128 devices in a mesh: seq: 8 (over z, core), tensor: 16 (over x, y).
Axes of the slice: x: 4, y: 4, z: 4, core: 2. Of those that a mesh axis runs over, the one named last changes fastest.
Arguments:
- span_tokens: bfloat16 [1024, 16, 1024], P(('seq', 'tensor')), may hold values from -6 to 6
- enc_dest: int32 [1024], replicated, may hold values from 0 to 1023, as said below
- passages: int32 [8], replicated, may hold values from 1 to 8, as said below
- req_slot: int32 [8], replicated, may hold values from 0 to 7, as said below
- block_mask: int32 [8, 8, 8], replicated, may hold values 0 or 1
- enc_qkv: bfloat16 [1024, 3072], P('tensor'), may hold values from -0.1875 to 0.1875
- enc_out: bfloat16 [1024, 1024], P('tensor'), may hold values from -0.1875 to 0.1875
- enc_up: bfloat16 [1024, 2048], P('tensor'), may hold values from -0.1875 to 0.1875
- enc_down: bfloat16 [2048, 1024], P('tensor'), may hold values from -0.125 to 0.125
- proj_in: bfloat16 [1024, 1024], replicated, may hold values from -0.1875 to 0.1875
- proj_out: bfloat16 [1024, 8192], P('tensor'), may hold values from -0.1875 to 0.1875
- norm_gain: float32 [8192], replicated, may hold values from 0.1 to 1.9
- q_weight: bfloat16 [8192, 8192], P(None, 'tensor'), may hold values from -0.0625 to 0.0625
- key_value_weight: bfloat16 [2, 8192, 1024], P(None, None, 'tensor'), may hold values from -0.0625 to 0.0625
- out_weight: bfloat16 [8192, 8192], P('tensor'), may hold values from -0.0625 to 0.0625
Outputs:
- mixed: bfloat16 [1024, 8192], P(('seq', 'tensor'))
The draws below stay inside these ranges and needn't reach their ends.
Inputs may be any that keep to these rules, and one draw needn't show every extreme that they name: `enc_dest`: every number once; the 8 slots of each device (in order of seq+tensor) hold exactly 1 spans of requests whose decoder slot lies with each index of seq. `req_slot`: every number once; decoder slot s is the request of seq index s. `passages`: some request has 8.
All inputs are finite; a program needn't handle non-finite values.
Results may differ from the reference program's by a relative error of at most 0.03.
Values may be sent and summed in bfloat16 or wider, within the bound.
No kernel may reach another device: no remote copies, remote signals or barrier semaphores. Data moves between devices by JAX's collectives and lax.ppermute only.
A program may use at most 128 MiB of HBM per device.

```python
import math
import jax
import jax.numpy as jnp
from jax import lax

MODEL_WIDTH = 8192
QUERY_HEAD_COUNT = 64
KEY_VALUE_HEADS = 8
HEAD_WIDTH = 128
ED = 1024
EH = 16
EFF = 2048
PH = 1024
CT = 16
CPP = 16
NP = 8
REQ_SHARD = 1
SPAN_LIMIT = 128
REQUEST_COUNT = 8
ROWS = 1024
ROWS_DEV = 8


def request_order(key):
    return jax.random.permutation(jax.random.fold_in(key, 101), REQUEST_COUNT).astype(jnp.int32)


def draw_req_slot(key, part):
    return request_order(key)


def draw_enc_dest(key, part):
    req_order = request_order(key)
    key = jax.random.fold_in(key, 7)
    first_key, second_key = jax.random.split(key)
    partition_rows = REQ_SHARD * SPAN_LIMIT
    group_count = ROWS // partition_rows
    device_count = ROWS // ROWS_DEV
    per_group = ROWS_DEV // group_count
    group_keys = jax.random.split(first_key, group_count)
    dealt = jax.vmap(lambda one_key: jax.random.permutation(one_key, partition_rows))(group_keys).astype(jnp.int32)
    dealt = dealt + (jnp.arange(group_count, dtype=jnp.int32) * partition_rows)[:, None]
    dealt = dealt.reshape(group_count, device_count, per_group).transpose(1, 0, 2).reshape(device_count, ROWS_DEV)
    device_keys = jax.random.split(second_key, device_count)
    shuffle = jax.vmap(lambda one_key: jax.random.permutation(one_key, ROWS_DEV))(device_keys).astype(jnp.int32)
    rows = jnp.take_along_axis(dealt, shuffle, axis=1).reshape(ROWS)
    slot_request = jnp.zeros((REQUEST_COUNT,), jnp.int32).at[req_order].set(jnp.arange(REQUEST_COUNT, dtype=jnp.int32))
    return (slot_request[rows // SPAN_LIMIT] * SPAN_LIMIT + rows % SPAN_LIMIT).astype(jnp.int32)


def draw_passages(key, part):
    key = jax.random.fold_in(key, 11)
    first_key, second_key = jax.random.split(key)
    counts = jax.random.randint(first_key, (REQUEST_COUNT,), 1, NP + 1)
    chosen = jax.random.randint(second_key, (), 0, REQUEST_COUNT)
    return counts.at[chosen].set(NP).astype(jnp.int32)


def set_ends(entries, rng, least, high):
    longest = entries.shape.index(max(entries.shape))
    spots = []
    for shift in (0, 1):
        where = [jax.random.randint(jax.random.fold_in(rng, axis), (), 0, length) for axis, length in enumerate(entries.shape)]
        where[longest] = (where[longest] + shift) % entries.shape[longest]
        spots.append(tuple(where))
    return entries.at[spots[0]].set(least).at[spots[1]].set(high)


def shard_levels(own_key, shape, cuts, least, high):
    factor_of = 1.0
    for dim, blocks in cuts:
        heights = jax.random.uniform(jax.random.fold_in(jax.random.fold_in(own_key, 6), dim), (blocks,), jnp.float32, least / len(cuts), high / len(cuts))
        factor_of = factor_of * jnp.repeat(jnp.exp(heights), shape[dim] // blocks).reshape((-1,) + (1,) * (len(shape) - 1 - dim))
    return factor_of


def gaussian(key, shape, scale, bound, cuts=(), kind=jnp.bfloat16):
    drawn = jax.random.normal(key, shape, jnp.float32) * scale
    if len(cuts) > 0:
        drawn = shard_levels(key, shape, cuts, -0.22, 0.18) * drawn
    return jnp.clip(drawn, min=-bound, max=bound).astype(kind)


def setup_inputs(seed: int = 0) -> dict:
    key_of = jax.random.split(jax.random.key(seed), 16)
    span_tokens = gaussian(key_of[0], (ROWS, CT, ED), 1.0, 6.0, ((0, 128),))
    enc_dest = draw_enc_dest(jax.random.fold_in(key_of[15], 71), 0)
    passages = draw_passages(jax.random.fold_in(key_of[15], 71), 0)
    req_slot = draw_req_slot(jax.random.fold_in(key_of[15], 71), 0)
    block_mask = set_ends((jax.random.randint(key_of[4], (REQUEST_COUNT, NP, NP), 0, 2) < 1).astype(jnp.int32), jax.random.fold_in(key_of[4], 1), 0, 1)
    enc_qkv = gaussian(key_of[5], (ED, 3 * ED), ED ** -0.5, 0.1875, ((0, 16),))
    enc_out = gaussian(key_of[6], (ED, ED), ED ** -0.5, 0.1875, ((0, 16),))
    enc_up = gaussian(key_of[7], (ED, EFF), ED ** -0.5, 0.1875, ((0, 16),))
    enc_down = gaussian(key_of[8], (EFF, ED), EFF ** -0.5, 0.125, ((0, 16),))
    proj_in = gaussian(key_of[9], (ED, PH), ED ** -0.5, 0.1875)
    proj_out = gaussian(key_of[10], (PH, MODEL_WIDTH), PH ** -0.5, 0.1875, ((0, 16),))
    norm_gain = jnp.clip(1.0 + 0.18 * jax.random.normal(key_of[11], (MODEL_WIDTH,), jnp.float32), 0.1, 1.9)
    q_weight = gaussian(key_of[12], (MODEL_WIDTH, QUERY_HEAD_COUNT * HEAD_WIDTH), MODEL_WIDTH ** -0.5, 0.0625, ((1, 16),))
    key_value_weight = gaussian(key_of[13], (2, MODEL_WIDTH, KEY_VALUE_HEADS * HEAD_WIDTH), MODEL_WIDTH ** -0.5, 0.0625, ((2, 16),))
    out_weight = gaussian(key_of[14], (QUERY_HEAD_COUNT * HEAD_WIDTH, MODEL_WIDTH), (QUERY_HEAD_COUNT * HEAD_WIDTH) ** -0.5, 0.0625, ((0, 16),))
    return {"span_tokens": span_tokens, "enc_dest": enc_dest, "passages": passages, "req_slot": req_slot, "block_mask": block_mask, "enc_qkv": enc_qkv, "enc_out": enc_out, "enc_up": enc_up, "enc_down": enc_down, "proj_in": proj_in, "proj_out": proj_out, "norm_gain": norm_gain, "q_weight": q_weight, "key_value_weight": key_value_weight, "out_weight": out_weight}


def layer_norm(values):
    mean_value = lax.optimization_barrier(jnp.mean(values, axis=-1, keepdims=True))
    centred = values - mean_value
    return centred * lax.rsqrt(lax.optimization_barrier(jnp.mean(centred * centred, axis=-1, keepdims=True)) + 1e-05)

def stored(values):
    return lax.optimization_barrier(values.astype(jnp.bfloat16)).astype(jnp.float32)

def encode_block(tokens, enc_qkv, enc_out, enc_up, enc_down):
    span_count = tokens.shape[0]
    flat_tokens = tokens.reshape(span_count * CT, ED)
    mixed_qkv = stored(jnp.dot(flat_tokens, enc_qkv, preferred_element_type=jnp.float32))
    split_qkv = mixed_qkv.reshape(span_count, CT, 3, EH, ED // EH)
    scores = jnp.einsum('nqhd,nkhd->nhqk', split_qkv[:, :, 0], split_qkv[:, :, 1]) / math.sqrt(ED // EH)
    weights = stored(jax.nn.softmax(scores, axis=-1))
    context = jnp.einsum('nhqk,nkhd->nqhd', weights, split_qkv[:, :, 2]).astype(jnp.bfloat16)
    attended = jnp.dot(context.reshape(span_count * CT, ED), enc_out, preferred_element_type=jnp.float32)
    first_out = layer_norm(flat_tokens.astype(jnp.float32) + attended).astype(jnp.bfloat16)
    inner_act = jax.nn.gelu(jnp.dot(first_out, enc_up, preferred_element_type=jnp.float32), approximate=False).astype(jnp.bfloat16)
    second = layer_norm(first_out.astype(jnp.float32) + jnp.dot(inner_act, enc_down, preferred_element_type=jnp.float32))
    return lax.optimization_barrier(jnp.mean(second.reshape(span_count, CT, ED), axis=1)).astype(jnp.bfloat16)

def rotate(values, col_start, positions):
    row_count, col_count = values.shape
    pair_index = (col_start + 2 * jnp.arange(col_count // 2)) % HEAD_WIDTH // 2
    frequency = jnp.exp(-(2.0 * pair_index.astype(jnp.float32) / HEAD_WIDTH) * math.log(500000.0))
    angles = positions.astype(jnp.float32)[:, None] * frequency[None, :]
    cosine = jnp.cos(angles)
    sine_part = jnp.sin(angles)
    paired = values.reshape(row_count, col_count // 2, 2)
    even_part = paired[:, :, 0]
    odd_part = paired[:, :, 1]
    turned = jnp.stack([even_part * cosine - odd_part * sine_part, even_part * sine_part + odd_part * cosine], axis=-1)
    return turned.reshape(row_count, col_count)

def visibility(masks, live_count):
    positions = jnp.arange(SPAN_LIMIT)
    passage = positions // CPP
    expanded = jnp.repeat(jnp.repeat(masks, CPP, axis=1), CPP, axis=2) > 0
    same_passage = passage[:, None] == passage[None, :]
    earlier = positions[None, :] <= positions[:, None]
    key_live = positions[None, None, :] < live_count[:, None, None]
    diagonal = positions[:, None] == positions[None, :]
    return diagonal[None] | earlier[None] & key_live & (same_passage[None] | expanded)

def reference(span_tokens, enc_dest, passages, req_slot, block_mask, enc_qkv, enc_out, enc_up, enc_down, proj_in, proj_out, norm_gain, q_weight, key_value_weight, out_weight):
    blocks = span_tokens.reshape(ROWS // SPAN_LIMIT, SPAN_LIMIT, CT, ED)
    pooled = lax.map(lambda block: encode_block(block, enc_qkv, enc_out, enc_up, enc_down), blocks).reshape(ROWS, ED)
    row_of_slot = (req_slot[enc_dest // SPAN_LIMIT] * SPAN_LIMIT + enc_dest % SPAN_LIMIT).astype(jnp.int32)
    arranged = jnp.zeros((ROWS, ED), jnp.bfloat16).at[row_of_slot].set(pooled)
    hidden = jax.nn.gelu(jnp.dot(arranged, proj_in, preferred_element_type=jnp.float32), approximate=False).astype(jnp.bfloat16)
    embedded = jnp.dot(hidden, proj_out, preferred_element_type=jnp.float32)
    scale_rows = lax.rsqrt(lax.optimization_barrier(jnp.mean(embedded * embedded, axis=-1, keepdims=True)) + 1e-05)
    normed = (embedded * scale_rows * norm_gain).astype(jnp.bfloat16)
    positions = jnp.arange(ROWS) % SPAN_LIMIT
    query_rows = stored(rotate(jnp.dot(normed, q_weight, preferred_element_type=jnp.float32), 0, positions))
    key_rows = stored(rotate(jnp.dot(normed, key_value_weight[0], preferred_element_type=jnp.float32), 0, positions))
    value_rows = stored(jnp.dot(normed, key_value_weight[1], preferred_element_type=jnp.float32))
    slot_request = jnp.zeros((REQUEST_COUNT,), jnp.int32).at[req_slot].set(jnp.arange(REQUEST_COUNT, dtype=jnp.int32))
    live_count = passages[slot_request] * CPP
    allowed = visibility(block_mask[slot_request], live_count)
    head_group = QUERY_HEAD_COUNT // KEY_VALUE_HEADS
    heads_query = query_rows.reshape(REQUEST_COUNT, SPAN_LIMIT, KEY_VALUE_HEADS, head_group, HEAD_WIDTH)
    heads_key = key_rows.reshape(REQUEST_COUNT, SPAN_LIMIT, KEY_VALUE_HEADS, HEAD_WIDTH)
    heads_value = value_rows.reshape(REQUEST_COUNT, SPAN_LIMIT, KEY_VALUE_HEADS, HEAD_WIDTH)
    scores = jnp.einsum('rqkgd,rpkd->rkgqp', heads_query, heads_key) / math.sqrt(HEAD_WIDTH)
    scores = jnp.where(allowed[:, None, None], scores, -1e+30)
    probs = stored(jax.nn.softmax(scores, axis=-1))
    context = jnp.einsum('rkgqp,rpkd->rqkgd', probs, heads_value).astype(jnp.bfloat16).reshape(ROWS, QUERY_HEAD_COUNT * HEAD_WIDTH)
    attended = jnp.dot(context, out_weight, preferred_element_type=jnp.float32)
    live_rows = (positions.reshape(REQUEST_COUNT, SPAN_LIMIT) < live_count[:, None]).reshape(ROWS)
    return jnp.where(live_rows[:, None], embedded + attended, 0.0).astype(jnp.bfloat16)
```

```python
import math

import jax
import jax.numpy as jnp
from jax import lax
from jax.sharding import PartitionSpec as P

QUERY_HEAD_COUNT = 64
KEY_VALUE_HEADS = 8
HEAD_WIDTH = 128
EH = 16
CPP = 16
SPAN_LIMIT = 128
SIDE = 4
AXES = ("seq", "tensor")


def device_id(plane, core, x, y):
    return ((plane * 2 + core) * SIDE + x) * SIDE + y


def every_device():
    return [
        (plane, core, x, y)
        for plane in range(SIDE)
        for core in range(2)
        for x in range(SIDE)
        for y in range(SIDE)
    ]


def first_axis_is_y(core, phase):
    return (core == 0) == (phase == 1)


def ring_pairs(phase, distance):
    pairs = []
    for plane, core, x, y in every_device():
        if first_axis_is_y(core, phase):
            target = device_id(plane, core, x, (y + distance) % SIDE)
        else:
            target = device_id(plane, core, (x + distance) % SIDE, y)
        pairs.append((device_id(plane, core, x, y), target))
    return pairs


def ring_groups(phase):
    groups = []
    for plane in range(SIDE):
        for core in range(2):
            for fixed in range(SIDE):
                groups.append(
                    [
                        device_id(plane, core, fixed, moving)
                        if first_axis_is_y(core, phase)
                        else device_id(plane, core, moving, fixed)
                        for moving in range(SIDE)
                    ]
                )
    return groups


def to_ring(value, phase, distance):
    return lax.ppermute(value, AXES, ring_pairs(phase, distance))


def to_core(value):
    return lax.ppermute(value, "seq", [(index, index ^ 1) for index in range(8)])


def short_gather(value):
    spread = jnp.broadcast_to(value[None], (SIDE,) + value.shape)
    return lax.all_to_all(spread, AXES, 0, 0, axis_index_groups=ring_groups(1))


def long_gather(block):
    left = to_ring(block, 2, 1)
    right = to_ring(block, 2, -1)
    opposite = jnp.concatenate([to_ring(left[:2], 2, 1), to_ring(right[2:], 2, -1)], axis=0)
    return jnp.stack([block, left, right, opposite])


def layer_norm(values):
    mean_value = jnp.mean(values, axis=-1, keepdims=True)
    centred = values - mean_value
    return centred * lax.rsqrt(jnp.mean(centred * centred, axis=-1, keepdims=True) + 1e-05)


def relative(blocks, position):
    order = [position, (position + 3) % SIDE, (position + 1) % SIDE, (position + 2) % SIDE]
    return jnp.concatenate(
        [lax.dynamic_slice_in_dim(blocks, index, 1, 1) for index in order], axis=1
    )


def column_orders(act, core, x, y):
    rows, width = act.shape
    share = width // (SIDE * SIDE)
    by_x = relative(act.reshape(rows, SIDE, SIDE * share), x).reshape(rows, width)
    turned = act.reshape(rows, SIDE, SIDE, share).transpose(0, 2, 1, 3)
    by_y = relative(turned.reshape(rows, SIDE, SIDE * share), y).reshape(rows, width)
    return jnp.where(core == 0, by_x, by_y), jnp.where(core == 0, by_y, by_x)


def half_dots(act, mine, other, place):
    core, x, y = place
    act_mine, act_other = column_orders(act, core, x, y)
    out_mine = jnp.dot(act_mine, mine, preferred_element_type=jnp.float32)
    out_other = jnp.dot(act_other, other, preferred_element_type=jnp.float32)
    low = jnp.where(core == 0, out_mine, out_other)
    high = jnp.where(core == 0, out_other, out_mine)
    return jnp.concatenate([low, high], axis=1)


def own_half(weight, core):
    width = weight.shape[1] // 2
    return lax.dynamic_slice_in_dim(weight, core * width, width, 1)


def encode_block(tokens, enc_qkv, enc_out, enc_up, enc_down, place):
    core = place[0]
    span_count, token_count, width = tokens.shape
    heads = EH
    flat_tokens = tokens.reshape(span_count * token_count, width)

    qkv_block = short_gather(own_half(enc_qkv, core))
    share = enc_qkv.shape[0]
    cols = width // 2
    up_half = own_half(enc_up, core)
    rest = jnp.concatenate(
        [
            own_half(enc_out, core),
            up_half[:, :cols],
            up_half[:, cols:],
            own_half(enc_down, core),
        ],
        axis=0,
    )
    rest_block = short_gather(rest)
    qkv_mine = long_gather(qkv_block).reshape(width, -1)
    qkv_other = to_core(qkv_mine)
    middle = long_gather(rest_block[:, : 3 * share])
    middle = middle.reshape(SIDE * SIDE, 3, share, cols).transpose(1, 0, 2, 3)
    middle = middle.reshape(3, width, cols)
    middle_other = to_core(middle)
    down_mine = long_gather(rest_block[:, 3 * share :]).reshape(-1, cols)
    down_other = to_core(down_mine)

    mixed_qkv = half_dots(flat_tokens, qkv_mine, qkv_other, place).astype(jnp.bfloat16)
    split_qkv = mixed_qkv.reshape(span_count, token_count, 3, heads, width // heads)
    scores = jnp.einsum(
        "nqhd,nkhd->nhqk",
        split_qkv[:, :, 0],
        split_qkv[:, :, 1],
        preferred_element_type=jnp.float32,
    ) / math.sqrt(width // heads)
    weights = jax.nn.softmax(scores, axis=-1).astype(jnp.bfloat16)
    context = jnp.einsum(
        "nhqk,nkhd->nqhd", weights, split_qkv[:, :, 2], preferred_element_type=jnp.float32
    ).astype(jnp.bfloat16)
    attended = half_dots(
        context.reshape(span_count * token_count, width), middle[0], middle_other[0], place
    )
    first_out = layer_norm(flat_tokens.astype(jnp.float32) + attended).astype(jnp.bfloat16)
    up_mine = jnp.concatenate([middle[1], middle[2]], axis=1)
    up_other = jnp.concatenate([middle_other[1], middle_other[2]], axis=1)
    inner_act = jax.nn.gelu(half_dots(first_out, up_mine, up_other, place), approximate=False)
    second = layer_norm(
        first_out.astype(jnp.float32)
        + half_dots(inner_act.astype(jnp.bfloat16), down_mine, down_other, place)
    )
    return jnp.mean(second.reshape(span_count, token_count, width), axis=1).astype(jnp.bfloat16)


def rotate(values, col_start, positions):
    row_count, col_count = values.shape
    pair_index = (col_start + 2 * jnp.arange(col_count // 2)) % HEAD_WIDTH // 2
    frequency = jnp.exp(-(2.0 * pair_index.astype(jnp.float32) / HEAD_WIDTH) * math.log(500000.0))
    angles = positions.astype(jnp.float32)[:, None] * frequency[None, :]
    cosine = jnp.cos(angles)
    sine_part = jnp.sin(angles)
    paired = values.reshape(row_count, col_count // 2, 2)
    even_part = paired[:, :, 0]
    odd_part = paired[:, :, 1]
    turned = jnp.stack(
        [even_part * cosine - odd_part * sine_part, even_part * sine_part + odd_part * cosine],
        axis=-1,
    )
    return turned.reshape(row_count, col_count)


def visibility(masks, live_count):
    positions = jnp.arange(SPAN_LIMIT)
    passage = positions // CPP
    expanded = jnp.repeat(jnp.repeat(masks, CPP, axis=0), CPP, axis=1) > 0
    same_passage = passage[:, None] == passage[None, :]
    earlier = positions[None, :] <= positions[:, None]
    key_live = positions[None, :] < live_count
    diagonal = positions[:, None] == positions[None, :]
    return diagonal | earlier & key_live & (same_passage | expanded)


def local(
    span_tokens,
    enc_dest,
    passages,
    req_slot,
    block_mask,
    enc_qkv,
    enc_out,
    enc_up,
    enc_down,
    proj_in,
    proj_out,
    norm_gain,
    q_weight,
    key_value_weight,
    out_weight,
):
    tensor_count = lax.axis_size("tensor")
    seq_count = lax.axis_size("seq")
    tensor_index = lax.axis_index("tensor")
    seq_index = lax.axis_index("seq")
    core = seq_index % 2
    device_count = tensor_count * seq_count
    rows = SPAN_LIMIT
    own_rows = rows // tensor_count
    width = span_tokens.shape[2]
    place = (core, tensor_index // SIDE, tensor_index % SIDE)

    pooled = encode_block(span_tokens, enc_qkv, enc_out, enc_up, enc_down, place)

    model_width = proj_out.shape[1]
    share_cols = model_width // tensor_count
    half_cols = share_cols // 2
    pieces = proj_out.reshape(proj_out.shape[0], tensor_count, 2, half_cols)
    pieces = lax.dynamic_slice_in_dim(pieces, core, 1, 2)[:, :, 0].transpose(1, 0, 2)
    out_mine = lax.all_to_all(pieces, "tensor", 0, 0).reshape(-1, half_cols)
    out_other = to_core(out_mine)
    proj_low = jnp.where(core == 0, out_mine, out_other)
    proj_high = jnp.where(core == 0, out_other, out_mine)

    requests = jnp.arange(req_slot.shape[0])
    dest_slot = jnp.sum(
        jnp.where(enc_dest[:, None] // SPAN_LIMIT == requests[None, :], req_slot[None, :], 0), axis=1
    ).reshape(device_count, own_rows)
    dest_place = (enc_dest % SPAN_LIMIT).reshape(device_count, own_rows)
    own_slots = lax.dynamic_slice_in_dim(
        dest_slot, seq_index * tensor_count + tensor_index, 1, 0
    )
    pick = (jnp.arange(seq_count)[:, None] == own_slots).astype(jnp.bfloat16)
    by_slot = jnp.dot(pick, pooled, preferred_element_type=jnp.float32).astype(jnp.bfloat16)
    outgoing = jnp.broadcast_to(
        by_slot.reshape(seq_count, 1, width // 128, 128),
        (seq_count, tensor_count, width // 128, 128),
    ).reshape(device_count, width // 128, 128)
    arrived = lax.all_to_all(outgoing, AXES, 0, 0).reshape(device_count, width)
    place_of = jnp.sum(jnp.where(dest_slot == seq_index, dest_place, 0), axis=1)
    order = (jnp.arange(rows)[:, None] == place_of[None, :]).astype(jnp.bfloat16)
    arranged = jnp.dot(order, arrived, preferred_element_type=jnp.float32).astype(jnp.bfloat16)

    hidden = jax.nn.gelu(
        jnp.dot(arranged, proj_in, preferred_element_type=jnp.float32), approximate=False
    ).astype(jnp.bfloat16)
    own_cols = jnp.concatenate(
        [
            jnp.dot(hidden, proj_low, preferred_element_type=jnp.float32).astype(jnp.bfloat16),
            jnp.dot(hidden, proj_high, preferred_element_type=jnp.float32).astype(jnp.bfloat16),
        ],
        axis=1,
    )
    embedded = lax.all_to_all(
        jnp.broadcast_to(own_cols[None], (tensor_count,) + own_cols.shape), "tensor", 0, 0
    )
    own_embedded = lax.dynamic_slice_in_dim(embedded, tensor_index * own_rows, own_rows, 1)
    own_embedded = own_embedded.transpose(1, 0, 2).reshape(own_rows, model_width)
    wide = embedded.astype(jnp.float32)
    scale_rows = lax.rsqrt(jnp.sum(wide * wide, axis=(0, 2)) / model_width + 1e-05)
    normed = wide * scale_rows[None, :, None] * norm_gain.reshape(tensor_count, 1, share_cols)
    normed = normed.astype(jnp.bfloat16).transpose(1, 0, 2).reshape(rows, model_width)

    positions = jnp.arange(rows)
    query_cols = q_weight.shape[1]
    kv_cols = key_value_weight.shape[2]
    keys_local = rotate(
        jnp.dot(normed, key_value_weight[0], preferred_element_type=jnp.float32),
        tensor_index * kv_cols,
        positions,
    ).astype(jnp.bfloat16)
    values_local = jnp.dot(normed, key_value_weight[1], preferred_element_type=jnp.float32).astype(
        jnp.bfloat16
    )
    collected = jnp.stack([keys_local, values_local])
    partner = lax.ppermute(
        collected, "tensor", [(index, index ^ 1) for index in range(tensor_count)]
    )
    collected = jnp.where(
        tensor_index % 2 == 1,
        jnp.concatenate([partner, collected], axis=2),
        jnp.concatenate([collected, partner], axis=2),
    )
    query_rows = rotate(
        jnp.dot(normed, q_weight, preferred_element_type=jnp.float32),
        tensor_index * query_cols,
        positions,
    ).astype(jnp.bfloat16)
    local_heads = query_cols // HEAD_WIDTH
    heads_query = query_rows.reshape(rows, local_heads, HEAD_WIDTH)
    chosen = jnp.sum(jnp.where(req_slot == seq_index, requests, 0))
    live_count = passages[chosen] * CPP
    allowed = visibility(block_mask[chosen], live_count)
    scores = jnp.einsum(
        "qhd,pd->hqp", heads_query, collected[0], preferred_element_type=jnp.float32
    ) / math.sqrt(HEAD_WIDTH)
    scores = jnp.where(allowed[None], scores, -1e30)
    probs = jax.nn.softmax(scores, axis=-1).astype(jnp.bfloat16)
    context = jnp.einsum(
        "hqp,pd->qhd", probs, collected[1], preferred_element_type=jnp.float32
    ).astype(jnp.bfloat16)
    context = context.reshape(rows, query_cols)
    partial = jnp.dot(context, out_weight, preferred_element_type=jnp.float32)
    partial = partial.astype(jnp.bfloat16).reshape(tensor_count, own_rows, model_width)
    terms = lax.all_to_all(partial, "tensor", 0, 0)
    own_attended = jnp.sum(terms.astype(jnp.float32), axis=0)
    live_own = tensor_index * own_rows + jnp.arange(own_rows) < live_count
    total = own_embedded.astype(jnp.float32) + own_attended
    return jnp.where(live_own[:, None], total, 0.0).astype(jnp.bfloat16)


def solution(mesh):
    return jax.shard_map(
        local,
        mesh=mesh,
        in_specs=(
            P(("seq", "tensor"), None, None),
            P(),
            P(),
            P(),
            P(),
            P("tensor", None),
            P("tensor", None),
            P("tensor", None),
            P("tensor", None),
            P(),
            P("tensor", None),
            P(),
            P(None, "tensor"),
            P(None, None, "tensor"),
            P("tensor", None),
        ),
        out_specs=P(("seq", "tensor"), None),
        check_vma=False,
    )
```

```python
import math

import jax
import jax.numpy as jnp
from jax import lax
from jax.experimental import pallas as pl
from jax.experimental.pallas import tpu as pltpu
from jax.sharding import PartitionSpec as P

QUERY_HEAD_COUNT = 64
KEY_VALUE_HEADS = 8
HEAD_WIDTH = 128
EH = 16
CPP = 16
SPAN_LIMIT = 128
SIDE = 4
AXES = ("seq", "tensor")


def device_id(plane, core, x, y):
    return ((plane * 2 + core) * SIDE + x) * SIDE + y


def every_device():
    return [
        (plane, core, x, y)
        for plane in range(SIDE)
        for core in range(2)
        for x in range(SIDE)
        for y in range(SIDE)
    ]


def first_axis_is_y(core, phase):
    return (core == 0) == (phase == 1)


def ring_pairs(phase, distance):
    pairs = []
    for plane, core, x, y in every_device():
        if first_axis_is_y(core, phase):
            target = device_id(plane, core, x, (y + distance) % SIDE)
        else:
            target = device_id(plane, core, (x + distance) % SIDE, y)
        pairs.append((device_id(plane, core, x, y), target))
    return pairs


def ring_groups(phase):
    groups = []
    for plane in range(SIDE):
        for core in range(2):
            for fixed in range(SIDE):
                groups.append(
                    [
                        device_id(plane, core, fixed, moving)
                        if first_axis_is_y(core, phase)
                        else device_id(plane, core, moving, fixed)
                        for moving in range(SIDE)
                    ]
                )
    return groups


def to_ring(value, phase, distance):
    return lax.ppermute(value, AXES, ring_pairs(phase, distance))


def to_core(value):
    return lax.ppermute(value, "seq", [(index, index ^ 1) for index in range(8)])


def short_gather(spread):
    return lax.all_to_all(spread, AXES, 0, 0, axis_index_groups=ring_groups(1))


VMEM = pl.BlockSpec(memory_space=pltpu.VMEM)
SMEM = pl.BlockSpec(memory_space=pltpu.SMEM)
MIB = 2**20


def shape_of(shape, dtype=jnp.bfloat16):
    return jax.ShapeDtypeStruct(shape, dtype)


def whole_call(body, name, info, arrays, outs, scratch=(), limit=24, flops=0):
    moved = sum(array.size * array.dtype.itemsize for array in arrays)
    return pl.pallas_call(
        body,
        name=name,
        out_shape=outs,
        in_specs=[SMEM] + [VMEM] * len(arrays),
        out_specs=jax.tree.map(lambda _: VMEM, outs),
        scratch_shapes=list(scratch),
        compiler_params=pltpu.CompilerParams(vmem_limit_bytes=limit * MIB),
        cost_estimate=pl.CostEstimate(flops=flops, bytes_accessed=moved, transcendentals=0),
    )(info, *arrays)


def dot32(left, right):
    return jnp.dot(left, right, preferred_element_type=jnp.float32)


def gelu_exact(values):
    return 0.5 * values * (1.0 + lax.erf(values * (0.5**0.5)))


def spread_qkv(info, weight, out):
    cols = weight.shape[1] // 6
    for part in range(3):
        start = pl.multiple_of((2 * part + info[16]) * cols, cols)
        piece = weight[:, pl.ds(start, cols)]
        for copy in range(SIDE):
            out[copy, :, part * cols : (part + 1) * cols] = piece


def spread_rest(info, out_weight, up_weight, down_weight, out):
    core = info[16]
    rows, width = out_weight.shape
    cols = width // 2
    units = down_weight.shape[0] // 2
    pieces = [out_weight[:, pl.ds(pl.multiple_of(core * cols, cols), cols)]]
    for pair in range(up_weight.shape[1] // (4 * units)):
        halves = []
        for step in range(2):
            low = (2 * pair + step) * 2 * units
            halves.append(
                jnp.where(
                    core == 0,
                    up_weight[:, low : low + units].astype(jnp.float32),
                    up_weight[:, low + units : low + 2 * units].astype(jnp.float32),
                )
            )
        pieces.append(jnp.concatenate(halves, axis=1).astype(jnp.bfloat16))
    pieces.append(down_weight[pl.ds(pl.multiple_of(core * units, units), units), :])
    for copy in range(SIDE):
        at = 0
        for piece in pieces:
            out[copy, :, at : at + piece.shape[1]] = piece
            at += piece.shape[1]


def spread_proj(info, weight, out):
    cols = out.shape[2]
    for index in range(out.shape[0]):
        start = pl.multiple_of((2 * index + info[16]) * cols, cols)
        out[index] = weight[:, pl.ds(start, cols)]


def both_rows(info, mine, other, rows_out, pieces_out):
    half, width = mine.shape
    core = info[16]
    rows_out[pl.ds(pl.multiple_of(core * half, half), half), :] = mine[...]
    rows_out[pl.ds(pl.multiple_of((1 - core) * half, half), half), :] = other[...]
    piece = pieces_out.shape[2]
    for index in range(width // piece):
        pieces_out[index] = rows_out[:, index * piece : (index + 1) * piece]


def ring_dot(info, pieces, blocks, low, high):
    total = None
    for at, block in enumerate(blocks):
        act = jnp.concatenate([pieces[info[4 * at + step]] for step in range(SIDE)], axis=1)
        weight = block[:, :, low:high].reshape(act.shape[1], high - low)
        part = dot32(act, weight)
        total = part if total is None else total + part
    return total


def span_attention(info, pieces, w0, w1, w2, w3, context, mixed):
    cols = w0.shape[2]
    third = cols // 3
    mixed[...] = ring_dot(info, pieces, (w0, w1, w2, w3), 0, cols).astype(jnp.bfloat16)
    size = context.shape[2]
    half = mixed.shape[0] // 2
    span = 16
    row = lax.broadcasted_iota(jnp.int32, (half, half), 0) // span
    col = lax.broadcasted_iota(jnp.int32, (half, half), 1) // span
    same = row == col
    for head in range(third // size):
        for part in range(2):
            rows = slice(part * half, (part + 1) * half)
            query = mixed[rows, head * size : (head + 1) * size]
            key = mixed[rows, third + head * size : third + (head + 1) * size]
            value = mixed[rows, 2 * third + head * size : 2 * third + (head + 1) * size]
            scores = lax.dot_general(
                query, key, (((1,), (1,)), ((), ())), preferred_element_type=jnp.float32
            ) / math.sqrt(size)
            scores = jnp.where(same, scores, -1e30)
            top = jnp.max(scores, axis=1, keepdims=True)
            powers = jnp.exp(scores - top)
            probs = powers / jnp.sum(powers, axis=1, keepdims=True)
            context[head, rows, :] = dot32(probs.astype(jnp.bfloat16), value).astype(jnp.bfloat16)


def context_out(info, mine, other, w0, w1, w2, w3, attended, pieces):
    heads = mine.shape[0]
    core = info[16]
    pieces[pl.ds(core * heads, heads)] = mine[...]
    pieces[pl.ds((1 - core) * heads, heads)] = other[...]
    cols = attended.shape[1]
    attended[...] = ring_dot(info, pieces, (w0, w1, w2, w3), 0, cols).astype(jnp.bfloat16)


def norm_up(info, rows, mine, other, w0, w1, w2, w3, first_out, inner, pieces):
    core = info[16]
    cols = mine.shape[1]
    width = rows.shape[1]
    near = mine[...].astype(jnp.float32)
    far = other[...].astype(jnp.float32)
    low = rows[:, :cols].astype(jnp.float32) + jnp.where(core == 0, near, far)
    high = rows[:, cols:].astype(jnp.float32) + jnp.where(core == 0, far, near)
    mean = (jnp.sum(low, 1, keepdims=True) + jnp.sum(high, 1, keepdims=True)) / width
    low, high = low - mean, high - mean
    var = (jnp.sum(low * low, 1, keepdims=True) + jnp.sum(high * high, 1, keepdims=True)) / width
    scale = lax.rsqrt(var + 1e-05)
    first_out[:, :cols] = (low * scale).astype(jnp.bfloat16)
    first_out[:, cols:] = (high * scale).astype(jnp.bfloat16)
    size = pieces.shape[2]
    for index in range(pieces.shape[0]):
        pieces[index] = first_out[:, index * size : (index + 1) * size]
    total = ring_dot(info, pieces, (w0, w1, w2, w3), cols, w0.shape[2])
    act = gelu_exact(total).astype(jnp.bfloat16)
    unit = inner.shape[2]
    for index in range(inner.shape[0]):
        inner[index] = act[:, index * unit : (index + 1) * unit]


def down(info, inner, w0, w1, w2, w3, kept, sent, total):
    core = info[16]
    total[...] = ring_dot(info, inner, (w0, w1, w2, w3), 0, w0.shape[2])
    half = kept.shape[0]
    kept[...] = total[pl.ds(pl.multiple_of(core * half, half), half), :]
    sent[...] = total[pl.ds(pl.multiple_of((1 - core) * half, half), half), :].astype(jnp.bfloat16)


def norm_pool(info, kept, arrived, first_out, pick, out, lanes):
    half, width = kept.shape
    rows = pl.ds(pl.multiple_of(info[16] * half, half), half)
    values = first_out[rows, :].astype(jnp.float32) + (
        kept[...] + arrived[...].astype(jnp.float32)
    )
    mean = jnp.mean(values, axis=1, keepdims=True)
    values = values - mean
    values = values * lax.rsqrt(jnp.mean(values * values, axis=1, keepdims=True) + 1e-05)
    spans = pick.shape[1]
    pooled = jnp.mean(values.reshape(spans, half // spans, width), axis=1).astype(jnp.bfloat16)
    by_slot = dot32(pick[...], pooled)
    for index in range(width // 128):
        lanes[:, index, :] = by_slot[:, index * 128 : (index + 1) * 128]
    out[...] = jnp.broadcast_to(lanes[...].astype(jnp.bfloat16)[:, None], out.shape)


def embed(info, arrived, order, proj_in, mine, other, out, lanes):
    core = info[16]
    lanes[...] = arrived[...].astype(jnp.float32)
    columns = [
        dot32(order[...], lanes[:, index, :].astype(jnp.bfloat16)).astype(jnp.bfloat16)
        for index in range(lanes.shape[1])
    ]
    arranged = jnp.concatenate(columns, axis=1)
    hidden = gelu_exact(dot32(arranged, proj_in[...])).astype(jnp.bfloat16)
    units = hidden.shape[1]
    cols = mine.shape[2]
    near = dot32(hidden, mine[...].reshape(units, cols))
    far = dot32(hidden, other[...].reshape(units, cols))
    low = jnp.where(core == 0, near, far).astype(jnp.bfloat16)
    high = jnp.where(core == 0, far, near).astype(jnp.bfloat16)
    for index in range(out.shape[0]):
        out[index, :, :cols] = low
        out[index, :, cols:] = high


def keys_values(emb, gain, weight, cosine, sine, swap, gained, scale, out, square, total_k, total_v):
    step = pl.program_id(0)

    @pl.when(step == 0)
    def _():
        square[...] = jnp.zeros_like(square)
        total_k[...] = jnp.zeros_like(total_k)
        total_v[...] = jnp.zeros_like(total_v)

    depth = emb.shape[2]
    for index in range(emb.shape[0]):
        wide = emb[index].astype(jnp.float32)
        square[...] += jnp.sum(wide * wide, axis=1, keepdims=True)
        act = (wide * gain[index]).astype(jnp.bfloat16)
        gained[index] = act
        total_k[...] += dot32(act, weight[0, index * depth : (index + 1) * depth, :])
        total_v[...] += dot32(act, weight[1, index * depth : (index + 1) * depth, :])

    @pl.when(step == pl.num_programs(0) - 1)
    def _():
        width = depth * emb.shape[0] * pl.num_programs(0)
        factor = lax.rsqrt(square[...] / width + 1e-05)
        scale[...] = factor
        key = total_k[...] * factor
        turned = jnp.dot(
            key, swap[...], preferred_element_type=jnp.float32, precision=lax.Precision.HIGHEST
        )
        out[0] = (key * cosine[...] + turned * sine[...]).astype(jnp.bfloat16)
        out[1] = (total_v[...] * factor).astype(jnp.bfloat16)


def queries(gained, weight, scale, cosine, sine, swap, out, total):
    step = pl.program_id(0)

    @pl.when(step == 0)
    def _():
        total[...] = jnp.zeros_like(total)

    act = jnp.concatenate([gained[index] for index in range(gained.shape[0])], axis=1)
    total[...] += dot32(act, weight[...])

    @pl.when(step == pl.num_programs(0) - 1)
    def _():
        for head in range(out.shape[1] // HEAD_WIDTH):
            lanes = slice(head * HEAD_WIDTH, (head + 1) * HEAD_WIDTH)
            query = total[:, lanes] * scale[...]
            turned = jnp.dot(
                query, swap[...], preferred_element_type=jnp.float32, precision=lax.Precision.HIGHEST
            )
            out[:, lanes] = (query * cosine[...] + turned * sine[...]).astype(jnp.bfloat16)


def attend_out(info, query, mine, partner, allowed, weight, out, context):
    @pl.when(pl.program_id(0) == 0)
    def _():
        odd = info[17] == 1
        own = mine[...].astype(jnp.float32)
        far = partner[...].astype(jnp.float32)
        low = jnp.where(odd, far, own)
        high = jnp.where(odd, own, far)
        pair = jnp.concatenate([low, high], axis=2).astype(jnp.bfloat16)
        key, value = pair[0], pair[1]
        for head in range(query.shape[1] // HEAD_WIDTH):
            lanes = slice(head * HEAD_WIDTH, (head + 1) * HEAD_WIDTH)
            scores = lax.dot_general(
                query[:, lanes], key, (((1,), (1,)), ((), ())), preferred_element_type=jnp.float32
            ) / math.sqrt(HEAD_WIDTH)
            scores = jnp.where(allowed[...] > 0, scores, -1e30)
            top = jnp.max(scores, axis=1, keepdims=True)
            powers = jnp.exp(scores - top)
            probs = powers / jnp.sum(powers, axis=1, keepdims=True)
            context[:, lanes] = dot32(probs.astype(jnp.bfloat16), value).astype(jnp.bfloat16)

    out[...] = dot32(context[...], weight[...]).astype(jnp.bfloat16)


def finish(info, terms, own, out):
    cols = own.shape[2]
    rows = own.shape[1]
    live = info[18] + lax.broadcasted_iota(jnp.int32, (rows, cols), 0) < info[19]
    for index in range(own.shape[0]):
        lanes = slice(index * cols, (index + 1) * cols)
        total = jnp.sum(terms[:, :, lanes].astype(jnp.float32), axis=0)
        total = total + own[index].astype(jnp.float32)
        out[:, lanes] = jnp.where(live, total, 0.0).astype(jnp.bfloat16)


def visibility(masks, live_count):
    positions = jnp.arange(SPAN_LIMIT)
    passage = positions // CPP
    expanded = jnp.repeat(jnp.repeat(masks, CPP, axis=0), CPP, axis=1) > 0
    same_passage = passage[:, None] == passage[None, :]
    earlier = positions[None, :] <= positions[:, None]
    key_live = positions[None, :] < live_count
    diagonal = positions[:, None] == positions[None, :]
    return diagonal | earlier & key_live & (same_passage | expanded)


def local(
    span_tokens,
    enc_dest,
    passages,
    req_slot,
    block_mask,
    enc_qkv,
    enc_out,
    enc_up,
    enc_down,
    proj_in,
    proj_out,
    norm_gain,
    q_weight,
    key_value_weight,
    out_weight,
):
    tensor_count = lax.axis_size("tensor")
    seq_count = lax.axis_size("seq")
    tensor_index = lax.axis_index("tensor")
    seq_index = lax.axis_index("seq")
    core = seq_index % 2
    device_count = tensor_count * seq_count
    rows = SPAN_LIMIT
    own_rows = rows // tensor_count
    spans, span_size, width = span_tokens.shape
    model_width = proj_out.shape[1]
    share = enc_qkv.shape[0]
    x_index, y_index = tensor_index // SIDE, tensor_index % SIDE

    requests = jnp.arange(req_slot.shape[0])
    dest_slot = jnp.sum(
        jnp.where(enc_dest[:, None] // SPAN_LIMIT == requests[None, :], req_slot[None, :], 0), axis=1
    ).reshape(device_count, own_rows)
    dest_place = (enc_dest % SPAN_LIMIT).reshape(device_count, own_rows)
    own_slots = lax.dynamic_slice_in_dim(
        dest_slot, seq_index * tensor_count + tensor_index, 1, 0
    )
    pick = (jnp.arange(seq_count)[:, None] == own_slots).astype(jnp.bfloat16)
    place_of = jnp.sum(jnp.where(dest_slot == seq_index, dest_place, 0), axis=1)
    order = (jnp.arange(rows)[:, None] == place_of[None, :]).astype(jnp.bfloat16)
    chosen = jnp.sum(jnp.where(req_slot == seq_index, requests, 0))
    live_count = jnp.sum(jnp.where(requests == chosen, passages, 0)) * CPP
    masks = jnp.sum(
        jnp.where(requests[:, None, None] == chosen, block_mask, 0), axis=0
    )
    allowed = visibility(masks, live_count).astype(jnp.float32)

    steps = jnp.array([0, SIDE - 1, 1, 2])[:, None]
    moving = jnp.arange(SIDE)[None, :]
    by_x = SIDE * ((x_index + steps) % SIDE) + moving
    by_y = SIDE * moving + (y_index + steps) % SIDE
    shards = jnp.where(core == 0, by_x, by_y).reshape(-1)
    scalars = jnp.stack([core, tensor_index % 2, tensor_index * own_rows, live_count])
    info = jnp.concatenate([shards, scalars]).astype(jnp.int32)

    positions = jnp.arange(rows).astype(jnp.float32)
    lane = jnp.arange(HEAD_WIDTH)
    frequency = jnp.exp(
        -(2.0 * (lane // 2).astype(jnp.float32) / HEAD_WIDTH) * math.log(500000.0)
    )
    angles = positions[:, None] * frequency[None, :]
    cosine, sine = jnp.cos(angles), jnp.sin(angles)
    swap = jnp.where(
        (lane[:, None] ^ 1) == lane[None, :], jnp.where(lane[None, :] % 2 == 0, -1.0, 1.0), 0.0
    ).astype(jnp.float32)

    own_tokens = span_tokens.reshape(spans * span_size, width)
    qkv_spread = whole_call(
        spread_qkv, "spread_qkv", info, [enc_qkv], shape_of((SIDE, share, 3 * width // 2))
    )
    qkv_block = short_gather(qkv_spread)
    units = enc_down.shape[0] // 2
    middle_cols = width // 2 + units * tensor_count
    rest_spread = whole_call(
        spread_rest,
        "spread_rest",
        info,
        [enc_out, enc_up, enc_down],
        shape_of((SIDE, share, middle_cols + width)),
    )
    rest_block = short_gather(rest_spread)
    other_tokens = to_core(own_tokens)
    token_rows, token_pieces = whole_call(
        both_rows,
        "both_rows",
        info,
        [own_tokens, other_tokens],
        (
            shape_of((2 * spans * span_size, width)),
            shape_of((tensor_count, 2 * spans * span_size, share)),
        ),
    )
    all_rows = token_rows.shape[0]

    def ring(block, relay):
        left = to_ring(block, 2, 1)
        right = to_ring(block, 2, -1)
        opposite = to_ring(left, 2, 1) if relay == 1 else to_ring(right, 2, -1)
        return [block, left, right, opposite]

    qkv = ring(qkv_block, 1)
    middle = ring(rest_block[:, :, :middle_cols], -1)
    lower = ring(rest_block[:, :, middle_cols:], 1)

    context = whole_call(
        span_attention,
        "span_attention",
        info,
        [token_pieces, *qkv],
        shape_of((tensor_count // 2, all_rows, share)),
        [pltpu.VMEM((all_rows, 3 * width // 2), jnp.bfloat16)],
        flops=2 * all_rows * width * 3 * width // 2,
    )
    attended = whole_call(
        context_out,
        "context_out",
        info,
        [context, to_core(context), *middle],
        shape_of((all_rows, width // 2)),
        [pltpu.VMEM((tensor_count, all_rows, share), jnp.bfloat16)],
        flops=2 * all_rows * width * width // 2,
    )
    first_out, inner = whole_call(
        norm_up,
        "norm_up",
        info,
        [token_rows, attended, to_core(attended), *middle],
        (shape_of((all_rows, width)), shape_of((tensor_count, all_rows, units))),
        [pltpu.VMEM((tensor_count, all_rows, share), jnp.bfloat16)],
        flops=2 * all_rows * width * width,
    )
    kept, sent = whole_call(
        down,
        "down",
        info,
        [inner, *lower],
        (
            shape_of((all_rows // 2, width), jnp.float32),
            shape_of((all_rows // 2, width)),
        ),
        [pltpu.VMEM((all_rows, width), jnp.float32)],
        flops=2 * all_rows * width * width,
    )
    outgoing = whole_call(
        norm_pool,
        "norm_pool",
        info,
        [kept, to_core(sent), first_out, pick],
        shape_of((seq_count, tensor_count, width // 128, 128)),
        [pltpu.VMEM((seq_count, width // 128, 128), jnp.float32)],
    )
    arrived = lax.all_to_all(
        outgoing.reshape(device_count, width // 128, 128), AXES, 0, 0
    )

    share_cols = model_width // tensor_count
    proj_mine = lax.all_to_all(
        whole_call(
            spread_proj,
            "spread_proj",
            info,
            [proj_out],
            shape_of((tensor_count, proj_out.shape[0], share_cols // 2)),
        ),
        "tensor",
        0,
        0,
    )
    proj_other = to_core(proj_mine)
    spread = whole_call(
        embed,
        "embed",
        info,
        [arrived, order, proj_in, proj_mine, proj_other],
        shape_of((tensor_count, rows, share_cols)),
        [pltpu.VMEM((device_count, width // 128, 128), jnp.float32)],
        flops=2 * rows * width * (width + share_cols),
    )
    embedded = lax.all_to_all(spread, "tensor", 0, 0)
    own_embedded = lax.dynamic_slice_in_dim(embedded, tensor_index * own_rows, own_rows, 1)

    query_cols = q_weight.shape[1]
    kv_cols = key_value_weight.shape[2]
    key_start = tensor_index * kv_cols % HEAD_WIDTH
    key_cosine = lax.dynamic_slice_in_dim(cosine, key_start, kv_cols, 1)
    key_sine = lax.dynamic_slice_in_dim(sine, key_start, kv_cols, 1)
    shards_step = 2
    grid = tensor_count // shards_step
    depth = shards_step * share_cols
    shard_spec = pl.BlockSpec((shards_step, rows, share_cols), lambda i: (i, 0, 0))

    def fixed(*shape):
        return pl.BlockSpec(shape, lambda i: (0,) * len(shape))

    gained, scale, own_kv = pl.pallas_call(
        keys_values,
        name="keys_values",
        grid=(grid,),
        out_shape=(
            shape_of((tensor_count, rows, share_cols)),
            shape_of((rows, 1), jnp.float32),
            shape_of((2, rows, kv_cols)),
        ),
        in_specs=[
            shard_spec,
            pl.BlockSpec((shards_step, 1, share_cols), lambda i: (i, 0, 0)),
            pl.BlockSpec((2, depth, kv_cols), lambda i: (0, i, 0)),
            fixed(rows, kv_cols),
            fixed(rows, kv_cols),
            fixed(kv_cols, kv_cols),
        ],
        out_specs=(shard_spec, fixed(rows, 1), fixed(2, rows, kv_cols)),
        scratch_shapes=[
            pltpu.VMEM((rows, 1), jnp.float32),
            pltpu.VMEM((rows, kv_cols), jnp.float32),
            pltpu.VMEM((rows, kv_cols), jnp.float32),
        ],
        compiler_params=pltpu.CompilerParams(vmem_limit_bytes=16 * MIB),
    )(
        embedded,
        norm_gain.reshape(tensor_count, 1, share_cols),
        key_value_weight,
        key_cosine,
        key_sine,
        swap[:kv_cols, :kv_cols],
    )
    partner_kv = lax.ppermute(
        own_kv, "tensor", [(index, index ^ 1) for index in range(tensor_count)]
    )
    query = pl.pallas_call(
        queries,
        name="queries",
        grid=(grid,),
        out_shape=shape_of((rows, query_cols)),
        in_specs=[
            shard_spec,
            pl.BlockSpec((depth, query_cols), lambda i: (i, 0)),
            fixed(rows, 1),
            fixed(rows, HEAD_WIDTH),
            fixed(rows, HEAD_WIDTH),
            fixed(HEAD_WIDTH, HEAD_WIDTH),
        ],
        out_specs=fixed(rows, query_cols),
        scratch_shapes=[pltpu.VMEM((rows, query_cols), jnp.float32)],
        compiler_params=pltpu.CompilerParams(vmem_limit_bytes=16 * MIB),
        cost_estimate=pl.CostEstimate(
            flops=2 * rows * model_width * query_cols,
            bytes_accessed=2 * model_width * query_cols,
            transcendentals=0,
        ),
    )(gained, q_weight, scale, cosine, sine, swap)
    out_step = 1024
    partial = pl.pallas_call(
        attend_out,
        name="attend_out",
        grid=(model_width // out_step,),
        out_shape=shape_of((rows, model_width)),
        in_specs=[
            SMEM,
            fixed(rows, query_cols),
            fixed(2, rows, kv_cols),
            fixed(2, rows, kv_cols),
            fixed(rows, rows),
            pl.BlockSpec((query_cols, out_step), lambda i: (0, i)),
        ],
        out_specs=pl.BlockSpec((rows, out_step), lambda i: (0, i)),
        scratch_shapes=[pltpu.VMEM((rows, query_cols), jnp.bfloat16)],
        compiler_params=pltpu.CompilerParams(vmem_limit_bytes=16 * MIB),
    )(info, query, own_kv, partner_kv, allowed, out_weight)
    terms = lax.all_to_all(
        partial.reshape(tensor_count, own_rows, model_width), "tensor", 0, 0
    )
    return whole_call(
        finish, "finish", info, [terms, own_embedded], shape_of((own_rows, model_width))
    )


def solution(mesh):
    return jax.shard_map(
        local,
        mesh=mesh,
        in_specs=(
            P(("seq", "tensor"), None, None),
            P(),
            P(),
            P(),
            P(),
            P("tensor", None),
            P("tensor", None),
            P("tensor", None),
            P("tensor", None),
            P(),
            P("tensor", None),
            P(),
            P(None, "tensor"),
            P(None, None, "tensor"),
            P("tensor", None),
        ),
        out_specs=P(("seq", "tensor"), None),
        check_vma=False,
    )
```

```python
import math

import jax
import jax.numpy as jnp
from jax import lax
from jax.experimental import pallas as pl
from jax.experimental.pallas import tpu as pltpu
from jax.sharding import PartitionSpec as P

QUERY_HEAD_COUNT = 64
KEY_VALUE_HEADS = 8
HEAD_WIDTH = 128
EH = 16
CPP = 16
SPAN_LIMIT = 128
SIDE = 4
AXES = ("seq", "tensor")


def device_id(plane, core, x, y):
    return ((plane * 2 + core) * SIDE + x) * SIDE + y


def every_device():
    return [
        (plane, core, x, y)
        for plane in range(SIDE)
        for core in range(2)
        for x in range(SIDE)
        for y in range(SIDE)
    ]


def first_axis_is_y(core, phase):
    return (core == 0) == (phase == 1)


def ring_pairs(phase, distance):
    pairs = []
    for plane, core, x, y in every_device():
        if first_axis_is_y(core, phase):
            target = device_id(plane, core, x, (y + distance) % SIDE)
        else:
            target = device_id(plane, core, (x + distance) % SIDE, y)
        pairs.append((device_id(plane, core, x, y), target))
    return pairs


def ring_groups(phase):
    groups = []
    for plane in range(SIDE):
        for core in range(2):
            for fixed in range(SIDE):
                groups.append(
                    [
                        device_id(plane, core, fixed, moving)
                        if first_axis_is_y(core, phase)
                        else device_id(plane, core, moving, fixed)
                        for moving in range(SIDE)
                    ]
                )
    return groups


def to_ring(value, phase, distance):
    return lax.ppermute(value, AXES, ring_pairs(phase, distance))


def to_core(value):
    return lax.ppermute(value, "seq", [(index, index ^ 1) for index in range(8)])


def short_ring(block):
    return [block] + [to_ring(block, 1, distance) for distance in (1, -1, 2)]


VMEM = pl.BlockSpec(memory_space=pltpu.VMEM)
SMEM = pl.BlockSpec(memory_space=pltpu.SMEM)
MIB = 2**20


def shape_of(shape, dtype=jnp.bfloat16):
    return jax.ShapeDtypeStruct(shape, dtype)


def whole_call(body, name, info, arrays, outs, scratch=(), limit=12, flops=0, out_space=pltpu.VMEM, after=()):
    count = len(arrays)

    def run(*refs):
        body(*refs[: 1 + count], *refs[1 + count + len(after) :])

    moved = sum(array.size * array.dtype.itemsize for array in arrays)
    return pl.pallas_call(
        run,
        name=name,
        out_shape=outs,
        in_specs=[SMEM] + [VMEM] * count + [pl.BlockSpec(memory_space=pl.ANY)] * len(after),
        out_specs=jax.tree.map(lambda _: pl.BlockSpec(memory_space=out_space), outs),
        scratch_shapes=list(scratch),
        compiler_params=pltpu.CompilerParams(vmem_limit_bytes=limit * MIB),
        cost_estimate=pl.CostEstimate(flops=flops, bytes_accessed=moved, transcendentals=0),
    )(info, *arrays, *after)


def dot32(left, right):
    return jnp.dot(left, right, preferred_element_type=jnp.float32)


def gelu_exact(values):
    return 0.5 * values * (1.0 + lax.erf(values * (0.5**0.5)))


def take_qkv(info, weight, out):
    cols = weight.shape[1] // 6
    for part in range(3):
        start = pl.multiple_of((2 * part + info[16]) * cols, cols)
        out[:, part * cols : (part + 1) * cols] = weight[:, pl.ds(start, cols)]


def take_rest(info, out_weight, up_weight, down_weight, out):
    core = info[16]
    rows, width = out_weight.shape
    cols = width // 2
    units = down_weight.shape[0] // 2
    out[:, :cols] = out_weight[:, pl.ds(pl.multiple_of(core * cols, cols), cols)]
    at = cols
    for pair in range(up_weight.shape[1] // (4 * units)):
        halves = []
        for step in range(2):
            low = (2 * pair + step) * 2 * units
            halves.append(
                jnp.where(
                    core == 0,
                    up_weight[:, low : low + units].astype(jnp.float32),
                    up_weight[:, low + units : low + 2 * units].astype(jnp.float32),
                )
            )
        piece = jnp.concatenate(halves, axis=1).astype(jnp.bfloat16)
        out[:, at : at + 2 * units] = piece
        at += 2 * units
    out[:, at:] = down_weight[pl.ds(pl.multiple_of(core * units, units), units), :]


def join_qkv(info, own, left, right, opposite, out):
    for index, block in enumerate((own, left, right, opposite)):
        out[index] = block[...]


def join_rest(info, own, left, right, opposite, middle, lower):
    cols = middle.shape[2]
    for index, block in enumerate((own, left, right, opposite)):
        middle[index] = block[:, :cols]
        lower[index] = block[:, cols:]


def spread_proj(info, weight, out):
    cols = out.shape[2]
    for index in range(out.shape[0]):
        start = pl.multiple_of((2 * index + info[16]) * cols, cols)
        out[index] = weight[:, pl.ds(start, cols)]


def both_rows(info, mine, other, pieces_out):
    half, width = mine.shape
    core = info[16]
    piece = pieces_out.shape[2]
    near = pl.ds(pl.multiple_of(core * half, half), half)
    far = pl.ds(pl.multiple_of((1 - core) * half, half), half)
    for index in range(width // piece):
        pieces_out[index, near, :] = mine[:, index * piece : (index + 1) * piece]
        pieces_out[index, far, :] = other[:, index * piece : (index + 1) * piece]


def ring_dot(info, pieces, blocks, low, high):
    total = None
    for at, block in enumerate(blocks):
        act = jnp.concatenate([pieces[info[4 * at + step]] for step in range(SIDE)], axis=1)
        weight = block[:, :, low:high].reshape(act.shape[1], high - low)
        part = dot32(act, weight)
        total = part if total is None else total + part
    return total


def masked_softmax(scores, seen, size):
    scores = [jnp.where(seen, score / math.sqrt(size), -1e30) for score in scores]
    tops = [jnp.max(score, axis=1, keepdims=True) for score in scores]
    powers = [jnp.exp(score - top) for score, top in zip(scores, tops)]
    sums = [jnp.sum(power, axis=1, keepdims=True) for power in powers]
    return [(power / total).astype(jnp.bfloat16) for power, total in zip(powers, sums)]


def span_attention(info, pieces, w0, w1, w2, w3, context, mixed):
    cols = w0.shape[2]
    third = cols // 3
    mixed[...] = ring_dot(info, pieces, (w0, w1, w2, w3), 0, cols).astype(jnp.bfloat16)
    size = context.shape[2]
    half = mixed.shape[0] // 2
    span = 16
    row = lax.broadcasted_iota(jnp.int32, (half, half), 0) // span
    col = lax.broadcasted_iota(jnp.int32, (half, half), 1) // span
    same = row == col
    heads = third // size
    units = [
        (head, slice(part * half, (part + 1) * half)) for head in range(heads) for part in range(2)
    ]
    scores = [
        lax.dot_general(
            mixed[rows, head * size : (head + 1) * size],
            mixed[rows, third + head * size : third + (head + 1) * size],
            (((1,), (1,)), ((), ())),
            preferred_element_type=jnp.float32,
        )
        for head, rows in units
    ]
    probs = masked_softmax(scores, same, size)
    for (head, rows), prob in zip(units, probs):
        value = mixed[rows, 2 * third + head * size : 2 * third + (head + 1) * size]
        context[head, rows, :] = dot32(prob, value).astype(jnp.bfloat16)


def context_out(info, mine, other, w0, w1, w2, w3, attended, pieces):
    heads = mine.shape[0]
    core = info[16]
    pieces[pl.ds(core * heads, heads)] = mine[...]
    pieces[pl.ds((1 - core) * heads, heads)] = other[...]
    cols = attended.shape[1]
    attended[...] = ring_dot(info, pieces, (w0, w1, w2, w3), 0, cols).astype(jnp.bfloat16)


def norm_up(info, near_rows, far_rows, mine, other, w0, w1, w2, w3, first_out, inner, pieces, rows):
    core = info[16]
    cols = mine.shape[1]
    half, width = near_rows.shape
    rows[pl.ds(pl.multiple_of(core * half, half), half), :] = near_rows[...]
    rows[pl.ds(pl.multiple_of((1 - core) * half, half), half), :] = far_rows[...]
    near = mine[...].astype(jnp.float32)
    far = other[...].astype(jnp.float32)
    low = rows[:, :cols].astype(jnp.float32) + jnp.where(core == 0, near, far)
    high = rows[:, cols:].astype(jnp.float32) + jnp.where(core == 0, far, near)
    mean = (jnp.sum(low, 1, keepdims=True) + jnp.sum(high, 1, keepdims=True)) / width
    low, high = low - mean, high - mean
    var = (jnp.sum(low * low, 1, keepdims=True) + jnp.sum(high * high, 1, keepdims=True)) / width
    scale = lax.rsqrt(var + 1e-05)
    first_out[:, :cols] = (low * scale).astype(jnp.bfloat16)
    first_out[:, cols:] = (high * scale).astype(jnp.bfloat16)
    size = pieces.shape[2]
    for index in range(pieces.shape[0]):
        pieces[index] = first_out[:, index * size : (index + 1) * size]
    total = ring_dot(info, pieces, (w0, w1, w2, w3), cols, w0.shape[2])
    act = gelu_exact(total).astype(jnp.bfloat16)
    unit = inner.shape[2]
    for index in range(inner.shape[0]):
        inner[index] = act[:, index * unit : (index + 1) * unit]


def down(info, inner, first_out, w0, w1, w2, w3, kept, sent, total):
    core = info[16]
    total[...] = ring_dot(info, inner, (w0, w1, w2, w3), 0, w0.shape[2])
    half = kept.shape[0]
    rows = pl.ds(pl.multiple_of(core * half, half), half)
    kept[...] = total[rows, :] + first_out[rows, :].astype(jnp.float32)
    sent[...] = total[pl.ds(pl.multiple_of((1 - core) * half, half), half), :].astype(jnp.bfloat16)


def norm_pool(info, kept, arrived, pick, out, lanes):
    half, width = kept.shape
    values = kept[...] + arrived[...].astype(jnp.float32)
    mean = jnp.mean(values, axis=1, keepdims=True)
    values = values - mean
    values = values * lax.rsqrt(jnp.mean(values * values, axis=1, keepdims=True) + 1e-05)
    spans = pick.shape[1]
    pooled = jnp.mean(values.reshape(spans, half // spans, width), axis=1).astype(jnp.bfloat16)
    by_slot = dot32(pick[...], pooled)
    for index in range(width // 128):
        lanes[:, index, :] = by_slot[:, index * 128 : (index + 1) * 128]
    out[...] = jnp.broadcast_to(lanes[...].astype(jnp.bfloat16)[:, None], out.shape)


def embed(info, arrived, order, proj_in, mine, other, out, lanes, result, sems):
    core = info[16]
    lanes[...] = arrived[...].astype(jnp.float32)
    columns = [
        dot32(order[...], lanes[:, index, :].astype(jnp.bfloat16)).astype(jnp.bfloat16)
        for index in range(lanes.shape[1])
    ]
    arranged = jnp.concatenate(columns, axis=1)
    hidden = gelu_exact(dot32(arranged, proj_in[...])).astype(jnp.bfloat16)
    units = hidden.shape[1]
    cols = mine.shape[2]
    near = dot32(hidden, mine[...].reshape(units, cols))
    far = dot32(hidden, other[...].reshape(units, cols))
    low = jnp.where(core == 0, near, far).astype(jnp.bfloat16)
    high = jnp.where(core == 0, far, near).astype(jnp.bfloat16)
    result[:, :cols] = low
    result[:, cols:] = high
    copies = [
        pltpu.make_async_copy(result, out.at[index], sems.at[index]) for index in range(out.shape[0])
    ]
    for copy in copies:
        copy.start()
    for copy in copies:
        copy.wait()


def keys_values(emb, gain, weight_hbm, cosine, sine, swap, gained, scale, out, weight, sems):
    count, rows, depth = emb.shape
    parts = sems.shape[0]
    step = weight.shape[1] // parts

    def fetch(part):
        span = pl.ds(part * step, step)
        return pltpu.make_async_copy(
            weight_hbm.at[:, span, :], weight.at[:, span, :], sems.at[part]
        )

    for part in range(parts):
        fetch(part).start()
    square = jnp.zeros((rows, 1), jnp.float32)
    for index in range(count):
        wide = emb[index].astype(jnp.float32)
        square += jnp.sum(wide * wide, axis=1, keepdims=True)
        gained[index] = (wide * gain[index]).astype(jnp.bfloat16)
    factor = lax.rsqrt(square / (count * depth) + 1e-05)
    scale[...] = factor
    key = jnp.zeros((rows, weight.shape[2]), jnp.float32)
    value = jnp.zeros((rows, weight.shape[2]), jnp.float32)
    for part in range(parts):
        fetch(part).wait()
        for index in range(part * step // depth, (part + 1) * step // depth):
            span = slice(index * depth, (index + 1) * depth)
            key += dot32(gained[index], weight[0, span, :])
            value += dot32(gained[index], weight[1, span, :])
    key = key * factor
    turned = jnp.dot(
        key, swap[...], preferred_element_type=jnp.float32, precision=lax.Precision.HIGHEST
    )
    out[0] = (key * cosine[...] + turned * sine[...]).astype(jnp.bfloat16)
    out[1] = (value * factor).astype(jnp.bfloat16)


def queries(gained, weight_hbm, scale, cosine, sine, swap, out, weight, total, sems):
    count, rows, depth = gained.shape
    parts = sems.shape[0]
    step = weight.shape[0] // parts

    def fetch(part):
        span = pl.ds(part * step, step)
        return pltpu.make_async_copy(weight_hbm.at[span, :], weight.at[span, :], sems.at[part])

    for part in range(parts):
        fetch(part).start()
    for part in range(parts):
        fetch(part).wait()
        span = range(part * step // depth, (part + 1) * step // depth)
        act = jnp.concatenate([gained[index] for index in span], axis=1)
        term = dot32(act, weight[part * step : (part + 1) * step, :])
        total[...] = term if part == 0 else total[...] + term
    for head in range(out.shape[1] // HEAD_WIDTH):
        lanes = slice(head * HEAD_WIDTH, (head + 1) * HEAD_WIDTH)
        query = total[:, lanes] * scale[...]
        turned = jnp.dot(
            query, swap[...], preferred_element_type=jnp.float32, precision=lax.Precision.HIGHEST
        )
        out[:, lanes] = (query * cosine[...] + turned * sine[...]).astype(jnp.bfloat16)


def attend_out(
    info, query, mine, partner, allowed, weight_hbm, out, weight, context, result, sems, out_sems
):
    parts = sems.shape[0]
    step = weight.shape[1] // parts

    def fetch(part):
        span = pl.ds(part * step, step)
        return pltpu.make_async_copy(weight_hbm.at[:, span], weight.at[:, span], sems.at[part])

    def store(part):
        span = pl.ds(part * step, step)
        return pltpu.make_async_copy(result.at[:, span], out.at[:, span], out_sems.at[part])

    for part in range(parts):
        fetch(part).start()
    odd = info[17] == 1
    own = mine[...].astype(jnp.float32)
    far = partner[...].astype(jnp.float32)
    low = jnp.where(odd, far, own)
    high = jnp.where(odd, own, far)
    pair = jnp.concatenate([low, high], axis=2).astype(jnp.bfloat16)
    key, value = pair[0], pair[1]
    heads = [
        slice(head * HEAD_WIDTH, (head + 1) * HEAD_WIDTH)
        for head in range(query.shape[1] // HEAD_WIDTH)
    ]
    scores = [
        lax.dot_general(
            query[:, lanes], key, (((1,), (1,)), ((), ())), preferred_element_type=jnp.float32
        )
        for lanes in heads
    ]
    for lanes, prob in zip(heads, masked_softmax(scores, allowed[...] > 0, HEAD_WIDTH)):
        context[:, lanes] = dot32(prob, value).astype(jnp.bfloat16)
    for part in range(parts):
        fetch(part).wait()
        span = slice(part * step, (part + 1) * step)
        result[:, span] = dot32(context[...], weight[:, span]).astype(jnp.bfloat16)
        store(part).start()
    for part in range(parts):
        store(part).wait()


def finish(info, terms, own, out):
    cols = own.shape[2]
    rows = own.shape[1]
    live = info[18] + lax.broadcasted_iota(jnp.int32, (rows, cols), 0) < info[19]
    for index in range(own.shape[0]):
        lanes = slice(index * cols, (index + 1) * cols)
        total = jnp.sum(terms[:, :, lanes].astype(jnp.float32), axis=0)
        total = total + own[index].astype(jnp.float32)
        out[:, lanes] = jnp.where(live, total, 0.0).astype(jnp.bfloat16)


def visibility(masks, live_count):
    positions = jnp.arange(SPAN_LIMIT)
    passage = positions // CPP
    expanded = jnp.repeat(jnp.repeat(masks, CPP, axis=0), CPP, axis=1) > 0
    same_passage = passage[:, None] == passage[None, :]
    earlier = positions[None, :] <= positions[:, None]
    key_live = positions[None, :] < live_count
    diagonal = positions[:, None] == positions[None, :]
    return diagonal | earlier & key_live & (same_passage | expanded)


def local(
    span_tokens,
    enc_dest,
    passages,
    req_slot,
    block_mask,
    enc_qkv,
    enc_out,
    enc_up,
    enc_down,
    proj_in,
    proj_out,
    norm_gain,
    q_weight,
    key_value_weight,
    out_weight,
):
    tensor_count = lax.axis_size("tensor")
    seq_count = lax.axis_size("seq")
    tensor_index = lax.axis_index("tensor")
    seq_index = lax.axis_index("seq")
    core = seq_index % 2
    device_count = tensor_count * seq_count
    rows = SPAN_LIMIT
    own_rows = rows // tensor_count
    spans, span_size, width = span_tokens.shape
    model_width = proj_out.shape[1]
    share = enc_qkv.shape[0]
    x_index, y_index = tensor_index // SIDE, tensor_index % SIDE

    steps = jnp.array([0, SIDE - 1, 1, 2])
    outer, inside = jnp.repeat(steps, SIDE), jnp.tile(steps, SIDE)
    by_x = SIDE * ((x_index + outer) % SIDE) + (y_index + inside) % SIDE
    by_y = SIDE * ((x_index + inside) % SIDE) + (y_index + outer) % SIDE
    shards = jnp.where(core == 0, by_x, by_y)
    scalars = jnp.stack([core, tensor_index % 2, tensor_index * own_rows])
    info = jnp.concatenate([shards, scalars]).astype(jnp.int32)

    requests = jnp.arange(req_slot.shape[0])
    dest_slot = jnp.sum(
        jnp.where(enc_dest[:, None] // SPAN_LIMIT == requests[None, :], req_slot[None, :], 0), axis=1
    ).reshape(device_count, own_rows)
    dest_place = (enc_dest % SPAN_LIMIT).reshape(device_count, own_rows)
    own_slots = lax.dynamic_slice_in_dim(
        dest_slot, seq_index * tensor_count + tensor_index, 1, 0
    )
    pick = (jnp.arange(seq_count)[:, None] == own_slots).astype(jnp.bfloat16)
    place_of = jnp.sum(jnp.where(dest_slot == seq_index, dest_place, 0), axis=1)
    order = (jnp.arange(rows)[:, None] == place_of[None, :]).astype(jnp.bfloat16)
    chosen = jnp.sum(jnp.where(req_slot == seq_index, requests, 0))
    live_count = jnp.sum(jnp.where(requests == chosen, passages, 0)) * CPP
    masks = jnp.sum(
        jnp.where(requests[:, None, None] == chosen, block_mask, 0), axis=0
    )
    allowed = visibility(masks, live_count).astype(jnp.float32)
    live_info = jnp.concatenate([info, live_count[None]]).astype(jnp.int32)

    positions = jnp.arange(rows).astype(jnp.float32)
    lane = jnp.arange(HEAD_WIDTH)
    frequency = jnp.exp(
        -(2.0 * (lane // 2).astype(jnp.float32) / HEAD_WIDTH) * math.log(500000.0)
    )
    angles = positions[:, None] * frequency[None, :]
    cosine, sine = jnp.cos(angles), jnp.sin(angles)
    swap = jnp.where(
        (lane[:, None] ^ 1) == lane[None, :], jnp.where(lane[None, :] % 2 == 0, -1.0, 1.0), 0.0
    ).astype(jnp.float32)

    own_tokens = span_tokens.reshape(spans * span_size, width)
    own_qkv = whole_call(
        take_qkv, "take_qkv", info, [enc_qkv], shape_of((share, 3 * width // 2)), limit=4
    )
    units = enc_down.shape[0] // 2
    middle_cols = width // 2 + units * tensor_count
    own_rest = whole_call(
        take_rest,
        "take_rest",
        info,
        [enc_out, enc_up, enc_down],
        shape_of((share, middle_cols + width)),
        limit=4,
    )
    qkv_block = whole_call(
        join_qkv,
        "join_qkv",
        info,
        short_ring(own_qkv),
        shape_of((SIDE, share, 3 * width // 2)),
        limit=6,
    )
    def ring(block, relay):
        left = to_ring(block, 2, 1)
        right = to_ring(block, 2, -1)
        opposite = to_ring(left, 2, 1) if relay == 1 else to_ring(right, 2, -1)
        return [block, left, right, opposite]

    qkv = ring(qkv_block, 1)
    middle_block, lower_block = whole_call(
        join_rest,
        "join_rest",
        info,
        short_ring(own_rest),
        (shape_of((SIDE, share, middle_cols)), shape_of((SIDE, share, width))),
        limit=8,
        after=qkv[1:3],
    )
    other_tokens = to_core(own_tokens)
    token_pieces = whole_call(
        both_rows,
        "both_rows",
        info,
        [own_tokens, other_tokens],
        shape_of((tensor_count, 2 * spans * span_size, share)),
    )
    all_rows = 2 * spans * span_size

    middle = ring(middle_block, -1)
    lower = ring(lower_block, 1)

    share_cols = model_width // tensor_count
    proj_mine = lax.all_to_all(
        whole_call(
            spread_proj,
            "spread_proj",
            info,
            [proj_out],
            shape_of((tensor_count, proj_out.shape[0], share_cols // 2)),
            after=[qkv_block],
        ),
        "tensor",
        0,
        0,
    )
    proj_other = to_core(proj_mine)
    context = whole_call(
        span_attention,
        "span_attention",
        info,
        [token_pieces, *qkv],
        shape_of((tensor_count // 2, all_rows, share)),
        [pltpu.VMEM((all_rows, 3 * width // 2), jnp.bfloat16)],
        flops=2 * all_rows * width * 3 * width // 2,
        after=[proj_mine],
    )
    attended = whole_call(
        context_out,
        "context_out",
        info,
        [context, to_core(context), *middle],
        shape_of((all_rows, width // 2)),
        [pltpu.VMEM((tensor_count, all_rows, share), jnp.bfloat16)],
        flops=2 * all_rows * width * width // 2,
    )
    first_out, inner = whole_call(
        norm_up,
        "norm_up",
        info,
        [own_tokens, other_tokens, attended, to_core(attended), *middle],
        (shape_of((all_rows, width)), shape_of((tensor_count, all_rows, units))),
        [
            pltpu.VMEM((tensor_count, all_rows, share), jnp.bfloat16),
            pltpu.VMEM((all_rows, width), jnp.bfloat16),
        ],
        flops=2 * all_rows * width * width,
    )
    kept, sent = whole_call(
        down,
        "down",
        info,
        [inner, first_out, *lower],
        (
            shape_of((all_rows // 2, width), jnp.float32),
            shape_of((all_rows // 2, width)),
        ),
        [pltpu.VMEM((all_rows, width), jnp.float32)],
        flops=2 * all_rows * width * width,
    )
    outgoing = whole_call(
        norm_pool,
        "norm_pool",
        info,
        [kept, to_core(sent), pick],
        shape_of((seq_count, tensor_count, width // 128, 128)),
        [pltpu.VMEM((seq_count, width // 128, 128), jnp.float32)],
    )
    arrived = lax.all_to_all(
        outgoing.reshape(device_count, width // 128, 128), AXES, 0, 0
    )

    spread = whole_call(
        embed,
        "embed",
        info,
        [arrived, order, proj_in, proj_mine, proj_other],
        shape_of((tensor_count, rows, share_cols)),
        [
            pltpu.VMEM((device_count, width // 128, 128), jnp.float32),
            pltpu.VMEM((rows, share_cols), jnp.bfloat16),
            pltpu.SemaphoreType.DMA((tensor_count,)),
        ],
        limit=50,
        flops=2 * rows * width * (width + share_cols),
        out_space=pltpu.HBM,
    )
    embedded = lax.all_to_all(spread, "tensor", 0, 0)
    own_embedded = lax.dynamic_slice_in_dim(embedded, tensor_index * own_rows, own_rows, 1)

    query_cols = q_weight.shape[1]
    kv_cols = key_value_weight.shape[2]
    key_start = tensor_index * kv_cols % HEAD_WIDTH
    key_cosine = lax.dynamic_slice_in_dim(cosine, key_start, kv_cols, 1)
    key_sine = lax.dynamic_slice_in_dim(sine, key_start, kv_cols, 1)
    parts = 8
    hbm = pl.BlockSpec(memory_space=pltpu.HBM)
    gained, scale, own_kv = pl.pallas_call(
        keys_values,
        name="keys_values",
        out_shape=(
            shape_of((tensor_count, rows, share_cols)),
            shape_of((rows, 1), jnp.float32),
            shape_of((2, rows, kv_cols)),
        ),
        in_specs=[VMEM, VMEM, hbm, VMEM, VMEM, VMEM],
        out_specs=(VMEM, VMEM, VMEM),
        scratch_shapes=[
            pltpu.VMEM((2, model_width, kv_cols), jnp.bfloat16),
            pltpu.SemaphoreType.DMA((parts,)),
        ],
        compiler_params=pltpu.CompilerParams(vmem_limit_bytes=56 * MIB),
    )(
        embedded,
        norm_gain.reshape(tensor_count, 1, share_cols),
        key_value_weight,
        key_cosine,
        key_sine,
        swap[:kv_cols, :kv_cols],
    )
    partner_kv = lax.ppermute(
        own_kv, "tensor", [(index, index ^ 1) for index in range(tensor_count)]
    )
    query = pl.pallas_call(
        queries,
        name="queries",
        out_shape=shape_of((rows, query_cols)),
        in_specs=[VMEM, hbm, VMEM, VMEM, VMEM, VMEM],
        out_specs=VMEM,
        scratch_shapes=[
            pltpu.VMEM((model_width, query_cols), jnp.bfloat16),
            pltpu.VMEM((rows, query_cols), jnp.float32),
            pltpu.SemaphoreType.DMA((parts,)),
        ],
        compiler_params=pltpu.CompilerParams(vmem_limit_bytes=52 * MIB),
        cost_estimate=pl.CostEstimate(
            flops=2 * rows * model_width * query_cols,
            bytes_accessed=2 * model_width * query_cols,
            transcendentals=0,
        ),
    )(gained, q_weight, scale, cosine, sine, swap)
    partial = pl.pallas_call(
        attend_out,
        name="attend_out",
        out_shape=shape_of((rows, model_width)),
        in_specs=[SMEM, VMEM, VMEM, VMEM, VMEM, hbm],
        out_specs=hbm,
        scratch_shapes=[
            pltpu.VMEM((query_cols, model_width), jnp.bfloat16),
            pltpu.VMEM((rows, query_cols), jnp.bfloat16),
            pltpu.VMEM((rows, model_width), jnp.bfloat16),
            pltpu.SemaphoreType.DMA((parts,)),
            pltpu.SemaphoreType.DMA((parts,)),
        ],
        compiler_params=pltpu.CompilerParams(vmem_limit_bytes=54 * MIB),
    )(info, query, own_kv, partner_kv, allowed, out_weight)
    terms = lax.all_to_all(
        partial.reshape(tensor_count, own_rows, model_width), "tensor", 0, 0
    )
    return whole_call(
        finish, "finish", live_info, [terms, own_embedded], shape_of((own_rows, model_width))
    )


def solution(mesh):
    return jax.shard_map(
        local,
        mesh=mesh,
        in_specs=(
            P(("seq", "tensor"), None, None),
            P(),
            P(),
            P(),
            P(),
            P("tensor", None),
            P("tensor", None),
            P("tensor", None),
            P("tensor", None),
            P(),
            P("tensor", None),
            P(),
            P(None, "tensor"),
            P(None, None, "tensor"),
            P("tensor", None),
        ),
        out_specs=P(("seq", "tensor"), None),
        check_vma=False,
    )
```

```python
import functools
import math

import jax
import jax.numpy as jnp
from jax import lax
from jax.experimental import pallas as pl
from jax.experimental.pallas import tpu as pltpu
from jax.sharding import PartitionSpec as P

QUERY_HEAD_COUNT = 64
KEY_VALUE_HEADS = 8
HEAD_WIDTH = 128
EH = 16
CPP = 16
SPAN_LIMIT = 128
SIDE = 4
AXES = ("seq", "tensor")


def device_id(plane, core, x, y):
    return ((plane * 2 + core) * SIDE + x) * SIDE + y


def every_device():
    return [
        (plane, core, x, y)
        for plane in range(SIDE)
        for core in range(2)
        for x in range(SIDE)
        for y in range(SIDE)
    ]


def first_axis_is_y(core, phase):
    return (core == 0) == (phase == 1)


def ring_pairs(phase, distance):
    pairs = []
    for plane, core, x, y in every_device():
        if first_axis_is_y(core, phase):
            target = device_id(plane, core, x, (y + distance) % SIDE)
        else:
            target = device_id(plane, core, (x + distance) % SIDE, y)
        pairs.append((device_id(plane, core, x, y), target))
    return pairs


def ring_groups(phase):
    groups = []
    for plane in range(SIDE):
        for core in range(2):
            for fixed in range(SIDE):
                groups.append(
                    [
                        device_id(plane, core, fixed, moving)
                        if first_axis_is_y(core, phase)
                        else device_id(plane, core, moving, fixed)
                        for moving in range(SIDE)
                    ]
                )
    return groups


def to_ring(value, phase, distance):
    return lax.ppermute(value, AXES, ring_pairs(phase, distance))


def to_core(value):
    return lax.ppermute(value, "seq", [(index, index ^ 1) for index in range(8)])


def short_ring(block):
    return [block] + [to_ring(block, 1, distance) for distance in (1, -1, 2)]


def short_relay(block):
    left = to_ring(block, 1, 1)
    right = to_ring(block, 1, -1)
    return [block, left, right, to_ring(right, 1, -1)]


VMEM = pl.BlockSpec(memory_space=pltpu.VMEM)
SMEM = pl.BlockSpec(memory_space=pltpu.SMEM)
MIB = 2**20


def shape_of(shape, dtype=jnp.bfloat16):
    return jax.ShapeDtypeStruct(shape, dtype)


def whole_call(body, name, info, arrays, outs, scratch=(), limit=12, flops=0, out_space=pltpu.VMEM, after=()):
    count = len(arrays)

    def run(*refs):
        body(*refs[: 1 + count], *refs[1 + count + len(after) :])

    moved = sum(array.size * array.dtype.itemsize for array in arrays)
    return pl.pallas_call(
        run,
        name=name,
        out_shape=outs,
        in_specs=[SMEM] + [VMEM] * count + [pl.BlockSpec(memory_space=pl.ANY)] * len(after),
        out_specs=jax.tree.map(lambda _: pl.BlockSpec(memory_space=out_space), outs),
        scratch_shapes=list(scratch),
        compiler_params=pltpu.CompilerParams(vmem_limit_bytes=limit * MIB),
        cost_estimate=pl.CostEstimate(flops=flops, bytes_accessed=moved, transcendentals=0),
    )(info, *arrays, *after)


def dot32(left, right):
    return jnp.dot(left, right, preferred_element_type=jnp.float32)


def gelu_exact(values):
    return 0.5 * values * (1.0 + lax.erf(values * (0.5**0.5)))


def take_qkv(info, weight, out):
    cols = weight.shape[1] // 6
    for part in range(3):
        start = pl.multiple_of((2 * part + info[16]) * cols, cols)
        out[:, part * cols : (part + 1) * cols] = weight[:, pl.ds(start, cols)]


def take_rest(info, out_weight, up_weight, down_weight, out):
    core = info[16]
    rows, width = out_weight.shape
    cols = width // 2
    units = down_weight.shape[0] // 2
    out[:, :cols] = out_weight[:, pl.ds(pl.multiple_of(core * cols, cols), cols)]
    at = cols
    for pair in range(up_weight.shape[1] // (4 * units)):
        halves = []
        for step in range(2):
            low = (2 * pair + step) * 2 * units
            halves.append(
                jnp.where(
                    core == 0,
                    up_weight[:, low : low + units].astype(jnp.float32),
                    up_weight[:, low + units : low + 2 * units].astype(jnp.float32),
                )
            )
        piece = jnp.concatenate(halves, axis=1).astype(jnp.bfloat16)
        out[:, at : at + 2 * units] = piece
        at += 2 * units
    out[:, at:] = down_weight[pl.ds(pl.multiple_of(core * units, units), units), :]


def join_blocks(info, own, left, right, opposite, out):
    for index, block in enumerate((own, left, right, opposite)):
        out[index] = block[...]


def join_rest(info, own, left, right, opposite, middle, lower):
    cols = middle.shape[2]
    for index, block in enumerate((own, left, right, opposite)):
        middle[index] = block[:, :cols]
        lower[index] = block[:, cols:]


def spread_proj(info, weight, out):
    cols = out.shape[2]
    for index in range(out.shape[0]):
        start = pl.multiple_of((2 * index + info[16]) * cols, cols)
        out[index] = weight[:, pl.ds(start, cols)]


def both_rows(info, mine, other, pieces_out):
    half, width = mine.shape
    core = info[16]
    piece = pieces_out.shape[2]
    near = pl.ds(pl.multiple_of(core * half, half), half)
    far = pl.ds(pl.multiple_of((1 - core) * half, half), half)
    for index in range(width // piece):
        pieces_out[index, near, :] = mine[:, index * piece : (index + 1) * piece]
        pieces_out[index, far, :] = other[:, index * piece : (index + 1) * piece]


def ring_dot(info, pieces, blocks, low, high):
    total = None
    for at, block in enumerate(blocks):
        act = jnp.concatenate([pieces[info[4 * at + step]] for step in range(SIDE)], axis=1)
        weight = block[:, :, low:high].reshape(act.shape[1], high - low)
        part = dot32(act, weight)
        total = part if total is None else total + part
    return total


def masked_softmax(scores, seen, size):
    scores = [jnp.where(seen, score / math.sqrt(size), -1e30) for score in scores]
    tops = [jnp.max(score, axis=1, keepdims=True) for score in scores]
    powers = [jnp.exp(score - top) for score, top in zip(scores, tops)]
    sums = [jnp.sum(power, axis=1, keepdims=True) for power in powers]
    return [(power / total).astype(jnp.bfloat16) for power, total in zip(powers, sums)]


def span_attention(info, pieces, w0, w1, w2, w3, context, mixed):
    cols = w0.shape[2]
    third = cols // 3
    mixed[...] = ring_dot(info, pieces, (w0, w1, w2, w3), 0, cols).astype(jnp.bfloat16)
    size = context.shape[2]
    half = mixed.shape[0] // 2
    span = 16
    row = lax.broadcasted_iota(jnp.int32, (half, half), 0) // span
    col = lax.broadcasted_iota(jnp.int32, (half, half), 1) // span
    same = row == col
    heads = third // size
    units = [
        (head, slice(part * half, (part + 1) * half)) for head in range(heads) for part in range(2)
    ]
    scores = [
        lax.dot_general(
            mixed[rows, head * size : (head + 1) * size],
            mixed[rows, third + head * size : third + (head + 1) * size],
            (((1,), (1,)), ((), ())),
            preferred_element_type=jnp.float32,
        )
        for head, rows in units
    ]
    probs = masked_softmax(scores, same, size)
    for (head, rows), prob in zip(units, probs):
        value = mixed[rows, 2 * third + head * size : 2 * third + (head + 1) * size]
        context[head, rows, :] = dot32(prob, value).astype(jnp.bfloat16)


def context_out(info, mine, other, w0, w1, w2, w3, attended, pieces):
    heads = mine.shape[0]
    core = info[16]
    pieces[pl.ds(core * heads, heads)] = mine[...]
    pieces[pl.ds((1 - core) * heads, heads)] = other[...]
    cols = attended.shape[1]
    attended[...] = ring_dot(info, pieces, (w0, w1, w2, w3), 0, cols).astype(jnp.bfloat16)


def norm_up(info, near_rows, far_rows, mine, other, w0, w1, w2, w3, first_out, inner, pieces, rows):
    core = info[16]
    cols = mine.shape[1]
    half, width = near_rows.shape
    rows[pl.ds(pl.multiple_of(core * half, half), half), :] = near_rows[...]
    rows[pl.ds(pl.multiple_of((1 - core) * half, half), half), :] = far_rows[...]
    near = mine[...].astype(jnp.float32)
    far = other[...].astype(jnp.float32)
    low = rows[:, :cols].astype(jnp.float32) + jnp.where(core == 0, near, far)
    high = rows[:, cols:].astype(jnp.float32) + jnp.where(core == 0, far, near)
    mean = (jnp.sum(low, 1, keepdims=True) + jnp.sum(high, 1, keepdims=True)) / width
    low, high = low - mean, high - mean
    var = (jnp.sum(low * low, 1, keepdims=True) + jnp.sum(high * high, 1, keepdims=True)) / width
    scale = lax.rsqrt(var + 1e-05)
    first_out[:, :cols] = (low * scale).astype(jnp.bfloat16)
    first_out[:, cols:] = (high * scale).astype(jnp.bfloat16)
    size = pieces.shape[2]
    for index in range(pieces.shape[0]):
        pieces[index] = first_out[:, index * size : (index + 1) * size]
    total = ring_dot(info, pieces, (w0, w1, w2, w3), cols, w0.shape[2])
    act = gelu_exact(total).astype(jnp.bfloat16)
    unit = inner.shape[2]
    for index in range(inner.shape[0]):
        inner[index] = act[:, index * unit : (index + 1) * unit]


def down(info, inner, first_out, w0, w1, w2, w3, kept, sent, total):
    core = info[16]
    total[...] = ring_dot(info, inner, (w0, w1, w2, w3), 0, w0.shape[2])
    half = kept.shape[0]
    rows = pl.ds(pl.multiple_of(core * half, half), half)
    kept[...] = total[rows, :] + first_out[rows, :].astype(jnp.float32)
    sent[...] = total[pl.ds(pl.multiple_of((1 - core) * half, half), half), :].astype(jnp.bfloat16)


def norm_pool(info, kept, arrived, pick, out, lanes):
    half, width = kept.shape
    values = kept[...] + arrived[...].astype(jnp.float32)
    mean = jnp.mean(values, axis=1, keepdims=True)
    values = values - mean
    values = values * lax.rsqrt(jnp.mean(values * values, axis=1, keepdims=True) + 1e-05)
    spans = pick.shape[1]
    pooled = jnp.mean(values.reshape(spans, half // spans, width), axis=1).astype(jnp.bfloat16)
    by_slot = dot32(pick[...], pooled)
    for index in range(width // 128):
        lanes[:, index, :] = by_slot[:, index * 128 : (index + 1) * 128]
    out[...] = jnp.broadcast_to(lanes[...].astype(jnp.bfloat16)[:, None], out.shape)


def embed(info, arrived, order, proj_in, mine, other, out, lanes):
    core = info[16]
    lanes[...] = arrived[...].astype(jnp.float32)
    columns = [
        dot32(order[...], lanes[:, index, :].astype(jnp.bfloat16)).astype(jnp.bfloat16)
        for index in range(lanes.shape[1])
    ]
    arranged = jnp.concatenate(columns, axis=1)
    hidden = gelu_exact(dot32(arranged, proj_in[...])).astype(jnp.bfloat16)
    units = hidden.shape[1]
    cols = mine.shape[2]
    near = dot32(hidden, mine[...].reshape(units, cols))
    far = dot32(hidden, other[...].reshape(units, cols))
    out[:, :cols] = jnp.where(core == 0, near, far).astype(jnp.bfloat16)
    out[:, cols:] = jnp.where(core == 0, far, near).astype(jnp.bfloat16)


def project(info, *refs, starts, count):
    blocks, refs = refs[:count], refs[count:]
    gain, q_weight, kv_weight = refs[:3]
    before = refs[3:6] if len(refs) > 6 else None
    q_total, kv_total, square = refs[-3:]
    depth = blocks[0].shape[2]
    queries, both = None, None
    squares = None
    for at, block in zip(starts, blocks):
        for step in range(SIDE):
            shard = info[SIDE * at + step]
            wide = block[step].astype(jnp.float32)
            act = (wide * gain[shard]).astype(jnp.bfloat16)
            span = pl.ds(pl.multiple_of(shard * depth, depth), depth)
            q_term = dot32(act, q_weight[span, :])
            kv_term = dot32(act, kv_weight[span, :])
            term = jnp.sum(wide * wide, axis=1, keepdims=True)
            queries = q_term if queries is None else queries + q_term
            both = kv_term if both is None else both + kv_term
            squares = term if squares is None else squares + term
    if before is not None:
        queries, both, squares = queries + before[0][...], both + before[1][...], squares + before[2][...]
    q_total[...] = queries
    kv_total[...] = both
    square[...] = squares


def turn(values, cosine, sine, swap):
    turned = jnp.dot(
        values, swap, preferred_element_type=jnp.float32, precision=lax.Precision.HIGHEST
    )
    return values * cosine + turned * sine


def last_keys(info, block, gain, kv_weight, kv_before, sq_before, cosine, sine, swap, out, scale):
    depth = block.shape[2]
    both = kv_before[...]
    squares = sq_before[...]
    for step in range(SIDE):
        shard = info[SIDE * 3 + step]
        wide = block[step].astype(jnp.float32)
        act = (wide * gain[shard]).astype(jnp.bfloat16)
        span = pl.ds(pl.multiple_of(shard * depth, depth), depth)
        both += dot32(act, kv_weight[span, :])
        squares += jnp.sum(wide * wide, axis=1, keepdims=True)
    factor = lax.rsqrt(squares / (depth * SIDE * SIDE) + 1e-05)
    scale[...] = factor
    both = both * factor
    cols = out.shape[2]
    out[0] = turn(both[:, :cols], cosine[...], sine[...], swap[...]).astype(jnp.bfloat16)
    out[1] = both[:, cols:].astype(jnp.bfloat16)


def last_queries(info, block, gain, q_weight, q_before, scale, cosine, sine, swap, out):
    depth = block.shape[2]
    total = q_before[...]
    for step in range(SIDE):
        shard = info[SIDE * 3 + step]
        act = (block[step].astype(jnp.float32) * gain[shard]).astype(jnp.bfloat16)
        span = pl.ds(pl.multiple_of(shard * depth, depth), depth)
        total += dot32(act, q_weight[span, :])
    for head in range(out.shape[1] // HEAD_WIDTH):
        lanes = slice(head * HEAD_WIDTH, (head + 1) * HEAD_WIDTH)
        query = total[:, lanes] * scale[...]
        out[:, lanes] = turn(query, cosine[...], sine[...], swap[...]).astype(jnp.bfloat16)


def attend_out(info, query, mine, partner, allowed, weight, out, context, result, out_sems):
    parts = out_sems.shape[0]
    step = weight.shape[1] // parts

    def store(part):
        span = pl.ds(part * step, step)
        return pltpu.make_async_copy(result.at[:, span], out.at[:, span], out_sems.at[part])

    odd = info[17] == 1
    own = mine[...].astype(jnp.float32)
    far = partner[...].astype(jnp.float32)
    low = jnp.where(odd, far, own)
    high = jnp.where(odd, own, far)
    both = jnp.concatenate([low, high], axis=2).astype(jnp.bfloat16)
    key, value = both[0], both[1]
    heads = [
        slice(head * HEAD_WIDTH, (head + 1) * HEAD_WIDTH)
        for head in range(query.shape[1] // HEAD_WIDTH)
    ]
    scores = [
        lax.dot_general(
            query[:, lanes], key, (((1,), (1,)), ((), ())), preferred_element_type=jnp.float32
        )
        for lanes in heads
    ]
    for lanes, prob in zip(heads, masked_softmax(scores, allowed[...] > 0, HEAD_WIDTH)):
        context[:, lanes] = dot32(prob, value).astype(jnp.bfloat16)
    for part in range(parts):
        span = slice(part * step, (part + 1) * step)
        result[:, span] = dot32(context[...], weight[:, span]).astype(jnp.bfloat16)
        store(part).start()
    for part in range(parts):
        store(part).wait()


def finish(info, terms, *refs):
    own, out = refs[:-1], refs[-1]
    rows, cols = own[0].shape[1:]
    live = info[18] + lax.broadcasted_iota(jnp.int32, (rows, cols), 0) < info[19]
    for at, block in enumerate(own):
        for step in range(SIDE):
            lanes = pl.ds(pl.multiple_of(info[SIDE * at + step] * cols, cols), cols)
            total = jnp.sum(terms[:, :, lanes].astype(jnp.float32), axis=0)
            total = total + block[step].astype(jnp.float32)
            out[:, lanes] = jnp.where(live, total, 0.0).astype(jnp.bfloat16)


def visibility(masks, live_count):
    positions = jnp.arange(SPAN_LIMIT)
    passage = positions // CPP
    expanded = jnp.repeat(jnp.repeat(masks, CPP, axis=0), CPP, axis=1) > 0
    same_passage = passage[:, None] == passage[None, :]
    earlier = positions[None, :] <= positions[:, None]
    key_live = positions[None, :] < live_count
    diagonal = positions[:, None] == positions[None, :]
    return diagonal | earlier & key_live & (same_passage | expanded)


def local(
    span_tokens,
    enc_dest,
    passages,
    req_slot,
    block_mask,
    enc_qkv,
    enc_out,
    enc_up,
    enc_down,
    proj_in,
    proj_out,
    norm_gain,
    q_weight,
    key_value_weight,
    out_weight,
):
    tensor_count = lax.axis_size("tensor")
    seq_count = lax.axis_size("seq")
    tensor_index = lax.axis_index("tensor")
    seq_index = lax.axis_index("seq")
    core = seq_index % 2
    device_count = tensor_count * seq_count
    rows = SPAN_LIMIT
    own_rows = rows // tensor_count
    spans, span_size, width = span_tokens.shape
    model_width = proj_out.shape[1]
    share = enc_qkv.shape[0]
    x_index, y_index = tensor_index // SIDE, tensor_index % SIDE

    steps = jnp.array([0, SIDE - 1, 1, 2])
    outer, inside = jnp.repeat(steps, SIDE), jnp.tile(steps, SIDE)
    by_x = SIDE * ((x_index + outer) % SIDE) + (y_index + inside) % SIDE
    by_y = SIDE * ((x_index + inside) % SIDE) + (y_index + outer) % SIDE
    shards = jnp.where(core == 0, by_x, by_y)
    scalars = jnp.stack([core, tensor_index % 2, tensor_index * own_rows])
    info = jnp.concatenate([shards, scalars]).astype(jnp.int32)

    requests = jnp.arange(req_slot.shape[0])
    dest_slot = jnp.sum(
        jnp.where(enc_dest[:, None] // SPAN_LIMIT == requests[None, :], req_slot[None, :], 0), axis=1
    ).reshape(device_count, own_rows)
    dest_place = (enc_dest % SPAN_LIMIT).reshape(device_count, own_rows)
    own_slots = lax.dynamic_slice_in_dim(
        dest_slot, seq_index * tensor_count + tensor_index, 1, 0
    )
    pick = (jnp.arange(seq_count)[:, None] == own_slots).astype(jnp.bfloat16)
    place_of = jnp.sum(jnp.where(dest_slot == seq_index, dest_place, 0), axis=1)
    order = (jnp.arange(rows)[:, None] == place_of[None, :]).astype(jnp.bfloat16)
    chosen = jnp.sum(jnp.where(req_slot == seq_index, requests, 0))
    live_count = jnp.sum(jnp.where(requests == chosen, passages, 0)) * CPP
    masks = jnp.sum(
        jnp.where(requests[:, None, None] == chosen, block_mask, 0), axis=0
    )
    allowed = visibility(masks, live_count).astype(jnp.float32)
    live_info = jnp.concatenate([info, live_count[None]]).astype(jnp.int32)

    positions = jnp.arange(rows).astype(jnp.float32)
    lane = jnp.arange(HEAD_WIDTH)
    frequency = jnp.exp(
        -(2.0 * (lane // 2).astype(jnp.float32) / HEAD_WIDTH) * math.log(500000.0)
    )
    angles = positions[:, None] * frequency[None, :]
    cosine, sine = jnp.cos(angles), jnp.sin(angles)
    swap = jnp.where(
        (lane[:, None] ^ 1) == lane[None, :], jnp.where(lane[None, :] % 2 == 0, -1.0, 1.0), 0.0
    ).astype(jnp.float32)

    own_tokens = span_tokens.reshape(spans * span_size, width)
    own_qkv = whole_call(
        take_qkv, "take_qkv", info, [enc_qkv], shape_of((share, 3 * width // 2)), limit=4
    )
    share_cols = model_width // tensor_count
    proj_mine = lax.all_to_all(
        whole_call(
            spread_proj,
            "spread_proj",
            info,
            [proj_out],
            shape_of((tensor_count, proj_out.shape[0], share_cols // 2)),
            after=[own_qkv],
        ),
        "tensor",
        0,
        0,
    )
    proj_other = to_core(proj_mine)
    units = enc_down.shape[0] // 2
    middle_cols = width // 2 + units * tensor_count
    own_rest = whole_call(
        take_rest,
        "take_rest",
        info,
        [enc_out, enc_up, enc_down],
        shape_of((share, middle_cols + width)),
        limit=4,
    )
    qkv_block = whole_call(
        join_blocks,
        "join_qkv",
        info,
        short_ring(own_qkv),
        shape_of((SIDE, share, 3 * width // 2)),
        limit=6,
    )
    def ring(block, relay):
        left = to_ring(block, 2, 1)
        right = to_ring(block, 2, -1)
        opposite = to_ring(left, 2, 1) if relay == 1 else to_ring(right, 2, -1)
        return [block, left, right, opposite]

    qkv = ring(qkv_block, 1)
    middle_block, lower_block = whole_call(
        join_rest,
        "join_rest",
        info,
        short_relay(own_rest),
        (shape_of((SIDE, share, middle_cols)), shape_of((SIDE, share, width))),
        limit=8,
        after=[*qkv[1:3], proj_mine],
    )
    other_tokens = to_core(own_tokens)
    token_pieces = whole_call(
        both_rows,
        "both_rows",
        info,
        [own_tokens, other_tokens],
        shape_of((tensor_count, 2 * spans * span_size, share)),
    )
    all_rows = 2 * spans * span_size

    middle = ring(middle_block, -1)
    lower = ring(lower_block, 1)

    context = whole_call(
        span_attention,
        "span_attention",
        info,
        [token_pieces, *qkv],
        shape_of((tensor_count // 2, all_rows, share)),
        [pltpu.VMEM((all_rows, 3 * width // 2), jnp.bfloat16)],
        flops=2 * all_rows * width * 3 * width // 2,
    )
    attended = whole_call(
        context_out,
        "context_out",
        info,
        [context, to_core(context), *middle],
        shape_of((all_rows, width // 2)),
        [pltpu.VMEM((tensor_count, all_rows, share), jnp.bfloat16)],
        flops=2 * all_rows * width * width // 2,
    )
    first_out, inner = whole_call(
        norm_up,
        "norm_up",
        info,
        [own_tokens, other_tokens, attended, to_core(attended), *middle],
        (shape_of((all_rows, width)), shape_of((tensor_count, all_rows, units))),
        [
            pltpu.VMEM((tensor_count, all_rows, share), jnp.bfloat16),
            pltpu.VMEM((all_rows, width), jnp.bfloat16),
        ],
        flops=2 * all_rows * width * width,
    )
    kept, sent = whole_call(
        down,
        "down",
        info,
        [inner, first_out, *lower],
        (
            shape_of((all_rows // 2, width), jnp.float32),
            shape_of((all_rows // 2, width)),
        ),
        [pltpu.VMEM((all_rows, width), jnp.float32)],
        flops=2 * all_rows * width * width,
    )
    outgoing = whole_call(
        norm_pool,
        "norm_pool",
        info,
        [kept, to_core(sent), pick],
        shape_of((seq_count, tensor_count, width // 128, 128)),
        [pltpu.VMEM((seq_count, width // 128, 128), jnp.float32)],
    )
    arrived = lax.all_to_all(
        outgoing.reshape(device_count, width // 128, 128), AXES, 0, 0
    )

    own_cols = whole_call(
        embed,
        "embed",
        info,
        [arrived, order, proj_in, proj_mine, proj_other],
        shape_of((rows, share_cols)),
        [pltpu.VMEM((device_count, width // 128, 128), jnp.float32)],
        flops=2 * rows * width * (width + share_cols),
    )
    first_block = whole_call(
        join_blocks,
        "join_columns",
        info,
        short_ring(own_cols),
        shape_of((SIDE, rows, share_cols)),
        limit=4,
    )
    embedded = ring(first_block, 1)

    query_cols = q_weight.shape[1]
    kv_cols = key_value_weight.shape[2]
    key_start = tensor_index * kv_cols % HEAD_WIDTH
    key_cosine = lax.dynamic_slice_in_dim(cosine, key_start, kv_cols, 1)
    key_sine = lax.dynamic_slice_in_dim(sine, key_start, kv_cols, 1)
    parts = 8
    gain = norm_gain.reshape(tensor_count, 1, share_cols)
    kv_pair = jnp.concatenate([key_value_weight[0], key_value_weight[1]], axis=1)
    sums = (
        shape_of((rows, query_cols), jnp.float32),
        shape_of((rows, 2 * kv_cols), jnp.float32),
        shape_of((rows, 1), jnp.float32),
    )
    block_flops = 2 * rows * model_width // SIDE * (query_cols + 2 * kv_cols)
    totals = whole_call(
        functools.partial(project, starts=(0,), count=1),
        "project_own",
        info,
        [embedded[0], gain, q_weight, kv_pair],
        sums,
        flops=block_flops,
    )
    totals = whole_call(
        functools.partial(project, starts=(1, 2), count=2),
        "project_near",
        info,
        [embedded[1], embedded[2], gain, q_weight, kv_pair, *totals],
        sums,
        flops=2 * block_flops,
    )
    own_kv, scale = whole_call(
        last_keys,
        "last_keys",
        info,
        [
            embedded[3],
            gain,
            kv_pair,
            totals[1],
            totals[2],
            key_cosine,
            key_sine,
            swap[:kv_cols, :kv_cols],
        ],
        (shape_of((2, rows, kv_cols)), shape_of((rows, 1), jnp.float32)),
    )
    partner_kv = lax.ppermute(
        own_kv, "tensor", [(index, index ^ 1) for index in range(tensor_count)]
    )
    query = whole_call(
        last_queries,
        "last_queries",
        info,
        [embedded[3], gain, q_weight, totals[0], scale, cosine, sine, swap],
        shape_of((rows, query_cols)),
        flops=block_flops,
    )
    partial = pl.pallas_call(
        attend_out,
        name="attend_out",
        out_shape=shape_of((rows, model_width)),
        in_specs=[SMEM, VMEM, VMEM, VMEM, VMEM, VMEM],
        out_specs=pl.BlockSpec(memory_space=pltpu.HBM),
        scratch_shapes=[
            pltpu.VMEM((rows, query_cols), jnp.bfloat16),
            pltpu.VMEM((rows, model_width), jnp.bfloat16),
            pltpu.SemaphoreType.DMA((parts,)),
        ],
        compiler_params=pltpu.CompilerParams(vmem_limit_bytes=16 * MIB),
    )(info, query, own_kv, partner_kv, allowed, out_weight)
    terms = lax.all_to_all(
        partial.reshape(tensor_count, own_rows, model_width), "tensor", 0, 0
    )
    own_embedded = [
        lax.dynamic_slice_in_dim(block, tensor_index * own_rows, own_rows, 1) for block in embedded
    ]
    return whole_call(
        finish, "finish", live_info, [terms, *own_embedded], shape_of((own_rows, model_width))
    )


def solution(mesh):
    return jax.shard_map(
        local,
        mesh=mesh,
        in_specs=(
            P(("seq", "tensor"), None, None),
            P(),
            P(),
            P(),
            P(),
            P("tensor", None),
            P("tensor", None),
            P("tensor", None),
            P("tensor", None),
            P(),
            P("tensor", None),
            P(),
            P(None, "tensor"),
            P(None, None, "tensor"),
            P("tensor", None),
        ),
        out_specs=P(("seq", "tensor"), None),
        check_vma=False,
    )
```

```python
import functools
import math

import jax
import jax.numpy as jnp
from jax import lax
from jax.experimental import pallas as pl
from jax.experimental.pallas import tpu as pltpu
from jax.sharding import PartitionSpec as P

QUERY_HEAD_COUNT = 64
KEY_VALUE_HEADS = 8
HEAD_WIDTH = 128
EH = 16
CPP = 16
SPAN_LIMIT = 128
SIDE = 4
AXES = ("seq", "tensor")


def device_id(plane, core, x, y):
    return ((plane * 2 + core) * SIDE + x) * SIDE + y


def every_device():
    return [
        (plane, core, x, y)
        for plane in range(SIDE)
        for core in range(2)
        for x in range(SIDE)
        for y in range(SIDE)
    ]


def first_axis_is_y(core, phase):
    return (core == 0) == (phase == 1)


def ring_pairs(phase, distance):
    pairs = []
    for plane, core, x, y in every_device():
        if first_axis_is_y(core, phase):
            target = device_id(plane, core, x, (y + distance) % SIDE)
        else:
            target = device_id(plane, core, (x + distance) % SIDE, y)
        pairs.append((device_id(plane, core, x, y), target))
    return pairs


def ring_groups(phase):
    groups = []
    for plane in range(SIDE):
        for core in range(2):
            for fixed in range(SIDE):
                groups.append(
                    [
                        device_id(plane, core, fixed, moving)
                        if first_axis_is_y(core, phase)
                        else device_id(plane, core, moving, fixed)
                        for moving in range(SIDE)
                    ]
                )
    return groups


def to_ring(value, phase, distance):
    return lax.ppermute(value, AXES, ring_pairs(phase, distance))


def to_core(value):
    return lax.ppermute(value, "seq", [(index, index ^ 1) for index in range(8)])


def short_ring(block):
    return [block] + [to_ring(block, 1, distance) for distance in (1, -1, 2)]


def short_relay(block):
    left = to_ring(block, 1, 1)
    right = to_ring(block, 1, -1)
    return [block, left, right, to_ring(right, 1, -1)]


VMEM = pl.BlockSpec(memory_space=pltpu.VMEM)
SMEM = pl.BlockSpec(memory_space=pltpu.SMEM)
MIB = 2**20


def shape_of(shape, dtype=jnp.bfloat16):
    return jax.ShapeDtypeStruct(shape, dtype)


def whole_call(body, name, info, arrays, outs, scratch=(), limit=12, flops=0, out_space=pltpu.VMEM, after=()):
    count = len(arrays)

    def run(*refs):
        body(*refs[: 1 + count], *refs[1 + count + len(after) :])

    moved = sum(array.size * array.dtype.itemsize for array in arrays)
    return pl.pallas_call(
        run,
        name=name,
        out_shape=outs,
        in_specs=[SMEM] + [VMEM] * count + [pl.BlockSpec(memory_space=pl.ANY)] * len(after),
        out_specs=jax.tree.map(lambda _: pl.BlockSpec(memory_space=out_space), outs),
        scratch_shapes=list(scratch),
        compiler_params=pltpu.CompilerParams(vmem_limit_bytes=limit * MIB),
        cost_estimate=pl.CostEstimate(flops=flops, bytes_accessed=moved, transcendentals=0),
    )(info, *arrays, *after)


def dot32(left, right):
    return jnp.dot(left, right, preferred_element_type=jnp.float32)


def dot_last(left, right):
    return lax.dot_general(
        left, right, (((1,), (1,)), ((), ())), preferred_element_type=jnp.float32
    )


def gelu_exact(values):
    return 0.5 * values * (1.0 + lax.erf(values * (0.5**0.5)))


def take_qkv(info, weight, out):
    cols = weight.shape[1] // 6
    for part in range(3):
        start = pl.multiple_of((2 * part + info[16]) * cols, cols)
        out[:, part * cols : (part + 1) * cols] = weight[:, pl.ds(start, cols)]


def take_halves(info, qkv, out_weight, up_weight, down_weight, qkv_out, rest_out):
    take_qkv(info, qkv, qkv_out)
    take_rest(info, out_weight, up_weight, down_weight, rest_out)


def take_rest(info, out_weight, up_weight, down_weight, out):
    core = info[16]
    rows, width = out_weight.shape
    cols = width // 2
    units = down_weight.shape[0] // 2
    out[:, :cols] = out_weight[:, pl.ds(pl.multiple_of(core * cols, cols), cols)]
    at = cols
    for pair in range(up_weight.shape[1] // (4 * units)):
        halves = []
        for step in range(2):
            low = (2 * pair + step) * 2 * units
            halves.append(
                jnp.where(
                    core == 0,
                    up_weight[:, low : low + units].astype(jnp.float32),
                    up_weight[:, low + units : low + 2 * units].astype(jnp.float32),
                )
            )
        piece = jnp.concatenate(halves, axis=1).astype(jnp.bfloat16)
        out[:, at : at + 2 * units] = piece
        at += 2 * units
    out[:, at:] = down_weight[pl.ds(pl.multiple_of(core * units, units), units), :]


def join_blocks(info, own, left, right, opposite, out):
    for index, block in enumerate((own, left, right, opposite)):
        out[index] = block[...]


def join_rest(info, own, left, right, opposite, middle, lower):
    cols = middle.shape[2]
    for index, block in enumerate((own, left, right, opposite)):
        middle[index] = block[:, :cols]
        lower[index] = block[:, cols:]


def deal_columns(info, weight, *outs):
    core, near = info[16], info[19]
    cols = outs[0].shape[2]
    for out, distance in zip(outs, (0, 1, SIDE - 1, 2)):
        target = lax.rem(near + distance, SIDE)
        for index in range(SIDE):
            shard = jnp.where(core == 0, SIDE * index + target, SIDE * target + index)
            start = pl.multiple_of((2 * shard + core) * cols, cols)
            out[index] = weight[:, pl.ds(start, cols)]


def deal_again(info, own, left, right, opposite, *outs):
    far = info[20]
    for out, distance in zip(outs, (0, 1, SIDE - 1, 2)):
        target = lax.rem(far + distance, SIDE)
        for index, block in enumerate((own, left, right, opposite)):
            out[index] = block[target]


def both_rows(info, mine, other, pieces_out):
    half, width = mine.shape
    core = info[16]
    piece = pieces_out.shape[2]
    near = pl.ds(pl.multiple_of(core * half, half), half)
    far = pl.ds(pl.multiple_of((1 - core) * half, half), half)
    for index in range(width // piece):
        pieces_out[index, near, :] = mine[:, index * piece : (index + 1) * piece]
        pieces_out[index, far, :] = other[:, index * piece : (index + 1) * piece]


def ring_dot(info, pieces, blocks, low, high):
    total = None
    for at, block in enumerate(blocks):
        act = jnp.concatenate([pieces[info[4 * at + step]] for step in range(SIDE)], axis=1)
        weight = block[:, :, low:high].reshape(act.shape[1], high - low)
        part = dot32(act, weight)
        total = part if total is None else total + part
    return total


def masked_softmax(scores, seen, size):
    scores = [jnp.where(seen, score / math.sqrt(size), -1e30) for score in scores]
    tops = [jnp.max(score, axis=1, keepdims=True) for score in scores]
    powers = [jnp.exp(score - top) for score, top in zip(scores, tops)]
    sums = [jnp.sum(power, axis=1, keepdims=True) for power in powers]
    return [(power / total).astype(jnp.bfloat16) for power, total in zip(powers, sums)]


def span_attention(info, pieces, w0, w1, w2, w3, context, mixed):
    cols = w0.shape[2]
    third = cols // 3
    mixed[...] = ring_dot(info, pieces, (w0, w1, w2, w3), 0, cols).astype(jnp.bfloat16)
    size = context.shape[2]
    half = mixed.shape[0] // 2
    span = 16
    row = lax.broadcasted_iota(jnp.int32, (half, half), 0) // span
    col = lax.broadcasted_iota(jnp.int32, (half, half), 1) // span
    same = row == col
    heads = third // size
    units = [
        (head, slice(part * half, (part + 1) * half)) for head in range(heads) for part in range(2)
    ]
    scores = [
        lax.dot_general(
            mixed[rows, head * size : (head + 1) * size],
            mixed[rows, third + head * size : third + (head + 1) * size],
            (((1,), (1,)), ((), ())),
            preferred_element_type=jnp.float32,
        )
        for head, rows in units
    ]
    probs = masked_softmax(scores, same, size)
    for (head, rows), prob in zip(units, probs):
        value = mixed[rows, 2 * third + head * size : 2 * third + (head + 1) * size]
        context[head, rows, :] = dot32(prob, value).astype(jnp.bfloat16)


def context_out(info, mine, other, w0, w1, w2, w3, attended, pieces):
    heads = mine.shape[0]
    core = info[16]
    pieces[pl.ds(core * heads, heads)] = mine[...]
    pieces[pl.ds((1 - core) * heads, heads)] = other[...]
    cols = attended.shape[1]
    attended[...] = ring_dot(info, pieces, (w0, w1, w2, w3), 0, cols).astype(jnp.bfloat16)


def norm_up(info, near_rows, far_rows, mine, other, w0, w1, w2, w3, first_out, inner, pieces, rows):
    core = info[16]
    cols = mine.shape[1]
    half, width = near_rows.shape
    rows[pl.ds(pl.multiple_of(core * half, half), half), :] = near_rows[...]
    rows[pl.ds(pl.multiple_of((1 - core) * half, half), half), :] = far_rows[...]
    near = mine[...].astype(jnp.float32)
    far = other[...].astype(jnp.float32)
    low = rows[:, :cols].astype(jnp.float32) + jnp.where(core == 0, near, far)
    high = rows[:, cols:].astype(jnp.float32) + jnp.where(core == 0, far, near)
    mean = (jnp.sum(low, 1, keepdims=True) + jnp.sum(high, 1, keepdims=True)) / width
    low, high = low - mean, high - mean
    var = (jnp.sum(low * low, 1, keepdims=True) + jnp.sum(high * high, 1, keepdims=True)) / width
    scale = lax.rsqrt(var + 1e-05)
    first_out[:, :cols] = (low * scale).astype(jnp.bfloat16)
    first_out[:, cols:] = (high * scale).astype(jnp.bfloat16)
    size = pieces.shape[2]
    for index in range(pieces.shape[0]):
        pieces[index] = first_out[:, index * size : (index + 1) * size]
    total = ring_dot(info, pieces, (w0, w1, w2, w3), cols, w0.shape[2])
    act = gelu_exact(total).astype(jnp.bfloat16)
    unit = inner.shape[2]
    for index in range(inner.shape[0]):
        inner[index] = act[:, index * unit : (index + 1) * unit]


def down(info, inner, first_out, w0, w1, w2, w3, kept, sent, total):
    core = info[16]
    total[...] = ring_dot(info, inner, (w0, w1, w2, w3), 0, w0.shape[2])
    half = kept.shape[0]
    rows = pl.ds(pl.multiple_of(core * half, half), half)
    kept[...] = total[rows, :] + first_out[rows, :].astype(jnp.float32)
    sent[...] = total[pl.ds(pl.multiple_of((1 - core) * half, half), half), :].astype(jnp.bfloat16)


def norm_pool(info, kept, arrived, pick, out, lanes):
    half, width = kept.shape
    values = kept[...] + arrived[...].astype(jnp.float32)
    mean = jnp.mean(values, axis=1, keepdims=True)
    values = values - mean
    values = values * lax.rsqrt(jnp.mean(values * values, axis=1, keepdims=True) + 1e-05)
    spans = pick.shape[1]
    pooled = jnp.mean(values.reshape(spans, half // spans, width), axis=1).astype(jnp.bfloat16)
    by_slot = dot32(pick[...], pooled)
    for index in range(width // 128):
        lanes[:, index, :] = by_slot[:, index * 128 : (index + 1) * 128]
    out[...] = jnp.broadcast_to(lanes[...].astype(jnp.bfloat16)[:, None], out.shape)


def embed(info, arrived, order, proj_in, mine, other, out, lanes, pieces):
    core = info[16]
    lanes[...] = arrived[...].astype(jnp.float32)
    columns = [
        dot32(order[...], lanes[:, index, :].astype(jnp.bfloat16)).astype(jnp.bfloat16)
        for index in range(lanes.shape[1])
    ]
    arranged = jnp.concatenate(columns, axis=1)
    hidden = gelu_exact(dot32(arranged, proj_in[...])).astype(jnp.bfloat16)
    units, cols = mine.shape[2:]
    for index in range(pieces.shape[0]):
        pieces[index] = hidden[:, index * units : (index + 1) * units]
    near, far = None, None
    for at in range(SIDE):
        act = jnp.concatenate([pieces[info[SIDE * at + step]] for step in range(SIDE)], axis=1)
        term = dot32(act, mine[at].reshape(SIDE * units, cols))
        near = term if near is None else near + term
        act = jnp.concatenate([pieces[info[22 + SIDE * at + step]] for step in range(SIDE)], axis=1)
        term = dot32(act, other[at].reshape(SIDE * units, cols))
        far = term if far is None else far + term
    out[:, :cols] = jnp.where(core == 0, near, far).astype(jnp.bfloat16)
    out[:, cols:] = jnp.where(core == 0, far, near).astype(jnp.bfloat16)


def project(info, *refs, starts, count):
    blocks, refs = refs[:count], refs[count:]
    gain, q_weight, kv_weight = refs[:3]
    before = refs[3:6] if len(refs) > 6 else None
    q_total, kv_total, square = refs[-3:]
    depth = blocks[0].shape[2]
    queries, both = None, None
    squares = None
    for at, block in zip(starts, blocks):
        for step in range(SIDE):
            shard = info[SIDE * at + step]
            wide = block[step].astype(jnp.float32)
            act = (wide * gain[shard]).astype(jnp.bfloat16)
            span = pl.ds(pl.multiple_of(shard * depth, depth), depth)
            q_term = dot32(act, q_weight[span, :])
            kv_term = dot_last(act, kv_weight[:, span])
            term = jnp.sum(wide * wide, axis=1, keepdims=True)
            queries = q_term if queries is None else queries + q_term
            both = kv_term if both is None else both + kv_term
            squares = term if squares is None else squares + term
    if before is not None:
        queries, both, squares = queries + before[0][...], both + before[1][...], squares + before[2][...]
    q_total[...] = queries
    kv_total[...] = both
    square[...] = squares


def turn(values, cosine, sine, swap):
    turned = jnp.dot(
        values, swap, preferred_element_type=jnp.float32, precision=lax.Precision.HIGHEST
    )
    return values * cosine + turned * sine


def last_keys(info, block, gain, kv_weight, kv_before, sq_before, cosine, sine, swap, out, scale):
    depth = block.shape[2]
    both = kv_before[...]
    squares = sq_before[...]
    for step in range(SIDE):
        shard = info[SIDE * 3 + step]
        wide = block[step].astype(jnp.float32)
        act = (wide * gain[shard]).astype(jnp.bfloat16)
        span = pl.ds(pl.multiple_of(shard * depth, depth), depth)
        both += dot_last(act, kv_weight[:, span])
        squares += jnp.sum(wide * wide, axis=1, keepdims=True)
    factor = lax.rsqrt(squares / (depth * SIDE * SIDE) + 1e-05)
    scale[...] = factor
    both = both * factor
    cols = out.shape[2]
    out[0] = turn(both[:, :cols], cosine[...], sine[...], swap[...]).astype(jnp.bfloat16)
    out[1] = both[:, cols:].astype(jnp.bfloat16)


def last_queries(info, block, gain, q_weight, q_before, scale, cosine, sine, swap, out):
    depth = block.shape[2]
    total = q_before[...]
    for step in range(SIDE):
        shard = info[SIDE * 3 + step]
        act = (block[step].astype(jnp.float32) * gain[shard]).astype(jnp.bfloat16)
        span = pl.ds(pl.multiple_of(shard * depth, depth), depth)
        total += dot32(act, q_weight[span, :])
    for head in range(out.shape[1] // HEAD_WIDTH):
        lanes = slice(head * HEAD_WIDTH, (head + 1) * HEAD_WIDTH)
        query = total[:, lanes] * scale[...]
        out[:, lanes] = turn(query, cosine[...], sine[...], swap[...]).astype(jnp.bfloat16)


def attend_out(info, query, mine, partner, allowed, weight, out, context, result, out_sems):
    parts = out_sems.shape[0]
    step = weight.shape[1] // parts

    def store(part):
        span = pl.ds(part * step, step)
        return pltpu.make_async_copy(result.at[:, span], out.at[:, span], out_sems.at[part])

    odd = info[17] == 1
    own = mine[...].astype(jnp.float32)
    far = partner[...].astype(jnp.float32)
    low = jnp.where(odd, far, own)
    high = jnp.where(odd, own, far)
    both = jnp.concatenate([low, high], axis=2).astype(jnp.bfloat16)
    key, value = both[0], both[1]
    heads = [
        slice(head * HEAD_WIDTH, (head + 1) * HEAD_WIDTH)
        for head in range(query.shape[1] // HEAD_WIDTH)
    ]
    scores = [
        lax.dot_general(
            query[:, lanes], key, (((1,), (1,)), ((), ())), preferred_element_type=jnp.float32
        )
        for lanes in heads
    ]
    for lanes, prob in zip(heads, masked_softmax(scores, allowed[...] > 0, HEAD_WIDTH)):
        context[:, lanes] = dot32(prob, value).astype(jnp.bfloat16)
    for part in range(parts):
        span = slice(part * step, (part + 1) * step)
        result[:, span] = dot32(context[...], weight[:, span]).astype(jnp.bfloat16)
        store(part).start()
    for part in range(parts):
        store(part).wait()


def finish(info, terms, *refs):
    own, out = refs[:-1], refs[-1]
    rows, cols = own[0].shape[1:]
    live = info[18] + lax.broadcasted_iota(jnp.int32, (rows, cols), 0) < info[21]
    for at, block in enumerate(own):
        for step in range(SIDE):
            lanes = pl.ds(pl.multiple_of(info[SIDE * at + step] * cols, cols), cols)
            total = jnp.sum(terms[:, :, lanes].astype(jnp.float32), axis=0)
            total = total + block[step].astype(jnp.float32)
            out[:, lanes] = jnp.where(live, total, 0.0).astype(jnp.bfloat16)


def visibility(masks, live_count):
    positions = jnp.arange(SPAN_LIMIT)
    passage = positions // CPP
    expanded = jnp.repeat(jnp.repeat(masks, CPP, axis=0), CPP, axis=1) > 0
    same_passage = passage[:, None] == passage[None, :]
    earlier = positions[None, :] <= positions[:, None]
    key_live = positions[None, :] < live_count
    diagonal = positions[:, None] == positions[None, :]
    return diagonal | earlier & key_live & (same_passage | expanded)


def local(
    span_tokens,
    enc_dest,
    passages,
    req_slot,
    block_mask,
    enc_qkv,
    enc_out,
    enc_up,
    enc_down,
    proj_in,
    proj_out,
    norm_gain,
    q_weight,
    key_value_weight,
    out_weight,
):
    tensor_count = lax.axis_size("tensor")
    seq_count = lax.axis_size("seq")
    tensor_index = lax.axis_index("tensor")
    seq_index = lax.axis_index("seq")
    core = seq_index % 2
    device_count = tensor_count * seq_count
    rows = SPAN_LIMIT
    own_rows = rows // tensor_count
    spans, span_size, width = span_tokens.shape
    model_width = proj_out.shape[1]
    share = enc_qkv.shape[0]
    x_index, y_index = tensor_index // SIDE, tensor_index % SIDE

    steps = jnp.array([0, SIDE - 1, 1, 2])
    outer, inside = jnp.repeat(steps, SIDE), jnp.tile(steps, SIDE)
    by_x = SIDE * ((x_index + outer) % SIDE) + (y_index + inside) % SIDE
    by_y = SIDE * ((x_index + inside) % SIDE) + (y_index + outer) % SIDE
    shards = jnp.where(core == 0, by_x, by_y)
    near = jnp.where(core == 0, y_index, x_index)
    far = jnp.where(core == 0, x_index, y_index)
    scalars = jnp.stack([core, tensor_index % 2, tensor_index * own_rows, near, far])
    other_shards = jnp.where(core == 0, by_y, by_x)
    info = jnp.concatenate([shards, scalars, core[None], other_shards]).astype(jnp.int32)

    requests = jnp.arange(req_slot.shape[0])
    dest_slot = jnp.sum(
        jnp.where(enc_dest[:, None] // SPAN_LIMIT == requests[None, :], req_slot[None, :], 0), axis=1
    ).reshape(device_count, own_rows)
    dest_place = (enc_dest % SPAN_LIMIT).reshape(device_count, own_rows)
    own_slots = lax.dynamic_slice_in_dim(
        dest_slot, seq_index * tensor_count + tensor_index, 1, 0
    )
    pick = (jnp.arange(seq_count)[:, None] == own_slots).astype(jnp.bfloat16)
    place_of = jnp.sum(jnp.where(dest_slot == seq_index, dest_place, 0), axis=1)
    order = (jnp.arange(rows)[:, None] == place_of[None, :]).astype(jnp.bfloat16)
    chosen = jnp.sum(jnp.where(req_slot == seq_index, requests, 0))
    live_count = jnp.sum(jnp.where(requests == chosen, passages, 0)) * CPP
    masks = jnp.sum(
        jnp.where(requests[:, None, None] == chosen, block_mask, 0), axis=0
    )
    allowed = visibility(masks, live_count).astype(jnp.float32)
    live_info = jnp.concatenate([info[:21], live_count[None]]).astype(jnp.int32)

    positions = jnp.arange(rows).astype(jnp.float32)
    lane = jnp.arange(HEAD_WIDTH)
    frequency = jnp.exp(
        -(2.0 * (lane // 2).astype(jnp.float32) / HEAD_WIDTH) * math.log(500000.0)
    )
    angles = positions[:, None] * frequency[None, :]
    cosine, sine = jnp.cos(angles), jnp.sin(angles)
    swap = jnp.where(
        (lane[:, None] ^ 1) == lane[None, :], jnp.where(lane[None, :] % 2 == 0, -1.0, 1.0), 0.0
    ).astype(jnp.float32)

    own_tokens = span_tokens.reshape(spans * span_size, width)
    units = enc_down.shape[0] // 2
    middle_cols = width // 2 + units * tensor_count
    own_qkv, own_rest = whole_call(
        take_halves,
        "take_halves",
        info,
        [enc_qkv, enc_out, enc_up, enc_down],
        (shape_of((share, 3 * width // 2)), shape_of((share, middle_cols + width))),
        limit=4,
    )
    rest_ring = short_relay(own_rest)
    qkv_block = whole_call(
        join_blocks,
        "join_qkv",
        info,
        short_ring(own_qkv),
        shape_of((SIDE, share, 3 * width // 2)),
        limit=6,
        after=rest_ring[1:3],
    )
    middle_block, lower_block = whole_call(
        join_rest,
        "join_rest",
        info,
        rest_ring,
        (shape_of((SIDE, share, middle_cols)), shape_of((SIDE, share, width))),
        limit=8,
    )
    other_tokens = to_core(own_tokens)
    token_pieces = whole_call(
        both_rows,
        "both_rows",
        info,
        [own_tokens, other_tokens],
        shape_of((tensor_count, 2 * spans * span_size, share)),
    )
    all_rows = 2 * spans * span_size

    def ring(block, relay):
        left = to_ring(block, 2, 1)
        right = to_ring(block, 2, -1)
        opposite = to_ring(left, 2, 1) if relay == 1 else to_ring(right, 2, -1)
        return [block, left, right, opposite]

    qkv = ring(qkv_block, 1)
    middle_down, _ = lax.optimization_barrier((middle_block, qkv[2]))
    middle_up, _ = lax.optimization_barrier((middle_block, qkv[3]))
    right = to_ring(middle_down, 2, -1)
    middle = [middle_block, to_ring(middle_up, 2, 1), right, to_ring(right, 2, -1)]
    lower_block, _ = lax.optimization_barrier((lower_block, right))
    lower = ring(lower_block, 1)

    share_cols = model_width // tensor_count
    dealt_shape = (SIDE, proj_out.shape[0], share_cols // 2)
    dealt = whole_call(
        deal_columns,
        "deal_columns",
        info,
        [proj_out],
        (shape_of(dealt_shape),) * 4,
        limit=8,
        after=[qkv[1]],
    )
    dealt = [dealt[0]] + [
        to_ring(part, 1, distance) for part, distance in zip(dealt[1:], (1, -1, 2))
    ]
    dealt = whole_call(
        deal_again, "deal_again", info, dealt, (shape_of(dealt_shape),) * 4, limit=8
    )
    dealt = [dealt[0]] + [
        to_ring(part, 2, distance) for part, distance in zip(dealt[1:], (1, -1, 2))
    ]
    proj_mine = whole_call(
        join_blocks, "join_proj", info, dealt, shape_of((SIDE,) + dealt_shape), limit=8
    )
    proj_other = to_core(proj_mine)

    context = whole_call(
        span_attention,
        "span_attention",
        info,
        [token_pieces, *qkv],
        shape_of((tensor_count // 2, all_rows, share)),
        [pltpu.VMEM((all_rows, 3 * width // 2), jnp.bfloat16)],
        flops=2 * all_rows * width * 3 * width // 2,
    )
    attended = whole_call(
        context_out,
        "context_out",
        info,
        [context, to_core(context), *middle],
        shape_of((all_rows, width // 2)),
        [pltpu.VMEM((tensor_count, all_rows, share), jnp.bfloat16)],
        flops=2 * all_rows * width * width // 2,
    )
    first_out, inner = whole_call(
        norm_up,
        "norm_up",
        info,
        [own_tokens, other_tokens, attended, to_core(attended), *middle],
        (shape_of((all_rows, width)), shape_of((tensor_count, all_rows, units))),
        [
            pltpu.VMEM((tensor_count, all_rows, share), jnp.bfloat16),
            pltpu.VMEM((all_rows, width), jnp.bfloat16),
        ],
        flops=2 * all_rows * width * width,
    )
    kept, sent = whole_call(
        down,
        "down",
        info,
        [inner, first_out, *lower],
        (
            shape_of((all_rows // 2, width), jnp.float32),
            shape_of((all_rows // 2, width)),
        ),
        [pltpu.VMEM((all_rows, width), jnp.float32)],
        flops=2 * all_rows * width * width,
    )
    outgoing = whole_call(
        norm_pool,
        "norm_pool",
        info,
        [kept, to_core(sent), pick],
        shape_of((seq_count, tensor_count, width // 128, 128)),
        [pltpu.VMEM((seq_count, width // 128, 128), jnp.float32)],
    )
    arrived = lax.all_to_all(
        outgoing.reshape(device_count, width // 128, 128), AXES, 0, 0
    )

    own_cols = whole_call(
        embed,
        "embed",
        info,
        [arrived, order, proj_in, proj_mine, proj_other],
        shape_of((rows, share_cols)),
        [
            pltpu.VMEM((device_count, width // 128, 128), jnp.float32),
            pltpu.VMEM((tensor_count, rows, proj_out.shape[0]), jnp.bfloat16),
        ],
        flops=2 * rows * width * (width + share_cols),
    )
    first_block = whole_call(
        join_blocks,
        "join_columns",
        info,
        short_ring(own_cols),
        shape_of((SIDE, rows, share_cols)),
        limit=4,
    )
    embedded = ring(first_block, 1)

    query_cols = q_weight.shape[1]
    kv_cols = key_value_weight.shape[2]
    key_start = tensor_index * kv_cols % HEAD_WIDTH
    key_cosine = lax.dynamic_slice_in_dim(cosine, key_start, kv_cols, 1)
    key_sine = lax.dynamic_slice_in_dim(sine, key_start, kv_cols, 1)
    parts = 8
    gain = norm_gain.reshape(tensor_count, 1, share_cols)
    kv_pair = key_value_weight.transpose(0, 2, 1).reshape(2 * kv_cols, model_width)
    sums = (
        shape_of((rows, query_cols), jnp.float32),
        shape_of((rows, 2 * kv_cols), jnp.float32),
        shape_of((rows, 1), jnp.float32),
    )
    block_flops = 2 * rows * model_width // SIDE * (query_cols + 2 * kv_cols)
    totals = whole_call(
        functools.partial(project, starts=(0,), count=1),
        "project_own",
        info,
        [embedded[0], gain, q_weight, kv_pair],
        sums,
        flops=block_flops,
    )
    totals = whole_call(
        functools.partial(project, starts=(1, 2), count=2),
        "project_near",
        info,
        [embedded[1], embedded[2], gain, q_weight, kv_pair, *totals],
        sums,
        flops=2 * block_flops,
    )
    own_kv, scale = whole_call(
        last_keys,
        "last_keys",
        info,
        [
            embedded[3],
            gain,
            kv_pair,
            totals[1],
            totals[2],
            key_cosine,
            key_sine,
            swap[:kv_cols, :kv_cols],
        ],
        (shape_of((2, rows, kv_cols)), shape_of((rows, 1), jnp.float32)),
    )
    partner_kv = lax.ppermute(
        own_kv, "tensor", [(index, index ^ 1) for index in range(tensor_count)]
    )
    query = whole_call(
        last_queries,
        "last_queries",
        info,
        [embedded[3], gain, q_weight, totals[0], scale, cosine, sine, swap],
        shape_of((rows, query_cols)),
        flops=block_flops,
    )
    partial = pl.pallas_call(
        attend_out,
        name="attend_out",
        out_shape=shape_of((rows, model_width)),
        in_specs=[SMEM, VMEM, VMEM, VMEM, VMEM, VMEM],
        out_specs=pl.BlockSpec(memory_space=pltpu.HBM),
        scratch_shapes=[
            pltpu.VMEM((rows, query_cols), jnp.bfloat16),
            pltpu.VMEM((rows, model_width), jnp.bfloat16),
            pltpu.SemaphoreType.DMA((parts,)),
        ],
        compiler_params=pltpu.CompilerParams(vmem_limit_bytes=16 * MIB),
    )(info, query, own_kv, partner_kv, allowed, out_weight)
    terms = lax.all_to_all(
        partial.reshape(tensor_count, own_rows, model_width), "tensor", 0, 0
    )
    own_embedded = [
        lax.dynamic_slice_in_dim(block, tensor_index * own_rows, own_rows, 1) for block in embedded
    ]
    return whole_call(
        finish, "finish", live_info, [terms, *own_embedded], shape_of((own_rows, model_width))
    )


def solution(mesh):
    return jax.shard_map(
        local,
        mesh=mesh,
        in_specs=(
            P(("seq", "tensor"), None, None),
            P(),
            P(),
            P(),
            P(),
            P("tensor", None),
            P("tensor", None),
            P("tensor", None),
            P("tensor", None),
            P(),
            P("tensor", None),
            P(),
            P(None, "tensor"),
            P(None, None, "tensor"),
            P("tensor", None),
        ),
        out_specs=P(("seq", "tensor"), None),
        check_vma=False,
    )
```

```python
import functools
import math

import jax
import jax.numpy as jnp
from jax import lax
from jax.experimental import pallas as pl
from jax.experimental.pallas import tpu as pltpu
from jax.sharding import PartitionSpec as P

QUERY_HEAD_COUNT = 64
KEY_VALUE_HEADS = 8
HEAD_WIDTH = 128
EH = 16
CPP = 16
SPAN_LIMIT = 128
SIDE = 4
AXES = ("seq", "tensor")


def device_id(plane, core, x, y):
    return ((plane * 2 + core) * SIDE + x) * SIDE + y


def every_device():
    return [
        (plane, core, x, y)
        for plane in range(SIDE)
        for core in range(2)
        for x in range(SIDE)
        for y in range(SIDE)
    ]


def first_axis_is_y(core, phase):
    return (core == 0) == (phase == 1)


def ring_pairs(phase, distance):
    pairs = []
    for plane, core, x, y in every_device():
        if first_axis_is_y(core, phase):
            target = device_id(plane, core, x, (y + distance) % SIDE)
        else:
            target = device_id(plane, core, (x + distance) % SIDE, y)
        pairs.append((device_id(plane, core, x, y), target))
    return pairs


def ring_groups(phase):
    groups = []
    for plane in range(SIDE):
        for core in range(2):
            for fixed in range(SIDE):
                groups.append(
                    [
                        device_id(plane, core, fixed, moving)
                        if first_axis_is_y(core, phase)
                        else device_id(plane, core, moving, fixed)
                        for moving in range(SIDE)
                    ]
                )
    return groups


def to_ring(value, phase, distance):
    return lax.ppermute(value, AXES, ring_pairs(phase, distance))


def to_core(value):
    return lax.ppermute(value, "seq", [(index, index ^ 1) for index in range(8)])


def short_ring(block):
    return [block] + [to_ring(block, 1, distance) for distance in (1, -1, 2)]


def short_relay(block):
    left = to_ring(block, 1, 1)
    right = to_ring(block, 1, -1)
    return [block, left, right, to_ring(right, 1, -1)]


VMEM = pl.BlockSpec(memory_space=pltpu.VMEM)
SMEM = pl.BlockSpec(memory_space=pltpu.SMEM)
ANYWHERE = pl.BlockSpec(memory_space=pl.ANY)
MIB = 2**20


def shape_of(shape, dtype=jnp.bfloat16):
    return jax.ShapeDtypeStruct(shape, dtype)


def whole_call(body, name, info, arrays, outs, scratch=(), limit=12, flops=0, far=(), after=()):
    count = len(arrays) + len(far)

    def run(*refs):
        body(*refs[: 1 + count], *refs[1 + count + len(after) :])

    moved = sum(array.size * array.dtype.itemsize for array in arrays)
    return pl.pallas_call(
        run,
        name=name,
        out_shape=outs,
        in_specs=[SMEM] + [VMEM] * len(arrays) + [ANYWHERE] * (len(far) + len(after)),
        out_specs=jax.tree.map(lambda _: VMEM, outs),
        scratch_shapes=list(scratch),
        compiler_params=pltpu.CompilerParams(vmem_limit_bytes=limit * MIB),
        cost_estimate=pl.CostEstimate(flops=flops, bytes_accessed=moved, transcendentals=0),
    )(info, *arrays, *far, *after)


def dot32(left, right):
    return jnp.dot(left, right, preferred_element_type=jnp.float32)


def dot_last(left, right):
    return lax.dot_general(
        left, right, (((1,), (1,)), ((), ())), preferred_element_type=jnp.float32
    )


def gelu_exact(values):
    return 0.5 * values * (1.0 + lax.erf(values * (0.5**0.5)))


def take_qkv(info, weight, out):
    cols = weight.shape[1] // 6
    for part in range(3):
        start = pl.multiple_of((2 * part + info[16]) * cols, cols)
        out[:, part * cols : (part + 1) * cols] = weight[:, pl.ds(start, cols)]


def take_halves(info, qkv, out_weight, up_weight, down_weight, qkv_out, rest_out):
    take_qkv(info, qkv, qkv_out)
    take_rest(info, out_weight, up_weight, down_weight, rest_out)


def take_rest(info, out_weight, up_weight, down_weight, out):
    core = info[16]
    rows, width = out_weight.shape
    cols = width // 2
    units = down_weight.shape[0] // 2
    out[:, :cols] = out_weight[:, pl.ds(pl.multiple_of(core * cols, cols), cols)]
    at = cols
    for pair in range(up_weight.shape[1] // (4 * units)):
        halves = []
        for step in range(2):
            low = (2 * pair + step) * 2 * units
            halves.append(
                jnp.where(
                    core == 0,
                    up_weight[:, low : low + units].astype(jnp.float32),
                    up_weight[:, low + units : low + 2 * units].astype(jnp.float32),
                )
            )
        piece = jnp.concatenate(halves, axis=1).astype(jnp.bfloat16)
        out[:, at : at + 2 * units] = piece
        at += 2 * units
    out[:, at:] = down_weight[pl.ds(pl.multiple_of(core * units, units), units), :]


def join_blocks(info, own, left, right, opposite, out):
    for index, block in enumerate((own, left, right, opposite)):
        out[index] = block[...]


def join_middle(info, own, left, right, opposite, out):
    for index, block in enumerate((own, left, right, opposite)):
        out[index] = block[:, : out.shape[2]]


def join_lower(info, own, left, right, opposite, out):
    for index, block in enumerate((own, left, right, opposite)):
        out[index] = block[:, block.shape[1] - out.shape[2] :]


def deal_columns(info, weight, *outs):
    core, near = info[16], info[19]
    cols = outs[0].shape[2]
    for out, distance in zip(outs, (0, 1, SIDE - 1, 2)):
        target = lax.rem(near + distance, SIDE)
        for index in range(SIDE):
            shard = jnp.where(core == 0, SIDE * index + target, SIDE * target + index)
            start = pl.multiple_of((2 * shard + core) * cols, cols)
            out[index] = weight[:, pl.ds(start, cols)]


def deal_again(info, own, left, right, opposite, *outs):
    far = info[20]
    for out, distance in zip(outs, (0, 1, SIDE - 1, 2)):
        target = lax.rem(far + distance, SIDE)
        for index, block in enumerate((own, left, right, opposite)):
            out[index] = block[target]


def both_rows(info, mine, other, pieces_out):
    half, width = mine.shape
    core = info[16]
    piece = pieces_out.shape[2]
    near = pl.ds(pl.multiple_of(core * half, half), half)
    far = pl.ds(pl.multiple_of((1 - core) * half, half), half)
    for index in range(width // piece):
        pieces_out[index, near, :] = mine[:, index * piece : (index + 1) * piece]
        pieces_out[index, far, :] = other[:, index * piece : (index + 1) * piece]


def ring_dot(info, pieces, blocks, low, high):
    total = None
    for at, block in enumerate(blocks):
        act = jnp.concatenate([pieces[info[4 * at + step]] for step in range(SIDE)], axis=1)
        weight = block[:, :, low:high].reshape(act.shape[1], high - low)
        part = dot32(act, weight)
        total = part if total is None else total + part
    return total


def masked_softmax(scores, seen, size):
    scores = [jnp.where(seen, score / math.sqrt(size), -1e30) for score in scores]
    tops = [jnp.max(score, axis=1, keepdims=True) for score in scores]
    powers = [jnp.exp(score - top) for score, top in zip(scores, tops)]
    sums = [jnp.sum(power, axis=1, keepdims=True) for power in powers]
    return [(power / total).astype(jnp.bfloat16) for power, total in zip(powers, sums)]


def span_qkv(info, pieces, w0, w1, w2, w3, mixed, mark):
    mixed[...] = ring_dot(info, pieces, (w0, w1, w2, w3), 0, w0.shape[2]).astype(jnp.bfloat16)
    mark[...] = jnp.zeros_like(mark)


def span_attention(info, mixed, context):
    third = mixed.shape[1] // 3
    size = context.shape[2]
    half = mixed.shape[0] // 2
    span = 16
    row = lax.broadcasted_iota(jnp.int32, (half, half), 0) // span
    col = lax.broadcasted_iota(jnp.int32, (half, half), 1) // span
    same = row == col
    heads = third // size
    units = [
        (head, slice(part * half, (part + 1) * half)) for head in range(heads) for part in range(2)
    ]
    scores = [
        lax.dot_general(
            mixed[rows, head * size : (head + 1) * size],
            mixed[rows, third + head * size : third + (head + 1) * size],
            (((1,), (1,)), ((), ())),
            preferred_element_type=jnp.float32,
        )
        for head, rows in units
    ]
    probs = masked_softmax(scores, same, size)
    for (head, rows), prob in zip(units, probs):
        value = mixed[rows, 2 * third + head * size : 2 * third + (head + 1) * size]
        context[head, rows, :] = dot32(prob, value).astype(jnp.bfloat16)


def context_out(info, mine, other, tokens, w0, w1, w2, w3, attended, pieces):
    heads = mine.shape[0]
    core = info[16]
    pieces[pl.ds(core * heads, heads)] = mine[...]
    pieces[pl.ds((1 - core) * heads, heads)] = other[...]
    cols = attended.shape[1]
    residual = jnp.concatenate([tokens[core * heads + index] for index in range(heads)], axis=1)
    total = ring_dot(info, pieces, (w0, w1, w2, w3), 0, cols)
    attended[...] = (residual.astype(jnp.float32) + total).astype(jnp.bfloat16)


def norm_up(info, mine, other, w0, w1, w2, w3, first_out, inner, pieces):
    core = info[16]
    cols = mine.shape[1]
    width = 2 * cols
    near = mine[...].astype(jnp.float32)
    far = other[...].astype(jnp.float32)
    low = jnp.where(core == 0, near, far)
    high = jnp.where(core == 0, far, near)
    mean = (jnp.sum(low, 1, keepdims=True) + jnp.sum(high, 1, keepdims=True)) / width
    low, high = low - mean, high - mean
    var = (jnp.sum(low * low, 1, keepdims=True) + jnp.sum(high * high, 1, keepdims=True)) / width
    scale = lax.rsqrt(var + 1e-05)
    first_out[:, :cols] = (low * scale).astype(jnp.bfloat16)
    first_out[:, cols:] = (high * scale).astype(jnp.bfloat16)
    size = pieces.shape[2]
    for index in range(pieces.shape[0]):
        pieces[index] = first_out[:, index * size : (index + 1) * size]
    total = ring_dot(info, pieces, (w0, w1, w2, w3), cols, w0.shape[2])
    act = gelu_exact(total).astype(jnp.bfloat16)
    unit = inner.shape[2]
    for index in range(inner.shape[0]):
        inner[index] = act[:, index * unit : (index + 1) * unit]


def down(info, inner, first_out, w0, w1, w2, w3, kept, sent, total):
    core = info[16]
    total[...] = ring_dot(info, inner, (w0, w1, w2, w3), 0, w0.shape[2])
    half = kept.shape[0]
    rows = pl.ds(pl.multiple_of(core * half, half), half)
    kept[...] = total[rows, :] + first_out[rows, :].astype(jnp.float32)
    sent[...] = total[pl.ds(pl.multiple_of((1 - core) * half, half), half), :].astype(jnp.bfloat16)


def norm_pool(info, kept, arrived, pick, out, lanes):
    half, width = kept.shape
    values = kept[...] + arrived[...].astype(jnp.float32)
    mean = jnp.mean(values, axis=1, keepdims=True)
    values = values - mean
    values = values * lax.rsqrt(jnp.mean(values * values, axis=1, keepdims=True) + 1e-05)
    spans = pick.shape[1]
    pooled = jnp.mean(values.reshape(spans, half // spans, width), axis=1).astype(jnp.bfloat16)
    by_slot = dot32(pick[...], pooled)
    for index in range(width // 128):
        lanes[:, index, :] = by_slot[:, index * 128 : (index + 1) * 128]
    out[...] = jnp.broadcast_to(lanes[...].astype(jnp.bfloat16)[:, None], out.shape)


def embed(info, arrived, order, proj_in, mine, other, out, lanes, pieces):
    core = info[16]
    lanes[...] = arrived[...].astype(jnp.float32)
    columns = [
        dot32(order[...], lanes[:, index, :].astype(jnp.bfloat16)).astype(jnp.bfloat16)
        for index in range(lanes.shape[1])
    ]
    arranged = jnp.concatenate(columns, axis=1)
    hidden = gelu_exact(dot32(arranged, proj_in[...])).astype(jnp.bfloat16)
    units, cols = mine.shape[2:]
    for index in range(pieces.shape[0]):
        pieces[index] = hidden[:, index * units : (index + 1) * units]
    near, far = None, None
    for at in range(SIDE):
        act = jnp.concatenate([pieces[info[SIDE * at + step]] for step in range(SIDE)], axis=1)
        term = dot32(act, mine[at].reshape(SIDE * units, cols))
        near = term if near is None else near + term
        act = jnp.concatenate([pieces[info[22 + SIDE * at + step]] for step in range(SIDE)], axis=1)
        term = dot32(act, other[at].reshape(SIDE * units, cols))
        far = term if far is None else far + term
    out[:, :cols] = jnp.where(core == 0, near, far).astype(jnp.bfloat16)
    out[:, cols:] = jnp.where(core == 0, far, near).astype(jnp.bfloat16)


def shard_rows(info, weight, buffer, sems, at, step, slot):
    depth = buffer.shape[1]
    start = pl.multiple_of(info[SIDE * at + step] * depth, depth)
    return pltpu.make_async_copy(
        weight.at[pl.ds(start, depth), :], buffer.at[slot], sems.at[slot]
    )


def project(info, *refs, starts, count):
    blocks, refs = refs[:count], refs[count:]
    gain, kv_weight = refs[:2]
    before = refs[2:5] if len(refs) > 8 else None
    q_weight, q_total, kv_total, square, buffer, sems = refs[-6:]
    depth = blocks[0].shape[2]
    places = [(at, step) for at in starts for step in range(SIDE)]
    copies = [
        shard_rows(info, q_weight, buffer, sems, at, step, slot)
        for slot, (at, step) in enumerate(places)
    ]
    for copy in copies:
        copy.start()
    queries, both, squares = None, None, None
    for slot, (at, step) in enumerate(places):
        shard = info[SIDE * at + step]
        wide = blocks[slot // SIDE][step].astype(jnp.float32)
        act = (wide * gain[shard]).astype(jnp.bfloat16)
        span = pl.ds(pl.multiple_of(shard * depth, depth), depth)
        kv_term = dot_last(act, kv_weight[:, span])
        term = jnp.sum(wide * wide, axis=1, keepdims=True)
        copies[slot].wait()
        q_term = dot32(act, buffer[slot])
        queries = q_term if queries is None else queries + q_term
        both = kv_term if both is None else both + kv_term
        squares = term if squares is None else squares + term
    if before is not None:
        queries, both, squares = queries + before[0][...], both + before[1][...], squares + before[2][...]
    q_total[...] = queries
    kv_total[...] = both
    square[...] = squares


def turn(values, cosine, sine, swap):
    turned = jnp.dot(
        values, swap, preferred_element_type=jnp.float32, precision=lax.Precision.HIGHEST
    )
    return values * cosine + turned * sine


def last_keys(info, block, gain, kv_weight, kv_before, sq_before, cosine, sine, swap, out, scale):
    depth = block.shape[2]
    both = kv_before[...]
    squares = sq_before[...]
    for step in range(SIDE):
        shard = info[SIDE * 3 + step]
        wide = block[step].astype(jnp.float32)
        act = (wide * gain[shard]).astype(jnp.bfloat16)
        span = pl.ds(pl.multiple_of(shard * depth, depth), depth)
        both += dot_last(act, kv_weight[:, span])
        squares += jnp.sum(wide * wide, axis=1, keepdims=True)
    factor = lax.rsqrt(squares / (depth * SIDE * SIDE) + 1e-05)
    scale[...] = factor
    both = both * factor
    cols = out.shape[2]
    out[0] = turn(both[:, :cols], cosine[...], sine[...], swap[...]).astype(jnp.bfloat16)
    out[1] = both[:, cols:].astype(jnp.bfloat16)


def last_queries(
    info, block, gain, q_before, scale, cosine, sine, swap, q_weight, out, buffer, sems
):
    copies = [shard_rows(info, q_weight, buffer, sems, 3, step, step) for step in range(SIDE)]
    for copy in copies:
        copy.start()
    total = q_before[...]
    for step in range(SIDE):
        shard = info[SIDE * 3 + step]
        act = (block[step].astype(jnp.float32) * gain[shard]).astype(jnp.bfloat16)
        copies[step].wait()
        total += dot32(act, buffer[step])
    for head in range(out.shape[1] // HEAD_WIDTH):
        lanes = slice(head * HEAD_WIDTH, (head + 1) * HEAD_WIDTH)
        query = total[:, lanes] * scale[...]
        out[:, lanes] = turn(query, cosine[...], sine[...], swap[...]).astype(jnp.bfloat16)


def attend_out(info, query, mine, partner, allowed, deal, weight_hbm, *refs):
    outs, context, weight, sems = refs[:4], refs[4], refs[5], refs[6]
    step = weight.shape[1] // sems.shape[0]

    def fetch(part):
        span = pl.ds(part * step, step)
        return pltpu.make_async_copy(weight_hbm.at[:, span], weight.at[:, span], sems.at[part])

    for part in range(sems.shape[0]):
        fetch(part).start()
    odd = info[17] == 1
    own = mine[...].astype(jnp.float32)
    far = partner[...].astype(jnp.float32)
    low = jnp.where(odd, far, own)
    high = jnp.where(odd, own, far)
    both = jnp.concatenate([low, high], axis=2).astype(jnp.bfloat16)
    key, value = both[0], both[1]
    heads = [
        slice(head * HEAD_WIDTH, (head + 1) * HEAD_WIDTH)
        for head in range(query.shape[1] // HEAD_WIDTH)
    ]
    scores = [
        lax.dot_general(
            query[:, lanes], key, (((1,), (1,)), ((), ())), preferred_element_type=jnp.float32
        )
        for lanes in heads
    ]
    for lanes, prob in zip(heads, masked_softmax(scores, allowed[...] > 0, HEAD_WIDTH)):
        context[:, lanes] = dot32(prob, value).astype(jnp.bfloat16)
    dealt = dot32(deal[...], context[...]).astype(jnp.bfloat16)
    rows = outs[0].shape[0]
    for part in range(sems.shape[0]):
        start = part * step
        fetch(part).wait()
        result = dot32(dealt, weight[:, start : start + step])
        for index, out in enumerate(outs):
            piece = result[index * rows : (index + 1) * rows]
            out[:, start : start + step] = piece.astype(jnp.bfloat16)


def add_ring(info, own, left, right, opposite, kept, *sent):
    rows = kept.shape[0]
    step = 1024
    for start in range(0, own.shape[1], step):
        lanes = slice(start, start + step)
        total = own[:, lanes].astype(jnp.float32)
        for block in (left, right, opposite):
            total = total + block[:, lanes].astype(jnp.float32)
        kept[:, lanes] = total[:rows]
        for index, out in enumerate(sent):
            piece = total[(index + 1) * rows : (index + 2) * rows]
            out[:, lanes] = piece.astype(jnp.bfloat16)


def finish(info, kept, left, right, opposite, *refs):
    own, out = refs[:-1], refs[-1]
    rows, cols = own[0].shape[1:]
    live = info[18] + lax.broadcasted_iota(jnp.int32, (rows, cols), 0) < info[21]
    for at, block in enumerate(own):
        for step in range(SIDE):
            lanes = pl.ds(pl.multiple_of(info[SIDE * at + step] * cols, cols), cols)
            total = kept[:, lanes] + block[step].astype(jnp.float32)
            for term in (left, right, opposite):
                total = total + term[:, lanes].astype(jnp.float32)
            out[:, lanes] = jnp.where(live, total, 0.0).astype(jnp.bfloat16)


def visibility(masks, live_count):
    positions = jnp.arange(SPAN_LIMIT)
    passage = positions // CPP
    expanded = jnp.repeat(jnp.repeat(masks, CPP, axis=0), CPP, axis=1) > 0
    same_passage = passage[:, None] == passage[None, :]
    earlier = positions[None, :] <= positions[:, None]
    key_live = positions[None, :] < live_count
    diagonal = positions[:, None] == positions[None, :]
    return diagonal | earlier & key_live & (same_passage | expanded)


def local(
    span_tokens,
    enc_dest,
    passages,
    req_slot,
    block_mask,
    enc_qkv,
    enc_out,
    enc_up,
    enc_down,
    proj_in,
    proj_out,
    norm_gain,
    q_weight,
    key_value_weight,
    out_weight,
):
    tensor_count = lax.axis_size("tensor")
    seq_count = lax.axis_size("seq")
    tensor_index = lax.axis_index("tensor")
    seq_index = lax.axis_index("seq")
    core = seq_index % 2
    device_count = tensor_count * seq_count
    rows = SPAN_LIMIT
    own_rows = rows // tensor_count
    spans, span_size, width = span_tokens.shape
    model_width = proj_out.shape[1]
    share = enc_qkv.shape[0]
    x_index, y_index = tensor_index // SIDE, tensor_index % SIDE

    steps = jnp.array([0, SIDE - 1, 1, 2])
    outer, inside = jnp.repeat(steps, SIDE), jnp.tile(steps, SIDE)
    by_x = SIDE * ((x_index + outer) % SIDE) + (y_index + inside) % SIDE
    by_y = SIDE * ((x_index + inside) % SIDE) + (y_index + outer) % SIDE
    shards = jnp.where(core == 0, by_x, by_y)
    near = jnp.where(core == 0, y_index, x_index)
    far = jnp.where(core == 0, x_index, y_index)
    scalars = jnp.stack([core, tensor_index % 2, tensor_index * own_rows, near, far])
    other_shards = jnp.where(core == 0, by_y, by_x)
    info = jnp.concatenate([shards, scalars, core[None], other_shards]).astype(jnp.int32)

    ahead = jnp.array([0, 1, SIDE - 1, 2])
    outer, inside = jnp.repeat(ahead, SIDE), jnp.tile(ahead, SIDE)
    owner_x = SIDE * ((x_index + outer) % SIDE) + (y_index + inside) % SIDE
    owner_y = SIDE * ((x_index + inside) % SIDE) + (y_index + outer) % SIDE
    owners = jnp.where(core == 0, owner_x, owner_y)
    from_row = (owners[:, None] * own_rows + jnp.arange(own_rows)[None, :]).reshape(-1)
    deal = (from_row[:, None] == jnp.arange(rows)[None, :]).astype(jnp.bfloat16)

    requests = jnp.arange(req_slot.shape[0])
    dest_slot = jnp.sum(
        jnp.where(enc_dest[:, None] // SPAN_LIMIT == requests[None, :], req_slot[None, :], 0), axis=1
    ).reshape(device_count, own_rows)
    dest_place = (enc_dest % SPAN_LIMIT).reshape(device_count, own_rows)
    own_slots = lax.dynamic_slice_in_dim(
        dest_slot, seq_index * tensor_count + tensor_index, 1, 0
    )
    pick = (jnp.arange(seq_count)[:, None] == own_slots).astype(jnp.bfloat16)
    place_of = jnp.sum(jnp.where(dest_slot == seq_index, dest_place, 0), axis=1)
    order = (jnp.arange(rows)[:, None] == place_of[None, :]).astype(jnp.bfloat16)
    chosen = jnp.sum(jnp.where(req_slot == seq_index, requests, 0))
    live_count = jnp.sum(jnp.where(requests == chosen, passages, 0)) * CPP
    masks = jnp.sum(
        jnp.where(requests[:, None, None] == chosen, block_mask, 0), axis=0
    )
    allowed = visibility(masks, live_count).astype(jnp.float32)
    live_info = jnp.concatenate([info[:21], live_count[None]]).astype(jnp.int32)

    positions = jnp.arange(rows).astype(jnp.float32)
    lane = jnp.arange(HEAD_WIDTH)
    frequency = jnp.exp(
        -(2.0 * (lane // 2).astype(jnp.float32) / HEAD_WIDTH) * math.log(500000.0)
    )
    angles = positions[:, None] * frequency[None, :]
    cosine, sine = jnp.cos(angles), jnp.sin(angles)
    swap = jnp.where(
        (lane[:, None] ^ 1) == lane[None, :], jnp.where(lane[None, :] % 2 == 0, -1.0, 1.0), 0.0
    ).astype(jnp.float32)

    own_tokens = span_tokens.reshape(spans * span_size, width)
    other_tokens = to_core(own_tokens)
    token_pieces = whole_call(
        both_rows,
        "both_rows",
        info,
        [own_tokens, other_tokens],
        shape_of((tensor_count, 2 * spans * span_size, share)),
    )
    units = enc_down.shape[0] // 2
    middle_cols = width // 2 + units * tensor_count
    own_qkv, own_rest = whole_call(
        take_halves,
        "take_halves",
        info,
        [enc_qkv, enc_out, enc_up, enc_down],
        (shape_of((share, 3 * width // 2)), shape_of((share, middle_cols + width))),
        limit=60,
    )
    rest_ring = short_relay(own_rest)
    qkv_block = whole_call(
        join_blocks,
        "join_qkv",
        info,
        short_ring(own_qkv),
        shape_of((SIDE, share, 3 * width // 2)),
        limit=6,
        after=rest_ring[1:3],
    )
    all_rows = 2 * spans * span_size

    qkv = [qkv_block] + [to_ring(qkv_block, 2, distance) for distance in (1, -1, 2)]

    share_cols = model_width // tensor_count
    dealt_shape = (SIDE, proj_out.shape[0], share_cols // 2)
    dealt = whole_call(
        deal_columns,
        "deal_columns",
        info,
        [proj_out],
        (shape_of(dealt_shape),) * 4,
        limit=8,
        after=[qkv_block],
    )
    dealt = [dealt[0]] + [
        to_ring(part, 1, distance) for part, distance in zip(dealt[1:], (1, -1, 2))
    ]

    dealt = whole_call(
        deal_again, "deal_again", info, dealt, (shape_of(dealt_shape),) * 4, limit=8
    )
    dealt = [dealt[0]] + [
        to_ring(part, 2, distance) for part, distance in zip(dealt[1:], (1, -1, 2))
    ]
    proj_mine = whole_call(
        join_blocks, "join_proj", info, dealt, shape_of((SIDE,) + dealt_shape), limit=8
    )
    proj_other = to_core(proj_mine)

    mixed, mark = whole_call(
        span_qkv,
        "span_qkv",
        info,
        [token_pieces, *qkv],
        (shape_of((all_rows, 3 * width // 2)), shape_of((8, 128), jnp.float32)),
        flops=2 * all_rows * width * 3 * width // 2,
        after=[proj_mine, *rest_ring],
    )
    middle_block = whole_call(
        join_middle,
        "join_middle",
        info,
        rest_ring,
        shape_of((SIDE, share, middle_cols)),
        limit=8,
        after=[mark],
    )
    right = to_ring(middle_block, 2, -1)
    middle = [middle_block, to_ring(middle_block, 2, 1), right, to_ring(right, 2, -1)]
    lower_block = whole_call(
        join_lower,
        "join_lower",
        info,
        rest_ring,
        shape_of((SIDE, share, width)),
        limit=8,
        after=[right],
    )
    left = to_ring(lower_block, 2, 1)
    lower = [lower_block, left, to_ring(lower_block, 2, -1), to_ring(left, 2, 1)]

    context = whole_call(
        span_attention,
        "span_attention",
        info,
        [mixed],
        shape_of((tensor_count // 2, all_rows, share)),
    )
    attended = whole_call(
        context_out,
        "context_out",
        info,
        [context, to_core(context), token_pieces, *middle],
        shape_of((all_rows, width // 2)),
        [pltpu.VMEM((tensor_count, all_rows, share), jnp.bfloat16)],
        flops=2 * all_rows * width * width // 2,
    )
    first_out, inner = whole_call(
        norm_up,
        "norm_up",
        info,
        [attended, to_core(attended), *middle],
        (shape_of((all_rows, width)), shape_of((tensor_count, all_rows, units))),
        [pltpu.VMEM((tensor_count, all_rows, share), jnp.bfloat16)],
        flops=2 * all_rows * width * width,
    )
    kept, sent = whole_call(
        down,
        "down",
        info,
        [inner, first_out, *lower],
        (
            shape_of((all_rows // 2, width), jnp.float32),
            shape_of((all_rows // 2, width)),
        ),
        [pltpu.VMEM((all_rows, width), jnp.float32)],
        flops=2 * all_rows * width * width,
    )
    outgoing = whole_call(
        norm_pool,
        "norm_pool",
        info,
        [kept, to_core(sent), pick],
        shape_of((seq_count, tensor_count, width // 128, 128)),
        [pltpu.VMEM((seq_count, width // 128, 128), jnp.float32)],
    )
    arrived = lax.all_to_all(
        outgoing.reshape(device_count, width // 128, 128), AXES, 0, 0
    )

    own_cols = whole_call(
        embed,
        "embed",
        info,
        [arrived, order, proj_in, proj_mine, proj_other],
        shape_of((rows, share_cols)),
        [
            pltpu.VMEM((device_count, width // 128, 128), jnp.float32),
            pltpu.VMEM((tensor_count, rows, proj_out.shape[0]), jnp.bfloat16),
        ],
        flops=2 * rows * width * (width + share_cols),
    )
    first_block = whole_call(
        join_blocks,
        "join_columns",
        info,
        short_ring(own_cols),
        shape_of((SIDE, rows, share_cols)),
        limit=4,
    )
    near_left = to_ring(first_block, 2, 1)
    near_right = to_ring(first_block, 2, -1)
    query_cols = q_weight.shape[1]
    kv_cols = key_value_weight.shape[2]
    key_start = tensor_index * kv_cols % HEAD_WIDTH
    key_cosine = lax.dynamic_slice_in_dim(cosine, key_start, kv_cols, 1)
    key_sine = lax.dynamic_slice_in_dim(sine, key_start, kv_cols, 1)
    gain = norm_gain.reshape(tensor_count, 1, share_cols)
    kv_pair = key_value_weight.transpose(0, 2, 1).reshape(2 * kv_cols, model_width)
    sums = (
        shape_of((rows, query_cols), jnp.float32),
        shape_of((rows, 2 * kv_cols), jnp.float32),
        shape_of((rows, 1), jnp.float32),
    )
    block_flops = 2 * rows * model_width // SIDE * (query_cols + 2 * kv_cols)
    totals = whole_call(
        functools.partial(project, starts=(0,), count=1),
        "project_own",
        info,
        [first_block, gain, kv_pair],
        sums,
        [
            pltpu.VMEM((SIDE, share_cols, query_cols), jnp.bfloat16),
            pltpu.SemaphoreType.DMA((SIDE,)),
        ],
        limit=56,
        far=[q_weight],
        flops=block_flops,
    )
    relayed, _ = lax.optimization_barrier((near_left, totals[2]))
    embedded = [first_block, relayed, near_right, to_ring(relayed, 2, 1)]
    totals = whole_call(
        functools.partial(project, starts=(1, 2), count=2),
        "project_near",
        info,
        [embedded[1], embedded[2], gain, kv_pair, *totals],
        sums,
        [
            pltpu.VMEM((2 * SIDE, share_cols, query_cols), jnp.bfloat16),
            pltpu.SemaphoreType.DMA((2 * SIDE,)),
        ],
        limit=56,
        far=[q_weight],
        flops=2 * block_flops,
    )
    own_kv, scale = whole_call(
        last_keys,
        "last_keys",
        info,
        [
            embedded[3],
            gain,
            kv_pair,
            totals[1],
            totals[2],
            key_cosine,
            key_sine,
            swap[:kv_cols, :kv_cols],
        ],
        (shape_of((2, rows, kv_cols)), shape_of((rows, 1), jnp.float32)),
    )
    partner_kv = lax.ppermute(
        own_kv, "tensor", [(index, index ^ 1) for index in range(tensor_count)]
    )
    query = whole_call(
        last_queries,
        "last_queries",
        info,
        [embedded[3], gain, totals[0], scale, cosine, sine, swap],
        shape_of((rows, query_cols)),
        [
            pltpu.VMEM((SIDE, share_cols, query_cols), jnp.bfloat16),
            pltpu.SemaphoreType.DMA((SIDE,)),
        ],
        limit=56,
        far=[q_weight],
        flops=block_flops,
    )
    partial = whole_call(
        attend_out,
        "attend_out",
        info,
        [query, own_kv, partner_kv, allowed, deal],
        (shape_of((rows // SIDE, model_width)),) * 4,
        [
            pltpu.VMEM((rows, query_cols), jnp.bfloat16),
            pltpu.VMEM((query_cols, model_width), jnp.bfloat16),
            pltpu.SemaphoreType.DMA((8,)),
        ],
        limit=56,
        far=[out_weight],
        flops=2 * rows * model_width * query_cols,
    )
    arrived_sums = [
        to_ring(part, 2, distance) for part, distance in zip(partial[1:], (1, -1, 2))
    ]
    kept_sum, *sent_sums = whole_call(
        add_ring,
        "add_ring",
        info,
        [partial[0], *arrived_sums],
        (shape_of((own_rows, model_width), jnp.float32),)
        + (shape_of((own_rows, model_width)),) * 3,
    )
    terms = [to_ring(part, 1, distance) for part, distance in zip(sent_sums, (1, -1, 2))]
    own_embedded = [
        lax.dynamic_slice_in_dim(block, tensor_index * own_rows, own_rows, 1) for block in embedded
    ]
    return whole_call(
        finish,
        "finish",
        live_info,
        [kept_sum, *terms, *own_embedded],
        shape_of((own_rows, model_width)),
    )


def solution(mesh):
    return jax.shard_map(
        local,
        mesh=mesh,
        in_specs=(
            P(("seq", "tensor"), None, None),
            P(),
            P(),
            P(),
            P(),
            P("tensor", None),
            P("tensor", None),
            P("tensor", None),
            P("tensor", None),
            P(),
            P("tensor", None),
            P(),
            P(None, "tensor"),
            P(None, None, "tensor"),
            P("tensor", None),
        ),
        out_specs=P(("seq", "tensor"), None),
        check_vma=False,
    )
```

```python
import functools
import math

import jax
import jax.numpy as jnp
from jax import lax
from jax.experimental import pallas as pl
from jax.experimental.pallas import tpu as pltpu
from jax.sharding import PartitionSpec as P

QUERY_HEAD_COUNT = 64
KEY_VALUE_HEADS = 8
HEAD_WIDTH = 128
EH = 16
CPP = 16
SPAN_LIMIT = 128
SIDE = 4
AXES = ("seq", "tensor")


def device_id(plane, core, x, y):
    return ((plane * 2 + core) * SIDE + x) * SIDE + y


def every_device():
    return [
        (plane, core, x, y)
        for plane in range(SIDE)
        for core in range(2)
        for x in range(SIDE)
        for y in range(SIDE)
    ]


def first_axis_is_y(core, phase):
    return (core == 0) == (phase == 1)


def ring_pairs(phase, distance):
    pairs = []
    for plane, core, x, y in every_device():
        if first_axis_is_y(core, phase):
            target = device_id(plane, core, x, (y + distance) % SIDE)
        else:
            target = device_id(plane, core, (x + distance) % SIDE, y)
        pairs.append((device_id(plane, core, x, y), target))
    return pairs


def ring_groups(phase):
    groups = []
    for plane in range(SIDE):
        for core in range(2):
            for fixed in range(SIDE):
                groups.append(
                    [
                        device_id(plane, core, fixed, moving)
                        if first_axis_is_y(core, phase)
                        else device_id(plane, core, moving, fixed)
                        for moving in range(SIDE)
                    ]
                )
    return groups


def to_ring(value, phase, distance):
    return lax.ppermute(value, AXES, ring_pairs(phase, distance))


def to_core(value):
    return lax.ppermute(value, "seq", [(index, index ^ 1) for index in range(8)])


def short_ring(block):
    return [block] + [to_ring(block, 1, distance) for distance in (1, -1, 2)]


def short_relay(block):
    left = to_ring(block, 1, 1)
    right = to_ring(block, 1, -1)
    return [block, left, right, to_ring(right, 1, -1)]


VMEM = pl.BlockSpec(memory_space=pltpu.VMEM)
SMEM = pl.BlockSpec(memory_space=pltpu.SMEM)
ANYWHERE = pl.BlockSpec(memory_space=pl.ANY)
MIB = 2**20


def shape_of(shape, dtype=jnp.bfloat16):
    return jax.ShapeDtypeStruct(shape, dtype)


def whole_call(body, name, info, arrays, outs, scratch=(), limit=12, flops=0, far=(), after=()):
    count = len(arrays) + len(far)

    def run(*refs):
        body(*refs[: 1 + count], *refs[1 + count + len(after) :])

    moved = sum(array.size * array.dtype.itemsize for array in arrays)
    return pl.pallas_call(
        run,
        name=name,
        out_shape=outs,
        in_specs=[SMEM] + [VMEM] * len(arrays) + [ANYWHERE] * (len(far) + len(after)),
        out_specs=jax.tree.map(lambda _: VMEM, outs),
        scratch_shapes=list(scratch),
        compiler_params=pltpu.CompilerParams(vmem_limit_bytes=limit * MIB),
        cost_estimate=pl.CostEstimate(flops=flops, bytes_accessed=moved, transcendentals=0),
    )(info, *arrays, *far, *after)


def dot32(left, right):
    return jnp.dot(left, right, preferred_element_type=jnp.float32)


def dot_last(left, right):
    return lax.dot_general(
        left, right, (((1,), (1,)), ((), ())), preferred_element_type=jnp.float32
    )


def gelu_exact(values):
    return 0.5 * values * (1.0 + lax.erf(values * (0.5**0.5)))


def take_qkv(info, weight, out):
    cols = weight.shape[1] // 6
    for part in range(3):
        start = pl.multiple_of((2 * part + info[16]) * cols, cols)
        out[:, part * cols : (part + 1) * cols] = weight[:, pl.ds(start, cols)]


def take_rest(info, out_weight, up_weight, down_weight, proj, up_out, down_out, kept, beyond):
    core, near = info[16], info[19]
    rows, width = out_weight.shape
    cols = width // 2
    units = down_weight.shape[0] // 2
    pieces = [out_weight[:, pl.ds(pl.multiple_of(core * cols, cols), cols)]]
    for pair in range(up_weight.shape[1] // (4 * units)):
        halves = []
        for step in range(2):
            low = (2 * pair + step) * 2 * units
            halves.append(
                jnp.where(
                    core == 0,
                    up_weight[:, low : low + units].astype(jnp.float32),
                    up_weight[:, low + units : low + 2 * units].astype(jnp.float32),
                )
            )
        pieces.append(jnp.concatenate(halves, axis=1).astype(jnp.bfloat16))
    pieces.append(down_weight[pl.ds(pl.multiple_of(core * units, units), units), :])
    at = 0
    for piece in pieces:
        for out in (up_out, down_out):
            out[:, at : at + piece.shape[1]] = piece
        at += piece.shape[1]
    block = kept.shape[1] // SIDE
    for out, start, distance in ((kept, 0, 0), (up_out, at, 1), (down_out, at, SIDE - 1), (beyond, 0, 2)):
        target = lax.rem(near + distance, SIDE)
        for index in range(SIDE):
            shard = jnp.where(core == 0, SIDE * index + target, SIDE * target + index)
            source = pl.multiple_of((2 * shard + core) * block, block)
            out[:, start + index * block : start + (index + 1) * block] = proj[:, pl.ds(source, block)]


def join_blocks(info, own, left, right, opposite, out):
    for index, block in enumerate((own, left, right, opposite)):
        out[index] = block[...]


def join_middle(info, own, left, right, opposite, out):
    for index, block in enumerate((own, left, right, opposite)):
        out[index] = block[:, : out.shape[2]]


def join_lower(info, own, left, right, opposite, kept, beyond, up_out, down_out, far_kept, far_beyond):
    far = info[20]
    block = far_kept.shape[2]
    width = up_out.shape[2] - block
    start = own.shape[1] - kept.shape[1] - width
    for index, part in enumerate((own, left, right, opposite)):
        for out in (up_out, down_out):
            out[index, :, :width] = part[:, start : start + width]
        columns, first = (part, start + width) if index in (1, 2) else (kept, 0)
        if index == 3:
            columns = beyond
        for out, at, distance in (
            (far_kept, 0, 0),
            (up_out, width, 1),
            (down_out, width, SIDE - 1),
            (far_beyond, 0, 2),
        ):
            target = lax.rem(far + distance, SIDE)
            source = pl.multiple_of(first + target * block, 128)
            out[index, :, at : at + block] = columns[:, pl.ds(source, block)]


def join_proj(info, own, left, right, opposite, out):
    block = own.shape[2]
    for index, part in enumerate((own, left, right, opposite)):
        out[index] = part[:, :, part.shape[2] - block :]


def both_rows(info, mine, other, pieces_out):
    half, width = mine.shape
    core = info[16]
    piece = pieces_out.shape[2]
    near = pl.ds(pl.multiple_of(core * half, half), half)
    far = pl.ds(pl.multiple_of((1 - core) * half, half), half)
    for index in range(width // piece):
        pieces_out[index, near, :] = mine[:, index * piece : (index + 1) * piece]
        pieces_out[index, far, :] = other[:, index * piece : (index + 1) * piece]


def ring_dot(info, pieces, blocks, low, high):
    total = None
    for at, block in enumerate(blocks):
        act = jnp.concatenate([pieces[info[4 * at + step]] for step in range(SIDE)], axis=1)
        weight = block[:, :, low:high].reshape(act.shape[1], high - low)
        part = dot32(act, weight)
        total = part if total is None else total + part
    return total


def masked_softmax(scores, seen, size):
    scores = [jnp.where(seen, score / math.sqrt(size), -1e30) for score in scores]
    tops = [jnp.max(score, axis=1, keepdims=True) for score in scores]
    powers = [jnp.exp(score - top) for score, top in zip(scores, tops)]
    sums = [jnp.sum(power, axis=1, keepdims=True) for power in powers]
    return [(power / total).astype(jnp.bfloat16) for power, total in zip(powers, sums)]


def span_qkv(info, pieces, w0, w1, w2, w3, mixed):
    mixed[...] = ring_dot(info, pieces, (w0, w1, w2, w3), 0, w0.shape[2]).astype(jnp.bfloat16)


def span_attention(info, mixed, context):
    third = mixed.shape[1] // 3
    size = context.shape[2]
    half = mixed.shape[0] // 2
    span = 16
    row = lax.broadcasted_iota(jnp.int32, (half, half), 0) // span
    col = lax.broadcasted_iota(jnp.int32, (half, half), 1) // span
    same = row == col
    heads = third // size
    units = [
        (head, slice(part * half, (part + 1) * half)) for head in range(heads) for part in range(2)
    ]
    scores = [
        lax.dot_general(
            mixed[rows, head * size : (head + 1) * size],
            mixed[rows, third + head * size : third + (head + 1) * size],
            (((1,), (1,)), ((), ())),
            preferred_element_type=jnp.float32,
        )
        for head, rows in units
    ]
    probs = masked_softmax(scores, same, size)
    for (head, rows), prob in zip(units, probs):
        value = mixed[rows, 2 * third + head * size : 2 * third + (head + 1) * size]
        context[head, rows, :] = dot32(prob, value).astype(jnp.bfloat16)


def context_out(info, mine, other, tokens, w0, w1, w2, w3, attended, pieces):
    heads = mine.shape[0]
    core = info[16]
    pieces[pl.ds(core * heads, heads)] = mine[...]
    pieces[pl.ds((1 - core) * heads, heads)] = other[...]
    cols = attended.shape[1]
    residual = jnp.concatenate([tokens[core * heads + index] for index in range(heads)], axis=1)
    total = ring_dot(info, pieces, (w0, w1, w2, w3), 0, cols)
    attended[...] = (residual.astype(jnp.float32) + total).astype(jnp.bfloat16)


def norm_up(info, mine, other, w0, w1, w2, w3, first_out, inner, pieces):
    core = info[16]
    cols = mine.shape[1]
    width = 2 * cols
    near = mine[...].astype(jnp.float32)
    far = other[...].astype(jnp.float32)
    low = jnp.where(core == 0, near, far)
    high = jnp.where(core == 0, far, near)
    mean = (jnp.sum(low, 1, keepdims=True) + jnp.sum(high, 1, keepdims=True)) / width
    low, high = low - mean, high - mean
    var = (jnp.sum(low * low, 1, keepdims=True) + jnp.sum(high * high, 1, keepdims=True)) / width
    scale = lax.rsqrt(var + 1e-05)
    first_out[:, :cols] = (low * scale).astype(jnp.bfloat16)
    first_out[:, cols:] = (high * scale).astype(jnp.bfloat16)
    size = pieces.shape[2]
    for index in range(pieces.shape[0]):
        pieces[index] = first_out[:, index * size : (index + 1) * size]
    total = ring_dot(info, pieces, (w0, w1, w2, w3), cols, w0.shape[2])
    act = gelu_exact(total).astype(jnp.bfloat16)
    unit = inner.shape[2]
    for index in range(inner.shape[0]):
        inner[index] = act[:, index * unit : (index + 1) * unit]


def down(info, inner, first_out, w0, w1, w2, w3, kept, sent, total):
    core = info[16]
    total[...] = ring_dot(info, inner, (w0, w1, w2, w3), 0, total.shape[1])
    half = kept.shape[0]
    rows = pl.ds(pl.multiple_of(core * half, half), half)
    kept[...] = total[rows, :] + first_out[rows, :].astype(jnp.float32)
    sent[...] = total[pl.ds(pl.multiple_of((1 - core) * half, half), half), :].astype(jnp.bfloat16)


def norm_pool(info, kept, arrived, pick, out, lanes):
    half, width = kept.shape
    values = kept[...] + arrived[...].astype(jnp.float32)
    mean = jnp.mean(values, axis=1, keepdims=True)
    values = values - mean
    values = values * lax.rsqrt(jnp.mean(values * values, axis=1, keepdims=True) + 1e-05)
    spans = pick.shape[1]
    pooled = jnp.mean(values.reshape(spans, half // spans, width), axis=1).astype(jnp.bfloat16)
    by_slot = dot32(pick[...], pooled)
    for index in range(width // 128):
        lanes[:, index, :] = by_slot[:, index * 128 : (index + 1) * 128]
    out[...] = jnp.broadcast_to(lanes[...].astype(jnp.bfloat16)[:, None], out.shape)


def embed(info, arrived, order, proj_in, mine, other, out, lanes, pieces):
    core = info[16]
    lanes[...] = arrived[...].astype(jnp.float32)
    columns = [
        dot32(order[...], lanes[:, index, :].astype(jnp.bfloat16)).astype(jnp.bfloat16)
        for index in range(lanes.shape[1])
    ]
    arranged = jnp.concatenate(columns, axis=1)
    hidden = gelu_exact(dot32(arranged, proj_in[...])).astype(jnp.bfloat16)
    units, cols = mine.shape[2:]
    for index in range(pieces.shape[0]):
        pieces[index] = hidden[:, index * units : (index + 1) * units]
    near, far = None, None
    for at in range(SIDE):
        act = jnp.concatenate([pieces[info[SIDE * at + step]] for step in range(SIDE)], axis=1)
        term = dot32(act, mine[at].reshape(SIDE * units, cols))
        near = term if near is None else near + term
        act = jnp.concatenate([pieces[info[22 + SIDE * at + step]] for step in range(SIDE)], axis=1)
        term = dot32(act, other[at].reshape(SIDE * units, cols))
        far = term if far is None else far + term
    out[:, :cols] = jnp.where(core == 0, near, far).astype(jnp.bfloat16)
    out[:, cols:] = jnp.where(core == 0, far, near).astype(jnp.bfloat16)


def project(info, *refs, starts, count):
    blocks, refs = refs[:count], refs[count:]
    gain, q_weight, kv_weight = refs[:3]
    before = refs[3:6] if len(refs) > 6 else None
    q_total, kv_total, square = refs[-3:]
    depth = blocks[0].shape[2]
    queries, both = None, None
    squares = None
    for at, block in zip(starts, blocks):
        for step in range(SIDE):
            shard = info[SIDE * at + step]
            wide = block[step].astype(jnp.float32)
            act = (wide * gain[shard]).astype(jnp.bfloat16)
            span = pl.ds(pl.multiple_of(shard * depth, depth), depth)
            q_term = dot32(act, q_weight[span, :])
            kv_term = dot_last(act, kv_weight[:, span])
            term = jnp.sum(wide * wide, axis=1, keepdims=True)
            queries = q_term if queries is None else queries + q_term
            both = kv_term if both is None else both + kv_term
            squares = term if squares is None else squares + term
    if before is not None:
        queries, both, squares = queries + before[0][...], both + before[1][...], squares + before[2][...]
    q_total[...] = queries
    kv_total[...] = both
    square[...] = squares


def turn(values, cosine, sine, swap):
    turned = jnp.dot(
        values, swap, preferred_element_type=jnp.float32, precision=lax.Precision.HIGHEST
    )
    return values * cosine + turned * sine


def last_keys(info, block, gain, kv_weight, kv_before, sq_before, cosine, sine, swap, out, scale):
    depth = block.shape[2]
    both = kv_before[...]
    squares = sq_before[...]
    for step in range(SIDE):
        shard = info[SIDE * 3 + step]
        wide = block[step].astype(jnp.float32)
        act = (wide * gain[shard]).astype(jnp.bfloat16)
        span = pl.ds(pl.multiple_of(shard * depth, depth), depth)
        both += dot_last(act, kv_weight[:, span])
        squares += jnp.sum(wide * wide, axis=1, keepdims=True)
    factor = lax.rsqrt(squares / (depth * SIDE * SIDE) + 1e-05)
    scale[...] = factor
    both = both * factor
    cols = out.shape[2]
    out[0] = turn(both[:, :cols], cosine[...], sine[...], swap[...]).astype(jnp.bfloat16)
    out[1] = both[:, cols:].astype(jnp.bfloat16)


def last_queries(info, block, gain, q_weight, q_before, scale, cosine, sine, swap, out):
    depth = block.shape[2]
    total = q_before[...]
    for step in range(SIDE):
        shard = info[SIDE * 3 + step]
        act = (block[step].astype(jnp.float32) * gain[shard]).astype(jnp.bfloat16)
        span = pl.ds(pl.multiple_of(shard * depth, depth), depth)
        total += dot32(act, q_weight[span, :])
    for head in range(out.shape[1] // HEAD_WIDTH):
        lanes = slice(head * HEAD_WIDTH, (head + 1) * HEAD_WIDTH)
        query = total[:, lanes] * scale[...]
        out[:, lanes] = turn(query, cosine[...], sine[...], swap[...]).astype(jnp.bfloat16)


def attend_out(info, query, mine, partner, allowed, deal, weight, *refs):
    outs, context = refs[:4], refs[4]
    odd = info[17] == 1
    own = mine[...].astype(jnp.float32)
    far = partner[...].astype(jnp.float32)
    low = jnp.where(odd, far, own)
    high = jnp.where(odd, own, far)
    both = jnp.concatenate([low, high], axis=2).astype(jnp.bfloat16)
    key, value = both[0], both[1]
    heads = [
        slice(head * HEAD_WIDTH, (head + 1) * HEAD_WIDTH)
        for head in range(query.shape[1] // HEAD_WIDTH)
    ]
    scores = [
        lax.dot_general(
            query[:, lanes], key, (((1,), (1,)), ((), ())), preferred_element_type=jnp.float32
        )
        for lanes in heads
    ]
    for lanes, prob in zip(heads, masked_softmax(scores, allowed[...] > 0, HEAD_WIDTH)):
        context[:, lanes] = dot32(prob, value).astype(jnp.bfloat16)
    dealt = dot32(deal[...], context[...]).astype(jnp.bfloat16)
    rows = outs[0].shape[0]
    step = weight.shape[1] // 8
    for start in range(0, weight.shape[1], step):
        result = dot32(dealt, weight[:, start : start + step])
        for index, out in enumerate(outs):
            piece = result[index * rows : (index + 1) * rows]
            out[:, start : start + step] = piece.astype(jnp.bfloat16)


def add_ring(info, own, left, right, opposite, kept, *sent):
    rows = kept.shape[0]
    step = 1024
    for start in range(0, own.shape[1], step):
        lanes = slice(start, start + step)
        total = own[:, lanes].astype(jnp.float32)
        for block in (left, right, opposite):
            total = total + block[:, lanes].astype(jnp.float32)
        kept[:, lanes] = total[:rows]
        for index, out in enumerate(sent):
            piece = total[(index + 1) * rows : (index + 2) * rows]
            out[:, lanes] = piece.astype(jnp.bfloat16)


def finish(info, kept, left, right, opposite, *refs):
    own, out = refs[:-1], refs[-1]
    rows, cols = own[0].shape[1:]
    live = info[18] + lax.broadcasted_iota(jnp.int32, (rows, cols), 0) < info[21]
    for at, block in enumerate(own):
        for step in range(SIDE):
            lanes = pl.ds(pl.multiple_of(info[SIDE * at + step] * cols, cols), cols)
            total = kept[:, lanes] + block[step].astype(jnp.float32)
            for term in (left, right, opposite):
                total = total + term[:, lanes].astype(jnp.float32)
            out[:, lanes] = jnp.where(live, total, 0.0).astype(jnp.bfloat16)


def visibility(masks, live_count):
    positions = jnp.arange(SPAN_LIMIT)
    passage = positions // CPP
    expanded = jnp.repeat(jnp.repeat(masks, CPP, axis=0), CPP, axis=1) > 0
    same_passage = passage[:, None] == passage[None, :]
    earlier = positions[None, :] <= positions[:, None]
    key_live = positions[None, :] < live_count
    diagonal = positions[:, None] == positions[None, :]
    return diagonal | earlier & key_live & (same_passage | expanded)


def local(
    span_tokens,
    enc_dest,
    passages,
    req_slot,
    block_mask,
    enc_qkv,
    enc_out,
    enc_up,
    enc_down,
    proj_in,
    proj_out,
    norm_gain,
    q_weight,
    key_value_weight,
    out_weight,
):
    tensor_count = lax.axis_size("tensor")
    seq_count = lax.axis_size("seq")
    tensor_index = lax.axis_index("tensor")
    seq_index = lax.axis_index("seq")
    core = seq_index % 2
    device_count = tensor_count * seq_count
    rows = SPAN_LIMIT
    own_rows = rows // tensor_count
    spans, span_size, width = span_tokens.shape
    model_width = proj_out.shape[1]
    share = enc_qkv.shape[0]
    x_index, y_index = tensor_index // SIDE, tensor_index % SIDE

    steps = jnp.array([0, SIDE - 1, 1, 2])
    outer, inside = jnp.repeat(steps, SIDE), jnp.tile(steps, SIDE)
    by_x = SIDE * ((x_index + outer) % SIDE) + (y_index + inside) % SIDE
    by_y = SIDE * ((x_index + inside) % SIDE) + (y_index + outer) % SIDE
    shards = jnp.where(core == 0, by_x, by_y)
    near = jnp.where(core == 0, y_index, x_index)
    far = jnp.where(core == 0, x_index, y_index)
    scalars = jnp.stack([core, tensor_index % 2, tensor_index * own_rows, near, far])
    other_shards = jnp.where(core == 0, by_y, by_x)
    info = jnp.concatenate([shards, scalars, core[None], other_shards]).astype(jnp.int32)

    ahead = jnp.array([0, 1, SIDE - 1, 2])
    outer, inside = jnp.repeat(ahead, SIDE), jnp.tile(ahead, SIDE)
    owner_x = SIDE * ((x_index + outer) % SIDE) + (y_index + inside) % SIDE
    owner_y = SIDE * ((x_index + inside) % SIDE) + (y_index + outer) % SIDE
    owners = jnp.where(core == 0, owner_x, owner_y)
    from_row = (owners[:, None] * own_rows + jnp.arange(own_rows)[None, :]).reshape(-1)
    deal = (from_row[:, None] == jnp.arange(rows)[None, :]).astype(jnp.bfloat16)

    requests = jnp.arange(req_slot.shape[0])
    dest_slot = jnp.sum(
        jnp.where(enc_dest[:, None] // SPAN_LIMIT == requests[None, :], req_slot[None, :], 0), axis=1
    ).reshape(device_count, own_rows)
    dest_place = (enc_dest % SPAN_LIMIT).reshape(device_count, own_rows)
    own_slots = lax.dynamic_slice_in_dim(
        dest_slot, seq_index * tensor_count + tensor_index, 1, 0
    )
    pick = (jnp.arange(seq_count)[:, None] == own_slots).astype(jnp.bfloat16)
    place_of = jnp.sum(jnp.where(dest_slot == seq_index, dest_place, 0), axis=1)
    order = (jnp.arange(rows)[:, None] == place_of[None, :]).astype(jnp.bfloat16)
    chosen = jnp.sum(jnp.where(req_slot == seq_index, requests, 0))
    live_count = jnp.sum(jnp.where(requests == chosen, passages, 0)) * CPP
    masks = jnp.sum(
        jnp.where(requests[:, None, None] == chosen, block_mask, 0), axis=0
    )
    allowed = visibility(masks, live_count).astype(jnp.float32)
    live_info = jnp.concatenate([info[:21], live_count[None]]).astype(jnp.int32)

    positions = jnp.arange(rows).astype(jnp.float32)
    lane = jnp.arange(HEAD_WIDTH)
    frequency = jnp.exp(
        -(2.0 * (lane // 2).astype(jnp.float32) / HEAD_WIDTH) * math.log(500000.0)
    )
    angles = positions[:, None] * frequency[None, :]
    cosine, sine = jnp.cos(angles), jnp.sin(angles)
    swap = jnp.where(
        (lane[:, None] ^ 1) == lane[None, :], jnp.where(lane[None, :] % 2 == 0, -1.0, 1.0), 0.0
    ).astype(jnp.float32)

    own_tokens = span_tokens.reshape(spans * span_size, width)
    other_tokens = to_core(own_tokens)
    token_pieces = whole_call(
        both_rows,
        "both_rows",
        info,
        [own_tokens, other_tokens],
        shape_of((tensor_count, 2 * spans * span_size, share)),
    )
    units = enc_down.shape[0] // 2
    middle_cols = width // 2 + units * tensor_count
    share_cols = model_width // tensor_count
    half_cols = share_cols // 2
    rest_shape = shape_of((share, middle_cols + width + SIDE * half_cols))
    dealt_shape = shape_of((share, SIDE * half_cols))
    own_qkv = whole_call(
        take_qkv, "take_qkv", info, [enc_qkv], shape_of((share, 3 * width // 2)), limit=4
    )
    rest_up, rest_down, kept_cols, beyond_cols = whole_call(
        take_rest,
        "take_rest",
        info,
        [enc_out, enc_up, enc_down, proj_out],
        (rest_shape, rest_shape, dealt_shape, dealt_shape),
        limit=60,
        after=[own_qkv],
    )
    qkv_ring = short_ring(own_qkv)
    rest_right = to_ring(rest_down, 1, -1)
    rest_ring = [rest_up, to_ring(rest_up, 1, 1), rest_right, to_ring(rest_right, 1, -1)]
    beyond_cols = to_ring(beyond_cols, 1, 2)
    qkv_block = whole_call(
        join_blocks,
        "join_qkv",
        info,
        qkv_ring,
        shape_of((SIDE, share, 3 * width // 2)),
        limit=6,
        after=rest_ring[1:3],
    )
    all_rows = 2 * spans * span_size

    qkv = [qkv_block] + [to_ring(qkv_block, 2, distance) for distance in (1, -1, 2)]
    mixed = whole_call(
        span_qkv,
        "span_qkv",
        info,
        [token_pieces, *qkv],
        shape_of((all_rows, 3 * width // 2)),
        flops=2 * all_rows * width * 3 * width // 2,
    )
    context = whole_call(
        span_attention,
        "span_attention",
        info,
        [mixed],
        shape_of((tensor_count // 2, all_rows, share)),
    )
    middle_block = whole_call(
        join_middle,
        "join_middle",
        info,
        rest_ring,
        shape_of((SIDE, share, middle_cols)),
        limit=8,
        after=[mixed],
    )
    right = to_ring(middle_block, 2, -1)
    middle = [middle_block, to_ring(middle_block, 2, 1), right, to_ring(right, 2, -1)]
    lower_shape = shape_of((SIDE, share, width + half_cols))
    far_shape = shape_of((SIDE, share, half_cols))
    lower_up, lower_down, far_kept, far_beyond = whole_call(
        join_lower,
        "join_lower",
        info,
        [*rest_ring, kept_cols, beyond_cols],
        (lower_shape, lower_shape, far_shape, far_shape),
        limit=8,
        after=[context, *middle[1:3]],
    )
    lower_left = to_ring(lower_up, 2, 1)
    lower = [lower_up, lower_left, to_ring(lower_down, 2, -1), to_ring(lower_left, 2, 1)]
    far_beyond = to_ring(far_beyond, 2, 2)
    attended = whole_call(
        context_out,
        "context_out",
        info,
        [context, to_core(context), token_pieces, *middle],
        shape_of((all_rows, width // 2)),
        [pltpu.VMEM((tensor_count, all_rows, share), jnp.bfloat16)],
        flops=2 * all_rows * width * width // 2,
    )
    first_out, inner = whole_call(
        norm_up,
        "norm_up",
        info,
        [attended, to_core(attended), *middle],
        (shape_of((all_rows, width)), shape_of((tensor_count, all_rows, units))),
        [pltpu.VMEM((tensor_count, all_rows, share), jnp.bfloat16)],
        flops=2 * all_rows * width * width,
    )
    kept, sent = whole_call(
        down,
        "down",
        info,
        [inner, first_out, *lower],
        (
            shape_of((all_rows // 2, width), jnp.float32),
            shape_of((all_rows // 2, width)),
        ),
        [pltpu.VMEM((all_rows, width), jnp.float32)],
        flops=2 * all_rows * width * width,
    )
    outgoing = whole_call(
        norm_pool,
        "norm_pool",
        info,
        [kept, to_core(sent), pick],
        shape_of((seq_count, tensor_count, width // 128, 128)),
        [pltpu.VMEM((seq_count, width // 128, 128), jnp.float32)],
    )
    arrived = lax.all_to_all(
        outgoing.reshape(device_count, width // 128, 128), AXES, 0, 0
    )

    proj_mine = whole_call(
        join_proj,
        "join_proj",
        info,
        [far_kept, lower[1], lower[2], far_beyond],
        shape_of((SIDE, SIDE, share, half_cols)),
        limit=8,
        after=[outgoing],
    )
    proj_other = to_core(proj_mine)
    own_cols = whole_call(
        embed,
        "embed",
        info,
        [arrived, order, proj_in, proj_mine, proj_other],
        shape_of((rows, share_cols)),
        [
            pltpu.VMEM((device_count, width // 128, 128), jnp.float32),
            pltpu.VMEM((tensor_count, rows, proj_out.shape[0]), jnp.bfloat16),
        ],
        flops=2 * rows * width * (width + share_cols),
    )
    first_block = whole_call(
        join_blocks,
        "join_columns",
        info,
        short_ring(own_cols),
        shape_of((SIDE, rows, share_cols)),
        limit=4,
    )
    near_left = to_ring(first_block, 2, 1)
    near_right = to_ring(first_block, 2, -1)
    query_cols = q_weight.shape[1]
    kv_cols = key_value_weight.shape[2]
    key_start = tensor_index * kv_cols % HEAD_WIDTH
    key_cosine = lax.dynamic_slice_in_dim(cosine, key_start, kv_cols, 1)
    key_sine = lax.dynamic_slice_in_dim(sine, key_start, kv_cols, 1)
    gain = norm_gain.reshape(tensor_count, 1, share_cols)
    kv_pair = key_value_weight.transpose(0, 2, 1).reshape(2 * kv_cols, model_width)
    sums = (
        shape_of((rows, query_cols), jnp.float32),
        shape_of((rows, 2 * kv_cols), jnp.float32),
        shape_of((rows, 1), jnp.float32),
    )
    block_flops = 2 * rows * model_width // SIDE * (query_cols + 2 * kv_cols)
    totals = whole_call(
        functools.partial(project, starts=(0,), count=1),
        "project_own",
        info,
        [first_block, gain, q_weight, kv_pair],
        sums,
        flops=block_flops,
    )
    embedded = [first_block, near_left, near_right, to_ring(near_left, 2, 1)]
    totals = whole_call(
        functools.partial(project, starts=(1, 2), count=2),
        "project_near",
        info,
        [embedded[1], embedded[2], gain, q_weight, kv_pair, *totals],
        sums,
        flops=2 * block_flops,
    )
    own_kv, scale = whole_call(
        last_keys,
        "last_keys",
        info,
        [
            embedded[3],
            gain,
            kv_pair,
            totals[1],
            totals[2],
            key_cosine,
            key_sine,
            swap[:kv_cols, :kv_cols],
        ],
        (shape_of((2, rows, kv_cols)), shape_of((rows, 1), jnp.float32)),
    )
    partner_kv = lax.ppermute(
        own_kv, "tensor", [(index, index ^ 1) for index in range(tensor_count)]
    )
    query = whole_call(
        last_queries,
        "last_queries",
        info,
        [embedded[3], gain, q_weight, totals[0], scale, cosine, sine, swap],
        shape_of((rows, query_cols)),
        flops=block_flops,
    )
    partial = whole_call(
        attend_out,
        "attend_out",
        info,
        [query, own_kv, partner_kv, allowed, deal, out_weight],
        (shape_of((rows // SIDE, model_width)),) * 4,
        [pltpu.VMEM((rows, query_cols), jnp.bfloat16)],
        flops=2 * rows * model_width * query_cols,
    )
    arrived_sums = [
        to_ring(part, 2, distance) for part, distance in zip(partial[1:], (1, -1, 2))
    ]
    kept_sum, *sent_sums = whole_call(
        add_ring,
        "add_ring",
        info,
        [partial[0], *arrived_sums],
        (shape_of((own_rows, model_width), jnp.float32),)
        + (shape_of((own_rows, model_width)),) * 3,
    )
    terms = [to_ring(part, 1, distance) for part, distance in zip(sent_sums, (1, -1, 2))]
    own_embedded = [
        lax.dynamic_slice_in_dim(block, tensor_index * own_rows, own_rows, 1) for block in embedded
    ]
    return whole_call(
        finish,
        "finish",
        live_info,
        [kept_sum, *terms, *own_embedded],
        shape_of((own_rows, model_width)),
    )


def solution(mesh):
    return jax.shard_map(
        local,
        mesh=mesh,
        in_specs=(
            P(("seq", "tensor"), None, None),
            P(),
            P(),
            P(),
            P(),
            P("tensor", None),
            P("tensor", None),
            P("tensor", None),
            P("tensor", None),
            P(),
            P("tensor", None),
            P(),
            P(None, "tensor"),
            P(None, None, "tensor"),
            P("tensor", None),
        ),
        out_specs=P(("seq", "tensor"), None),
        check_vma=False,
    )
```

```python
import functools
import math

import jax
import jax.numpy as jnp
from jax import lax
from jax.experimental import pallas as pl
from jax.experimental.pallas import tpu as pltpu
from jax.sharding import PartitionSpec as P

QUERY_HEAD_COUNT = 64
KEY_VALUE_HEADS = 8
HEAD_WIDTH = 128
EH = 16
CPP = 16
SPAN_LIMIT = 128
SIDE = 4
AXES = ("seq", "tensor")


def device_id(plane, core, x, y):
    return ((plane * 2 + core) * SIDE + x) * SIDE + y


def every_device():
    return [
        (plane, core, x, y)
        for plane in range(SIDE)
        for core in range(2)
        for x in range(SIDE)
        for y in range(SIDE)
    ]


def first_axis_is_y(core, phase):
    return (core == 0) == (phase == 1)


def ring_pairs(phase, distance):
    pairs = []
    for plane, core, x, y in every_device():
        if first_axis_is_y(core, phase):
            target = device_id(plane, core, x, (y + distance) % SIDE)
        else:
            target = device_id(plane, core, (x + distance) % SIDE, y)
        pairs.append((device_id(plane, core, x, y), target))
    return pairs


def ring_groups(phase):
    groups = []
    for plane in range(SIDE):
        for core in range(2):
            for fixed in range(SIDE):
                groups.append(
                    [
                        device_id(plane, core, fixed, moving)
                        if first_axis_is_y(core, phase)
                        else device_id(plane, core, moving, fixed)
                        for moving in range(SIDE)
                    ]
                )
    return groups


def to_ring(value, phase, distance):
    return lax.ppermute(value, AXES, ring_pairs(phase, distance))


def to_core(value):
    return lax.ppermute(value, "seq", [(index, index ^ 1) for index in range(8)])


def short_ring(block):
    return [block] + [to_ring(block, 1, distance) for distance in (1, -1, 2)]


def short_relay(block):
    left = to_ring(block, 1, 1)
    right = to_ring(block, 1, -1)
    return [block, left, right, to_ring(right, 1, -1)]


VMEM = pl.BlockSpec(memory_space=pltpu.VMEM)
SMEM = pl.BlockSpec(memory_space=pltpu.SMEM)
ANYWHERE = pl.BlockSpec(memory_space=pl.ANY)
MIB = 2**20


def shape_of(shape, dtype=jnp.bfloat16):
    return jax.ShapeDtypeStruct(shape, dtype)


def whole_call(body, name, info, arrays, outs, scratch=(), limit=12, flops=0, far=(), after=()):
    count = len(arrays) + len(far)

    def run(*refs):
        body(*refs[: 1 + count], *refs[1 + count + len(after) :])

    moved = sum(array.size * array.dtype.itemsize for array in arrays)
    return pl.pallas_call(
        run,
        name=name,
        out_shape=outs,
        in_specs=[SMEM] + [VMEM] * len(arrays) + [ANYWHERE] * (len(far) + len(after)),
        out_specs=jax.tree.map(lambda _: VMEM, outs),
        scratch_shapes=list(scratch),
        compiler_params=pltpu.CompilerParams(vmem_limit_bytes=limit * MIB),
        cost_estimate=pl.CostEstimate(flops=flops, bytes_accessed=moved, transcendentals=0),
    )(info, *arrays, *far, *after)


def dot32(left, right):
    return jnp.dot(left, right, preferred_element_type=jnp.float32)


def dot_last(left, right):
    return lax.dot_general(
        left, right, (((1,), (1,)), ((), ())), preferred_element_type=jnp.float32
    )


def gelu_exact(values):
    return 0.5 * values * (1.0 + lax.erf(values * (0.5**0.5)))


def take_qkv(info, weight, out):
    cols = weight.shape[1] // 6
    for part in range(3):
        start = pl.multiple_of((2 * part + info[16]) * cols, cols)
        out[:, part * cols : (part + 1) * cols] = weight[:, pl.ds(start, cols)]


def take_rest(info, out_weight, up_weight, down_weight, proj, up_out, down_out, kept, beyond):
    core, near = info[16], info[19]
    rows, width = out_weight.shape
    cols = width // 2
    units = down_weight.shape[0] // 2
    pieces = [out_weight[:, pl.ds(pl.multiple_of(core * cols, cols), cols)]]
    for pair in range(up_weight.shape[1] // (4 * units)):
        halves = []
        for step in range(2):
            low = (2 * pair + step) * 2 * units
            halves.append(
                jnp.where(
                    core == 0,
                    up_weight[:, low : low + units].astype(jnp.float32),
                    up_weight[:, low + units : low + 2 * units].astype(jnp.float32),
                )
            )
        pieces.append(jnp.concatenate(halves, axis=1).astype(jnp.bfloat16))
    pieces.append(down_weight[pl.ds(pl.multiple_of(core * units, units), units), :])
    at = 0
    for piece in pieces:
        for out in (up_out, down_out):
            out[:, at : at + piece.shape[1]] = piece
        at += piece.shape[1]
    block = kept.shape[1] // SIDE
    for out, start, distance in ((kept, 0, 0), (up_out, at, 1), (down_out, at, SIDE - 1), (beyond, 0, 2)):
        target = lax.rem(near + distance, SIDE)
        for index in range(SIDE):
            shard = jnp.where(core == 0, SIDE * index + target, SIDE * target + index)
            source = pl.multiple_of((2 * shard + core) * block, block)
            out[:, start + index * block : start + (index + 1) * block] = proj[:, pl.ds(source, block)]


def join_blocks(info, own, left, right, opposite, out):
    for index, block in enumerate((own, left, right, opposite)):
        out[index] = block[...]


def join_middle(info, own, left, right, opposite, out):
    for index, block in enumerate((own, left, right, opposite)):
        out[index] = block[:, : out.shape[2]]


def join_lower(info, own, left, right, opposite, kept, beyond, up_out, down_out, far_kept, far_beyond):
    far = info[20]
    block = far_kept.shape[2]
    width = up_out.shape[2] - block
    start = own.shape[1] - kept.shape[1] - width
    for index, part in enumerate((own, left, right, opposite)):
        for out in (up_out, down_out):
            out[index, :, :width] = part[:, start : start + width]
        columns, first = (part, start + width) if index in (1, 2) else (kept, 0)
        if index == 3:
            columns = beyond
        for out, at, distance in (
            (far_kept, 0, 0),
            (up_out, width, 1),
            (down_out, width, SIDE - 1),
            (far_beyond, 0, 2),
        ):
            target = lax.rem(far + distance, SIDE)
            source = pl.multiple_of(first + target * block, 128)
            out[index, :, at : at + block] = columns[:, pl.ds(source, block)]


def join_proj(info, own, left, right, opposite, out):
    block = own.shape[2]
    for index, part in enumerate((own, left, right, opposite)):
        out[index] = part[:, :, part.shape[2] - block :]


def both_rows(info, mine, other, pieces_out):
    half, width = mine.shape
    core = info[16]
    piece = pieces_out.shape[2]
    near = pl.ds(pl.multiple_of(core * half, half), half)
    far = pl.ds(pl.multiple_of((1 - core) * half, half), half)
    for index in range(width // piece):
        pieces_out[index, near, :] = mine[:, index * piece : (index + 1) * piece]
        pieces_out[index, far, :] = other[:, index * piece : (index + 1) * piece]


def ring_dot(info, pieces, blocks, low, high):
    total = None
    for at, block in enumerate(blocks):
        act = jnp.concatenate([pieces[info[4 * at + step]] for step in range(SIDE)], axis=1)
        weight = block[:, :, low:high].reshape(act.shape[1], high - low)
        part = dot32(act, weight)
        total = part if total is None else total + part
    return total


def masked_softmax(scores, seen, size):
    scores = [jnp.where(seen, score / math.sqrt(size), -1e30) for score in scores]
    tops = [jnp.max(score, axis=1, keepdims=True) for score in scores]
    powers = [jnp.exp(score - top) for score, top in zip(scores, tops)]
    sums = [jnp.sum(power, axis=1, keepdims=True) for power in powers]
    return [(power / total).astype(jnp.bfloat16) for power, total in zip(powers, sums)]


def span_attention(info, pieces, w0, w1, w2, w3, context, mixed):
    cols = w0.shape[2]
    third = cols // 3
    mixed[...] = ring_dot(info, pieces, (w0, w1, w2, w3), 0, cols).astype(jnp.bfloat16)
    size = context.shape[2]
    half = mixed.shape[0] // 2
    span = 16
    row = lax.broadcasted_iota(jnp.int32, (half, half), 0) // span
    col = lax.broadcasted_iota(jnp.int32, (half, half), 1) // span
    same = row == col
    heads = third // size
    units = [
        (head, slice(part * half, (part + 1) * half)) for head in range(heads) for part in range(2)
    ]
    scores = [
        lax.dot_general(
            mixed[rows, head * size : (head + 1) * size],
            mixed[rows, third + head * size : third + (head + 1) * size],
            (((1,), (1,)), ((), ())),
            preferred_element_type=jnp.float32,
        )
        for head, rows in units
    ]
    probs = masked_softmax(scores, same, size)
    for (head, rows), prob in zip(units, probs):
        value = mixed[rows, 2 * third + head * size : 2 * third + (head + 1) * size]
        context[head, rows, :] = dot32(prob, value).astype(jnp.bfloat16)


def context_out(info, mine, other, tokens, w0, w1, w2, w3, attended, pieces):
    heads = mine.shape[0]
    core = info[16]
    pieces[pl.ds(core * heads, heads)] = mine[...]
    pieces[pl.ds((1 - core) * heads, heads)] = other[...]
    cols = attended.shape[1]
    residual = jnp.concatenate([tokens[core * heads + index] for index in range(heads)], axis=1)
    total = ring_dot(info, pieces, (w0, w1, w2, w3), 0, cols)
    attended[...] = (residual.astype(jnp.float32) + total).astype(jnp.bfloat16)


def norm_up(info, mine, other, w0, w1, w2, w3, first_out, inner, pieces):
    core = info[16]
    cols = mine.shape[1]
    width = 2 * cols
    near = mine[...].astype(jnp.float32)
    far = other[...].astype(jnp.float32)
    low = jnp.where(core == 0, near, far)
    high = jnp.where(core == 0, far, near)
    mean = (jnp.sum(low, 1, keepdims=True) + jnp.sum(high, 1, keepdims=True)) / width
    low, high = low - mean, high - mean
    var = (jnp.sum(low * low, 1, keepdims=True) + jnp.sum(high * high, 1, keepdims=True)) / width
    scale = lax.rsqrt(var + 1e-05)
    first_out[:, :cols] = (low * scale).astype(jnp.bfloat16)
    first_out[:, cols:] = (high * scale).astype(jnp.bfloat16)
    size = pieces.shape[2]
    for index in range(pieces.shape[0]):
        pieces[index] = first_out[:, index * size : (index + 1) * size]
    total = ring_dot(info, pieces, (w0, w1, w2, w3), cols, w0.shape[2])
    act = gelu_exact(total).astype(jnp.bfloat16)
    unit = inner.shape[2]
    for index in range(inner.shape[0]):
        inner[index] = act[:, index * unit : (index + 1) * unit]


def down(info, inner, first_out, w0, w1, w2, w3, kept, sent, total):
    core = info[16]
    total[...] = ring_dot(info, inner, (w0, w1, w2, w3), 0, total.shape[1])
    half = kept.shape[0]
    rows = pl.ds(pl.multiple_of(core * half, half), half)
    kept[...] = total[rows, :] + first_out[rows, :].astype(jnp.float32)
    sent[...] = total[pl.ds(pl.multiple_of((1 - core) * half, half), half), :].astype(jnp.bfloat16)


def norm_pool(info, kept, arrived, pick, out, lanes):
    half, width = kept.shape
    values = kept[...] + arrived[...].astype(jnp.float32)
    mean = jnp.mean(values, axis=1, keepdims=True)
    values = values - mean
    values = values * lax.rsqrt(jnp.mean(values * values, axis=1, keepdims=True) + 1e-05)
    spans = pick.shape[1]
    pooled = jnp.mean(values.reshape(spans, half // spans, width), axis=1).astype(jnp.bfloat16)
    by_slot = dot32(pick[...], pooled)
    for index in range(width // 128):
        lanes[:, index, :] = by_slot[:, index * 128 : (index + 1) * 128]
    out[...] = jnp.broadcast_to(lanes[...].astype(jnp.bfloat16)[:, None], out.shape)


def embed(info, arrived, order, proj_in, mine, other, out, lanes, pieces):
    core = info[16]
    lanes[...] = arrived[...].astype(jnp.float32)
    columns = [
        dot32(order[...], lanes[:, index, :].astype(jnp.bfloat16)).astype(jnp.bfloat16)
        for index in range(lanes.shape[1])
    ]
    arranged = jnp.concatenate(columns, axis=1)
    hidden = gelu_exact(dot32(arranged, proj_in[...])).astype(jnp.bfloat16)
    units, cols = mine.shape[2:]
    for index in range(pieces.shape[0]):
        pieces[index] = hidden[:, index * units : (index + 1) * units]
    near, far = None, None
    for at in range(SIDE):
        act = jnp.concatenate([pieces[info[SIDE * at + step]] for step in range(SIDE)], axis=1)
        term = dot32(act, mine[at].reshape(SIDE * units, cols))
        near = term if near is None else near + term
        act = jnp.concatenate([pieces[info[22 + SIDE * at + step]] for step in range(SIDE)], axis=1)
        term = dot32(act, other[at].reshape(SIDE * units, cols))
        far = term if far is None else far + term
    out[:, :cols] = jnp.where(core == 0, near, far).astype(jnp.bfloat16)
    out[:, cols:] = jnp.where(core == 0, far, near).astype(jnp.bfloat16)


def project(info, *refs, starts, count):
    blocks, refs = refs[:count], refs[count:]
    gain, q_weight, kv_weight = refs[:3]
    before = refs[3:6] if len(refs) > 6 else None
    q_total, kv_total, square = refs[-3:]
    depth = blocks[0].shape[2]
    queries, both = None, None
    squares = None
    for at, block in zip(starts, blocks):
        for step in range(SIDE):
            shard = info[SIDE * at + step]
            wide = block[step].astype(jnp.float32)
            act = (wide * gain[shard]).astype(jnp.bfloat16)
            span = pl.ds(pl.multiple_of(shard * depth, depth), depth)
            q_term = dot32(act, q_weight[span, :])
            kv_term = dot_last(act, kv_weight[:, span])
            term = jnp.sum(wide * wide, axis=1, keepdims=True)
            queries = q_term if queries is None else queries + q_term
            both = kv_term if both is None else both + kv_term
            squares = term if squares is None else squares + term
    if before is not None:
        queries, both, squares = queries + before[0][...], both + before[1][...], squares + before[2][...]
    q_total[...] = queries
    kv_total[...] = both
    square[...] = squares


def turn(values, cosine, sine, swap):
    turned = jnp.dot(
        values, swap, preferred_element_type=jnp.float32, precision=lax.Precision.HIGHEST
    )
    return values * cosine + turned * sine


def last_keys(info, block, gain, kv_weight, kv_before, sq_before, cosine, sine, swap, out, scale):
    depth = block.shape[2]
    both = kv_before[...]
    squares = sq_before[...]
    for step in range(SIDE):
        shard = info[SIDE * 3 + step]
        wide = block[step].astype(jnp.float32)
        act = (wide * gain[shard]).astype(jnp.bfloat16)
        span = pl.ds(pl.multiple_of(shard * depth, depth), depth)
        both += dot_last(act, kv_weight[:, span])
        squares += jnp.sum(wide * wide, axis=1, keepdims=True)
    factor = lax.rsqrt(squares / (depth * SIDE * SIDE) + 1e-05)
    scale[...] = factor
    both = both * factor
    cols = out.shape[2]
    out[0] = turn(both[:, :cols], cosine[...], sine[...], swap[...]).astype(jnp.bfloat16)
    out[1] = both[:, cols:].astype(jnp.bfloat16)


def last_queries(info, block, gain, q_weight, q_before, scale, cosine, sine, swap, out):
    depth = block.shape[2]
    total = q_before[...]
    for step in range(SIDE):
        shard = info[SIDE * 3 + step]
        act = (block[step].astype(jnp.float32) * gain[shard]).astype(jnp.bfloat16)
        span = pl.ds(pl.multiple_of(shard * depth, depth), depth)
        total += dot32(act, q_weight[span, :])
    for head in range(out.shape[1] // HEAD_WIDTH):
        lanes = slice(head * HEAD_WIDTH, (head + 1) * HEAD_WIDTH)
        query = total[:, lanes] * scale[...]
        out[:, lanes] = turn(query, cosine[...], sine[...], swap[...]).astype(jnp.bfloat16)


def attend_out(info, query, mine, partner, allowed, deal, weight, *refs):
    outs, context = refs[:4], refs[4]
    odd = info[17] == 1
    own = mine[...].astype(jnp.float32)
    far = partner[...].astype(jnp.float32)
    low = jnp.where(odd, far, own)
    high = jnp.where(odd, own, far)
    both = jnp.concatenate([low, high], axis=2).astype(jnp.bfloat16)
    key, value = both[0], both[1]
    heads = [
        slice(head * HEAD_WIDTH, (head + 1) * HEAD_WIDTH)
        for head in range(query.shape[1] // HEAD_WIDTH)
    ]
    scores = [
        lax.dot_general(
            query[:, lanes], key, (((1,), (1,)), ((), ())), preferred_element_type=jnp.float32
        )
        for lanes in heads
    ]
    for lanes, prob in zip(heads, masked_softmax(scores, allowed[...] > 0, HEAD_WIDTH)):
        context[:, lanes] = dot32(prob, value).astype(jnp.bfloat16)
    dealt = dot32(deal[...], context[...]).astype(jnp.bfloat16)
    rows = outs[0].shape[0]
    step = weight.shape[1] // 8
    for start in range(0, weight.shape[1], step):
        result = dot32(dealt, weight[:, start : start + step])
        for index, out in enumerate(outs):
            piece = result[index * rows : (index + 1) * rows]
            out[:, start : start + step] = piece.astype(jnp.bfloat16)


def add_ring(info, own, left, right, opposite, kept, *sent):
    rows = kept.shape[0]
    step = 1024
    for start in range(0, own.shape[1], step):
        lanes = slice(start, start + step)
        total = own[:, lanes].astype(jnp.float32)
        for block in (left, right, opposite):
            total = total + block[:, lanes].astype(jnp.float32)
        kept[:, lanes] = total[:rows]
        for index, out in enumerate(sent):
            piece = total[(index + 1) * rows : (index + 2) * rows]
            out[:, lanes] = piece.astype(jnp.bfloat16)


def finish(info, kept, left, right, opposite, *refs):
    own, out = refs[:-1], refs[-1]
    rows, cols = own[0].shape[1:]
    live = info[18] + lax.broadcasted_iota(jnp.int32, (rows, cols), 0) < info[21]
    for at, block in enumerate(own):
        for step in range(SIDE):
            lanes = pl.ds(pl.multiple_of(info[SIDE * at + step] * cols, cols), cols)
            total = kept[:, lanes] + block[step].astype(jnp.float32)
            for term in (left, right, opposite):
                total = total + term[:, lanes].astype(jnp.float32)
            out[:, lanes] = jnp.where(live, total, 0.0).astype(jnp.bfloat16)


def visibility(masks, live_count):
    positions = jnp.arange(SPAN_LIMIT)
    passage = positions // CPP
    expanded = jnp.repeat(jnp.repeat(masks, CPP, axis=0), CPP, axis=1) > 0
    same_passage = passage[:, None] == passage[None, :]
    earlier = positions[None, :] <= positions[:, None]
    key_live = positions[None, :] < live_count
    diagonal = positions[:, None] == positions[None, :]
    return diagonal | earlier & key_live & (same_passage | expanded)


def local(
    span_tokens,
    enc_dest,
    passages,
    req_slot,
    block_mask,
    enc_qkv,
    enc_out,
    enc_up,
    enc_down,
    proj_in,
    proj_out,
    norm_gain,
    q_weight,
    key_value_weight,
    out_weight,
):
    tensor_count = lax.axis_size("tensor")
    seq_count = lax.axis_size("seq")
    tensor_index = lax.axis_index("tensor")
    seq_index = lax.axis_index("seq")
    core = seq_index % 2
    device_count = tensor_count * seq_count
    rows = SPAN_LIMIT
    own_rows = rows // tensor_count
    spans, span_size, width = span_tokens.shape
    model_width = proj_out.shape[1]
    share = enc_qkv.shape[0]
    x_index, y_index = tensor_index // SIDE, tensor_index % SIDE

    steps = jnp.array([0, SIDE - 1, 1, 2])
    outer, inside = jnp.repeat(steps, SIDE), jnp.tile(steps, SIDE)
    by_x = SIDE * ((x_index + outer) % SIDE) + (y_index + inside) % SIDE
    by_y = SIDE * ((x_index + inside) % SIDE) + (y_index + outer) % SIDE
    shards = jnp.where(core == 0, by_x, by_y)
    near = jnp.where(core == 0, y_index, x_index)
    far = jnp.where(core == 0, x_index, y_index)
    scalars = jnp.stack([core, tensor_index % 2, tensor_index * own_rows, near, far])
    other_shards = jnp.where(core == 0, by_y, by_x)
    info = jnp.concatenate([shards, scalars, core[None], other_shards]).astype(jnp.int32)

    ahead = jnp.array([0, 1, SIDE - 1, 2])
    outer, inside = jnp.repeat(ahead, SIDE), jnp.tile(ahead, SIDE)
    owner_x = SIDE * ((x_index + outer) % SIDE) + (y_index + inside) % SIDE
    owner_y = SIDE * ((x_index + inside) % SIDE) + (y_index + outer) % SIDE
    owners = jnp.where(core == 0, owner_x, owner_y)
    from_row = (owners[:, None] * own_rows + jnp.arange(own_rows)[None, :]).reshape(-1)
    deal = (from_row[:, None] == jnp.arange(rows)[None, :]).astype(jnp.bfloat16)

    requests = jnp.arange(req_slot.shape[0])
    dest_slot = jnp.sum(
        jnp.where(enc_dest[:, None] // SPAN_LIMIT == requests[None, :], req_slot[None, :], 0), axis=1
    ).reshape(device_count, own_rows)
    dest_place = (enc_dest % SPAN_LIMIT).reshape(device_count, own_rows)
    own_slots = lax.dynamic_slice_in_dim(
        dest_slot, seq_index * tensor_count + tensor_index, 1, 0
    )
    pick = (jnp.arange(seq_count)[:, None] == own_slots).astype(jnp.bfloat16)
    place_of = jnp.sum(jnp.where(dest_slot == seq_index, dest_place, 0), axis=1)
    order = (jnp.arange(rows)[:, None] == place_of[None, :]).astype(jnp.bfloat16)
    chosen = jnp.sum(jnp.where(req_slot == seq_index, requests, 0))
    live_count = jnp.sum(jnp.where(requests == chosen, passages, 0)) * CPP
    masks = jnp.sum(
        jnp.where(requests[:, None, None] == chosen, block_mask, 0), axis=0
    )
    allowed = visibility(masks, live_count).astype(jnp.float32)
    live_info = jnp.concatenate([info[:21], live_count[None]]).astype(jnp.int32)

    positions = jnp.arange(rows).astype(jnp.float32)
    lane = jnp.arange(HEAD_WIDTH)
    frequency = jnp.exp(
        -(2.0 * (lane // 2).astype(jnp.float32) / HEAD_WIDTH) * math.log(500000.0)
    )
    angles = positions[:, None] * frequency[None, :]
    cosine, sine = jnp.cos(angles), jnp.sin(angles)
    swap = jnp.where(
        (lane[:, None] ^ 1) == lane[None, :], jnp.where(lane[None, :] % 2 == 0, -1.0, 1.0), 0.0
    ).astype(jnp.float32)

    own_tokens = span_tokens.reshape(spans * span_size, width)
    other_tokens = to_core(own_tokens)
    token_pieces = whole_call(
        both_rows,
        "both_rows",
        info,
        [own_tokens, other_tokens],
        shape_of((tensor_count, 2 * spans * span_size, share)),
    )
    units = enc_down.shape[0] // 2
    middle_cols = width // 2 + units * tensor_count
    share_cols = model_width // tensor_count
    half_cols = share_cols // 2
    rest_shape = shape_of((share, middle_cols + width + SIDE * half_cols))
    dealt_shape = shape_of((share, SIDE * half_cols))
    own_qkv = whole_call(
        take_qkv, "take_qkv", info, [enc_qkv], shape_of((share, 3 * width // 2)), limit=4
    )
    rest_up, rest_down, kept_cols, beyond_cols = whole_call(
        take_rest,
        "take_rest",
        info,
        [enc_out, enc_up, enc_down, proj_out],
        (rest_shape, rest_shape, dealt_shape, dealt_shape),
        limit=60,
        after=[own_qkv],
    )
    qkv_ring = short_ring(own_qkv)
    rest_left = to_ring(rest_up, 1, 1)
    rest_ring = [rest_up, rest_left, to_ring(rest_down, 1, -1), to_ring(rest_left, 1, 1)]
    beyond_cols = to_ring(beyond_cols, 1, 2)
    qkv_block = whole_call(
        join_blocks,
        "join_qkv",
        info,
        qkv_ring,
        shape_of((SIDE, share, 3 * width // 2)),
        limit=6,
    )
    all_rows = 2 * spans * span_size

    qkv_right = to_ring(qkv_block, 2, -1)
    qkv = [qkv_block, to_ring(qkv_block, 2, 1), qkv_right, to_ring(qkv_right, 2, -1)]
    middle_block = whole_call(
        join_middle,
        "join_middle",
        info,
        rest_ring,
        shape_of((SIDE, share, middle_cols)),
        limit=8,
        after=[*qkv[1:3], token_pieces],
    )
    left = to_ring(middle_block, 2, 1)
    middle = [middle_block, left, to_ring(middle_block, 2, -1), to_ring(left, 2, 1)]
    context = whole_call(
        span_attention,
        "span_attention",
        info,
        [token_pieces, *qkv],
        shape_of((tensor_count // 2, all_rows, share)),
        [pltpu.VMEM((all_rows, 3 * width // 2), jnp.bfloat16)],
        flops=2 * all_rows * width * 3 * width // 2,
    )
    lower_shape = shape_of((SIDE, share, width + half_cols))
    far_shape = shape_of((SIDE, share, half_cols))
    lower_up, lower_down, far_kept, far_beyond = whole_call(
        join_lower,
        "join_lower",
        info,
        [*rest_ring, kept_cols, beyond_cols],
        (lower_shape, lower_shape, far_shape, far_shape),
        limit=8,
        after=[context],
    )
    lower_left = to_ring(lower_up, 2, 1)
    lower = [lower_up, lower_left, to_ring(lower_down, 2, -1), to_ring(lower_left, 2, 1)]
    far_beyond = to_ring(far_beyond, 2, 2)
    attended = whole_call(
        context_out,
        "context_out",
        info,
        [context, to_core(context), token_pieces, *middle],
        shape_of((all_rows, width // 2)),
        [pltpu.VMEM((tensor_count, all_rows, share), jnp.bfloat16)],
        flops=2 * all_rows * width * width // 2,
    )
    first_out, inner = whole_call(
        norm_up,
        "norm_up",
        info,
        [attended, to_core(attended), *middle],
        (shape_of((all_rows, width)), shape_of((tensor_count, all_rows, units))),
        [pltpu.VMEM((tensor_count, all_rows, share), jnp.bfloat16)],
        flops=2 * all_rows * width * width,
    )
    kept, sent = whole_call(
        down,
        "down",
        info,
        [inner, first_out, *lower],
        (
            shape_of((all_rows // 2, width), jnp.float32),
            shape_of((all_rows // 2, width)),
        ),
        [pltpu.VMEM((all_rows, width), jnp.float32)],
        flops=2 * all_rows * width * width,
    )
    outgoing = whole_call(
        norm_pool,
        "norm_pool",
        info,
        [kept, to_core(sent), pick],
        shape_of((seq_count, tensor_count, width // 128, 128)),
        [pltpu.VMEM((seq_count, width // 128, 128), jnp.float32)],
    )
    arrived = lax.all_to_all(
        outgoing.reshape(device_count, width // 128, 128), AXES, 0, 0
    )

    proj_mine = whole_call(
        join_proj,
        "join_proj",
        info,
        [far_kept, lower[1], lower[2], far_beyond],
        shape_of((SIDE, SIDE, share, half_cols)),
        limit=8,
        after=[outgoing],
    )
    proj_other = to_core(proj_mine)
    own_cols = whole_call(
        embed,
        "embed",
        info,
        [arrived, order, proj_in, proj_mine, proj_other],
        shape_of((rows, share_cols)),
        [
            pltpu.VMEM((device_count, width // 128, 128), jnp.float32),
            pltpu.VMEM((tensor_count, rows, proj_out.shape[0]), jnp.bfloat16),
        ],
        flops=2 * rows * width * (width + share_cols),
    )
    first_block = whole_call(
        join_blocks,
        "join_columns",
        info,
        short_ring(own_cols),
        shape_of((SIDE, rows, share_cols)),
        limit=4,
    )
    near_left = to_ring(first_block, 2, 1)
    near_right = to_ring(first_block, 2, -1)
    query_cols = q_weight.shape[1]
    kv_cols = key_value_weight.shape[2]
    key_start = tensor_index * kv_cols % HEAD_WIDTH
    key_cosine = lax.dynamic_slice_in_dim(cosine, key_start, kv_cols, 1)
    key_sine = lax.dynamic_slice_in_dim(sine, key_start, kv_cols, 1)
    gain = norm_gain.reshape(tensor_count, 1, share_cols)
    kv_pair = key_value_weight.transpose(0, 2, 1).reshape(2 * kv_cols, model_width)
    sums = (
        shape_of((rows, query_cols), jnp.float32),
        shape_of((rows, 2 * kv_cols), jnp.float32),
        shape_of((rows, 1), jnp.float32),
    )
    block_flops = 2 * rows * model_width // SIDE * (query_cols + 2 * kv_cols)
    totals = whole_call(
        functools.partial(project, starts=(0,), count=1),
        "project_own",
        info,
        [first_block, gain, q_weight, kv_pair],
        sums,
        flops=block_flops,
    )
    embedded = [first_block, near_left, near_right, to_ring(near_left, 2, 1)]
    totals = whole_call(
        functools.partial(project, starts=(1, 2), count=2),
        "project_near",
        info,
        [embedded[1], embedded[2], gain, q_weight, kv_pair, *totals],
        sums,
        flops=2 * block_flops,
    )
    own_kv, scale = whole_call(
        last_keys,
        "last_keys",
        info,
        [
            embedded[3],
            gain,
            kv_pair,
            totals[1],
            totals[2],
            key_cosine,
            key_sine,
            swap[:kv_cols, :kv_cols],
        ],
        (shape_of((2, rows, kv_cols)), shape_of((rows, 1), jnp.float32)),
    )
    partner_kv = lax.ppermute(
        own_kv, "tensor", [(index, index ^ 1) for index in range(tensor_count)]
    )
    query = whole_call(
        last_queries,
        "last_queries",
        info,
        [embedded[3], gain, q_weight, totals[0], scale, cosine, sine, swap],
        shape_of((rows, query_cols)),
        flops=block_flops,
    )
    partial = whole_call(
        attend_out,
        "attend_out",
        info,
        [query, own_kv, partner_kv, allowed, deal, out_weight],
        (shape_of((rows // SIDE, model_width)),) * 4,
        [pltpu.VMEM((rows, query_cols), jnp.bfloat16)],
        flops=2 * rows * model_width * query_cols,
    )
    arrived_sums = [
        to_ring(part, 2, distance) for part, distance in zip(partial[1:], (1, -1, 2))
    ]
    kept_sum, *sent_sums = whole_call(
        add_ring,
        "add_ring",
        info,
        [partial[0], *arrived_sums],
        (shape_of((own_rows, model_width), jnp.float32),)
        + (shape_of((own_rows, model_width)),) * 3,
    )
    terms = [to_ring(part, 1, distance) for part, distance in zip(sent_sums, (1, -1, 2))]
    own_embedded = [
        lax.dynamic_slice_in_dim(block, tensor_index * own_rows, own_rows, 1) for block in embedded
    ]
    return whole_call(
        finish,
        "finish",
        live_info,
        [kept_sum, *terms, *own_embedded],
        shape_of((own_rows, model_width)),
    )


def solution(mesh):
    return jax.shard_map(
        local,
        mesh=mesh,
        in_specs=(
            P(("seq", "tensor"), None, None),
            P(),
            P(),
            P(),
            P(),
            P("tensor", None),
            P("tensor", None),
            P("tensor", None),
            P("tensor", None),
            P(),
            P("tensor", None),
            P(),
            P(None, "tensor"),
            P(None, None, "tensor"),
            P("tensor", None),
        ),
        out_specs=P(("seq", "tensor"), None),
        check_vma=False,
    )
```

```python
import functools
import math

import jax
import jax.numpy as jnp
from jax import lax
from jax.experimental import pallas as pl
from jax.experimental.pallas import tpu as pltpu
from jax.sharding import PartitionSpec as P

QUERY_HEAD_COUNT = 64
KEY_VALUE_HEADS = 8
HEAD_WIDTH = 128
EH = 16
CPP = 16
SPAN_LIMIT = 128
SIDE = 4
AXES = ("seq", "tensor")


def device_id(plane, core, x, y):
    return ((plane * 2 + core) * SIDE + x) * SIDE + y


def every_device():
    return [
        (plane, core, x, y)
        for plane in range(SIDE)
        for core in range(2)
        for x in range(SIDE)
        for y in range(SIDE)
    ]


def first_axis_is_y(core, phase):
    return (core == 0) == (phase == 1)


def ring_pairs(phase, distance):
    pairs = []
    for plane, core, x, y in every_device():
        if first_axis_is_y(core, phase):
            target = device_id(plane, core, x, (y + distance) % SIDE)
        else:
            target = device_id(plane, core, (x + distance) % SIDE, y)
        pairs.append((device_id(plane, core, x, y), target))
    return pairs


def ring_groups(phase):
    groups = []
    for plane in range(SIDE):
        for core in range(2):
            for fixed in range(SIDE):
                groups.append(
                    [
                        device_id(plane, core, fixed, moving)
                        if first_axis_is_y(core, phase)
                        else device_id(plane, core, moving, fixed)
                        for moving in range(SIDE)
                    ]
                )
    return groups


def to_ring(value, phase, distance):
    return lax.ppermute(value, AXES, ring_pairs(phase, distance))


def to_core(value):
    return lax.ppermute(value, "seq", [(index, index ^ 1) for index in range(8)])


def short_ring(block):
    return [block] + [to_ring(block, 1, distance) for distance in (1, -1, 2)]


def short_relay(block):
    left = to_ring(block, 1, 1)
    right = to_ring(block, 1, -1)
    return [block, left, right, to_ring(right, 1, -1)]


VMEM = pl.BlockSpec(memory_space=pltpu.VMEM)
SMEM = pl.BlockSpec(memory_space=pltpu.SMEM)
ANYWHERE = pl.BlockSpec(memory_space=pl.ANY)
MIB = 2**20


def shape_of(shape, dtype=jnp.bfloat16):
    return jax.ShapeDtypeStruct(shape, dtype)


def whole_call(body, name, info, arrays, outs, scratch=(), limit=12, flops=0, far=(), after=()):
    count = len(arrays) + len(far)

    def run(*refs):
        body(*refs[: 1 + count], *refs[1 + count + len(after) :])

    moved = sum(array.size * array.dtype.itemsize for array in arrays)
    return pl.pallas_call(
        run,
        name=name,
        out_shape=outs,
        in_specs=[SMEM] + [VMEM] * len(arrays) + [ANYWHERE] * (len(far) + len(after)),
        out_specs=jax.tree.map(lambda _: VMEM, outs),
        scratch_shapes=list(scratch),
        compiler_params=pltpu.CompilerParams(vmem_limit_bytes=limit * MIB),
        cost_estimate=pl.CostEstimate(flops=flops, bytes_accessed=moved, transcendentals=0),
    )(info, *arrays, *far, *after)


def dot32(left, right):
    return jnp.dot(left, right, preferred_element_type=jnp.float32)


def dot_last(left, right):
    return lax.dot_general(
        left, right, (((1,), (1,)), ((), ())), preferred_element_type=jnp.float32
    )


def gelu_exact(values):
    return 0.5 * values * (1.0 + lax.erf(values * (0.5**0.5)))


def take_qkv(info, weight, out):
    cols = weight.shape[1] // 6
    for part in range(3):
        start = pl.multiple_of((2 * part + info[16]) * cols, cols)
        out[:, part * cols : (part + 1) * cols] = weight[:, pl.ds(start, cols)]


def take_rest(info, out_weight, up_weight, down_weight, proj, up_out, down_out, kept, beyond):
    core, near = info[16], info[19]
    rows, width = out_weight.shape
    cols = width // 2
    units = down_weight.shape[0] // 2
    pieces = [out_weight[:, pl.ds(pl.multiple_of(core * cols, cols), cols)]]
    for pair in range(up_weight.shape[1] // (4 * units)):
        halves = []
        for step in range(2):
            low = (2 * pair + step) * 2 * units
            halves.append(
                jnp.where(
                    core == 0,
                    up_weight[:, low : low + units].astype(jnp.float32),
                    up_weight[:, low + units : low + 2 * units].astype(jnp.float32),
                )
            )
        pieces.append(jnp.concatenate(halves, axis=1).astype(jnp.bfloat16))
    pieces.append(down_weight[pl.ds(pl.multiple_of(core * units, units), units), :])
    at = 0
    for piece in pieces:
        for out in (up_out, down_out):
            out[:, at : at + piece.shape[1]] = piece
        at += piece.shape[1]
    block = kept.shape[1] // SIDE
    for out, start, distance in ((kept, 0, 0), (up_out, at, 1), (down_out, at, SIDE - 1), (beyond, 0, 2)):
        target = lax.rem(near + distance, SIDE)
        for index in range(SIDE):
            shard = jnp.where(core == 0, SIDE * index + target, SIDE * target + index)
            source = pl.multiple_of((2 * shard + core) * block, block)
            out[:, start + index * block : start + (index + 1) * block] = proj[:, pl.ds(source, block)]


def join_blocks(info, own, left, right, opposite, out):
    for index, block in enumerate((own, left, right, opposite)):
        out[index] = block[...]


def join_middle(info, own, left, right, opposite, out):
    for index, block in enumerate((own, left, right, opposite)):
        out[index] = block[:, : out.shape[2]]


def join_lower(info, own, left, right, opposite, kept, beyond, up_out, down_out, far_kept, far_beyond):
    far = info[20]
    block = far_kept.shape[2]
    width = up_out.shape[2] - block
    start = own.shape[1] - kept.shape[1] - width
    for index, part in enumerate((own, left, right, opposite)):
        for out in (up_out, down_out):
            out[index, :, :width] = part[:, start : start + width]
        columns, first = (part, start + width) if index in (1, 2) else (kept, 0)
        if index == 3:
            columns = beyond
        for out, at, distance in (
            (far_kept, 0, 0),
            (up_out, width, 1),
            (down_out, width, SIDE - 1),
            (far_beyond, 0, 2),
        ):
            target = lax.rem(far + distance, SIDE)
            source = pl.multiple_of(first + target * block, 128)
            out[index, :, at : at + block] = columns[:, pl.ds(source, block)]


def join_proj(info, own, left, right, opposite, out):
    block = own.shape[2]
    for index, part in enumerate((own, left, right, opposite)):
        out[index] = part[:, :, part.shape[2] - block :]


def both_rows(info, mine, other, pieces_out):
    half, width = mine.shape
    core = info[16]
    piece = pieces_out.shape[2]
    near = pl.ds(pl.multiple_of(core * half, half), half)
    far = pl.ds(pl.multiple_of((1 - core) * half, half), half)
    for index in range(width // piece):
        pieces_out[index, near, :] = mine[:, index * piece : (index + 1) * piece]
        pieces_out[index, far, :] = other[:, index * piece : (index + 1) * piece]


def ring_dot(info, pieces, blocks, low, high):
    total = None
    for at, block in enumerate(blocks):
        act = jnp.concatenate([pieces[info[4 * at + step]] for step in range(SIDE)], axis=1)
        weight = block[:, :, low:high].reshape(act.shape[1], high - low)
        part = dot32(act, weight)
        total = part if total is None else total + part
    return total


def masked_softmax(scores, seen, size):
    scores = [jnp.where(seen, score / math.sqrt(size), -1e30) for score in scores]
    tops = [jnp.max(score, axis=1, keepdims=True) for score in scores]
    powers = [jnp.exp(score - top) for score, top in zip(scores, tops)]
    sums = [jnp.sum(power, axis=1, keepdims=True) for power in powers]
    return [(power / total).astype(jnp.bfloat16) for power, total in zip(powers, sums)]


def span_attention(info, pieces, w0, w1, w2, w3, context, mixed):
    cols = w0.shape[2]
    third = cols // 3
    mixed[...] = ring_dot(info, pieces, (w0, w1, w2, w3), 0, cols).astype(jnp.bfloat16)
    size = context.shape[2]
    half = mixed.shape[0] // 2
    span = 16
    row = lax.broadcasted_iota(jnp.int32, (half, half), 0) // span
    col = lax.broadcasted_iota(jnp.int32, (half, half), 1) // span
    same = row == col
    heads = third // size
    units = [
        (head, slice(part * half, (part + 1) * half)) for head in range(heads) for part in range(2)
    ]
    scores = [
        lax.dot_general(
            mixed[rows, head * size : (head + 1) * size],
            mixed[rows, third + head * size : third + (head + 1) * size],
            (((1,), (1,)), ((), ())),
            preferred_element_type=jnp.float32,
        )
        for head, rows in units
    ]
    probs = masked_softmax(scores, same, size)
    for (head, rows), prob in zip(units, probs):
        value = mixed[rows, 2 * third + head * size : 2 * third + (head + 1) * size]
        context[head, rows, :] = dot32(prob, value).astype(jnp.bfloat16)


def context_out(info, mine, other, tokens, w0, w1, w2, w3, attended, pieces):
    heads = mine.shape[0]
    core = info[16]
    pieces[pl.ds(core * heads, heads)] = mine[...]
    pieces[pl.ds((1 - core) * heads, heads)] = other[...]
    cols = attended.shape[1]
    residual = jnp.concatenate([tokens[core * heads + index] for index in range(heads)], axis=1)
    total = ring_dot(info, pieces, (w0, w1, w2, w3), 0, cols)
    attended[...] = (residual.astype(jnp.float32) + total).astype(jnp.bfloat16)


def norm_up(info, mine, other, w0, w1, w2, w3, first_out, inner, pieces):
    core = info[16]
    cols = mine.shape[1]
    width = 2 * cols
    near = mine[...].astype(jnp.float32)
    far = other[...].astype(jnp.float32)
    low = jnp.where(core == 0, near, far)
    high = jnp.where(core == 0, far, near)
    mean = (jnp.sum(low, 1, keepdims=True) + jnp.sum(high, 1, keepdims=True)) / width
    low, high = low - mean, high - mean
    var = (jnp.sum(low * low, 1, keepdims=True) + jnp.sum(high * high, 1, keepdims=True)) / width
    scale = lax.rsqrt(var + 1e-05)
    first_out[:, :cols] = (low * scale).astype(jnp.bfloat16)
    first_out[:, cols:] = (high * scale).astype(jnp.bfloat16)
    size = pieces.shape[2]
    for index in range(pieces.shape[0]):
        pieces[index] = first_out[:, index * size : (index + 1) * size]
    total = ring_dot(info, pieces, (w0, w1, w2, w3), cols, w0.shape[2])
    act = gelu_exact(total).astype(jnp.bfloat16)
    unit = inner.shape[2]
    for index in range(inner.shape[0]):
        inner[index] = act[:, index * unit : (index + 1) * unit]


def down(info, inner, first_out, w0, w1, w2, w3, kept, sent, total):
    core = info[16]
    total[...] = ring_dot(info, inner, (w0, w1, w2, w3), 0, total.shape[1])
    half = kept.shape[0]
    rows = pl.ds(pl.multiple_of(core * half, half), half)
    kept[...] = total[rows, :] + first_out[rows, :].astype(jnp.float32)
    sent[...] = total[pl.ds(pl.multiple_of((1 - core) * half, half), half), :].astype(jnp.bfloat16)


def norm_pool(info, kept, arrived, pick, out, lanes):
    half, width = kept.shape
    values = kept[...] + arrived[...].astype(jnp.float32)
    mean = jnp.mean(values, axis=1, keepdims=True)
    values = values - mean
    values = values * lax.rsqrt(jnp.mean(values * values, axis=1, keepdims=True) + 1e-05)
    spans = pick.shape[1]
    pooled = jnp.mean(values.reshape(spans, half // spans, width), axis=1).astype(jnp.bfloat16)
    by_slot = dot32(pick[...], pooled)
    for index in range(width // 128):
        lanes[:, index, :] = by_slot[:, index * 128 : (index + 1) * 128]
    out[...] = jnp.broadcast_to(lanes[...].astype(jnp.bfloat16)[:, None], out.shape)


def embed(info, arrived, order, proj_in, mine, other, out, lanes, pieces):
    core = info[16]
    lanes[...] = arrived[...].astype(jnp.float32)
    columns = [
        dot32(order[...], lanes[:, index, :].astype(jnp.bfloat16)).astype(jnp.bfloat16)
        for index in range(lanes.shape[1])
    ]
    arranged = jnp.concatenate(columns, axis=1)
    hidden = gelu_exact(dot32(arranged, proj_in[...])).astype(jnp.bfloat16)
    units, cols = mine.shape[2:]
    for index in range(pieces.shape[0]):
        pieces[index] = hidden[:, index * units : (index + 1) * units]
    near, far = None, None
    for at in range(SIDE):
        act = jnp.concatenate([pieces[info[SIDE * at + step]] for step in range(SIDE)], axis=1)
        term = dot32(act, mine[at].reshape(SIDE * units, cols))
        near = term if near is None else near + term
        act = jnp.concatenate([pieces[info[22 + SIDE * at + step]] for step in range(SIDE)], axis=1)
        term = dot32(act, other[at].reshape(SIDE * units, cols))
        far = term if far is None else far + term
    out[:, :cols] = jnp.where(core == 0, near, far).astype(jnp.bfloat16)
    out[:, cols:] = jnp.where(core == 0, far, near).astype(jnp.bfloat16)


def project(info, *refs, starts, count):
    blocks, refs = refs[:count], refs[count:]
    gain, q_weight, kv_weight = refs[:3]
    before = refs[3:6] if len(refs) > 6 else None
    q_total, kv_total, square = refs[-3:]
    depth = blocks[0].shape[2]
    queries, both = None, None
    squares = None
    for at, block in zip(starts, blocks):
        for step in range(SIDE):
            shard = info[SIDE * at + step]
            wide = block[step].astype(jnp.float32)
            act = (wide * gain[shard]).astype(jnp.bfloat16)
            span = pl.ds(pl.multiple_of(shard * depth, depth), depth)
            q_term = dot32(act, q_weight[span, :])
            kv_term = dot_last(act, kv_weight[:, span])
            term = jnp.sum(wide * wide, axis=1, keepdims=True)
            queries = q_term if queries is None else queries + q_term
            both = kv_term if both is None else both + kv_term
            squares = term if squares is None else squares + term
    if before is not None:
        queries, both, squares = queries + before[0][...], both + before[1][...], squares + before[2][...]
    q_total[...] = queries
    kv_total[...] = both
    square[...] = squares


def turn(values, cosine, sine, swap):
    turned = jnp.dot(
        values, swap, preferred_element_type=jnp.float32, precision=lax.Precision.HIGHEST
    )
    return values * cosine + turned * sine


def last_keys(info, block, gain, kv_weight, kv_before, sq_before, cosine, sine, swap, out, scale):
    depth = block.shape[2]
    both = kv_before[...]
    squares = sq_before[...]
    for step in range(SIDE):
        shard = info[SIDE * 3 + step]
        wide = block[step].astype(jnp.float32)
        act = (wide * gain[shard]).astype(jnp.bfloat16)
        span = pl.ds(pl.multiple_of(shard * depth, depth), depth)
        both += dot_last(act, kv_weight[:, span])
        squares += jnp.sum(wide * wide, axis=1, keepdims=True)
    factor = lax.rsqrt(squares / (depth * SIDE * SIDE) + 1e-05)
    scale[...] = factor
    both = both * factor
    cols = out.shape[2]
    out[0] = turn(both[:, :cols], cosine[...], sine[...], swap[...]).astype(jnp.bfloat16)
    out[1] = both[:, cols:].astype(jnp.bfloat16)


def last_queries(info, block, gain, q_weight, q_before, scale, cosine, sine, swap, out):
    depth = block.shape[2]
    total = q_before[...]
    for step in range(SIDE):
        shard = info[SIDE * 3 + step]
        act = (block[step].astype(jnp.float32) * gain[shard]).astype(jnp.bfloat16)
        span = pl.ds(pl.multiple_of(shard * depth, depth), depth)
        total += dot32(act, q_weight[span, :])
    for head in range(out.shape[1] // HEAD_WIDTH):
        lanes = slice(head * HEAD_WIDTH, (head + 1) * HEAD_WIDTH)
        query = total[:, lanes] * scale[...]
        out[:, lanes] = turn(query, cosine[...], sine[...], swap[...]).astype(jnp.bfloat16)


def attend_out(info, query, mine, partner, allowed, deal, weight, *refs):
    outs, context = refs[:4], refs[4]
    odd = info[17] == 1
    own = mine[...].astype(jnp.float32)
    far = partner[...].astype(jnp.float32)
    low = jnp.where(odd, far, own)
    high = jnp.where(odd, own, far)
    both = jnp.concatenate([low, high], axis=2).astype(jnp.bfloat16)
    key, value = both[0], both[1]
    heads = [
        slice(head * HEAD_WIDTH, (head + 1) * HEAD_WIDTH)
        for head in range(query.shape[1] // HEAD_WIDTH)
    ]
    scores = [
        lax.dot_general(
            query[:, lanes], key, (((1,), (1,)), ((), ())), preferred_element_type=jnp.float32
        )
        for lanes in heads
    ]
    for lanes, prob in zip(heads, masked_softmax(scores, allowed[...] > 0, HEAD_WIDTH)):
        context[:, lanes] = dot32(prob, value).astype(jnp.bfloat16)
    dealt = dot32(deal[...], context[...]).astype(jnp.bfloat16)
    rows = outs[0].shape[0]
    step = weight.shape[1] // 8
    for start in range(0, weight.shape[1], step):
        result = dot32(dealt, weight[:, start : start + step])
        for index, out in enumerate(outs):
            piece = result[index * rows : (index + 1) * rows]
            out[:, start : start + step] = piece.astype(jnp.bfloat16)


def add_ring(info, own, left, right, opposite, kept, *sent):
    rows = kept.shape[0]
    step = 1024
    for start in range(0, own.shape[1], step):
        lanes = slice(start, start + step)
        total = own[:, lanes].astype(jnp.float32)
        for block in (left, right, opposite):
            total = total + block[:, lanes].astype(jnp.float32)
        kept[:, lanes] = total[:rows]
        for index, out in enumerate(sent):
            piece = total[(index + 1) * rows : (index + 2) * rows]
            out[:, lanes] = piece.astype(jnp.bfloat16)


def finish(info, kept, left, right, opposite, *refs):
    own, out = refs[:-1], refs[-1]
    rows, cols = own[0].shape[1:]
    live = info[18] + lax.broadcasted_iota(jnp.int32, (rows, cols), 0) < info[21]
    for at, block in enumerate(own):
        for step in range(SIDE):
            lanes = pl.ds(pl.multiple_of(info[SIDE * at + step] * cols, cols), cols)
            total = kept[:, lanes] + block[step].astype(jnp.float32)
            for term in (left, right, opposite):
                total = total + term[:, lanes].astype(jnp.float32)
            out[:, lanes] = jnp.where(live, total, 0.0).astype(jnp.bfloat16)


def visibility(masks, live_count):
    positions = jnp.arange(SPAN_LIMIT)
    passage = positions // CPP
    expanded = jnp.repeat(jnp.repeat(masks, CPP, axis=0), CPP, axis=1) > 0
    same_passage = passage[:, None] == passage[None, :]
    earlier = positions[None, :] <= positions[:, None]
    key_live = positions[None, :] < live_count
    diagonal = positions[:, None] == positions[None, :]
    return diagonal | earlier & key_live & (same_passage | expanded)


def local(
    span_tokens,
    enc_dest,
    passages,
    req_slot,
    block_mask,
    enc_qkv,
    enc_out,
    enc_up,
    enc_down,
    proj_in,
    proj_out,
    norm_gain,
    q_weight,
    key_value_weight,
    out_weight,
):
    tensor_count = lax.axis_size("tensor")
    seq_count = lax.axis_size("seq")
    tensor_index = lax.axis_index("tensor")
    seq_index = lax.axis_index("seq")
    core = seq_index % 2
    device_count = tensor_count * seq_count
    rows = SPAN_LIMIT
    own_rows = rows // tensor_count
    spans, span_size, width = span_tokens.shape
    model_width = proj_out.shape[1]
    share = enc_qkv.shape[0]
    x_index, y_index = tensor_index // SIDE, tensor_index % SIDE

    steps = jnp.array([0, SIDE - 1, 1, 2])
    outer, inside = jnp.repeat(steps, SIDE), jnp.tile(steps, SIDE)
    by_x = SIDE * ((x_index + outer) % SIDE) + (y_index + inside) % SIDE
    by_y = SIDE * ((x_index + inside) % SIDE) + (y_index + outer) % SIDE
    shards = jnp.where(core == 0, by_x, by_y)
    near = jnp.where(core == 0, y_index, x_index)
    far = jnp.where(core == 0, x_index, y_index)
    scalars = jnp.stack([core, tensor_index % 2, tensor_index * own_rows, near, far])
    other_shards = jnp.where(core == 0, by_y, by_x)
    info = jnp.concatenate([shards, scalars, core[None], other_shards]).astype(jnp.int32)

    ahead = jnp.array([0, 1, SIDE - 1, 2])
    outer, inside = jnp.repeat(ahead, SIDE), jnp.tile(ahead, SIDE)
    owner_x = SIDE * ((x_index + outer) % SIDE) + (y_index + inside) % SIDE
    owner_y = SIDE * ((x_index + inside) % SIDE) + (y_index + outer) % SIDE
    owners = jnp.where(core == 0, owner_x, owner_y)
    from_row = (owners[:, None] * own_rows + jnp.arange(own_rows)[None, :]).reshape(-1)
    deal = (from_row[:, None] == jnp.arange(rows)[None, :]).astype(jnp.bfloat16)

    requests = jnp.arange(req_slot.shape[0])
    dest_slot = jnp.sum(
        jnp.where(enc_dest[:, None] // SPAN_LIMIT == requests[None, :], req_slot[None, :], 0), axis=1
    ).reshape(device_count, own_rows)
    dest_place = (enc_dest % SPAN_LIMIT).reshape(device_count, own_rows)
    own_slots = lax.dynamic_slice_in_dim(
        dest_slot, seq_index * tensor_count + tensor_index, 1, 0
    )
    pick = (jnp.arange(seq_count)[:, None] == own_slots).astype(jnp.bfloat16)
    place_of = jnp.sum(jnp.where(dest_slot == seq_index, dest_place, 0), axis=1)
    order = (jnp.arange(rows)[:, None] == place_of[None, :]).astype(jnp.bfloat16)
    chosen = jnp.sum(jnp.where(req_slot == seq_index, requests, 0))
    live_count = jnp.sum(jnp.where(requests == chosen, passages, 0)) * CPP
    masks = jnp.sum(
        jnp.where(requests[:, None, None] == chosen, block_mask, 0), axis=0
    )
    allowed = visibility(masks, live_count).astype(jnp.float32)
    live_info = jnp.concatenate([info[:21], live_count[None]]).astype(jnp.int32)

    positions = jnp.arange(rows).astype(jnp.float32)
    lane = jnp.arange(HEAD_WIDTH)
    frequency = jnp.exp(
        -(2.0 * (lane // 2).astype(jnp.float32) / HEAD_WIDTH) * math.log(500000.0)
    )
    angles = positions[:, None] * frequency[None, :]
    cosine, sine = jnp.cos(angles), jnp.sin(angles)
    swap = jnp.where(
        (lane[:, None] ^ 1) == lane[None, :], jnp.where(lane[None, :] % 2 == 0, -1.0, 1.0), 0.0
    ).astype(jnp.float32)

    kv_cols = key_value_weight.shape[2]
    key_start = tensor_index * kv_cols % HEAD_WIDTH
    key_cosine = lax.dynamic_slice_in_dim(cosine, key_start, kv_cols, 1)
    key_sine = lax.dynamic_slice_in_dim(sine, key_start, kv_cols, 1)
    early = [pick, order, deal, allowed, cosine, sine, key_cosine, key_sine, swap]

    own_tokens = span_tokens.reshape(spans * span_size, width)
    other_tokens = to_core(own_tokens)
    token_pieces = whole_call(
        both_rows,
        "both_rows",
        info,
        [own_tokens, other_tokens],
        shape_of((tensor_count, 2 * spans * span_size, share)),
    )
    units = enc_down.shape[0] // 2
    middle_cols = width // 2 + units * tensor_count
    share_cols = model_width // tensor_count
    half_cols = share_cols // 2
    rest_shape = shape_of((share, middle_cols + width + SIDE * half_cols))
    dealt_shape = shape_of((share, SIDE * half_cols))
    own_qkv = whole_call(
        take_qkv, "take_qkv", info, [enc_qkv], shape_of((share, 3 * width // 2)), limit=4
    )
    rest_up, rest_down, kept_cols, beyond_cols = whole_call(
        take_rest,
        "take_rest",
        info,
        [enc_out, enc_up, enc_down, proj_out],
        (rest_shape, rest_shape, dealt_shape, dealt_shape),
        limit=60,
        after=[own_qkv],
    )
    qkv_ring = short_ring(own_qkv)
    rest_left = to_ring(rest_up, 1, 1)
    rest_ring = [rest_up, rest_left, to_ring(rest_down, 1, -1), to_ring(rest_left, 1, 1)]
    beyond_cols = to_ring(beyond_cols, 1, 2)
    qkv_block = whole_call(
        join_blocks,
        "join_qkv",
        info,
        qkv_ring,
        shape_of((SIDE, share, 3 * width // 2)),
        limit=6,
    )
    all_rows = 2 * spans * span_size

    qkv_right = to_ring(qkv_block, 2, -1)
    qkv = [qkv_block, to_ring(qkv_block, 2, 1), qkv_right, to_ring(qkv_right, 2, -1)]
    middle_block = whole_call(
        join_middle,
        "join_middle",
        info,
        rest_ring,
        shape_of((SIDE, share, middle_cols)),
        limit=8,
        after=[*qkv[1:3], token_pieces, *early],
    )
    left = to_ring(middle_block, 2, 1)
    middle = [middle_block, left, to_ring(middle_block, 2, -1), to_ring(left, 2, 1)]
    context = whole_call(
        span_attention,
        "span_attention",
        info,
        [token_pieces, *qkv],
        shape_of((tensor_count // 2, all_rows, share)),
        [pltpu.VMEM((all_rows, 3 * width // 2), jnp.bfloat16)],
        flops=2 * all_rows * width * 3 * width // 2,
    )
    lower_shape = shape_of((SIDE, share, width + half_cols))
    far_shape = shape_of((SIDE, share, half_cols))
    lower_up, lower_down, far_kept, far_beyond = whole_call(
        join_lower,
        "join_lower",
        info,
        [*rest_ring, kept_cols, beyond_cols],
        (lower_shape, lower_shape, far_shape, far_shape),
        limit=8,
        after=[context, left],
    )
    lower_right = to_ring(lower_down, 2, -1)
    lower = [lower_up, to_ring(lower_up, 2, 1), lower_right, to_ring(lower_right, 2, -1)]
    far_beyond = to_ring(far_beyond, 2, 2)
    attended = whole_call(
        context_out,
        "context_out",
        info,
        [context, to_core(context), token_pieces, *middle],
        shape_of((all_rows, width // 2)),
        [pltpu.VMEM((tensor_count, all_rows, share), jnp.bfloat16)],
        flops=2 * all_rows * width * width // 2,
    )
    first_out, inner = whole_call(
        norm_up,
        "norm_up",
        info,
        [attended, to_core(attended), *middle],
        (shape_of((all_rows, width)), shape_of((tensor_count, all_rows, units))),
        [pltpu.VMEM((tensor_count, all_rows, share), jnp.bfloat16)],
        flops=2 * all_rows * width * width,
    )
    proj_mine = whole_call(
        join_proj,
        "join_proj",
        info,
        [far_kept, lower[1], lower[2], far_beyond],
        shape_of((SIDE, SIDE, share, half_cols)),
        limit=8,
    )
    proj_other = to_core(proj_mine)
    kept, sent = whole_call(
        down,
        "down",
        info,
        [inner, first_out, *lower],
        (
            shape_of((all_rows // 2, width), jnp.float32),
            shape_of((all_rows // 2, width)),
        ),
        [pltpu.VMEM((all_rows, width), jnp.float32)],
        flops=2 * all_rows * width * width,
        after=[proj_mine],
    )
    outgoing = whole_call(
        norm_pool,
        "norm_pool",
        info,
        [kept, to_core(sent), pick],
        shape_of((seq_count, tensor_count, width // 128, 128)),
        [pltpu.VMEM((seq_count, width // 128, 128), jnp.float32)],
    )
    arrived = lax.all_to_all(
        outgoing.reshape(device_count, width // 128, 128), AXES, 0, 0
    )

    own_cols = whole_call(
        embed,
        "embed",
        info,
        [arrived, order, proj_in, proj_mine, proj_other],
        shape_of((rows, share_cols)),
        [
            pltpu.VMEM((device_count, width // 128, 128), jnp.float32),
            pltpu.VMEM((tensor_count, rows, proj_out.shape[0]), jnp.bfloat16),
        ],
        flops=2 * rows * width * (width + share_cols),
    )
    first_block = whole_call(
        join_blocks,
        "join_columns",
        info,
        short_ring(own_cols),
        shape_of((SIDE, rows, share_cols)),
        limit=4,
    )
    near_left = to_ring(first_block, 2, 1)
    near_right = to_ring(first_block, 2, -1)
    query_cols = q_weight.shape[1]
    kv_cols = key_value_weight.shape[2]
    gain = norm_gain.reshape(tensor_count, 1, share_cols)
    kv_pair = key_value_weight.transpose(0, 2, 1).reshape(2 * kv_cols, model_width)
    sums = (
        shape_of((rows, query_cols), jnp.float32),
        shape_of((rows, 2 * kv_cols), jnp.float32),
        shape_of((rows, 1), jnp.float32),
    )
    block_flops = 2 * rows * model_width // SIDE * (query_cols + 2 * kv_cols)
    totals = whole_call(
        functools.partial(project, starts=(0,), count=1),
        "project_own",
        info,
        [first_block, gain, q_weight, kv_pair],
        sums,
        flops=block_flops,
    )
    relayed, _ = lax.optimization_barrier((near_left, totals[2]))
    embedded = [first_block, relayed, near_right, to_ring(relayed, 2, 1)]
    totals = whole_call(
        functools.partial(project, starts=(1, 2), count=2),
        "project_near",
        info,
        [embedded[1], embedded[2], gain, q_weight, kv_pair, *totals],
        sums,
        flops=2 * block_flops,
    )
    own_kv, scale = whole_call(
        last_keys,
        "last_keys",
        info,
        [
            embedded[3],
            gain,
            kv_pair,
            totals[1],
            totals[2],
            key_cosine,
            key_sine,
            swap[:kv_cols, :kv_cols],
        ],
        (shape_of((2, rows, kv_cols)), shape_of((rows, 1), jnp.float32)),
    )
    partner_kv = lax.ppermute(
        own_kv, "tensor", [(index, index ^ 1) for index in range(tensor_count)]
    )
    query = whole_call(
        last_queries,
        "last_queries",
        info,
        [embedded[3], gain, q_weight, totals[0], scale, cosine, sine, swap],
        shape_of((rows, query_cols)),
        flops=block_flops,
    )
    partial = whole_call(
        attend_out,
        "attend_out",
        info,
        [query, own_kv, partner_kv, allowed, deal, out_weight],
        (shape_of((rows // SIDE, model_width)),) * 4,
        [pltpu.VMEM((rows, query_cols), jnp.bfloat16)],
        flops=2 * rows * model_width * query_cols,
    )
    arrived_sums = [
        to_ring(part, 2, distance) for part, distance in zip(partial[1:], (1, -1, 2))
    ]
    kept_sum, *sent_sums = whole_call(
        add_ring,
        "add_ring",
        info,
        [partial[0], *arrived_sums],
        (shape_of((own_rows, model_width), jnp.float32),)
        + (shape_of((own_rows, model_width)),) * 3,
    )
    terms = [to_ring(part, 1, distance) for part, distance in zip(sent_sums, (1, -1, 2))]
    own_embedded = [
        lax.dynamic_slice_in_dim(block, tensor_index * own_rows, own_rows, 1) for block in embedded
    ]
    return whole_call(
        finish,
        "finish",
        live_info,
        [kept_sum, *terms, *own_embedded],
        shape_of((own_rows, model_width)),
    )


def solution(mesh):
    return jax.shard_map(
        local,
        mesh=mesh,
        in_specs=(
            P(("seq", "tensor"), None, None),
            P(),
            P(),
            P(),
            P(),
            P("tensor", None),
            P("tensor", None),
            P("tensor", None),
            P("tensor", None),
            P(),
            P("tensor", None),
            P(),
            P(None, "tensor"),
            P(None, None, "tensor"),
            P("tensor", None),
        ),
        out_specs=P(("seq", "tensor"), None),
        check_vma=False,
    )
```

```python
import functools
import math

import jax
import jax.numpy as jnp
from jax import lax
from jax.experimental import pallas as pl
from jax.experimental.pallas import tpu as pltpu
from jax.sharding import PartitionSpec as P

QUERY_HEAD_COUNT = 64
KEY_VALUE_HEADS = 8
HEAD_WIDTH = 128
EH = 16
CPP = 16
SPAN_LIMIT = 128
SIDE = 4
AXES = ("seq", "tensor")


def device_id(plane, core, x, y):
    return ((plane * 2 + core) * SIDE + x) * SIDE + y


def every_device():
    return [
        (plane, core, x, y)
        for plane in range(SIDE)
        for core in range(2)
        for x in range(SIDE)
        for y in range(SIDE)
    ]


def first_axis_is_y(core, phase):
    return (core == 0) == (phase == 1)


def ring_pairs(phase, distance):
    pairs = []
    for plane, core, x, y in every_device():
        if first_axis_is_y(core, phase):
            target = device_id(plane, core, x, (y + distance) % SIDE)
        else:
            target = device_id(plane, core, (x + distance) % SIDE, y)
        pairs.append((device_id(plane, core, x, y), target))
    return pairs


def ring_groups(phase):
    groups = []
    for plane in range(SIDE):
        for core in range(2):
            for fixed in range(SIDE):
                groups.append(
                    [
                        device_id(plane, core, fixed, moving)
                        if first_axis_is_y(core, phase)
                        else device_id(plane, core, moving, fixed)
                        for moving in range(SIDE)
                    ]
                )
    return groups


def to_ring(value, phase, distance):
    return lax.ppermute(value, AXES, ring_pairs(phase, distance))


def to_core(value):
    return lax.ppermute(value, "seq", [(index, index ^ 1) for index in range(8)])


def short_ring(block):
    return [block] + [to_ring(block, 1, distance) for distance in (1, -1, 2)]


def short_relay(block):
    left = to_ring(block, 1, 1)
    right = to_ring(block, 1, -1)
    return [block, left, right, to_ring(right, 1, -1)]


VMEM = pl.BlockSpec(memory_space=pltpu.VMEM)
SMEM = pl.BlockSpec(memory_space=pltpu.SMEM)
ANYWHERE = pl.BlockSpec(memory_space=pl.ANY)
MIB = 2**20


def shape_of(shape, dtype=jnp.bfloat16):
    return jax.ShapeDtypeStruct(shape, dtype)


def whole_call(body, name, info, arrays, outs, scratch=(), limit=12, flops=0, far=(), after=()):
    count = len(arrays) + len(far)

    def run(*refs):
        body(*refs[: 1 + count], *refs[1 + count + len(after) :])

    moved = sum(array.size * array.dtype.itemsize for array in arrays)
    return pl.pallas_call(
        run,
        name=name,
        out_shape=outs,
        in_specs=[SMEM] + [VMEM] * len(arrays) + [ANYWHERE] * (len(far) + len(after)),
        out_specs=jax.tree.map(lambda _: VMEM, outs),
        scratch_shapes=list(scratch),
        compiler_params=pltpu.CompilerParams(vmem_limit_bytes=limit * MIB),
        cost_estimate=pl.CostEstimate(flops=flops, bytes_accessed=moved, transcendentals=0),
    )(info, *arrays, *far, *after)


def dot32(left, right):
    return jnp.dot(left, right, preferred_element_type=jnp.float32)


def dot_last(left, right):
    return lax.dot_general(
        left, right, (((1,), (1,)), ((), ())), preferred_element_type=jnp.float32
    )


def gelu_exact(values):
    return 0.5 * values * (1.0 + lax.erf(values * (0.5**0.5)))


def take_qkv(info, weight, out):
    cols = weight.shape[1] // 6
    for part in range(3):
        start = pl.multiple_of((2 * part + info[16]) * cols, cols)
        out[:, part * cols : (part + 1) * cols] = weight[:, pl.ds(start, cols)]


def take_rest(info, out_weight, up_weight, down_weight, proj, up_out, down_out, kept, beyond):
    core, near = info[16], info[19]
    rows, width = out_weight.shape
    cols = width // 2
    units = down_weight.shape[0] // 2
    pieces = [out_weight[:, pl.ds(pl.multiple_of(core * cols, cols), cols)]]
    for pair in range(up_weight.shape[1] // (4 * units)):
        halves = []
        for step in range(2):
            low = (2 * pair + step) * 2 * units
            halves.append(
                jnp.where(
                    core == 0,
                    up_weight[:, low : low + units].astype(jnp.float32),
                    up_weight[:, low + units : low + 2 * units].astype(jnp.float32),
                )
            )
        pieces.append(jnp.concatenate(halves, axis=1).astype(jnp.bfloat16))
    pieces.append(down_weight[pl.ds(pl.multiple_of(core * units, units), units), :])
    at = 0
    for piece in pieces:
        for out in (up_out, down_out):
            out[:, at : at + piece.shape[1]] = piece
        at += piece.shape[1]
    block = kept.shape[1] // SIDE
    for out, start, distance in ((kept, 0, 0), (up_out, at, 1), (down_out, at, SIDE - 1), (beyond, 0, 2)):
        target = lax.rem(near + distance, SIDE)
        for index in range(SIDE):
            shard = jnp.where(core == 0, SIDE * index + target, SIDE * target + index)
            source = pl.multiple_of((2 * shard + core) * block, block)
            out[:, start + index * block : start + (index + 1) * block] = proj[:, pl.ds(source, block)]


def join_blocks(info, own, left, right, opposite, out):
    for index, block in enumerate((own, left, right, opposite)):
        out[index] = block[...]


def join_middle(info, own, left, right, opposite, out):
    for index, block in enumerate((own, left, right, opposite)):
        out[index] = block[:, : out.shape[2]]


def join_lower(info, own, left, right, opposite, kept, beyond, up_out, down_out, far_kept, far_beyond):
    far = info[20]
    block = far_kept.shape[2]
    width = up_out.shape[2] - block
    start = own.shape[1] - kept.shape[1] - width
    for index, part in enumerate((own, left, right, opposite)):
        for out in (up_out, down_out):
            out[index, :, :width] = part[:, start : start + width]
        columns, first = (part, start + width) if index in (1, 2) else (kept, 0)
        if index == 3:
            columns = beyond
        for out, at, distance in (
            (far_kept, 0, 0),
            (up_out, width, 1),
            (down_out, width, SIDE - 1),
            (far_beyond, 0, 2),
        ):
            target = lax.rem(far + distance, SIDE)
            source = pl.multiple_of(first + target * block, 128)
            out[index, :, at : at + block] = columns[:, pl.ds(source, block)]


def join_proj(info, own, left, right, opposite, out):
    block = own.shape[2]
    for index, part in enumerate((own, left, right, opposite)):
        out[index] = part[:, :, part.shape[2] - block :]


def both_rows(info, mine, other, pieces_out):
    half, width = mine.shape
    core = info[16]
    piece = pieces_out.shape[2]
    near = pl.ds(pl.multiple_of(core * half, half), half)
    far = pl.ds(pl.multiple_of((1 - core) * half, half), half)
    for index in range(width // piece):
        pieces_out[index, near, :] = mine[:, index * piece : (index + 1) * piece]
        pieces_out[index, far, :] = other[:, index * piece : (index + 1) * piece]


def ring_dot(info, pieces, blocks, low, high):
    total = None
    for at, block in enumerate(blocks):
        act = jnp.concatenate([pieces[info[4 * at + step]] for step in range(SIDE)], axis=1)
        weight = block[:, :, low:high].reshape(act.shape[1], high - low)
        part = dot32(act, weight)
        total = part if total is None else total + part
    return total


def masked_softmax(scores, seen, size):
    scores = [jnp.where(seen, score / math.sqrt(size), -1e30) for score in scores]
    tops = [jnp.max(score, axis=1, keepdims=True) for score in scores]
    powers = [jnp.exp(score - top) for score, top in zip(scores, tops)]
    sums = [jnp.sum(power, axis=1, keepdims=True) for power in powers]
    return [(power / total).astype(jnp.bfloat16) for power, total in zip(powers, sums)]


def span_attention(info, pieces, w0, w1, w2, w3, context, mixed):
    cols = w0.shape[2]
    third = cols // 3
    mixed[...] = ring_dot(info, pieces, (w0, w1, w2, w3), 0, cols).astype(jnp.bfloat16)
    size = context.shape[2]
    half = mixed.shape[0] // 2
    span = 16
    row = lax.broadcasted_iota(jnp.int32, (half, half), 0) // span
    col = lax.broadcasted_iota(jnp.int32, (half, half), 1) // span
    same = row == col
    heads = third // size
    units = [
        (head, slice(part * half, (part + 1) * half)) for head in range(heads) for part in range(2)
    ]
    scores = [
        lax.dot_general(
            mixed[rows, head * size : (head + 1) * size],
            mixed[rows, third + head * size : third + (head + 1) * size],
            (((1,), (1,)), ((), ())),
            preferred_element_type=jnp.float32,
        )
        for head, rows in units
    ]
    probs = masked_softmax(scores, same, size)
    for (head, rows), prob in zip(units, probs):
        value = mixed[rows, 2 * third + head * size : 2 * third + (head + 1) * size]
        context[head, rows, :] = dot32(prob, value).astype(jnp.bfloat16)


def context_out(info, mine, other, tokens, w0, w1, w2, w3, attended, pieces):
    heads = mine.shape[0]
    core = info[16]
    pieces[pl.ds(core * heads, heads)] = mine[...]
    pieces[pl.ds((1 - core) * heads, heads)] = other[...]
    cols = attended.shape[1]
    residual = jnp.concatenate([tokens[core * heads + index] for index in range(heads)], axis=1)
    total = ring_dot(info, pieces, (w0, w1, w2, w3), 0, cols)
    attended[...] = (residual.astype(jnp.float32) + total).astype(jnp.bfloat16)


def norm_up(info, mine, other, w0, w1, w2, w3, first_out, inner, pieces):
    core = info[16]
    cols = mine.shape[1]
    width = 2 * cols
    near = mine[...].astype(jnp.float32)
    far = other[...].astype(jnp.float32)
    low = jnp.where(core == 0, near, far)
    high = jnp.where(core == 0, far, near)
    mean = (jnp.sum(low, 1, keepdims=True) + jnp.sum(high, 1, keepdims=True)) / width
    low, high = low - mean, high - mean
    var = (jnp.sum(low * low, 1, keepdims=True) + jnp.sum(high * high, 1, keepdims=True)) / width
    scale = lax.rsqrt(var + 1e-05)
    first_out[:, :cols] = (low * scale).astype(jnp.bfloat16)
    first_out[:, cols:] = (high * scale).astype(jnp.bfloat16)
    size = pieces.shape[2]
    for index in range(pieces.shape[0]):
        pieces[index] = first_out[:, index * size : (index + 1) * size]
    total = ring_dot(info, pieces, (w0, w1, w2, w3), cols, w0.shape[2])
    act = gelu_exact(total).astype(jnp.bfloat16)
    unit = inner.shape[2]
    for index in range(inner.shape[0]):
        inner[index] = act[:, index * unit : (index + 1) * unit]


def down(info, inner, first_out, w0, w1, w2, w3, kept, sent, total):
    core = info[16]
    total[...] = ring_dot(info, inner, (w0, w1, w2, w3), 0, total.shape[1])
    half = kept.shape[0]
    rows = pl.ds(pl.multiple_of(core * half, half), half)
    kept[...] = total[rows, :] + first_out[rows, :].astype(jnp.float32)
    sent[...] = total[pl.ds(pl.multiple_of((1 - core) * half, half), half), :].astype(jnp.bfloat16)


def norm_pool(info, kept, arrived, pick, out, lanes):
    half, width = kept.shape
    values = kept[...] + arrived[...].astype(jnp.float32)
    mean = jnp.mean(values, axis=1, keepdims=True)
    values = values - mean
    values = values * lax.rsqrt(jnp.mean(values * values, axis=1, keepdims=True) + 1e-05)
    spans = pick.shape[1]
    pooled = jnp.mean(values.reshape(spans, half // spans, width), axis=1).astype(jnp.bfloat16)
    by_slot = dot32(pick[...], pooled)
    for index in range(width // 128):
        lanes[:, index, :] = by_slot[:, index * 128 : (index + 1) * 128]
    out[...] = jnp.broadcast_to(lanes[...].astype(jnp.bfloat16)[:, None], out.shape)


def embed(info, arrived, order, proj_in, mine, other, out, lanes, pieces):
    core = info[16]
    lanes[...] = arrived[...].astype(jnp.float32)
    columns = [
        dot32(order[...], lanes[:, index, :].astype(jnp.bfloat16)).astype(jnp.bfloat16)
        for index in range(lanes.shape[1])
    ]
    arranged = jnp.concatenate(columns, axis=1)
    hidden = gelu_exact(dot32(arranged, proj_in[...])).astype(jnp.bfloat16)
    units, cols = mine.shape[2:]
    for index in range(pieces.shape[0]):
        pieces[index] = hidden[:, index * units : (index + 1) * units]
    near, far = None, None
    for at in range(SIDE):
        act = jnp.concatenate([pieces[info[SIDE * at + step]] for step in range(SIDE)], axis=1)
        term = dot32(act, mine[at].reshape(SIDE * units, cols))
        near = term if near is None else near + term
        act = jnp.concatenate([pieces[info[22 + SIDE * at + step]] for step in range(SIDE)], axis=1)
        term = dot32(act, other[at].reshape(SIDE * units, cols))
        far = term if far is None else far + term
    out[:, :cols] = jnp.where(core == 0, near, far).astype(jnp.bfloat16)
    out[:, cols:] = jnp.where(core == 0, far, near).astype(jnp.bfloat16)


def project(info, *refs, starts, count):
    blocks, refs = refs[:count], refs[count:]
    gain, q_weight, kv_weight = refs[:3]
    before = refs[3:6] if len(refs) > 6 else None
    q_total, kv_total, square = refs[-3:]
    depth = blocks[0].shape[2]
    queries, both = None, None
    squares = None
    for at, block in zip(starts, blocks):
        for step in range(SIDE):
            shard = info[SIDE * at + step]
            wide = block[step].astype(jnp.float32)
            act = (wide * gain[shard]).astype(jnp.bfloat16)
            span = pl.ds(pl.multiple_of(shard * depth, depth), depth)
            q_term = dot32(act, q_weight[span, :])
            kv_term = dot_last(act, kv_weight[:, span])
            term = jnp.sum(wide * wide, axis=1, keepdims=True)
            queries = q_term if queries is None else queries + q_term
            both = kv_term if both is None else both + kv_term
            squares = term if squares is None else squares + term
    if before is not None:
        queries, both, squares = queries + before[0][...], both + before[1][...], squares + before[2][...]
    q_total[...] = queries
    kv_total[...] = both
    square[...] = squares


def turn(values, cosine, sine, swap):
    turned = jnp.dot(
        values, swap, preferred_element_type=jnp.float32, precision=lax.Precision.HIGHEST
    )
    return values * cosine + turned * sine


def last_keys(info, block, gain, kv_weight, kv_before, sq_before, cosine, sine, swap, out, scale):
    depth = block.shape[2]
    both = kv_before[...]
    squares = sq_before[...]
    for step in range(SIDE):
        shard = info[SIDE * 3 + step]
        wide = block[step].astype(jnp.float32)
        act = (wide * gain[shard]).astype(jnp.bfloat16)
        span = pl.ds(pl.multiple_of(shard * depth, depth), depth)
        both += dot_last(act, kv_weight[:, span])
        squares += jnp.sum(wide * wide, axis=1, keepdims=True)
    factor = lax.rsqrt(squares / (depth * SIDE * SIDE) + 1e-05)
    scale[...] = factor
    both = both * factor
    cols = out.shape[2]
    out[0] = turn(both[:, :cols], cosine[...], sine[...], swap[...]).astype(jnp.bfloat16)
    out[1] = both[:, cols:].astype(jnp.bfloat16)


def last_queries(info, block, gain, q_weight, q_before, scale, cosine, sine, swap, out):
    depth = block.shape[2]
    total = q_before[...]
    for step in range(SIDE):
        shard = info[SIDE * 3 + step]
        act = (block[step].astype(jnp.float32) * gain[shard]).astype(jnp.bfloat16)
        span = pl.ds(pl.multiple_of(shard * depth, depth), depth)
        total += dot32(act, q_weight[span, :])
    for head in range(out.shape[1] // HEAD_WIDTH):
        lanes = slice(head * HEAD_WIDTH, (head + 1) * HEAD_WIDTH)
        query = total[:, lanes] * scale[...]
        out[:, lanes] = turn(query, cosine[...], sine[...], swap[...]).astype(jnp.bfloat16)


def attend_out(info, query, mine, partner, allowed, deal, weight, *refs):
    outs, context = refs[:4], refs[4]
    odd = info[17] == 1
    own = mine[...].astype(jnp.float32)
    far = partner[...].astype(jnp.float32)
    low = jnp.where(odd, far, own)
    high = jnp.where(odd, own, far)
    both = jnp.concatenate([low, high], axis=2).astype(jnp.bfloat16)
    key, value = both[0], both[1]
    heads = [
        slice(head * HEAD_WIDTH, (head + 1) * HEAD_WIDTH)
        for head in range(query.shape[1] // HEAD_WIDTH)
    ]
    scores = [
        lax.dot_general(
            query[:, lanes], key, (((1,), (1,)), ((), ())), preferred_element_type=jnp.float32
        )
        for lanes in heads
    ]
    for lanes, prob in zip(heads, masked_softmax(scores, allowed[...] > 0, HEAD_WIDTH)):
        context[:, lanes] = dot32(prob, value).astype(jnp.bfloat16)
    dealt = dot32(deal[...], context[...]).astype(jnp.bfloat16)
    rows = outs[0].shape[0]
    step = weight.shape[1] // 8
    for start in range(0, weight.shape[1], step):
        result = dot32(dealt, weight[:, start : start + step])
        for index, out in enumerate(outs):
            piece = result[index * rows : (index + 1) * rows]
            out[:, start : start + step] = piece.astype(jnp.bfloat16)


def add_ring(info, own, left, right, opposite, kept, *sent):
    rows = kept.shape[0]
    step = 1024
    for start in range(0, own.shape[1], step):
        lanes = slice(start, start + step)
        total = own[:, lanes].astype(jnp.float32)
        for block in (left, right, opposite):
            total = total + block[:, lanes].astype(jnp.float32)
        kept[:, lanes] = total[:rows]
        for index, out in enumerate(sent):
            piece = total[(index + 1) * rows : (index + 2) * rows]
            out[:, lanes] = piece.astype(jnp.bfloat16)


def finish(info, kept, left, right, opposite, *refs):
    own, out = refs[:-1], refs[-1]
    rows, cols = own[0].shape[1:]
    live = info[18] + lax.broadcasted_iota(jnp.int32, (rows, cols), 0) < info[21]
    for at, block in enumerate(own):
        for step in range(SIDE):
            lanes = pl.ds(pl.multiple_of(info[SIDE * at + step] * cols, cols), cols)
            total = kept[:, lanes] + block[step].astype(jnp.float32)
            for term in (left, right, opposite):
                total = total + term[:, lanes].astype(jnp.float32)
            out[:, lanes] = jnp.where(live, total, 0.0).astype(jnp.bfloat16)


def visibility(masks, live_count):
    positions = jnp.arange(SPAN_LIMIT)
    passage = positions // CPP
    expanded = jnp.repeat(jnp.repeat(masks, CPP, axis=0), CPP, axis=1) > 0
    same_passage = passage[:, None] == passage[None, :]
    earlier = positions[None, :] <= positions[:, None]
    key_live = positions[None, :] < live_count
    diagonal = positions[:, None] == positions[None, :]
    return diagonal | earlier & key_live & (same_passage | expanded)


def local(
    span_tokens,
    enc_dest,
    passages,
    req_slot,
    block_mask,
    enc_qkv,
    enc_out,
    enc_up,
    enc_down,
    proj_in,
    proj_out,
    norm_gain,
    q_weight,
    key_value_weight,
    out_weight,
):
    tensor_count = lax.axis_size("tensor")
    seq_count = lax.axis_size("seq")
    tensor_index = lax.axis_index("tensor")
    seq_index = lax.axis_index("seq")
    core = seq_index % 2
    device_count = tensor_count * seq_count
    rows = SPAN_LIMIT
    own_rows = rows // tensor_count
    spans, span_size, width = span_tokens.shape
    model_width = proj_out.shape[1]
    share = enc_qkv.shape[0]
    x_index, y_index = tensor_index // SIDE, tensor_index % SIDE

    steps = jnp.array([0, SIDE - 1, 1, 2])
    outer, inside = jnp.repeat(steps, SIDE), jnp.tile(steps, SIDE)
    by_x = SIDE * ((x_index + outer) % SIDE) + (y_index + inside) % SIDE
    by_y = SIDE * ((x_index + inside) % SIDE) + (y_index + outer) % SIDE
    shards = jnp.where(core == 0, by_x, by_y)
    near = jnp.where(core == 0, y_index, x_index)
    far = jnp.where(core == 0, x_index, y_index)
    scalars = jnp.stack([core, tensor_index % 2, tensor_index * own_rows, near, far])
    other_shards = jnp.where(core == 0, by_y, by_x)
    info = jnp.concatenate([shards, scalars, core[None], other_shards]).astype(jnp.int32)

    ahead = jnp.array([0, 1, SIDE - 1, 2])
    outer, inside = jnp.repeat(ahead, SIDE), jnp.tile(ahead, SIDE)
    owner_x = SIDE * ((x_index + outer) % SIDE) + (y_index + inside) % SIDE
    owner_y = SIDE * ((x_index + inside) % SIDE) + (y_index + outer) % SIDE
    owners = jnp.where(core == 0, owner_x, owner_y)
    from_row = (owners[:, None] * own_rows + jnp.arange(own_rows)[None, :]).reshape(-1)
    deal = (from_row[:, None] == jnp.arange(rows)[None, :]).astype(jnp.bfloat16)

    requests = jnp.arange(req_slot.shape[0])
    dest_slot = jnp.sum(
        jnp.where(enc_dest[:, None] // SPAN_LIMIT == requests[None, :], req_slot[None, :], 0), axis=1
    ).reshape(device_count, own_rows)
    dest_place = (enc_dest % SPAN_LIMIT).reshape(device_count, own_rows)
    own_slots = lax.dynamic_slice_in_dim(
        dest_slot, seq_index * tensor_count + tensor_index, 1, 0
    )
    pick = (jnp.arange(seq_count)[:, None] == own_slots).astype(jnp.bfloat16)
    place_of = jnp.sum(jnp.where(dest_slot == seq_index, dest_place, 0), axis=1)
    order = (jnp.arange(rows)[:, None] == place_of[None, :]).astype(jnp.bfloat16)
    chosen = jnp.sum(jnp.where(req_slot == seq_index, requests, 0))
    live_count = jnp.sum(jnp.where(requests == chosen, passages, 0)) * CPP
    masks = jnp.sum(
        jnp.where(requests[:, None, None] == chosen, block_mask, 0), axis=0
    )
    allowed = visibility(masks, live_count).astype(jnp.float32)
    live_info = jnp.concatenate([info[:21], live_count[None]]).astype(jnp.int32)

    positions = jnp.arange(rows).astype(jnp.float32)
    lane = jnp.arange(HEAD_WIDTH)
    frequency = jnp.exp(
        -(2.0 * (lane // 2).astype(jnp.float32) / HEAD_WIDTH) * math.log(500000.0)
    )
    angles = positions[:, None] * frequency[None, :]
    cosine, sine = jnp.cos(angles), jnp.sin(angles)
    swap = jnp.where(
        (lane[:, None] ^ 1) == lane[None, :], jnp.where(lane[None, :] % 2 == 0, -1.0, 1.0), 0.0
    ).astype(jnp.float32)

    kv_cols = key_value_weight.shape[2]
    key_start = tensor_index * kv_cols % HEAD_WIDTH
    key_cosine = lax.dynamic_slice_in_dim(cosine, key_start, kv_cols, 1)
    key_sine = lax.dynamic_slice_in_dim(sine, key_start, kv_cols, 1)
    early = [pick, order, deal, allowed, cosine, sine, key_cosine, key_sine, swap]

    own_tokens = span_tokens.reshape(spans * span_size, width)
    other_tokens = to_core(own_tokens)
    token_pieces = whole_call(
        both_rows,
        "both_rows",
        info,
        [own_tokens, other_tokens],
        shape_of((tensor_count, 2 * spans * span_size, share)),
    )
    units = enc_down.shape[0] // 2
    middle_cols = width // 2 + units * tensor_count
    share_cols = model_width // tensor_count
    half_cols = share_cols // 2
    rest_shape = shape_of((share, middle_cols + width + SIDE * half_cols))
    dealt_shape = shape_of((share, SIDE * half_cols))
    own_qkv = whole_call(
        take_qkv, "take_qkv", info, [enc_qkv], shape_of((share, 3 * width // 2)), limit=4
    )
    rest_up, rest_down, kept_cols, beyond_cols = whole_call(
        take_rest,
        "take_rest",
        info,
        [enc_out, enc_up, enc_down, proj_out],
        (rest_shape, rest_shape, dealt_shape, dealt_shape),
        limit=60,
        after=[own_qkv],
    )
    qkv_ring = short_ring(own_qkv)
    rest_left = to_ring(rest_up, 1, 1)
    rest_ring = [rest_up, rest_left, to_ring(rest_down, 1, -1), to_ring(rest_left, 1, 1)]
    beyond_cols = to_ring(beyond_cols, 1, 2)
    qkv_block = whole_call(
        join_blocks,
        "join_qkv",
        info,
        qkv_ring,
        shape_of((SIDE, share, 3 * width // 2)),
        limit=6,
    )
    all_rows = 2 * spans * span_size

    qkv_right = to_ring(qkv_block, 2, -1)
    qkv = [qkv_block, to_ring(qkv_block, 2, 1), qkv_right, to_ring(qkv_right, 2, -1)]
    middle_block = whole_call(
        join_middle,
        "join_middle",
        info,
        rest_ring,
        shape_of((SIDE, share, middle_cols)),
        limit=8,
        after=[*qkv[1:3], token_pieces],
    )
    left = to_ring(middle_block, 2, 1)
    middle = [middle_block, left, to_ring(middle_block, 2, -1), to_ring(left, 2, 1)]
    context = whole_call(
        span_attention,
        "span_attention",
        info,
        [token_pieces, *qkv],
        shape_of((tensor_count // 2, all_rows, share)),
        [pltpu.VMEM((all_rows, 3 * width // 2), jnp.bfloat16)],
        flops=2 * all_rows * width * 3 * width // 2,
    )
    lower_shape = shape_of((SIDE, share, width + half_cols))
    far_shape = shape_of((SIDE, share, half_cols))
    lower_up, lower_down, far_kept, far_beyond = whole_call(
        join_lower,
        "join_lower",
        info,
        [*rest_ring, kept_cols, beyond_cols],
        (lower_shape, lower_shape, far_shape, far_shape),
        limit=8,
        after=[context, *middle[1:3]],
    )
    lower_right = to_ring(lower_down, 2, -1)
    lower = [lower_up, to_ring(lower_up, 2, 1), lower_right, to_ring(lower_right, 2, -1)]
    far_beyond = to_ring(far_beyond, 2, 2)
    attended = whole_call(
        context_out,
        "context_out",
        info,
        [context, to_core(context), token_pieces, *middle],
        shape_of((all_rows, width // 2)),
        [pltpu.VMEM((tensor_count, all_rows, share), jnp.bfloat16)],
        flops=2 * all_rows * width * width // 2,
        after=[far_beyond],
    )
    first_out, inner = whole_call(
        norm_up,
        "norm_up",
        info,
        [attended, to_core(attended), *middle],
        (shape_of((all_rows, width)), shape_of((tensor_count, all_rows, units))),
        [pltpu.VMEM((tensor_count, all_rows, share), jnp.bfloat16)],
        flops=2 * all_rows * width * width,
    )
    proj_mine = whole_call(
        join_proj,
        "join_proj",
        info,
        [far_kept, lower[1], lower[2], far_beyond],
        shape_of((SIDE, SIDE, share, half_cols)),
        limit=8,
    )
    proj_other = to_core(proj_mine)
    kept, sent = whole_call(
        down,
        "down",
        info,
        [inner, first_out, *lower],
        (
            shape_of((all_rows // 2, width), jnp.float32),
            shape_of((all_rows // 2, width)),
        ),
        [pltpu.VMEM((all_rows, width), jnp.float32)],
        flops=2 * all_rows * width * width,
        after=[proj_mine],
    )
    outgoing = whole_call(
        norm_pool,
        "norm_pool",
        info,
        [kept, to_core(sent), pick],
        shape_of((seq_count, tensor_count, width // 128, 128)),
        [pltpu.VMEM((seq_count, width // 128, 128), jnp.float32)],
    )
    arrived = lax.all_to_all(
        outgoing.reshape(device_count, width // 128, 128), AXES, 0, 0
    )

    own_cols = whole_call(
        embed,
        "embed",
        info,
        [arrived, order, proj_in, proj_mine, proj_other],
        shape_of((rows, share_cols)),
        [
            pltpu.VMEM((device_count, width // 128, 128), jnp.float32),
            pltpu.VMEM((tensor_count, rows, proj_out.shape[0]), jnp.bfloat16),
        ],
        flops=2 * rows * width * (width + share_cols),
    )
    first_block = whole_call(
        join_blocks,
        "join_columns",
        info,
        short_ring(own_cols),
        shape_of((SIDE, rows, share_cols)),
        limit=4,
    )
    near_left = to_ring(first_block, 2, 1)
    near_right = to_ring(first_block, 2, -1)
    query_cols = q_weight.shape[1]
    kv_cols = key_value_weight.shape[2]
    gain = norm_gain.reshape(tensor_count, 1, share_cols)
    kv_pair = key_value_weight.transpose(0, 2, 1).reshape(2 * kv_cols, model_width)
    sums = (
        shape_of((rows, query_cols), jnp.float32),
        shape_of((rows, 2 * kv_cols), jnp.float32),
        shape_of((rows, 1), jnp.float32),
    )
    block_flops = 2 * rows * model_width // SIDE * (query_cols + 2 * kv_cols)
    totals = whole_call(
        functools.partial(project, starts=(0,), count=1),
        "project_own",
        info,
        [first_block, gain, q_weight, kv_pair],
        sums,
        flops=block_flops,
    )
    relayed, _ = lax.optimization_barrier((near_left, totals[2]))
    embedded = [first_block, relayed, near_right, to_ring(relayed, 2, 1)]
    totals = whole_call(
        functools.partial(project, starts=(1, 2), count=2),
        "project_near",
        info,
        [embedded[1], embedded[2], gain, q_weight, kv_pair, *totals],
        sums,
        flops=2 * block_flops,
    )
    own_kv, scale = whole_call(
        last_keys,
        "last_keys",
        info,
        [
            embedded[3],
            gain,
            kv_pair,
            totals[1],
            totals[2],
            key_cosine,
            key_sine,
            swap[:kv_cols, :kv_cols],
        ],
        (shape_of((2, rows, kv_cols)), shape_of((rows, 1), jnp.float32)),
    )
    partner_kv = lax.ppermute(
        own_kv, "tensor", [(index, index ^ 1) for index in range(tensor_count)]
    )
    query = whole_call(
        last_queries,
        "last_queries",
        info,
        [embedded[3], gain, q_weight, totals[0], scale, cosine, sine, swap],
        shape_of((rows, query_cols)),
        flops=block_flops,
    )
    partial = whole_call(
        attend_out,
        "attend_out",
        info,
        [query, own_kv, partner_kv, allowed, deal, out_weight],
        (shape_of((rows // SIDE, model_width)),) * 4,
        [pltpu.VMEM((rows, query_cols), jnp.bfloat16)],
        flops=2 * rows * model_width * query_cols,
    )
    arrived_sums = [
        to_ring(part, 2, distance) for part, distance in zip(partial[1:], (1, -1, 2))
    ]
    kept_sum, *sent_sums = whole_call(
        add_ring,
        "add_ring",
        info,
        [partial[0], *arrived_sums],
        (shape_of((own_rows, model_width), jnp.float32),)
        + (shape_of((own_rows, model_width)),) * 3,
    )
    terms = [to_ring(part, 1, distance) for part, distance in zip(sent_sums, (1, -1, 2))]
    own_embedded = [
        lax.dynamic_slice_in_dim(block, tensor_index * own_rows, own_rows, 1) for block in embedded
    ]
    return whole_call(
        finish,
        "finish",
        live_info,
        [kept_sum, *terms, *own_embedded],
        shape_of((own_rows, model_width)),
    )


def solution(mesh):
    return jax.shard_map(
        local,
        mesh=mesh,
        in_specs=(
            P(("seq", "tensor"), None, None),
            P(),
            P(),
            P(),
            P(),
            P("tensor", None),
            P("tensor", None),
            P("tensor", None),
            P("tensor", None),
            P(),
            P("tensor", None),
            P(),
            P(None, "tensor"),
            P(None, None, "tensor"),
            P("tensor", None),
        ),
        out_specs=P(("seq", "tensor"), None),
        check_vma=False,
    )
```

```python
import functools
import math

import jax
import jax.numpy as jnp
from jax import lax
from jax.experimental import pallas as pl
from jax.experimental.pallas import tpu as pltpu
from jax.sharding import PartitionSpec as P

QUERY_HEAD_COUNT = 64
KEY_VALUE_HEADS = 8
HEAD_WIDTH = 128
EH = 16
CPP = 16
SPAN_LIMIT = 128
SIDE = 4
AXES = ("seq", "tensor")


def device_id(plane, core, x, y):
    return ((plane * 2 + core) * SIDE + x) * SIDE + y


def every_device():
    return [
        (plane, core, x, y)
        for plane in range(SIDE)
        for core in range(2)
        for x in range(SIDE)
        for y in range(SIDE)
    ]


def first_axis_is_y(core, phase):
    return (core == 0) == (phase == 1)


def ring_pairs(phase, distance):
    pairs = []
    for plane, core, x, y in every_device():
        if first_axis_is_y(core, phase):
            target = device_id(plane, core, x, (y + distance) % SIDE)
        else:
            target = device_id(plane, core, (x + distance) % SIDE, y)
        pairs.append((device_id(plane, core, x, y), target))
    return pairs


def ring_groups(phase):
    groups = []
    for plane in range(SIDE):
        for core in range(2):
            for fixed in range(SIDE):
                groups.append(
                    [
                        device_id(plane, core, fixed, moving)
                        if first_axis_is_y(core, phase)
                        else device_id(plane, core, moving, fixed)
                        for moving in range(SIDE)
                    ]
                )
    return groups


def to_ring(value, phase, distance):
    return lax.ppermute(value, AXES, ring_pairs(phase, distance))


def to_core(value):
    return lax.ppermute(value, "seq", [(index, index ^ 1) for index in range(8)])


def short_ring(block):
    return [block] + [to_ring(block, 1, distance) for distance in (1, -1, 2)]


def short_relay(block):
    left = to_ring(block, 1, 1)
    right = to_ring(block, 1, -1)
    return [block, left, right, to_ring(right, 1, -1)]


VMEM = pl.BlockSpec(memory_space=pltpu.VMEM)
SMEM = pl.BlockSpec(memory_space=pltpu.SMEM)
ANYWHERE = pl.BlockSpec(memory_space=pl.ANY)
MIB = 2**20


def shape_of(shape, dtype=jnp.bfloat16):
    return jax.ShapeDtypeStruct(shape, dtype)


def whole_call(body, name, info, arrays, outs, scratch=(), limit=12, flops=0, far=(), after=()):
    count = len(arrays) + len(far)

    def run(*refs):
        body(*refs[: 1 + count], *refs[1 + count + len(after) :])

    moved = sum(array.size * array.dtype.itemsize for array in arrays)
    return pl.pallas_call(
        run,
        name=name,
        out_shape=outs,
        in_specs=[SMEM] + [VMEM] * len(arrays) + [ANYWHERE] * (len(far) + len(after)),
        out_specs=jax.tree.map(lambda _: VMEM, outs),
        scratch_shapes=list(scratch),
        compiler_params=pltpu.CompilerParams(vmem_limit_bytes=limit * MIB),
        cost_estimate=pl.CostEstimate(flops=flops, bytes_accessed=moved, transcendentals=0),
    )(info, *arrays, *far, *after)


def dot32(left, right):
    return jnp.dot(left, right, preferred_element_type=jnp.float32)


def dot_last(left, right):
    return lax.dot_general(
        left, right, (((1,), (1,)), ((), ())), preferred_element_type=jnp.float32
    )


def gelu_exact(values):
    return 0.5 * values * (1.0 + lax.erf(values * (0.5**0.5)))


def take_qkv(info, weight, out):
    cols = weight.shape[1] // 6
    for part in range(3):
        start = pl.multiple_of((2 * part + info[16]) * cols, cols)
        out[:, part * cols : (part + 1) * cols] = weight[:, pl.ds(start, cols)]


def take_rest(info, out_weight, up_weight, down_weight, proj, up_out, down_out, kept, beyond):
    core, near = info[16], info[19]
    rows, width = out_weight.shape
    cols = width // 2
    units = down_weight.shape[0] // 2
    pieces = [out_weight[:, pl.ds(pl.multiple_of(core * cols, cols), cols)]]
    for pair in range(up_weight.shape[1] // (4 * units)):
        halves = []
        for step in range(2):
            low = (2 * pair + step) * 2 * units
            halves.append(
                jnp.where(
                    core == 0,
                    up_weight[:, low : low + units].astype(jnp.float32),
                    up_weight[:, low + units : low + 2 * units].astype(jnp.float32),
                )
            )
        pieces.append(jnp.concatenate(halves, axis=1).astype(jnp.bfloat16))
    pieces.append(down_weight[pl.ds(pl.multiple_of(core * units, units), units), :])
    at = 0
    for piece in pieces:
        for out in (up_out, down_out):
            out[:, at : at + piece.shape[1]] = piece
        at += piece.shape[1]
    block = kept.shape[1] // SIDE
    for out, start, distance in ((kept, 0, 0), (up_out, at, 1), (down_out, at, SIDE - 1), (beyond, 0, 2)):
        target = lax.rem(near + distance, SIDE)
        for index in range(SIDE):
            shard = jnp.where(core == 0, SIDE * index + target, SIDE * target + index)
            source = pl.multiple_of((2 * shard + core) * block, block)
            out[:, start + index * block : start + (index + 1) * block] = proj[:, pl.ds(source, block)]


def join_blocks(info, own, left, right, opposite, out):
    for index, block in enumerate((own, left, right, opposite)):
        out[index] = block[...]


def join_middle(info, own, left, right, opposite, out):
    for index, block in enumerate((own, left, right, opposite)):
        out[index] = block[:, : out.shape[2]]


def join_lower(info, own, left, right, opposite, kept, beyond, up_out, down_out, far_kept, far_beyond):
    far = info[20]
    block = far_kept.shape[2]
    width = up_out.shape[2] - block
    start = own.shape[1] - kept.shape[1] - width
    for index, part in enumerate((own, left, right, opposite)):
        for out in (up_out, down_out):
            out[index, :, :width] = part[:, start : start + width]
        columns, first = (part, start + width) if index in (1, 2) else (kept, 0)
        if index == 3:
            columns = beyond
        for out, at, distance in (
            (far_kept, 0, 0),
            (up_out, width, 1),
            (down_out, width, SIDE - 1),
            (far_beyond, 0, 2),
        ):
            target = lax.rem(far + distance, SIDE)
            source = pl.multiple_of(first + target * block, 128)
            out[index, :, at : at + block] = columns[:, pl.ds(source, block)]


def join_proj(info, own, left, right, opposite, out):
    block = own.shape[2]
    for index, part in enumerate((own, left, right, opposite)):
        out[index] = part[:, :, part.shape[2] - block :]


def both_rows(info, mine, other, pieces_out):
    half, width = mine.shape
    core = info[16]
    piece = pieces_out.shape[2]
    near = pl.ds(pl.multiple_of(core * half, half), half)
    far = pl.ds(pl.multiple_of((1 - core) * half, half), half)
    for index in range(width // piece):
        pieces_out[index, near, :] = mine[:, index * piece : (index + 1) * piece]
        pieces_out[index, far, :] = other[:, index * piece : (index + 1) * piece]


def ring_dot(info, pieces, blocks, low, high):
    total = None
    for at, block in enumerate(blocks):
        act = jnp.concatenate([pieces[info[4 * at + step]] for step in range(SIDE)], axis=1)
        weight = block[:, :, low:high].reshape(act.shape[1], high - low)
        part = dot32(act, weight)
        total = part if total is None else total + part
    return total


def masked_softmax(scores, seen, size):
    scores = [jnp.where(seen, score / math.sqrt(size), -1e30) for score in scores]
    tops = [jnp.max(score, axis=1, keepdims=True) for score in scores]
    powers = [jnp.exp(score - top) for score, top in zip(scores, tops)]
    sums = [jnp.sum(power, axis=1, keepdims=True) for power in powers]
    return [(power / total).astype(jnp.bfloat16) for power, total in zip(powers, sums)]


def span_attention(info, pieces, w0, w1, w2, w3, context, mixed):
    cols = w0.shape[2]
    third = cols // 3
    mixed[...] = ring_dot(info, pieces, (w0, w1, w2, w3), 0, cols).astype(jnp.bfloat16)
    size = context.shape[2]
    half = mixed.shape[0] // 2
    span = 16
    row = lax.broadcasted_iota(jnp.int32, (half, half), 0) // span
    col = lax.broadcasted_iota(jnp.int32, (half, half), 1) // span
    same = row == col
    heads = third // size
    units = [
        (head, slice(part * half, (part + 1) * half)) for head in range(heads) for part in range(2)
    ]
    scores = [
        lax.dot_general(
            mixed[rows, head * size : (head + 1) * size],
            mixed[rows, third + head * size : third + (head + 1) * size],
            (((1,), (1,)), ((), ())),
            preferred_element_type=jnp.float32,
        )
        for head, rows in units
    ]
    probs = masked_softmax(scores, same, size)
    for (head, rows), prob in zip(units, probs):
        value = mixed[rows, 2 * third + head * size : 2 * third + (head + 1) * size]
        context[head, rows, :] = dot32(prob, value).astype(jnp.bfloat16)


def context_out(info, mine, other, tokens, w0, w1, w2, w3, attended, pieces):
    heads = mine.shape[0]
    core = info[16]
    pieces[pl.ds(core * heads, heads)] = mine[...]
    pieces[pl.ds((1 - core) * heads, heads)] = other[...]
    cols = attended.shape[1]
    residual = jnp.concatenate([tokens[core * heads + index] for index in range(heads)], axis=1)
    total = ring_dot(info, pieces, (w0, w1, w2, w3), 0, cols)
    attended[...] = (residual.astype(jnp.float32) + total).astype(jnp.bfloat16)


def norm_up(info, mine, other, w0, w1, w2, w3, first_out, inner, pieces):
    core = info[16]
    cols = mine.shape[1]
    width = 2 * cols
    near = mine[...].astype(jnp.float32)
    far = other[...].astype(jnp.float32)
    low = jnp.where(core == 0, near, far)
    high = jnp.where(core == 0, far, near)
    mean = (jnp.sum(low, 1, keepdims=True) + jnp.sum(high, 1, keepdims=True)) / width
    low, high = low - mean, high - mean
    var = (jnp.sum(low * low, 1, keepdims=True) + jnp.sum(high * high, 1, keepdims=True)) / width
    scale = lax.rsqrt(var + 1e-05)
    first_out[:, :cols] = (low * scale).astype(jnp.bfloat16)
    first_out[:, cols:] = (high * scale).astype(jnp.bfloat16)
    size = pieces.shape[2]
    for index in range(pieces.shape[0]):
        pieces[index] = first_out[:, index * size : (index + 1) * size]
    total = ring_dot(info, pieces, (w0, w1, w2, w3), cols, w0.shape[2])
    act = gelu_exact(total).astype(jnp.bfloat16)
    unit = inner.shape[2]
    for index in range(inner.shape[0]):
        inner[index] = act[:, index * unit : (index + 1) * unit]


def down(info, inner, first_out, w0, w1, w2, w3, kept, sent, total):
    core = info[16]
    total[...] = ring_dot(info, inner, (w0, w1, w2, w3), 0, total.shape[1])
    half = kept.shape[0]
    rows = pl.ds(pl.multiple_of(core * half, half), half)
    kept[...] = total[rows, :] + first_out[rows, :].astype(jnp.float32)
    sent[...] = total[pl.ds(pl.multiple_of((1 - core) * half, half), half), :].astype(jnp.bfloat16)


def norm_pool(info, kept, arrived, pick, out, lanes):
    half, width = kept.shape
    values = kept[...] + arrived[...].astype(jnp.float32)
    mean = jnp.mean(values, axis=1, keepdims=True)
    values = values - mean
    values = values * lax.rsqrt(jnp.mean(values * values, axis=1, keepdims=True) + 1e-05)
    spans = pick.shape[1]
    pooled = jnp.mean(values.reshape(spans, half // spans, width), axis=1).astype(jnp.bfloat16)
    by_slot = dot32(pick[...], pooled)
    for index in range(width // 128):
        lanes[:, index, :] = by_slot[:, index * 128 : (index + 1) * 128]
    out[...] = jnp.broadcast_to(lanes[...].astype(jnp.bfloat16)[:, None], out.shape)


def embed(info, arrived, order, proj_in, mine, other, out, lanes, pieces):
    core = info[16]
    lanes[...] = arrived[...].astype(jnp.float32)
    columns = [
        dot32(order[...], lanes[:, index, :].astype(jnp.bfloat16)).astype(jnp.bfloat16)
        for index in range(lanes.shape[1])
    ]
    arranged = jnp.concatenate(columns, axis=1)
    hidden = gelu_exact(dot32(arranged, proj_in[...])).astype(jnp.bfloat16)
    units, cols = mine.shape[2:]
    for index in range(pieces.shape[0]):
        pieces[index] = hidden[:, index * units : (index + 1) * units]
    near, far = None, None
    for at in range(SIDE):
        act = jnp.concatenate([pieces[info[SIDE * at + step]] for step in range(SIDE)], axis=1)
        term = dot32(act, mine[at].reshape(SIDE * units, cols))
        near = term if near is None else near + term
        act = jnp.concatenate([pieces[info[22 + SIDE * at + step]] for step in range(SIDE)], axis=1)
        term = dot32(act, other[at].reshape(SIDE * units, cols))
        far = term if far is None else far + term
    out[:, :cols] = jnp.where(core == 0, near, far).astype(jnp.bfloat16)
    out[:, cols:] = jnp.where(core == 0, far, near).astype(jnp.bfloat16)


def project(info, *refs, starts, count):
    blocks, refs = refs[:count], refs[count:]
    gain, q_weight, kv_weight = refs[:3]
    before = refs[3:6] if len(refs) > 6 else None
    q_total, kv_total, square = refs[-3:]
    depth = blocks[0].shape[2]
    queries, both = None, None
    squares = None
    for at, block in zip(starts, blocks):
        for step in range(SIDE):
            shard = info[SIDE * at + step]
            wide = block[step].astype(jnp.float32)
            act = (wide * gain[shard]).astype(jnp.bfloat16)
            span = pl.ds(pl.multiple_of(shard * depth, depth), depth)
            q_term = dot32(act, q_weight[span, :])
            kv_term = dot_last(act, kv_weight[:, span])
            term = jnp.sum(wide * wide, axis=1, keepdims=True)
            queries = q_term if queries is None else queries + q_term
            both = kv_term if both is None else both + kv_term
            squares = term if squares is None else squares + term
    if before is not None:
        queries, both, squares = queries + before[0][...], both + before[1][...], squares + before[2][...]
    q_total[...] = queries
    kv_total[...] = both
    square[...] = squares


def turn(values, cosine, sine, swap):
    turned = jnp.dot(
        values, swap, preferred_element_type=jnp.float32, precision=lax.Precision.HIGHEST
    )
    return values * cosine + turned * sine


def last_keys(info, block, gain, kv_weight, kv_before, sq_before, cosine, sine, swap, out, scale):
    depth = block.shape[2]
    both = kv_before[...]
    squares = sq_before[...]
    for step in range(SIDE):
        shard = info[SIDE * 3 + step]
        wide = block[step].astype(jnp.float32)
        act = (wide * gain[shard]).astype(jnp.bfloat16)
        span = pl.ds(pl.multiple_of(shard * depth, depth), depth)
        both += dot_last(act, kv_weight[:, span])
        squares += jnp.sum(wide * wide, axis=1, keepdims=True)
    factor = lax.rsqrt(squares / (depth * SIDE * SIDE) + 1e-05)
    scale[...] = factor
    both = both * factor
    cols = out.shape[2]
    out[0] = turn(both[:, :cols], cosine[...], sine[...], swap[...]).astype(jnp.bfloat16)
    out[1] = both[:, cols:].astype(jnp.bfloat16)


def last_queries(info, block, gain, q_weight, q_before, scale, cosine, sine, swap, out):
    depth = block.shape[2]
    total = q_before[...]
    for step in range(SIDE):
        shard = info[SIDE * 3 + step]
        act = (block[step].astype(jnp.float32) * gain[shard]).astype(jnp.bfloat16)
        span = pl.ds(pl.multiple_of(shard * depth, depth), depth)
        total += dot32(act, q_weight[span, :])
    for head in range(out.shape[1] // HEAD_WIDTH):
        lanes = slice(head * HEAD_WIDTH, (head + 1) * HEAD_WIDTH)
        query = total[:, lanes] * scale[...]
        out[:, lanes] = turn(query, cosine[...], sine[...], swap[...]).astype(jnp.bfloat16)


def attend_out(info, query, mine, partner, allowed, deal, weight, *refs):
    outs, context = refs[:4], refs[4]
    odd = info[17] == 1
    own = mine[...].astype(jnp.float32)
    far = partner[...].astype(jnp.float32)
    low = jnp.where(odd, far, own)
    high = jnp.where(odd, own, far)
    both = jnp.concatenate([low, high], axis=2).astype(jnp.bfloat16)
    key, value = both[0], both[1]
    heads = [
        slice(head * HEAD_WIDTH, (head + 1) * HEAD_WIDTH)
        for head in range(query.shape[1] // HEAD_WIDTH)
    ]
    scores = [
        lax.dot_general(
            query[:, lanes], key, (((1,), (1,)), ((), ())), preferred_element_type=jnp.float32
        )
        for lanes in heads
    ]
    for lanes, prob in zip(heads, masked_softmax(scores, allowed[...] > 0, HEAD_WIDTH)):
        context[:, lanes] = dot32(prob, value).astype(jnp.bfloat16)
    dealt = dot32(deal[...], context[...]).astype(jnp.bfloat16)
    rows = outs[0].shape[0]
    step = weight.shape[1] // 8
    for start in range(0, weight.shape[1], step):
        result = dot32(dealt, weight[:, start : start + step])
        for index, out in enumerate(outs):
            piece = result[index * rows : (index + 1) * rows]
            out[:, start : start + step] = piece.astype(jnp.bfloat16)


def add_ring(info, own, left, right, opposite, kept, *sent):
    rows = kept.shape[0]
    step = 1024
    for start in range(0, own.shape[1], step):
        lanes = slice(start, start + step)
        total = own[:, lanes].astype(jnp.float32)
        for block in (left, right, opposite):
            total = total + block[:, lanes].astype(jnp.float32)
        kept[:, lanes] = total[:rows]
        for index, out in enumerate(sent):
            piece = total[(index + 1) * rows : (index + 2) * rows]
            out[:, lanes] = piece.astype(jnp.bfloat16)


def finish(info, kept, left, right, opposite, *refs):
    own, out = refs[:-1], refs[-1]
    rows, cols = own[0].shape[1:]
    live = info[18] + lax.broadcasted_iota(jnp.int32, (rows, cols), 0) < info[21]
    for at, block in enumerate(own):
        for step in range(SIDE):
            lanes = pl.ds(pl.multiple_of(info[SIDE * at + step] * cols, cols), cols)
            total = kept[:, lanes] + block[step].astype(jnp.float32)
            for term in (left, right, opposite):
                total = total + term[:, lanes].astype(jnp.float32)
            out[:, lanes] = jnp.where(live, total, 0.0).astype(jnp.bfloat16)


def visibility(masks, live_count):
    positions = jnp.arange(SPAN_LIMIT)
    passage = positions // CPP
    expanded = jnp.repeat(jnp.repeat(masks, CPP, axis=0), CPP, axis=1) > 0
    same_passage = passage[:, None] == passage[None, :]
    earlier = positions[None, :] <= positions[:, None]
    key_live = positions[None, :] < live_count
    diagonal = positions[:, None] == positions[None, :]
    return diagonal | earlier & key_live & (same_passage | expanded)


def local(
    span_tokens,
    enc_dest,
    passages,
    req_slot,
    block_mask,
    enc_qkv,
    enc_out,
    enc_up,
    enc_down,
    proj_in,
    proj_out,
    norm_gain,
    q_weight,
    key_value_weight,
    out_weight,
):
    tensor_count = lax.axis_size("tensor")
    seq_count = lax.axis_size("seq")
    tensor_index = lax.axis_index("tensor")
    seq_index = lax.axis_index("seq")
    core = seq_index % 2
    device_count = tensor_count * seq_count
    rows = SPAN_LIMIT
    own_rows = rows // tensor_count
    spans, span_size, width = span_tokens.shape
    model_width = proj_out.shape[1]
    share = enc_qkv.shape[0]
    x_index, y_index = tensor_index // SIDE, tensor_index % SIDE

    steps = jnp.array([0, SIDE - 1, 1, 2])
    outer, inside = jnp.repeat(steps, SIDE), jnp.tile(steps, SIDE)
    by_x = SIDE * ((x_index + outer) % SIDE) + (y_index + inside) % SIDE
    by_y = SIDE * ((x_index + inside) % SIDE) + (y_index + outer) % SIDE
    shards = jnp.where(core == 0, by_x, by_y)
    near = jnp.where(core == 0, y_index, x_index)
    far = jnp.where(core == 0, x_index, y_index)
    scalars = jnp.stack([core, tensor_index % 2, tensor_index * own_rows, near, far])
    other_shards = jnp.where(core == 0, by_y, by_x)
    info = jnp.concatenate([shards, scalars, core[None], other_shards]).astype(jnp.int32)

    ahead = jnp.array([0, 1, SIDE - 1, 2])
    outer, inside = jnp.repeat(ahead, SIDE), jnp.tile(ahead, SIDE)
    owner_x = SIDE * ((x_index + outer) % SIDE) + (y_index + inside) % SIDE
    owner_y = SIDE * ((x_index + inside) % SIDE) + (y_index + outer) % SIDE
    owners = jnp.where(core == 0, owner_x, owner_y)
    from_row = (owners[:, None] * own_rows + jnp.arange(own_rows)[None, :]).reshape(-1)
    deal = (from_row[:, None] == jnp.arange(rows)[None, :]).astype(jnp.bfloat16)

    requests = jnp.arange(req_slot.shape[0])
    dest_slot = jnp.sum(
        jnp.where(enc_dest[:, None] // SPAN_LIMIT == requests[None, :], req_slot[None, :], 0), axis=1
    ).reshape(device_count, own_rows)
    dest_place = (enc_dest % SPAN_LIMIT).reshape(device_count, own_rows)
    own_slots = lax.dynamic_slice_in_dim(
        dest_slot, seq_index * tensor_count + tensor_index, 1, 0
    )
    pick = (jnp.arange(seq_count)[:, None] == own_slots).astype(jnp.bfloat16)
    place_of = jnp.sum(jnp.where(dest_slot == seq_index, dest_place, 0), axis=1)
    order = (jnp.arange(rows)[:, None] == place_of[None, :]).astype(jnp.bfloat16)
    chosen = jnp.sum(jnp.where(req_slot == seq_index, requests, 0))
    live_count = jnp.sum(jnp.where(requests == chosen, passages, 0)) * CPP
    masks = jnp.sum(
        jnp.where(requests[:, None, None] == chosen, block_mask, 0), axis=0
    )
    allowed = visibility(masks, live_count).astype(jnp.float32)
    live_info = jnp.concatenate([info[:21], live_count[None]]).astype(jnp.int32)

    positions = jnp.arange(rows).astype(jnp.float32)
    lane = jnp.arange(HEAD_WIDTH)
    frequency = jnp.exp(
        -(2.0 * (lane // 2).astype(jnp.float32) / HEAD_WIDTH) * math.log(500000.0)
    )
    angles = positions[:, None] * frequency[None, :]
    cosine, sine = jnp.cos(angles), jnp.sin(angles)
    swap = jnp.where(
        (lane[:, None] ^ 1) == lane[None, :], jnp.where(lane[None, :] % 2 == 0, -1.0, 1.0), 0.0
    ).astype(jnp.float32)

    kv_cols = key_value_weight.shape[2]
    key_start = tensor_index * kv_cols % HEAD_WIDTH
    key_cosine = lax.dynamic_slice_in_dim(cosine, key_start, kv_cols, 1)
    key_sine = lax.dynamic_slice_in_dim(sine, key_start, kv_cols, 1)
    early = [pick, order, deal, allowed, cosine, sine, key_cosine, key_sine, swap]

    own_tokens = span_tokens.reshape(spans * span_size, width)
    other_tokens = to_core(own_tokens)
    token_pieces = whole_call(
        both_rows,
        "both_rows",
        info,
        [own_tokens, other_tokens],
        shape_of((tensor_count, 2 * spans * span_size, share)),
    )
    units = enc_down.shape[0] // 2
    middle_cols = width // 2 + units * tensor_count
    share_cols = model_width // tensor_count
    half_cols = share_cols // 2
    rest_shape = shape_of((share, middle_cols + width + SIDE * half_cols))
    dealt_shape = shape_of((share, SIDE * half_cols))
    own_qkv = whole_call(
        take_qkv, "take_qkv", info, [enc_qkv], shape_of((share, 3 * width // 2)), limit=4
    )
    rest_up, rest_down, kept_cols, beyond_cols = whole_call(
        take_rest,
        "take_rest",
        info,
        [enc_out, enc_up, enc_down, proj_out],
        (rest_shape, rest_shape, dealt_shape, dealt_shape),
        limit=60,
        after=[own_qkv],
    )
    qkv_ring = short_ring(own_qkv)
    rest_left = to_ring(rest_up, 1, 1)
    rest_ring = [rest_up, rest_left, to_ring(rest_down, 1, -1), to_ring(rest_left, 1, 1)]
    beyond_cols = to_ring(beyond_cols, 1, 2)
    qkv_block = whole_call(
        join_blocks,
        "join_qkv",
        info,
        qkv_ring,
        shape_of((SIDE, share, 3 * width // 2)),
        limit=6,
    )
    all_rows = 2 * spans * span_size

    qkv_right = to_ring(qkv_block, 2, -1)
    qkv = [qkv_block, to_ring(qkv_block, 2, 1), qkv_right, to_ring(qkv_right, 2, -1)]
    middle_block = whole_call(
        join_middle,
        "join_middle",
        info,
        rest_ring,
        shape_of((SIDE, share, middle_cols)),
        limit=8,
        after=[*qkv[1:3], token_pieces],
    )
    left = to_ring(middle_block, 2, 1)
    middle = [middle_block, left, to_ring(middle_block, 2, -1), to_ring(left, 2, 1)]
    context = whole_call(
        span_attention,
        "span_attention",
        info,
        [token_pieces, *qkv],
        shape_of((tensor_count // 2, all_rows, share)),
        [pltpu.VMEM((all_rows, 3 * width // 2), jnp.bfloat16)],
        flops=2 * all_rows * width * 3 * width // 2,
    )
    lower_shape = shape_of((SIDE, share, width + half_cols))
    far_shape = shape_of((SIDE, share, half_cols))
    lower_up, lower_down, far_kept, far_beyond = whole_call(
        join_lower,
        "join_lower",
        info,
        [*rest_ring, kept_cols, beyond_cols],
        (lower_shape, lower_shape, far_shape, far_shape),
        limit=8,
        after=[context],
    )
    lower_left = to_ring(lower_up, 2, 1)
    lower = [lower_up, lower_left, to_ring(lower_down, 2, -1), to_ring(lower_left, 2, 1)]
    far_beyond = to_ring(far_beyond, 2, 2)
    attended = whole_call(
        context_out,
        "context_out",
        info,
        [context, to_core(context), token_pieces, *middle],
        shape_of((all_rows, width // 2)),
        [pltpu.VMEM((tensor_count, all_rows, share), jnp.bfloat16)],
        flops=2 * all_rows * width * width // 2,
    )
    first_out, inner = whole_call(
        norm_up,
        "norm_up",
        info,
        [attended, to_core(attended), *middle],
        (shape_of((all_rows, width)), shape_of((tensor_count, all_rows, units))),
        [pltpu.VMEM((tensor_count, all_rows, share), jnp.bfloat16)],
        flops=2 * all_rows * width * width,
        after=[*early],
    )
    kept, sent = whole_call(
        down,
        "down",
        info,
        [inner, first_out, *lower],
        (
            shape_of((all_rows // 2, width), jnp.float32),
            shape_of((all_rows // 2, width)),
        ),
        [pltpu.VMEM((all_rows, width), jnp.float32)],
        flops=2 * all_rows * width * width,
    )
    outgoing = whole_call(
        norm_pool,
        "norm_pool",
        info,
        [kept, to_core(sent), pick],
        shape_of((seq_count, tensor_count, width // 128, 128)),
        [pltpu.VMEM((seq_count, width // 128, 128), jnp.float32)],
    )
    arrived = lax.all_to_all(
        outgoing.reshape(device_count, width // 128, 128), AXES, 0, 0
    )

    proj_mine = whole_call(
        join_proj,
        "join_proj",
        info,
        [far_kept, lower[1], lower[2], far_beyond],
        shape_of((SIDE, SIDE, share, half_cols)),
        limit=8,
        after=[outgoing],
    )
    proj_other = to_core(proj_mine)
    own_cols = whole_call(
        embed,
        "embed",
        info,
        [arrived, order, proj_in, proj_mine, proj_other],
        shape_of((rows, share_cols)),
        [
            pltpu.VMEM((device_count, width // 128, 128), jnp.float32),
            pltpu.VMEM((tensor_count, rows, proj_out.shape[0]), jnp.bfloat16),
        ],
        flops=2 * rows * width * (width + share_cols),
    )
    first_block = whole_call(
        join_blocks,
        "join_columns",
        info,
        short_ring(own_cols),
        shape_of((SIDE, rows, share_cols)),
        limit=4,
    )
    near_left = to_ring(first_block, 2, 1)
    near_right = to_ring(first_block, 2, -1)
    query_cols = q_weight.shape[1]
    kv_cols = key_value_weight.shape[2]
    gain = norm_gain.reshape(tensor_count, 1, share_cols)
    kv_pair = key_value_weight.transpose(0, 2, 1).reshape(2 * kv_cols, model_width)
    sums = (
        shape_of((rows, query_cols), jnp.float32),
        shape_of((rows, 2 * kv_cols), jnp.float32),
        shape_of((rows, 1), jnp.float32),
    )
    block_flops = 2 * rows * model_width // SIDE * (query_cols + 2 * kv_cols)
    totals = whole_call(
        functools.partial(project, starts=(0,), count=1),
        "project_own",
        info,
        [first_block, gain, q_weight, kv_pair],
        sums,
        flops=block_flops,
    )
    relayed, _ = lax.optimization_barrier((near_left, totals[2]))
    embedded = [first_block, relayed, near_right, to_ring(relayed, 2, 1)]
    totals = whole_call(
        functools.partial(project, starts=(1, 2), count=2),
        "project_near",
        info,
        [embedded[1], embedded[2], gain, q_weight, kv_pair, *totals],
        sums,
        flops=2 * block_flops,
    )
    own_kv, scale = whole_call(
        last_keys,
        "last_keys",
        info,
        [
            embedded[3],
            gain,
            kv_pair,
            totals[1],
            totals[2],
            key_cosine,
            key_sine,
            swap[:kv_cols, :kv_cols],
        ],
        (shape_of((2, rows, kv_cols)), shape_of((rows, 1), jnp.float32)),
    )
    partner_kv = lax.ppermute(
        own_kv, "tensor", [(index, index ^ 1) for index in range(tensor_count)]
    )
    query = whole_call(
        last_queries,
        "last_queries",
        info,
        [embedded[3], gain, q_weight, totals[0], scale, cosine, sine, swap],
        shape_of((rows, query_cols)),
        flops=block_flops,
    )
    partial = whole_call(
        attend_out,
        "attend_out",
        info,
        [query, own_kv, partner_kv, allowed, deal, out_weight],
        (shape_of((rows // SIDE, model_width)),) * 4,
        [pltpu.VMEM((rows, query_cols), jnp.bfloat16)],
        flops=2 * rows * model_width * query_cols,
    )
    arrived_sums = [
        to_ring(part, 2, distance) for part, distance in zip(partial[1:], (1, -1, 2))
    ]
    kept_sum, *sent_sums = whole_call(
        add_ring,
        "add_ring",
        info,
        [partial[0], *arrived_sums],
        (shape_of((own_rows, model_width), jnp.float32),)
        + (shape_of((own_rows, model_width)),) * 3,
    )
    terms = [to_ring(part, 1, distance) for part, distance in zip(sent_sums, (1, -1, 2))]
    own_embedded = [
        lax.dynamic_slice_in_dim(block, tensor_index * own_rows, own_rows, 1) for block in embedded
    ]
    return whole_call(
        finish,
        "finish",
        live_info,
        [kept_sum, *terms, *own_embedded],
        shape_of((own_rows, model_width)),
    )


def solution(mesh):
    return jax.shard_map(
        local,
        mesh=mesh,
        in_specs=(
            P(("seq", "tensor"), None, None),
            P(),
            P(),
            P(),
            P(),
            P("tensor", None),
            P("tensor", None),
            P("tensor", None),
            P("tensor", None),
            P(),
            P("tensor", None),
            P(),
            P(None, "tensor"),
            P(None, None, "tensor"),
            P("tensor", None),
        ),
        out_specs=P(("seq", "tensor"), None),
        check_vma=False,
    )
```

```python
import functools
import math

import jax
import jax.numpy as jnp
from jax import lax
from jax.experimental import pallas as pl
from jax.experimental.pallas import tpu as pltpu
from jax.sharding import PartitionSpec as P

QUERY_HEAD_COUNT = 64
KEY_VALUE_HEADS = 8
HEAD_WIDTH = 128
EH = 16
CPP = 16
SPAN_LIMIT = 128
SIDE = 4
AXES = ("seq", "tensor")


def device_id(plane, core, x, y):
    return ((plane * 2 + core) * SIDE + x) * SIDE + y


def every_device():
    return [
        (plane, core, x, y)
        for plane in range(SIDE)
        for core in range(2)
        for x in range(SIDE)
        for y in range(SIDE)
    ]


def first_axis_is_y(core, phase):
    return (core == 0) == (phase == 1)


def ring_pairs(phase, distance):
    pairs = []
    for plane, core, x, y in every_device():
        if first_axis_is_y(core, phase):
            target = device_id(plane, core, x, (y + distance) % SIDE)
        else:
            target = device_id(plane, core, (x + distance) % SIDE, y)
        pairs.append((device_id(plane, core, x, y), target))
    return pairs


def ring_groups(phase):
    groups = []
    for plane in range(SIDE):
        for core in range(2):
            for fixed in range(SIDE):
                groups.append(
                    [
                        device_id(plane, core, fixed, moving)
                        if first_axis_is_y(core, phase)
                        else device_id(plane, core, moving, fixed)
                        for moving in range(SIDE)
                    ]
                )
    return groups


def to_ring(value, phase, distance):
    return lax.ppermute(value, AXES, ring_pairs(phase, distance))


def to_core(value):
    return lax.ppermute(value, "seq", [(index, index ^ 1) for index in range(8)])


def short_ring(block):
    return [block] + [to_ring(block, 1, distance) for distance in (1, -1, 2)]


def short_relay(block):
    left = to_ring(block, 1, 1)
    right = to_ring(block, 1, -1)
    return [block, left, right, to_ring(right, 1, -1)]


VMEM = pl.BlockSpec(memory_space=pltpu.VMEM)
SMEM = pl.BlockSpec(memory_space=pltpu.SMEM)
ANYWHERE = pl.BlockSpec(memory_space=pl.ANY)
MIB = 2**20


def shape_of(shape, dtype=jnp.bfloat16):
    return jax.ShapeDtypeStruct(shape, dtype)


def whole_call(body, name, info, arrays, outs, scratch=(), limit=12, flops=0, far=(), after=()):
    count = len(arrays) + len(far)

    def run(*refs):
        body(*refs[: 1 + count], *refs[1 + count + len(after) :])

    moved = sum(array.size * array.dtype.itemsize for array in arrays)
    return pl.pallas_call(
        run,
        name=name,
        out_shape=outs,
        in_specs=[SMEM] + [VMEM] * len(arrays) + [ANYWHERE] * (len(far) + len(after)),
        out_specs=jax.tree.map(lambda _: VMEM, outs),
        scratch_shapes=list(scratch),
        compiler_params=pltpu.CompilerParams(vmem_limit_bytes=limit * MIB),
        cost_estimate=pl.CostEstimate(flops=flops, bytes_accessed=moved, transcendentals=0),
    )(info, *arrays, *far, *after)


def dot32(left, right):
    return jnp.dot(left, right, preferred_element_type=jnp.float32)


def dot_last(left, right):
    return lax.dot_general(
        left, right, (((1,), (1,)), ((), ())), preferred_element_type=jnp.float32
    )


def gelu_exact(values):
    return 0.5 * values * (1.0 + lax.erf(values * (0.5**0.5)))


def take_qkv(info, weight, out):
    cols = weight.shape[1] // 6
    for part in range(3):
        start = pl.multiple_of((2 * part + info[16]) * cols, cols)
        out[:, part * cols : (part + 1) * cols] = weight[:, pl.ds(start, cols)]


def take_rest(info, out_weight, up_weight, down_weight, proj, up_out, down_out, kept, beyond):
    core, near = info[16], info[19]
    rows, width = out_weight.shape
    cols = width // 2
    units = down_weight.shape[0] // 2
    pieces = [out_weight[:, pl.ds(pl.multiple_of(core * cols, cols), cols)]]
    for pair in range(up_weight.shape[1] // (4 * units)):
        halves = []
        for step in range(2):
            low = (2 * pair + step) * 2 * units
            halves.append(
                jnp.where(
                    core == 0,
                    up_weight[:, low : low + units].astype(jnp.float32),
                    up_weight[:, low + units : low + 2 * units].astype(jnp.float32),
                )
            )
        pieces.append(jnp.concatenate(halves, axis=1).astype(jnp.bfloat16))
    pieces.append(down_weight[pl.ds(pl.multiple_of(core * units, units), units), :])
    at = 0
    for piece in pieces:
        for out in (up_out, down_out):
            out[:, at : at + piece.shape[1]] = piece
        at += piece.shape[1]
    block = kept.shape[1] // SIDE
    for out, start, distance in ((kept, 0, 0), (up_out, at, 1), (down_out, at, SIDE - 1), (beyond, 0, 2)):
        target = lax.rem(near + distance, SIDE)
        for index in range(SIDE):
            shard = jnp.where(core == 0, SIDE * index + target, SIDE * target + index)
            source = pl.multiple_of((2 * shard + core) * block, block)
            out[:, start + index * block : start + (index + 1) * block] = proj[:, pl.ds(source, block)]


def join_blocks(info, own, left, right, opposite, out):
    for index, block in enumerate((own, left, right, opposite)):
        out[index] = block[...]


def join_middle(info, own, left, right, opposite, out):
    for index, block in enumerate((own, left, right, opposite)):
        out[index] = block[:, : out.shape[2]]


def join_lower(info, own, left, right, opposite, kept, beyond, up_out, down_out, far_kept, far_beyond):
    far = info[20]
    block = far_kept.shape[2]
    width = up_out.shape[2] - block
    start = own.shape[1] - kept.shape[1] - width
    for index, part in enumerate((own, left, right, opposite)):
        for out in (up_out, down_out):
            out[index, :, :width] = part[:, start : start + width]
        columns, first = (part, start + width) if index in (1, 2) else (kept, 0)
        if index == 3:
            columns = beyond
        for out, at, distance in (
            (far_kept, 0, 0),
            (up_out, width, 1),
            (down_out, width, SIDE - 1),
            (far_beyond, 0, 2),
        ):
            target = lax.rem(far + distance, SIDE)
            source = pl.multiple_of(first + target * block, 128)
            out[index, :, at : at + block] = columns[:, pl.ds(source, block)]


def join_proj(info, own, left, right, opposite, out):
    block = own.shape[2]
    for index, part in enumerate((own, left, right, opposite)):
        out[index] = part[:, :, part.shape[2] - block :]


def both_rows(info, mine, other, pieces_out):
    half, width = mine.shape
    core = info[16]
    piece = pieces_out.shape[2]
    near = pl.ds(pl.multiple_of(core * half, half), half)
    far = pl.ds(pl.multiple_of((1 - core) * half, half), half)
    for index in range(width // piece):
        pieces_out[index, near, :] = mine[:, index * piece : (index + 1) * piece]
        pieces_out[index, far, :] = other[:, index * piece : (index + 1) * piece]


def ring_dot(info, pieces, blocks, low, high):
    total = None
    for at, block in enumerate(blocks):
        act = jnp.concatenate([pieces[info[4 * at + step]] for step in range(SIDE)], axis=1)
        weight = block[:, :, low:high].reshape(act.shape[1], high - low)
        part = dot32(act, weight)
        total = part if total is None else total + part
    return total


def masked_softmax(scores, seen, size):
    scores = [jnp.where(seen, score / math.sqrt(size), -1e30) for score in scores]
    tops = [jnp.max(score, axis=1, keepdims=True) for score in scores]
    powers = [jnp.exp(score - top) for score, top in zip(scores, tops)]
    sums = [jnp.sum(power, axis=1, keepdims=True) for power in powers]
    return [(power / total).astype(jnp.bfloat16) for power, total in zip(powers, sums)]


def span_attention(info, pieces, w0, w1, w2, w3, context, mixed):
    cols = w0.shape[2]
    third = cols // 3
    mixed[...] = ring_dot(info, pieces, (w0, w1, w2, w3), 0, cols).astype(jnp.bfloat16)
    size = context.shape[2]
    half = mixed.shape[0] // 2
    span = 16
    row = lax.broadcasted_iota(jnp.int32, (half, half), 0) // span
    col = lax.broadcasted_iota(jnp.int32, (half, half), 1) // span
    same = row == col
    heads = third // size
    units = [
        (head, slice(part * half, (part + 1) * half)) for head in range(heads) for part in range(2)
    ]
    scores = [
        lax.dot_general(
            mixed[rows, head * size : (head + 1) * size],
            mixed[rows, third + head * size : third + (head + 1) * size],
            (((1,), (1,)), ((), ())),
            preferred_element_type=jnp.float32,
        )
        for head, rows in units
    ]
    probs = masked_softmax(scores, same, size)
    for (head, rows), prob in zip(units, probs):
        value = mixed[rows, 2 * third + head * size : 2 * third + (head + 1) * size]
        context[head, rows, :] = dot32(prob, value).astype(jnp.bfloat16)


def context_out(info, mine, other, tokens, w0, w1, w2, w3, attended, pieces):
    heads = mine.shape[0]
    core = info[16]
    pieces[pl.ds(core * heads, heads)] = mine[...]
    pieces[pl.ds((1 - core) * heads, heads)] = other[...]
    cols = attended.shape[1]
    residual = jnp.concatenate([tokens[core * heads + index] for index in range(heads)], axis=1)
    total = ring_dot(info, pieces, (w0, w1, w2, w3), 0, cols)
    attended[...] = (residual.astype(jnp.float32) + total).astype(jnp.bfloat16)


def norm_up(info, mine, other, w0, w1, w2, w3, first_out, inner, pieces):
    core = info[16]
    cols = mine.shape[1]
    width = 2 * cols
    near = mine[...].astype(jnp.float32)
    far = other[...].astype(jnp.float32)
    low = jnp.where(core == 0, near, far)
    high = jnp.where(core == 0, far, near)
    mean = (jnp.sum(low, 1, keepdims=True) + jnp.sum(high, 1, keepdims=True)) / width
    low, high = low - mean, high - mean
    var = (jnp.sum(low * low, 1, keepdims=True) + jnp.sum(high * high, 1, keepdims=True)) / width
    scale = lax.rsqrt(var + 1e-05)
    first_out[:, :cols] = (low * scale).astype(jnp.bfloat16)
    first_out[:, cols:] = (high * scale).astype(jnp.bfloat16)
    size = pieces.shape[2]
    for index in range(pieces.shape[0]):
        pieces[index] = first_out[:, index * size : (index + 1) * size]
    total = ring_dot(info, pieces, (w0, w1, w2, w3), cols, w0.shape[2])
    act = gelu_exact(total).astype(jnp.bfloat16)
    unit = inner.shape[2]
    for index in range(inner.shape[0]):
        inner[index] = act[:, index * unit : (index + 1) * unit]


def down(info, inner, first_out, w0, w1, w2, w3, kept, sent, total):
    core = info[16]
    total[...] = ring_dot(info, inner, (w0, w1, w2, w3), 0, total.shape[1])
    half = kept.shape[0]
    rows = pl.ds(pl.multiple_of(core * half, half), half)
    kept[...] = total[rows, :] + first_out[rows, :].astype(jnp.float32)
    sent[...] = total[pl.ds(pl.multiple_of((1 - core) * half, half), half), :].astype(jnp.bfloat16)


def norm_pool(info, kept, arrived, pick, out, lanes):
    half, width = kept.shape
    values = kept[...] + arrived[...].astype(jnp.float32)
    mean = jnp.mean(values, axis=1, keepdims=True)
    values = values - mean
    values = values * lax.rsqrt(jnp.mean(values * values, axis=1, keepdims=True) + 1e-05)
    spans = pick.shape[1]
    pooled = jnp.mean(values.reshape(spans, half // spans, width), axis=1).astype(jnp.bfloat16)
    by_slot = dot32(pick[...], pooled)
    for index in range(width // 128):
        lanes[:, index, :] = by_slot[:, index * 128 : (index + 1) * 128]
    out[...] = jnp.broadcast_to(lanes[...].astype(jnp.bfloat16)[:, None], out.shape)


def embed(info, arrived, order, proj_in, mine, other, out, lanes, pieces):
    core = info[16]
    lanes[...] = arrived[...].astype(jnp.float32)
    columns = [
        dot32(order[...], lanes[:, index, :].astype(jnp.bfloat16)).astype(jnp.bfloat16)
        for index in range(lanes.shape[1])
    ]
    arranged = jnp.concatenate(columns, axis=1)
    hidden = gelu_exact(dot32(arranged, proj_in[...])).astype(jnp.bfloat16)
    units, cols = mine.shape[2:]
    for index in range(pieces.shape[0]):
        pieces[index] = hidden[:, index * units : (index + 1) * units]
    near, far = None, None
    for at in range(SIDE):
        act = jnp.concatenate([pieces[info[SIDE * at + step]] for step in range(SIDE)], axis=1)
        term = dot32(act, mine[at].reshape(SIDE * units, cols))
        near = term if near is None else near + term
        act = jnp.concatenate([pieces[info[22 + SIDE * at + step]] for step in range(SIDE)], axis=1)
        term = dot32(act, other[at].reshape(SIDE * units, cols))
        far = term if far is None else far + term
    out[:, :cols] = jnp.where(core == 0, near, far).astype(jnp.bfloat16)
    out[:, cols:] = jnp.where(core == 0, far, near).astype(jnp.bfloat16)


def project(info, *refs, starts, count):
    blocks, refs = refs[:count], refs[count:]
    gain, q_weight, kv_weight = refs[:3]
    before = refs[3:6] if len(refs) > 6 else None
    q_total, kv_total, square = refs[-3:]
    depth = blocks[0].shape[2]
    queries, both = None, None
    squares = None
    for at, block in zip(starts, blocks):
        for step in range(SIDE):
            shard = info[SIDE * at + step]
            wide = block[step].astype(jnp.float32)
            act = (wide * gain[shard]).astype(jnp.bfloat16)
            span = pl.ds(pl.multiple_of(shard * depth, depth), depth)
            q_term = dot32(act, q_weight[span, :])
            kv_term = dot_last(act, kv_weight[:, span])
            term = jnp.sum(wide * wide, axis=1, keepdims=True)
            queries = q_term if queries is None else queries + q_term
            both = kv_term if both is None else both + kv_term
            squares = term if squares is None else squares + term
    if before is not None:
        queries, both, squares = queries + before[0][...], both + before[1][...], squares + before[2][...]
    q_total[...] = queries
    kv_total[...] = both
    square[...] = squares


def turn(values, cosine, sine, swap):
    turned = jnp.dot(
        values, swap, preferred_element_type=jnp.float32, precision=lax.Precision.HIGHEST
    )
    return values * cosine + turned * sine


def last_keys(info, block, gain, kv_weight, kv_before, sq_before, cosine, sine, swap, out, scale):
    depth = block.shape[2]
    both = kv_before[...]
    squares = sq_before[...]
    for step in range(SIDE):
        shard = info[SIDE * 3 + step]
        wide = block[step].astype(jnp.float32)
        act = (wide * gain[shard]).astype(jnp.bfloat16)
        span = pl.ds(pl.multiple_of(shard * depth, depth), depth)
        both += dot_last(act, kv_weight[:, span])
        squares += jnp.sum(wide * wide, axis=1, keepdims=True)
    factor = lax.rsqrt(squares / (depth * SIDE * SIDE) + 1e-05)
    scale[...] = factor
    both = both * factor
    cols = out.shape[2]
    out[0] = turn(both[:, :cols], cosine[...], sine[...], swap[...]).astype(jnp.bfloat16)
    out[1] = both[:, cols:].astype(jnp.bfloat16)


def last_queries(info, block, gain, q_weight, q_before, scale, cosine, sine, swap, out):
    depth = block.shape[2]
    total = q_before[...]
    for step in range(SIDE):
        shard = info[SIDE * 3 + step]
        act = (block[step].astype(jnp.float32) * gain[shard]).astype(jnp.bfloat16)
        span = pl.ds(pl.multiple_of(shard * depth, depth), depth)
        total += dot32(act, q_weight[span, :])
    for head in range(out.shape[1] // HEAD_WIDTH):
        lanes = slice(head * HEAD_WIDTH, (head + 1) * HEAD_WIDTH)
        query = total[:, lanes] * scale[...]
        out[:, lanes] = turn(query, cosine[...], sine[...], swap[...]).astype(jnp.bfloat16)


def attend_out(info, query, mine, partner, allowed, deal, weight, *refs):
    outs, context = refs[:4], refs[4]
    odd = info[17] == 1
    own = mine[...].astype(jnp.float32)
    far = partner[...].astype(jnp.float32)
    low = jnp.where(odd, far, own)
    high = jnp.where(odd, own, far)
    both = jnp.concatenate([low, high], axis=2).astype(jnp.bfloat16)
    key, value = both[0], both[1]
    heads = [
        slice(head * HEAD_WIDTH, (head + 1) * HEAD_WIDTH)
        for head in range(query.shape[1] // HEAD_WIDTH)
    ]
    scores = [
        lax.dot_general(
            query[:, lanes], key, (((1,), (1,)), ((), ())), preferred_element_type=jnp.float32
        )
        for lanes in heads
    ]
    for lanes, prob in zip(heads, masked_softmax(scores, allowed[...] > 0, HEAD_WIDTH)):
        context[:, lanes] = dot32(prob, value).astype(jnp.bfloat16)
    dealt = dot32(deal[...], context[...]).astype(jnp.bfloat16)
    rows = outs[0].shape[0]
    step = weight.shape[1] // 8
    for start in range(0, weight.shape[1], step):
        result = dot32(dealt, weight[:, start : start + step])
        for index, out in enumerate(outs):
            piece = result[index * rows : (index + 1) * rows]
            out[:, start : start + step] = piece.astype(jnp.bfloat16)


def add_ring(info, own, left, right, opposite, kept, *sent):
    rows = kept.shape[0]
    step = 1024
    for start in range(0, own.shape[1], step):
        lanes = slice(start, start + step)
        total = own[:, lanes].astype(jnp.float32)
        for block in (left, right, opposite):
            total = total + block[:, lanes].astype(jnp.float32)
        kept[:, lanes] = total[:rows]
        for index, out in enumerate(sent):
            piece = total[(index + 1) * rows : (index + 2) * rows]
            out[:, lanes] = piece.astype(jnp.bfloat16)


def finish(info, kept, left, right, opposite, *refs):
    own, out = refs[:-1], refs[-1]
    rows, cols = own[0].shape[1:]
    live = info[18] + lax.broadcasted_iota(jnp.int32, (rows, cols), 0) < info[21]
    for at, block in enumerate(own):
        for step in range(SIDE):
            lanes = pl.ds(pl.multiple_of(info[SIDE * at + step] * cols, cols), cols)
            total = kept[:, lanes] + block[step].astype(jnp.float32)
            for term in (left, right, opposite):
                total = total + term[:, lanes].astype(jnp.float32)
            out[:, lanes] = jnp.where(live, total, 0.0).astype(jnp.bfloat16)


def visibility(masks, live_count):
    positions = jnp.arange(SPAN_LIMIT)
    passage = positions // CPP
    expanded = jnp.repeat(jnp.repeat(masks, CPP, axis=0), CPP, axis=1) > 0
    same_passage = passage[:, None] == passage[None, :]
    earlier = positions[None, :] <= positions[:, None]
    key_live = positions[None, :] < live_count
    diagonal = positions[:, None] == positions[None, :]
    return diagonal | earlier & key_live & (same_passage | expanded)


def local(
    span_tokens,
    enc_dest,
    passages,
    req_slot,
    block_mask,
    enc_qkv,
    enc_out,
    enc_up,
    enc_down,
    proj_in,
    proj_out,
    norm_gain,
    q_weight,
    key_value_weight,
    out_weight,
):
    tensor_count = lax.axis_size("tensor")
    seq_count = lax.axis_size("seq")
    tensor_index = lax.axis_index("tensor")
    seq_index = lax.axis_index("seq")
    core = seq_index % 2
    device_count = tensor_count * seq_count
    rows = SPAN_LIMIT
    own_rows = rows // tensor_count
    spans, span_size, width = span_tokens.shape
    model_width = proj_out.shape[1]
    share = enc_qkv.shape[0]
    x_index, y_index = tensor_index // SIDE, tensor_index % SIDE

    steps = jnp.array([0, SIDE - 1, 1, 2])
    outer, inside = jnp.repeat(steps, SIDE), jnp.tile(steps, SIDE)
    by_x = SIDE * ((x_index + outer) % SIDE) + (y_index + inside) % SIDE
    by_y = SIDE * ((x_index + inside) % SIDE) + (y_index + outer) % SIDE
    shards = jnp.where(core == 0, by_x, by_y)
    near = jnp.where(core == 0, y_index, x_index)
    far = jnp.where(core == 0, x_index, y_index)
    scalars = jnp.stack([core, tensor_index % 2, tensor_index * own_rows, near, far])
    other_shards = jnp.where(core == 0, by_y, by_x)
    info = jnp.concatenate([shards, scalars, core[None], other_shards]).astype(jnp.int32)

    ahead = jnp.array([0, 1, SIDE - 1, 2])
    outer, inside = jnp.repeat(ahead, SIDE), jnp.tile(ahead, SIDE)
    owner_x = SIDE * ((x_index + outer) % SIDE) + (y_index + inside) % SIDE
    owner_y = SIDE * ((x_index + inside) % SIDE) + (y_index + outer) % SIDE
    owners = jnp.where(core == 0, owner_x, owner_y)
    from_row = (owners[:, None] * own_rows + jnp.arange(own_rows)[None, :]).reshape(-1)
    deal = (from_row[:, None] == jnp.arange(rows)[None, :]).astype(jnp.bfloat16)

    requests = jnp.arange(req_slot.shape[0])
    dest_slot = jnp.sum(
        jnp.where(enc_dest[:, None] // SPAN_LIMIT == requests[None, :], req_slot[None, :], 0), axis=1
    ).reshape(device_count, own_rows)
    dest_place = (enc_dest % SPAN_LIMIT).reshape(device_count, own_rows)
    own_slots = lax.dynamic_slice_in_dim(
        dest_slot, seq_index * tensor_count + tensor_index, 1, 0
    )
    pick = (jnp.arange(seq_count)[:, None] == own_slots).astype(jnp.bfloat16)
    place_of = jnp.sum(jnp.where(dest_slot == seq_index, dest_place, 0), axis=1)
    order = (jnp.arange(rows)[:, None] == place_of[None, :]).astype(jnp.bfloat16)
    chosen = jnp.sum(jnp.where(req_slot == seq_index, requests, 0))
    live_count = jnp.sum(jnp.where(requests == chosen, passages, 0)) * CPP
    masks = jnp.sum(
        jnp.where(requests[:, None, None] == chosen, block_mask, 0), axis=0
    )
    allowed = visibility(masks, live_count).astype(jnp.float32)
    live_info = jnp.concatenate([info[:21], live_count[None]]).astype(jnp.int32)

    positions = jnp.arange(rows).astype(jnp.float32)
    lane = jnp.arange(HEAD_WIDTH)
    frequency = jnp.exp(
        -(2.0 * (lane // 2).astype(jnp.float32) / HEAD_WIDTH) * math.log(500000.0)
    )
    angles = positions[:, None] * frequency[None, :]
    cosine, sine = jnp.cos(angles), jnp.sin(angles)
    swap = jnp.where(
        (lane[:, None] ^ 1) == lane[None, :], jnp.where(lane[None, :] % 2 == 0, -1.0, 1.0), 0.0
    ).astype(jnp.float32)

    own_tokens = span_tokens.reshape(spans * span_size, width)
    other_tokens = to_core(own_tokens)
    token_pieces = whole_call(
        both_rows,
        "both_rows",
        info,
        [own_tokens, other_tokens],
        shape_of((tensor_count, 2 * spans * span_size, share)),
    )
    units = enc_down.shape[0] // 2
    middle_cols = width // 2 + units * tensor_count
    share_cols = model_width // tensor_count
    half_cols = share_cols // 2
    rest_shape = shape_of((share, middle_cols + width + SIDE * half_cols))
    dealt_shape = shape_of((share, SIDE * half_cols))
    own_qkv = whole_call(
        take_qkv, "take_qkv", info, [enc_qkv], shape_of((share, 3 * width // 2)), limit=4
    )
    rest_up, rest_down, kept_cols, beyond_cols = whole_call(
        take_rest,
        "take_rest",
        info,
        [enc_out, enc_up, enc_down, proj_out],
        (rest_shape, rest_shape, dealt_shape, dealt_shape),
        limit=60,
        after=[own_qkv],
    )
    qkv_ring = short_ring(own_qkv)
    rest_left = to_ring(rest_up, 1, 1)
    rest_ring = [rest_up, rest_left, to_ring(rest_down, 1, -1), to_ring(rest_left, 1, 1)]
    beyond_cols = to_ring(beyond_cols, 1, 2)
    qkv_block = whole_call(
        join_blocks,
        "join_qkv",
        info,
        qkv_ring,
        shape_of((SIDE, share, 3 * width // 2)),
        limit=6,
    )
    all_rows = 2 * spans * span_size

    qkv_right = to_ring(qkv_block, 2, -1)
    qkv = [qkv_block, to_ring(qkv_block, 2, 1), qkv_right, to_ring(qkv_right, 2, -1)]
    middle_block = whole_call(
        join_middle,
        "join_middle",
        info,
        rest_ring,
        shape_of((SIDE, share, middle_cols)),
        limit=8,
        after=[*qkv[1:3], token_pieces],
    )
    left = to_ring(middle_block, 2, 1)
    middle = [middle_block, left, to_ring(middle_block, 2, -1), to_ring(left, 2, 1)]
    context = whole_call(
        span_attention,
        "span_attention",
        info,
        [token_pieces, *qkv],
        shape_of((tensor_count // 2, all_rows, share)),
        [pltpu.VMEM((all_rows, 3 * width // 2), jnp.bfloat16)],
        flops=2 * all_rows * width * 3 * width // 2,
    )
    lower_shape = shape_of((SIDE, share, width + half_cols))
    far_shape = shape_of((SIDE, share, half_cols))
    lower_up, lower_down, far_kept, far_beyond = whole_call(
        join_lower,
        "join_lower",
        info,
        [*rest_ring, kept_cols, beyond_cols],
        (lower_shape, lower_shape, far_shape, far_shape),
        limit=8,
        after=[context],
    )
    lower_left = to_ring(lower_up, 2, 1)
    lower = [lower_up, lower_left, to_ring(lower_down, 2, -1), to_ring(lower_left, 2, 1)]
    far_beyond = to_ring(far_beyond, 2, 2)
    attended = whole_call(
        context_out,
        "context_out",
        info,
        [context, to_core(context), token_pieces, *middle],
        shape_of((all_rows, width // 2)),
        [pltpu.VMEM((tensor_count, all_rows, share), jnp.bfloat16)],
        flops=2 * all_rows * width * width // 2,
    )
    first_out, inner = whole_call(
        norm_up,
        "norm_up",
        info,
        [attended, to_core(attended), *middle],
        (shape_of((all_rows, width)), shape_of((tensor_count, all_rows, units))),
        [pltpu.VMEM((tensor_count, all_rows, share), jnp.bfloat16)],
        flops=2 * all_rows * width * width,
    )
    kept, sent = whole_call(
        down,
        "down",
        info,
        [inner, first_out, *lower],
        (
            shape_of((all_rows // 2, width), jnp.float32),
            shape_of((all_rows // 2, width)),
        ),
        [pltpu.VMEM((all_rows, width), jnp.float32)],
        flops=2 * all_rows * width * width,
        after=[far_beyond],
    )
    outgoing = whole_call(
        norm_pool,
        "norm_pool",
        info,
        [kept, to_core(sent), pick],
        shape_of((seq_count, tensor_count, width // 128, 128)),
        [pltpu.VMEM((seq_count, width // 128, 128), jnp.float32)],
    )
    arrived = lax.all_to_all(
        outgoing.reshape(device_count, width // 128, 128), AXES, 0, 0
    )

    proj_mine = whole_call(
        join_proj,
        "join_proj",
        info,
        [far_kept, lower[1], lower[2], far_beyond],
        shape_of((SIDE, SIDE, share, half_cols)),
        limit=8,
        after=[outgoing],
    )
    proj_other = to_core(proj_mine)
    own_cols = whole_call(
        embed,
        "embed",
        info,
        [arrived, order, proj_in, proj_mine, proj_other],
        shape_of((rows, share_cols)),
        [
            pltpu.VMEM((device_count, width // 128, 128), jnp.float32),
            pltpu.VMEM((tensor_count, rows, proj_out.shape[0]), jnp.bfloat16),
        ],
        flops=2 * rows * width * (width + share_cols),
    )
    first_block = whole_call(
        join_blocks,
        "join_columns",
        info,
        short_ring(own_cols),
        shape_of((SIDE, rows, share_cols)),
        limit=4,
    )
    near_left = to_ring(first_block, 2, 1)
    near_right = to_ring(first_block, 2, -1)
    query_cols = q_weight.shape[1]
    kv_cols = key_value_weight.shape[2]
    key_start = tensor_index * kv_cols % HEAD_WIDTH
    key_cosine = lax.dynamic_slice_in_dim(cosine, key_start, kv_cols, 1)
    key_sine = lax.dynamic_slice_in_dim(sine, key_start, kv_cols, 1)
    gain = norm_gain.reshape(tensor_count, 1, share_cols)
    kv_pair = key_value_weight.transpose(0, 2, 1).reshape(2 * kv_cols, model_width)
    sums = (
        shape_of((rows, query_cols), jnp.float32),
        shape_of((rows, 2 * kv_cols), jnp.float32),
        shape_of((rows, 1), jnp.float32),
    )
    block_flops = 2 * rows * model_width // SIDE * (query_cols + 2 * kv_cols)
    totals = whole_call(
        functools.partial(project, starts=(0,), count=1),
        "project_own",
        info,
        [first_block, gain, q_weight, kv_pair],
        sums,
        flops=block_flops,
    )
    embedded = [first_block, near_left, near_right, to_ring(near_left, 2, 1)]
    totals = whole_call(
        functools.partial(project, starts=(1, 2), count=2),
        "project_near",
        info,
        [embedded[1], embedded[2], gain, q_weight, kv_pair, *totals],
        sums,
        flops=2 * block_flops,
    )
    own_kv, scale = whole_call(
        last_keys,
        "last_keys",
        info,
        [
            embedded[3],
            gain,
            kv_pair,
            totals[1],
            totals[2],
            key_cosine,
            key_sine,
            swap[:kv_cols, :kv_cols],
        ],
        (shape_of((2, rows, kv_cols)), shape_of((rows, 1), jnp.float32)),
    )
    partner_kv = lax.ppermute(
        own_kv, "tensor", [(index, index ^ 1) for index in range(tensor_count)]
    )
    query = whole_call(
        last_queries,
        "last_queries",
        info,
        [embedded[3], gain, q_weight, totals[0], scale, cosine, sine, swap],
        shape_of((rows, query_cols)),
        flops=block_flops,
    )
    partial = whole_call(
        attend_out,
        "attend_out",
        info,
        [query, own_kv, partner_kv, allowed, deal, out_weight],
        (shape_of((rows // SIDE, model_width)),) * 4,
        [pltpu.VMEM((rows, query_cols), jnp.bfloat16)],
        flops=2 * rows * model_width * query_cols,
    )
    arrived_sums = [
        to_ring(part, 2, distance) for part, distance in zip(partial[1:], (1, -1, 2))
    ]
    kept_sum, *sent_sums = whole_call(
        add_ring,
        "add_ring",
        info,
        [partial[0], *arrived_sums],
        (shape_of((own_rows, model_width), jnp.float32),)
        + (shape_of((own_rows, model_width)),) * 3,
    )
    terms = [to_ring(part, 1, distance) for part, distance in zip(sent_sums, (1, -1, 2))]
    own_embedded = [
        lax.dynamic_slice_in_dim(block, tensor_index * own_rows, own_rows, 1) for block in embedded
    ]
    return whole_call(
        finish,
        "finish",
        live_info,
        [kept_sum, *terms, *own_embedded],
        shape_of((own_rows, model_width)),
    )


def solution(mesh):
    return jax.shard_map(
        local,
        mesh=mesh,
        in_specs=(
            P(("seq", "tensor"), None, None),
            P(),
            P(),
            P(),
            P(),
            P("tensor", None),
            P("tensor", None),
            P("tensor", None),
            P("tensor", None),
            P(),
            P("tensor", None),
            P(),
            P(None, "tensor"),
            P(None, None, "tensor"),
            P("tensor", None),
        ),
        out_specs=P(("seq", "tensor"), None),
        check_vma=False,
    )
```

```python
import functools
import math

import jax
import jax.numpy as jnp
from jax import lax
from jax.experimental import pallas as pl
from jax.experimental.pallas import tpu as pltpu
from jax.sharding import PartitionSpec as P

QUERY_HEAD_COUNT = 64
KEY_VALUE_HEADS = 8
HEAD_WIDTH = 128
EH = 16
CPP = 16
SPAN_LIMIT = 128
SIDE = 4
AXES = ("seq", "tensor")


def device_id(plane, core, x, y):
    return ((plane * 2 + core) * SIDE + x) * SIDE + y


def every_device():
    return [
        (plane, core, x, y)
        for plane in range(SIDE)
        for core in range(2)
        for x in range(SIDE)
        for y in range(SIDE)
    ]


def first_axis_is_y(core, phase):
    return (core == 0) == (phase == 1)


def ring_pairs(phase, distance):
    pairs = []
    for plane, core, x, y in every_device():
        if first_axis_is_y(core, phase):
            target = device_id(plane, core, x, (y + distance) % SIDE)
        else:
            target = device_id(plane, core, (x + distance) % SIDE, y)
        pairs.append((device_id(plane, core, x, y), target))
    return pairs


def ring_groups(phase):
    groups = []
    for plane in range(SIDE):
        for core in range(2):
            for fixed in range(SIDE):
                groups.append(
                    [
                        device_id(plane, core, fixed, moving)
                        if first_axis_is_y(core, phase)
                        else device_id(plane, core, moving, fixed)
                        for moving in range(SIDE)
                    ]
                )
    return groups


def to_ring(value, phase, distance):
    return lax.ppermute(value, AXES, ring_pairs(phase, distance))


def to_core(value):
    return lax.ppermute(value, "seq", [(index, index ^ 1) for index in range(8)])


def short_ring(block):
    return [block] + [to_ring(block, 1, distance) for distance in (1, -1, 2)]


def short_relay(block):
    left = to_ring(block, 1, 1)
    right = to_ring(block, 1, -1)
    return [block, left, right, to_ring(right, 1, -1)]


VMEM = pl.BlockSpec(memory_space=pltpu.VMEM)
SMEM = pl.BlockSpec(memory_space=pltpu.SMEM)
ANYWHERE = pl.BlockSpec(memory_space=pl.ANY)
MIB = 2**20


def shape_of(shape, dtype=jnp.bfloat16):
    return jax.ShapeDtypeStruct(shape, dtype)


def whole_call(body, name, info, arrays, outs, scratch=(), limit=12, flops=0, far=(), after=()):
    count = len(arrays) + len(far)

    def run(*refs):
        body(*refs[: 1 + count], *refs[1 + count + len(after) :])

    moved = sum(array.size * array.dtype.itemsize for array in arrays)
    return pl.pallas_call(
        run,
        name=name,
        out_shape=outs,
        in_specs=[SMEM] + [VMEM] * len(arrays) + [ANYWHERE] * (len(far) + len(after)),
        out_specs=jax.tree.map(lambda _: VMEM, outs),
        scratch_shapes=list(scratch),
        compiler_params=pltpu.CompilerParams(vmem_limit_bytes=limit * MIB),
        cost_estimate=pl.CostEstimate(flops=flops, bytes_accessed=moved, transcendentals=0),
    )(info, *arrays, *far, *after)


def dot32(left, right):
    return jnp.dot(left, right, preferred_element_type=jnp.float32)


def dot_last(left, right):
    return lax.dot_general(
        left, right, (((1,), (1,)), ((), ())), preferred_element_type=jnp.float32
    )


def gelu_exact(values):
    return 0.5 * values * (1.0 + lax.erf(values * (0.5**0.5)))


def take_qkv(info, weight, out):
    cols = weight.shape[1] // 6
    for part in range(3):
        start = pl.multiple_of((2 * part + info[16]) * cols, cols)
        out[:, part * cols : (part + 1) * cols] = weight[:, pl.ds(start, cols)]


def take_rest(info, out_weight, up_weight, down_weight, proj, up_out, down_out, kept, beyond):
    core, near = info[16], info[19]
    rows, width = out_weight.shape
    cols = width // 2
    units = down_weight.shape[0] // 2
    pieces = [out_weight[:, pl.ds(pl.multiple_of(core * cols, cols), cols)]]
    for pair in range(up_weight.shape[1] // (4 * units)):
        halves = []
        for step in range(2):
            low = (2 * pair + step) * 2 * units
            halves.append(
                jnp.where(
                    core == 0,
                    up_weight[:, low : low + units].astype(jnp.float32),
                    up_weight[:, low + units : low + 2 * units].astype(jnp.float32),
                )
            )
        pieces.append(jnp.concatenate(halves, axis=1).astype(jnp.bfloat16))
    pieces.append(down_weight[pl.ds(pl.multiple_of(core * units, units), units), :])
    at = 0
    for piece in pieces:
        for out in (up_out, down_out):
            out[:, at : at + piece.shape[1]] = piece
        at += piece.shape[1]
    block = kept.shape[1] // SIDE
    for out, start, distance in ((kept, 0, 0), (up_out, at, 1), (down_out, at, SIDE - 1), (beyond, 0, 2)):
        target = lax.rem(near + distance, SIDE)
        for index in range(SIDE):
            shard = jnp.where(core == 0, SIDE * index + target, SIDE * target + index)
            source = pl.multiple_of((2 * shard + core) * block, block)
            out[:, start + index * block : start + (index + 1) * block] = proj[:, pl.ds(source, block)]


def join_blocks(info, own, left, right, opposite, out):
    for index, block in enumerate((own, left, right, opposite)):
        out[index] = block[...]


def join_middle(info, own, left, right, opposite, out):
    for index, block in enumerate((own, left, right, opposite)):
        out[index] = block[:, : out.shape[2]]


def join_lower(info, own, left, right, opposite, kept, beyond, up_out, down_out, far_kept, far_beyond):
    far = info[20]
    block = far_kept.shape[2]
    width = up_out.shape[2] - block
    start = own.shape[1] - kept.shape[1] - width
    for index, part in enumerate((own, left, right, opposite)):
        for out in (up_out, down_out):
            out[index, :, :width] = part[:, start : start + width]
        columns, first = (part, start + width) if index in (1, 2) else (kept, 0)
        if index == 3:
            columns = beyond
        for out, at, distance in (
            (far_kept, 0, 0),
            (up_out, width, 1),
            (down_out, width, SIDE - 1),
            (far_beyond, 0, 2),
        ):
            target = lax.rem(far + distance, SIDE)
            source = pl.multiple_of(first + target * block, 128)
            out[index, :, at : at + block] = columns[:, pl.ds(source, block)]


def join_proj(info, own, left, right, opposite, out):
    block = own.shape[2]
    for index, part in enumerate((own, left, right, opposite)):
        out[index] = part[:, :, part.shape[2] - block :]


def both_rows(info, mine, other, pieces_out):
    half, width = mine.shape
    core = info[16]
    piece = pieces_out.shape[2]
    near = pl.ds(pl.multiple_of(core * half, half), half)
    far = pl.ds(pl.multiple_of((1 - core) * half, half), half)
    for index in range(width // piece):
        pieces_out[index, near, :] = mine[:, index * piece : (index + 1) * piece]
        pieces_out[index, far, :] = other[:, index * piece : (index + 1) * piece]


def ring_dot(info, pieces, blocks, low, high):
    total = None
    for at, block in enumerate(blocks):
        act = jnp.concatenate([pieces[info[4 * at + step]] for step in range(SIDE)], axis=1)
        weight = block[:, :, low:high].reshape(act.shape[1], high - low)
        part = dot32(act, weight)
        total = part if total is None else total + part
    return total


def masked_softmax(scores, seen, size):
    scores = [jnp.where(seen, score / math.sqrt(size), -1e30) for score in scores]
    tops = [jnp.max(score, axis=1, keepdims=True) for score in scores]
    powers = [jnp.exp(score - top) for score, top in zip(scores, tops)]
    sums = [jnp.sum(power, axis=1, keepdims=True) for power in powers]
    return [(power / total).astype(jnp.bfloat16) for power, total in zip(powers, sums)]


def span_attention(info, pieces, w0, w1, w2, w3, context, mixed):
    cols = w0.shape[2]
    third = cols // 3
    mixed[...] = ring_dot(info, pieces, (w0, w1, w2, w3), 0, cols).astype(jnp.bfloat16)
    size = context.shape[2]
    half = mixed.shape[0] // 2
    span = 16
    row = lax.broadcasted_iota(jnp.int32, (half, half), 0) // span
    col = lax.broadcasted_iota(jnp.int32, (half, half), 1) // span
    same = row == col
    heads = third // size
    units = [
        (head, slice(part * half, (part + 1) * half)) for head in range(heads) for part in range(2)
    ]
    scores = [
        lax.dot_general(
            mixed[rows, head * size : (head + 1) * size],
            mixed[rows, third + head * size : third + (head + 1) * size],
            (((1,), (1,)), ((), ())),
            preferred_element_type=jnp.float32,
        )
        for head, rows in units
    ]
    probs = masked_softmax(scores, same, size)
    for (head, rows), prob in zip(units, probs):
        value = mixed[rows, 2 * third + head * size : 2 * third + (head + 1) * size]
        context[head, rows, :] = dot32(prob, value).astype(jnp.bfloat16)


def context_out(info, mine, other, tokens, w0, w1, w2, w3, attended, pieces):
    heads = mine.shape[0]
    core = info[16]
    pieces[pl.ds(core * heads, heads)] = mine[...]
    pieces[pl.ds((1 - core) * heads, heads)] = other[...]
    cols = attended.shape[1]
    residual = jnp.concatenate([tokens[core * heads + index] for index in range(heads)], axis=1)
    total = ring_dot(info, pieces, (w0, w1, w2, w3), 0, cols)
    attended[...] = (residual.astype(jnp.float32) + total).astype(jnp.bfloat16)


def norm_up(info, mine, other, w0, w1, w2, w3, first_out, inner, pieces):
    core = info[16]
    cols = mine.shape[1]
    width = 2 * cols
    near = mine[...].astype(jnp.float32)
    far = other[...].astype(jnp.float32)
    low = jnp.where(core == 0, near, far)
    high = jnp.where(core == 0, far, near)
    mean = (jnp.sum(low, 1, keepdims=True) + jnp.sum(high, 1, keepdims=True)) / width
    low, high = low - mean, high - mean
    var = (jnp.sum(low * low, 1, keepdims=True) + jnp.sum(high * high, 1, keepdims=True)) / width
    scale = lax.rsqrt(var + 1e-05)
    first_out[:, :cols] = (low * scale).astype(jnp.bfloat16)
    first_out[:, cols:] = (high * scale).astype(jnp.bfloat16)
    size = pieces.shape[2]
    for index in range(pieces.shape[0]):
        pieces[index] = first_out[:, index * size : (index + 1) * size]
    total = ring_dot(info, pieces, (w0, w1, w2, w3), cols, w0.shape[2])
    act = gelu_exact(total).astype(jnp.bfloat16)
    unit = inner.shape[2]
    for index in range(inner.shape[0]):
        inner[index] = act[:, index * unit : (index + 1) * unit]


def down(info, inner, first_out, w0, w1, w2, w3, kept, sent, total):
    core = info[16]
    total[...] = ring_dot(info, inner, (w0, w1, w2, w3), 0, total.shape[1])
    half = kept.shape[0]
    rows = pl.ds(pl.multiple_of(core * half, half), half)
    kept[...] = total[rows, :] + first_out[rows, :].astype(jnp.float32)
    sent[...] = total[pl.ds(pl.multiple_of((1 - core) * half, half), half), :].astype(jnp.bfloat16)


def norm_pool(info, kept, arrived, pick, out, lanes):
    half, width = kept.shape
    values = kept[...] + arrived[...].astype(jnp.float32)
    mean = jnp.mean(values, axis=1, keepdims=True)
    values = values - mean
    values = values * lax.rsqrt(jnp.mean(values * values, axis=1, keepdims=True) + 1e-05)
    spans = pick.shape[1]
    pooled = jnp.mean(values.reshape(spans, half // spans, width), axis=1).astype(jnp.bfloat16)
    by_slot = dot32(pick[...], pooled)
    for index in range(width // 128):
        lanes[:, index, :] = by_slot[:, index * 128 : (index + 1) * 128]
    out[...] = jnp.broadcast_to(lanes[...].astype(jnp.bfloat16)[:, None], out.shape)


def embed(info, arrived, order, proj_in, mine, other, out, lanes, pieces):
    core = info[16]
    lanes[...] = arrived[...].astype(jnp.float32)
    columns = [
        dot32(order[...], lanes[:, index, :].astype(jnp.bfloat16)).astype(jnp.bfloat16)
        for index in range(lanes.shape[1])
    ]
    arranged = jnp.concatenate(columns, axis=1)
    hidden = gelu_exact(dot32(arranged, proj_in[...])).astype(jnp.bfloat16)
    units, cols = mine.shape[2:]
    for index in range(pieces.shape[0]):
        pieces[index] = hidden[:, index * units : (index + 1) * units]
    near, far = None, None
    for at in range(SIDE):
        act = jnp.concatenate([pieces[info[SIDE * at + step]] for step in range(SIDE)], axis=1)
        term = dot32(act, mine[at].reshape(SIDE * units, cols))
        near = term if near is None else near + term
        act = jnp.concatenate([pieces[info[22 + SIDE * at + step]] for step in range(SIDE)], axis=1)
        term = dot32(act, other[at].reshape(SIDE * units, cols))
        far = term if far is None else far + term
    out[:, :cols] = jnp.where(core == 0, near, far).astype(jnp.bfloat16)
    out[:, cols:] = jnp.where(core == 0, far, near).astype(jnp.bfloat16)


def project(info, *refs, starts, count):
    blocks, refs = refs[:count], refs[count:]
    gain, q_weight, kv_weight = refs[:3]
    before = refs[3:6] if len(refs) > 6 else None
    q_total, kv_total, square = refs[-3:]
    depth = blocks[0].shape[2]
    queries, both = None, None
    squares = None
    for at, block in zip(starts, blocks):
        for step in range(SIDE):
            shard = info[SIDE * at + step]
            wide = block[step].astype(jnp.float32)
            act = (wide * gain[shard]).astype(jnp.bfloat16)
            span = pl.ds(pl.multiple_of(shard * depth, depth), depth)
            q_term = dot32(act, q_weight[span, :])
            kv_term = dot_last(act, kv_weight[:, span])
            term = jnp.sum(wide * wide, axis=1, keepdims=True)
            queries = q_term if queries is None else queries + q_term
            both = kv_term if both is None else both + kv_term
            squares = term if squares is None else squares + term
    if before is not None:
        queries, both, squares = queries + before[0][...], both + before[1][...], squares + before[2][...]
    q_total[...] = queries
    kv_total[...] = both
    square[...] = squares


def turn(values, cosine, sine, swap):
    turned = jnp.dot(
        values, swap, preferred_element_type=jnp.float32, precision=lax.Precision.HIGHEST
    )
    return values * cosine + turned * sine


def last_keys(info, block, gain, kv_weight, kv_before, sq_before, cosine, sine, swap, out, scale):
    depth = block.shape[2]
    both = kv_before[...]
    squares = sq_before[...]
    for step in range(SIDE):
        shard = info[SIDE * 3 + step]
        wide = block[step].astype(jnp.float32)
        act = (wide * gain[shard]).astype(jnp.bfloat16)
        span = pl.ds(pl.multiple_of(shard * depth, depth), depth)
        both += dot_last(act, kv_weight[:, span])
        squares += jnp.sum(wide * wide, axis=1, keepdims=True)
    factor = lax.rsqrt(squares / (depth * SIDE * SIDE) + 1e-05)
    scale[...] = factor
    both = both * factor
    cols = out.shape[2]
    out[0] = turn(both[:, :cols], cosine[...], sine[...], swap[...]).astype(jnp.bfloat16)
    out[1] = both[:, cols:].astype(jnp.bfloat16)


def last_queries(info, block, gain, q_weight, q_before, scale, cosine, sine, swap, out):
    depth = block.shape[2]
    total = q_before[...]
    for step in range(SIDE):
        shard = info[SIDE * 3 + step]
        act = (block[step].astype(jnp.float32) * gain[shard]).astype(jnp.bfloat16)
        span = pl.ds(pl.multiple_of(shard * depth, depth), depth)
        total += dot32(act, q_weight[span, :])
    for head in range(out.shape[1] // HEAD_WIDTH):
        lanes = slice(head * HEAD_WIDTH, (head + 1) * HEAD_WIDTH)
        query = total[:, lanes] * scale[...]
        out[:, lanes] = turn(query, cosine[...], sine[...], swap[...]).astype(jnp.bfloat16)


def attend_out(info, query, mine, partner, allowed, deal, weight, *refs):
    outs, context = refs[:5], refs[5]
    odd = info[17] == 1
    own = mine[...].astype(jnp.float32)
    far = partner[...].astype(jnp.float32)
    low = jnp.where(odd, far, own)
    high = jnp.where(odd, own, far)
    both = jnp.concatenate([low, high], axis=2).astype(jnp.bfloat16)
    key, value = both[0], both[1]
    heads = [
        slice(head * HEAD_WIDTH, (head + 1) * HEAD_WIDTH)
        for head in range(query.shape[1] // HEAD_WIDTH)
    ]
    scores = [
        lax.dot_general(
            query[:, lanes], key, (((1,), (1,)), ((), ())), preferred_element_type=jnp.float32
        )
        for lanes in heads
    ]
    for lanes, prob in zip(heads, masked_softmax(scores, allowed[...] > 0, HEAD_WIDTH)):
        context[:, lanes] = dot32(prob, value).astype(jnp.bfloat16)
    dealt = dot32(deal[...], context[...]).astype(jnp.bfloat16)
    rows = outs[0].shape[0]
    step = weight.shape[1] // 8
    for start in range(0, weight.shape[1], step):
        result = dot32(dealt, weight[:, start : start + step])
        for index in range(SIDE):
            piece = result[index * rows : (index + 1) * rows].astype(jnp.bfloat16)
            out, at = outs[index], start
            if index == 3 and start >= out.shape[1]:
                out, at = outs[4], start - out.shape[1]
            out[:, at : at + step] = piece


def add_ring(info, own, left, right, far_low, far_high, kept, *sent):
    rows = kept.shape[0]
    step = 1024
    for start in range(0, own.shape[1], step):
        lanes = slice(start, start + step)
        total = own[:, lanes].astype(jnp.float32)
        for block in (left, right):
            total = total + block[:, lanes].astype(jnp.float32)
        far, at = (far_low, start)
        if start >= far_low.shape[1]:
            far, at = far_high, start - far_low.shape[1]
        total = total + far[:, at : at + step].astype(jnp.float32)
        kept[:, lanes] = total[:rows]
        for index, out in enumerate(sent):
            piece = total[(index + 1) * rows : (index + 2) * rows]
            out[:, lanes] = piece.astype(jnp.bfloat16)


def finish(info, kept, left, right, opposite, *refs):
    own, out = refs[:-1], refs[-1]
    rows, cols = own[0].shape[1:]
    live = info[18] + lax.broadcasted_iota(jnp.int32, (rows, cols), 0) < info[21]
    for at, block in enumerate(own):
        for step in range(SIDE):
            lanes = pl.ds(pl.multiple_of(info[SIDE * at + step] * cols, cols), cols)
            total = kept[:, lanes] + block[step].astype(jnp.float32)
            for term in (left, right, opposite):
                total = total + term[:, lanes].astype(jnp.float32)
            out[:, lanes] = jnp.where(live, total, 0.0).astype(jnp.bfloat16)


def visibility(masks, live_count):
    positions = jnp.arange(SPAN_LIMIT)
    passage = positions // CPP
    expanded = jnp.repeat(jnp.repeat(masks, CPP, axis=0), CPP, axis=1) > 0
    same_passage = passage[:, None] == passage[None, :]
    earlier = positions[None, :] <= positions[:, None]
    key_live = positions[None, :] < live_count
    diagonal = positions[:, None] == positions[None, :]
    return diagonal | earlier & key_live & (same_passage | expanded)


def local(
    span_tokens,
    enc_dest,
    passages,
    req_slot,
    block_mask,
    enc_qkv,
    enc_out,
    enc_up,
    enc_down,
    proj_in,
    proj_out,
    norm_gain,
    q_weight,
    key_value_weight,
    out_weight,
):
    tensor_count = lax.axis_size("tensor")
    seq_count = lax.axis_size("seq")
    tensor_index = lax.axis_index("tensor")
    seq_index = lax.axis_index("seq")
    core = seq_index % 2
    device_count = tensor_count * seq_count
    rows = SPAN_LIMIT
    own_rows = rows // tensor_count
    spans, span_size, width = span_tokens.shape
    model_width = proj_out.shape[1]
    share = enc_qkv.shape[0]
    x_index, y_index = tensor_index // SIDE, tensor_index % SIDE

    steps = jnp.array([0, SIDE - 1, 1, 2])
    outer, inside = jnp.repeat(steps, SIDE), jnp.tile(steps, SIDE)
    by_x = SIDE * ((x_index + outer) % SIDE) + (y_index + inside) % SIDE
    by_y = SIDE * ((x_index + inside) % SIDE) + (y_index + outer) % SIDE
    shards = jnp.where(core == 0, by_x, by_y)
    near = jnp.where(core == 0, y_index, x_index)
    far = jnp.where(core == 0, x_index, y_index)
    scalars = jnp.stack([core, tensor_index % 2, tensor_index * own_rows, near, far])
    other_shards = jnp.where(core == 0, by_y, by_x)
    info = jnp.concatenate([shards, scalars, core[None], other_shards]).astype(jnp.int32)

    ahead = jnp.array([0, 1, SIDE - 1, 2])
    outer, inside = jnp.repeat(ahead, SIDE), jnp.tile(ahead, SIDE)
    owner_x = SIDE * ((x_index + outer) % SIDE) + (y_index + inside) % SIDE
    owner_y = SIDE * ((x_index + inside) % SIDE) + (y_index + outer) % SIDE
    owners = jnp.where(core == 0, owner_x, owner_y)
    from_row = (owners[:, None] * own_rows + jnp.arange(own_rows)[None, :]).reshape(-1)
    deal = (from_row[:, None] == jnp.arange(rows)[None, :]).astype(jnp.bfloat16)

    requests = jnp.arange(req_slot.shape[0])
    dest_slot = jnp.sum(
        jnp.where(enc_dest[:, None] // SPAN_LIMIT == requests[None, :], req_slot[None, :], 0), axis=1
    ).reshape(device_count, own_rows)
    dest_place = (enc_dest % SPAN_LIMIT).reshape(device_count, own_rows)
    own_slots = lax.dynamic_slice_in_dim(
        dest_slot, seq_index * tensor_count + tensor_index, 1, 0
    )
    pick = (jnp.arange(seq_count)[:, None] == own_slots).astype(jnp.bfloat16)
    place_of = jnp.sum(jnp.where(dest_slot == seq_index, dest_place, 0), axis=1)
    order = (jnp.arange(rows)[:, None] == place_of[None, :]).astype(jnp.bfloat16)
    chosen = jnp.sum(jnp.where(req_slot == seq_index, requests, 0))
    live_count = jnp.sum(jnp.where(requests == chosen, passages, 0)) * CPP
    masks = jnp.sum(
        jnp.where(requests[:, None, None] == chosen, block_mask, 0), axis=0
    )
    allowed = visibility(masks, live_count).astype(jnp.float32)
    live_info = jnp.concatenate([info[:21], live_count[None]]).astype(jnp.int32)

    positions = jnp.arange(rows).astype(jnp.float32)
    lane = jnp.arange(HEAD_WIDTH)
    frequency = jnp.exp(
        -(2.0 * (lane // 2).astype(jnp.float32) / HEAD_WIDTH) * math.log(500000.0)
    )
    angles = positions[:, None] * frequency[None, :]
    cosine, sine = jnp.cos(angles), jnp.sin(angles)
    swap = jnp.where(
        (lane[:, None] ^ 1) == lane[None, :], jnp.where(lane[None, :] % 2 == 0, -1.0, 1.0), 0.0
    ).astype(jnp.float32)

    own_tokens = span_tokens.reshape(spans * span_size, width)
    other_tokens = to_core(own_tokens)
    token_pieces = whole_call(
        both_rows,
        "both_rows",
        info,
        [own_tokens, other_tokens],
        shape_of((tensor_count, 2 * spans * span_size, share)),
    )
    units = enc_down.shape[0] // 2
    middle_cols = width // 2 + units * tensor_count
    share_cols = model_width // tensor_count
    half_cols = share_cols // 2
    rest_shape = shape_of((share, middle_cols + width + SIDE * half_cols))
    dealt_shape = shape_of((share, SIDE * half_cols))
    own_qkv = whole_call(
        take_qkv, "take_qkv", info, [enc_qkv], shape_of((share, 3 * width // 2)), limit=4
    )
    rest_up, rest_down, kept_cols, beyond_cols = whole_call(
        take_rest,
        "take_rest",
        info,
        [enc_out, enc_up, enc_down, proj_out],
        (rest_shape, rest_shape, dealt_shape, dealt_shape),
        limit=60,
        after=[own_qkv],
    )
    qkv_ring = short_ring(own_qkv)
    rest_left = to_ring(rest_up, 1, 1)
    rest_ring = [rest_up, rest_left, to_ring(rest_down, 1, -1), to_ring(rest_left, 1, 1)]
    beyond_cols = to_ring(beyond_cols, 1, 2)
    qkv_block = whole_call(
        join_blocks,
        "join_qkv",
        info,
        qkv_ring,
        shape_of((SIDE, share, 3 * width // 2)),
        limit=6,
    )
    all_rows = 2 * spans * span_size

    qkv_right = to_ring(qkv_block, 2, -1)
    qkv = [qkv_block, to_ring(qkv_block, 2, 1), qkv_right, to_ring(qkv_right, 2, -1)]
    middle_block = whole_call(
        join_middle,
        "join_middle",
        info,
        rest_ring,
        shape_of((SIDE, share, middle_cols)),
        limit=8,
        after=[*qkv[1:3], token_pieces],
    )
    left = to_ring(middle_block, 2, 1)
    middle = [middle_block, left, to_ring(middle_block, 2, -1), to_ring(left, 2, 1)]
    context = whole_call(
        span_attention,
        "span_attention",
        info,
        [token_pieces, *qkv],
        shape_of((tensor_count // 2, all_rows, share)),
        [pltpu.VMEM((all_rows, 3 * width // 2), jnp.bfloat16)],
        flops=2 * all_rows * width * 3 * width // 2,
    )
    lower_shape = shape_of((SIDE, share, width + half_cols))
    far_shape = shape_of((SIDE, share, half_cols))
    lower_up, lower_down, far_kept, far_beyond = whole_call(
        join_lower,
        "join_lower",
        info,
        [*rest_ring, kept_cols, beyond_cols],
        (lower_shape, lower_shape, far_shape, far_shape),
        limit=8,
        after=[context],
    )
    lower_left = to_ring(lower_up, 2, 1)
    lower = [lower_up, lower_left, to_ring(lower_down, 2, -1), to_ring(lower_left, 2, 1)]
    far_beyond = to_ring(far_beyond, 2, 2)
    attended = whole_call(
        context_out,
        "context_out",
        info,
        [context, to_core(context), token_pieces, *middle],
        shape_of((all_rows, width // 2)),
        [pltpu.VMEM((tensor_count, all_rows, share), jnp.bfloat16)],
        flops=2 * all_rows * width * width // 2,
    )
    first_out, inner = whole_call(
        norm_up,
        "norm_up",
        info,
        [attended, to_core(attended), *middle],
        (shape_of((all_rows, width)), shape_of((tensor_count, all_rows, units))),
        [pltpu.VMEM((tensor_count, all_rows, share), jnp.bfloat16)],
        flops=2 * all_rows * width * width,
    )
    kept, sent = whole_call(
        down,
        "down",
        info,
        [inner, first_out, *lower],
        (
            shape_of((all_rows // 2, width), jnp.float32),
            shape_of((all_rows // 2, width)),
        ),
        [pltpu.VMEM((all_rows, width), jnp.float32)],
        flops=2 * all_rows * width * width,
    )
    outgoing = whole_call(
        norm_pool,
        "norm_pool",
        info,
        [kept, to_core(sent), pick],
        shape_of((seq_count, tensor_count, width // 128, 128)),
        [pltpu.VMEM((seq_count, width // 128, 128), jnp.float32)],
    )
    arrived = lax.all_to_all(
        outgoing.reshape(device_count, width // 128, 128), AXES, 0, 0
    )

    proj_mine = whole_call(
        join_proj,
        "join_proj",
        info,
        [far_kept, lower[1], lower[2], far_beyond],
        shape_of((SIDE, SIDE, share, half_cols)),
        limit=8,
        after=[outgoing],
    )
    proj_other = to_core(proj_mine)
    own_cols = whole_call(
        embed,
        "embed",
        info,
        [arrived, order, proj_in, proj_mine, proj_other],
        shape_of((rows, share_cols)),
        [
            pltpu.VMEM((device_count, width // 128, 128), jnp.float32),
            pltpu.VMEM((tensor_count, rows, proj_out.shape[0]), jnp.bfloat16),
        ],
        flops=2 * rows * width * (width + share_cols),
    )
    first_block = whole_call(
        join_blocks,
        "join_columns",
        info,
        short_ring(own_cols),
        shape_of((SIDE, rows, share_cols)),
        limit=4,
    )
    near_left = to_ring(first_block, 2, 1)
    near_right = to_ring(first_block, 2, -1)
    query_cols = q_weight.shape[1]
    kv_cols = key_value_weight.shape[2]
    key_start = tensor_index * kv_cols % HEAD_WIDTH
    key_cosine = lax.dynamic_slice_in_dim(cosine, key_start, kv_cols, 1)
    key_sine = lax.dynamic_slice_in_dim(sine, key_start, kv_cols, 1)
    gain = norm_gain.reshape(tensor_count, 1, share_cols)
    kv_pair = key_value_weight.transpose(0, 2, 1).reshape(2 * kv_cols, model_width)
    sums = (
        shape_of((rows, query_cols), jnp.float32),
        shape_of((rows, 2 * kv_cols), jnp.float32),
        shape_of((rows, 1), jnp.float32),
    )
    block_flops = 2 * rows * model_width // SIDE * (query_cols + 2 * kv_cols)
    totals = whole_call(
        functools.partial(project, starts=(0,), count=1),
        "project_own",
        info,
        [first_block, gain, q_weight, kv_pair],
        sums,
        flops=block_flops,
    )
    embedded = [first_block, near_left, near_right, to_ring(near_left, 2, 1)]
    totals = whole_call(
        functools.partial(project, starts=(1, 2), count=2),
        "project_near",
        info,
        [embedded[1], embedded[2], gain, q_weight, kv_pair, *totals],
        sums,
        flops=2 * block_flops,
    )
    own_kv, scale = whole_call(
        last_keys,
        "last_keys",
        info,
        [
            embedded[3],
            gain,
            kv_pair,
            totals[1],
            totals[2],
            key_cosine,
            key_sine,
            swap[:kv_cols, :kv_cols],
        ],
        (shape_of((2, rows, kv_cols)), shape_of((rows, 1), jnp.float32)),
    )
    partner_kv = lax.ppermute(
        own_kv, "tensor", [(index, index ^ 1) for index in range(tensor_count)]
    )
    query = whole_call(
        last_queries,
        "last_queries",
        info,
        [embedded[3], gain, q_weight, totals[0], scale, cosine, sine, swap],
        shape_of((rows, query_cols)),
        flops=block_flops,
    )
    partial = whole_call(
        attend_out,
        "attend_out",
        info,
        [query, own_kv, partner_kv, allowed, deal, out_weight],
        (shape_of((rows // SIDE, model_width)),) * 3
        + (shape_of((rows // SIDE, model_width // 2)),) * 2,
        [pltpu.VMEM((rows, query_cols), jnp.bfloat16)],
        flops=2 * rows * model_width * query_cols,
    )
    passing = to_ring(partial[4], 2, -1)
    arrived_sums = [
        to_ring(part, 2, distance) for part, distance in zip(partial[1:4], (1, -1, 2))
    ] + [to_ring(passing, 2, -1)]
    kept_sum, *sent_sums = whole_call(
        add_ring,
        "add_ring",
        info,
        [partial[0], *arrived_sums],
        (shape_of((own_rows, model_width), jnp.float32),)
        + (shape_of((own_rows, model_width)),) * 3,
    )
    terms = [to_ring(part, 1, distance) for part, distance in zip(sent_sums, (1, -1, 2))]
    own_embedded = [
        lax.dynamic_slice_in_dim(block, tensor_index * own_rows, own_rows, 1) for block in embedded
    ]
    return whole_call(
        finish,
        "finish",
        live_info,
        [kept_sum, *terms, *own_embedded],
        shape_of((own_rows, model_width)),
    )


def solution(mesh):
    return jax.shard_map(
        local,
        mesh=mesh,
        in_specs=(
            P(("seq", "tensor"), None, None),
            P(),
            P(),
            P(),
            P(),
            P("tensor", None),
            P("tensor", None),
            P("tensor", None),
            P("tensor", None),
            P(),
            P("tensor", None),
            P(),
            P(None, "tensor"),
            P(None, None, "tensor"),
            P("tensor", None),
        ),
        out_specs=P(("seq", "tensor"), None),
        check_vma=False,
    )
```
